32 devices in a mesh: group: 2 (over y), patch: 4 (over z), visit: 2 (over x), band: 2 (over core).
Axes of the slice: x: 2, y: 2, z: 4, core: 2. Of those that a mesh axis runs over, the one named last changes fastest.
Arguments:
- template: bfloat16 [4096, 512], P(('group', 'patch')), parts along dimension 0, may hold values from -6 to 6
- science: bfloat16 [4096, 4, 512], P(('group', 'patch'), ('visit', 'band')), parts along dimension 0, may hold values from -6 to 6
- offsets: int32 [8, 4], P(('group', 'patch'), ('visit', 'band')), parts along dimension 0, may hold values from 0 to 496
- live_flags: int32 [8, 4], P(('group', 'patch'), ('visit', 'band')), parts along dimension 0, may hold values 0 or 1
- bank: bfloat16 [16, 31], replicated, may hold values from -1 to 1
- basis_index: int32 [8, 15, 2], P(('group', 'visit', 'band')), parts along dimension 0, may hold values from 0 to 15, as said below
- coeff: float32 [8, 15], P(('group', 'visit', 'band')), parts along dimension 0, may hold values from -4 to 4
- psf_profile: bfloat16 [31], replicated, may hold values from -1 to 1
Outputs:
- difference: bfloat16 [4096, 4, 512], P(('group', 'patch'), ('visit', 'band')), parts along dimension 0
- detection: float32 [4096, 512], P(('group', 'patch', 'visit', 'band')), parts along dimension 0
The draws below stay inside these ranges and needn't reach their ends.
There are 2 independent parts, one for each index of `group`. The reference program is written for one: setup_inputs(seed, part) draws one part's arguments, and reference() takes and returns one part's arrays. A program takes and returns all parts, laid end to end along the dimension named above; an argument that names none is the same for every part. Nothing has to cross between parts.
Inputs may be any that keep to these rules, and one draw needn't show every extreme that they name: For each visit w, the 15 row profile indices basis_index[w, :, 0] are distinct, and so are the 15 column profile indices basis_index[w, :, 1].
All inputs are finite; a program needn't handle non-finite values. No bound on the sum of `live_flags` on one device may be relied on, other than what follows from the above.
Results may differ from the reference program's by a relative error of at most 0.0056.
Values may be sent and summed in bfloat16 or wider, within the bound.
No kernel may reach another device: no remote copies, remote signals or barrier semaphores. Data moves between devices by JAX's collectives and lax.ppermute only.
A program may use at most 64 MiB of HBM per device.

```python
import jax
import jax.numpy as jnp
from jax import lax

TR = 512
TC = 512
NK = 15
KS = 31
NB = 16
VISITS = 4
ROWS = 2048
N_PATCH = 4


def draw_basis_index(key, part):
    keys = jax.random.split(jax.random.fold_in(key, 7), VISITS * 2)
    orders = jax.vmap(lambda single: jax.random.permutation(single, NB))(keys)
    picked = orders[:, :NK].reshape(VISITS, 2, NK)
    return jnp.transpose(picked, (0, 2, 1)).astype(jnp.int32)


def with_ends(array, key, least, high):
    longest = array.shape.index(max(array.shape))
    spots = []
    for shift in (0, 1):
        where = [jax.random.randint(jax.random.fold_in(key, axis), (), 0, length) for axis, length in enumerate(array.shape)]
        where[longest] = (where[longest] + shift) % array.shape[longest]
        spots.append(tuple(where))
    return array.at[spots[0]].set(least).at[spots[1]].set(high)


def shard_levels(stream_key, dims, pieces, smallest, high):
    def one(dim, parts):
        heights = jax.random.uniform(jax.random.fold_in(jax.random.fold_in(stream_key, 6), dim), (parts,), jnp.float32, smallest / len(pieces), high / len(pieces))
        return jnp.repeat(jnp.exp(heights), dims[dim] // parts).reshape((-1,) + (1,) * (len(dims) - dim - 1))

    factor_of = one(*pieces[0])
    for cut in pieces[1:]:
        factor_of = factor_of * one(*cut)
    return factor_of


def noise(own_key, extent, scale, bound, pieces=(), kind=jnp.bfloat16):
    drawn = scale * jax.random.normal(own_key, extent, jnp.float32)
    if pieces:
        drawn = drawn * shard_levels(own_key, extent, pieces, -0.22, 0.18)
    return jnp.clip(drawn, -bound, bound).astype(kind)


def setup_inputs(seed: int = 0, part: int = 0) -> dict:
    seeds = jax.random.split(jax.random.key(seed), 9)
    part_splits = jax.random.split(jax.random.fold_in(seeds[8], part), 9)
    template = noise(part_splits[0], (ROWS, TC), 1.0, 6.0, ((0, 4),))
    science = noise(part_splits[1], (ROWS, VISITS, TC), 1.0, 6.0, ((0, 4), (1, 4)))
    offsets = with_ends(jax.random.randint(part_splits[2], (N_PATCH, VISITS), 0, TR - KS // 2), jax.random.fold_in(part_splits[2], 1), 0, (TR - KS // 2) - 1).astype(jnp.int32)
    live_flags = with_ends((jax.random.randint(part_splits[3], (N_PATCH, VISITS), 0, 4) < 3).astype(jnp.int32), jax.random.fold_in(part_splits[3], 1), 0, 1)
    bank = noise(seeds[4], (NB, KS), KS ** -0.5, 1.0)
    basis_index = draw_basis_index(jax.random.fold_in(jax.random.fold_in(seeds[8], part), 71), part)
    coeff = noise(part_splits[6], (VISITS, NK), 0.26, 4.0, ((0, 4),), jnp.float32)
    psf_profile = noise(seeds[7], (KS,), KS ** -0.5, 1.0)
    return {"template": template, "science": science, "offsets": offsets, "live_flags": live_flags, "bank": bank, "basis_index": basis_index, "coeff": coeff, "psf_profile": psf_profile}


def toeplitz(profile, count):
    width = profile.shape[-1]
    lead = profile.shape[:-1]
    padded = jnp.concatenate([profile, jnp.zeros(lead + (count,), profile.dtype)], axis=-1)
    tiled = jnp.tile(padded, (1,) * len(lead) + (count,))
    tiled = tiled[..., :count * (count + width - 1)]
    return tiled.reshape(lead + (count, count + width - 1))

def profiles(bank, basis_index, coeff):
    table = bank.astype(jnp.float32)
    labels = jnp.arange(table.shape[0], dtype=jnp.int32)
    pick_row = (basis_index[:, 0:1] == labels[None, :]).astype(jnp.float32)
    pick_col = (basis_index[:, 1:2] == labels[None, :]).astype(jnp.float32)
    row_raw = jnp.dot(pick_row, table, precision=lax.Precision.HIGHEST)
    col_raw = jnp.dot(pick_col, table, precision=lax.Precision.HIGHEST)
    rowprof = (coeff[:, None] * row_raw).astype(jnp.bfloat16)
    colprof = col_raw.astype(jnp.bfloat16)
    return (rowprof, colprof)

def match_tile(window, sci, rowprof, colprof, psf):
    tile_rows, tile_cols = sci.shape
    half = psf.shape[0] // 2
    padded = jnp.pad(window, ((0, 0), (half, half)))
    colmat = toeplitz(colprof, tile_cols)
    smoothed = jnp.einsum('ri,kci->krc', padded.astype(jnp.float32), colmat.astype(jnp.float32)).astype(jnp.bfloat16)
    rowmat = toeplitz(rowprof, tile_rows)
    matched = jnp.einsum('kri,kic->rc', rowmat.astype(jnp.float32), smoothed.astype(jnp.float32))
    difference = (sci.astype(jnp.float32) - matched).astype(jnp.bfloat16)
    dpad = jnp.pad(difference, ((0, 0), (half, half)))
    pcol = toeplitz(psf, tile_cols)
    filtrow = jnp.dot(dpad, pcol.T, preferred_element_type=jnp.float32).astype(jnp.bfloat16)
    fpad = jnp.pad(filtrow, ((half, half), (0, 0)))
    prow = toeplitz(psf, tile_rows)
    filtered = jnp.dot(prow, fpad, preferred_element_type=jnp.float32)
    return (difference, filtered)

def split_rows(filtered, shift_rows, live):
    tile_rows = filtered.shape[0]
    rolled = jnp.roll(filtered, shift_rows, axis=0)
    rowid = jnp.arange(tile_rows, dtype=jnp.int32)
    mine = (rowid >= shift_rows).astype(jnp.float32) * live
    spilled = (rowid < shift_rows).astype(jnp.float32) * live
    return (rolled * mine[:, None], rolled * spilled[:, None], mine, spilled)

def reference(template, science, offsets, live_flags, bank, basis_index, coeff, psf_profile):
    half = KS // 2
    padded_tpl = jnp.concatenate([jnp.zeros((half, TC), jnp.bfloat16), template, jnp.zeros((TR + half, TC), jnp.bfloat16)], axis=0)

    def one_patch(patch_id):

        def one_visit(visit_id):
            shift_rows = offsets[patch_id, visit_id]
            start = (patch_id * TR + shift_rows).astype(jnp.int32)
            window = lax.dynamic_slice(padded_tpl, (start, jnp.int32(0)), (TR + 2 * half, TC))
            sci = lax.dynamic_slice(science, ((patch_id * TR).astype(jnp.int32), visit_id.astype(jnp.int32), jnp.int32(0)), (TR, 1, TC))[:, 0, :]
            rowprof, colprof = profiles(bank, basis_index[visit_id], coeff[visit_id])
            difference, filtered = match_tile(window, sci, rowprof, colprof, psf_profile)
            live = live_flags[patch_id, visit_id].astype(jnp.float32)
            mine, spill, mine_cover, spill_cover = split_rows(filtered, shift_rows, live)
            return (difference, mine, spill, mine_cover, spill_cover)
        diffs, mine, spill, mine_cover, spill_cover = lax.map(one_visit, jnp.arange(VISITS, dtype=jnp.int32))
        return (diffs, lax.optimization_barrier(jnp.sum(mine, axis=0)), lax.optimization_barrier(jnp.sum(spill, axis=0)), lax.optimization_barrier(jnp.sum(mine_cover, axis=0)), lax.optimization_barrier(jnp.sum(spill_cover, axis=0)))
    diffs, mine, spill, mine_cover, spill_cover = lax.map(one_patch, jnp.arange(N_PATCH, dtype=jnp.int32))
    difference = jnp.transpose(diffs, (0, 2, 1, 3)).reshape(N_PATCH * TR, VISITS, TC)
    spill_in = jnp.concatenate([jnp.zeros_like(spill[:1]), spill[:-1]], axis=0)
    cover_in = jnp.concatenate([jnp.zeros_like(spill_cover[:1]), spill_cover[:-1]], axis=0)
    accum = mine + spill_in
    cover = mine_cover + cover_in
    detection = accum * lax.rsqrt(jnp.maximum(cover, 1.0))[:, :, None]
    return (difference, detection.reshape(N_PATCH * TR, TC))
```

```python
import functools

import jax
import jax.numpy as jnp
from jax import lax
from jax.experimental import pallas as pl
from jax.experimental.pallas import tpu as pltpu
from jax.sharding import PartitionSpec as P

B = 16
CH = B * B
LANES = 128
GROUPS = LANES // B
F32 = jnp.float32
BF16 = jnp.bfloat16


def shifted(shard, axis, by):
    devices = lax.axis_size(axis)
    pairs = [(i, i + by) for i in range(devices) if 0 <= i + by < devices]
    return lax.ppermute(shard, axis, pairs)


def iota(shape, dim):
    return lax.broadcasted_iota(jnp.int32, shape, dim)


def params():
    return pltpu.CompilerParams(vmem_limit_bytes=48 * 1024 * 1024)


VM = pl.BlockSpec(memory_space=pltpu.VMEM)
SM = pl.BlockSpec(memory_space=pltpu.SMEM)


def group_transpose(parts):
    parts = list(parts)
    group = iota(parts[0].shape, 1) // B
    for step in (1, 2, 4):
        low = (group & step) == 0
        for m in range(GROUPS):
            if m & step:
                continue
            x, y = parts[m], parts[m + step]
            parts[m] = jnp.where(low, x, pltpu.roll(y, step * B, 1))
            parts[m + step] = jnp.where(low, pltpu.roll(x, LANES - step * B, 1), y)
    return parts


def conv_blocks(src, count, w_ref, xs, rs, dst, dst_row, batch):
    chunks = src.shape[0]
    blocks = chunks * GROUPS
    for q in range(3):
        xs[q, 0] = jnp.zeros((count, CH), xs.dtype)
        xs[q, blocks + 1] = jnp.zeros((count, CH), xs.dtype)
    for c in range(chunks):
        for h in range(2):
            rows = [src[c, pl.ds(GROUPS * h + i, count, stride=B), :] for i in range(GROUPS)]
            cols = group_transpose(rows)
            for g in range(GROUPS):
                for q in range(3):
                    moved = cols[g] if q == 1 else pltpu.roll(cols[g], (1 - q) % count, 0)
                    xs[q, 1 + c * GROUPS + g, :, h * LANES : (h + 1) * LANES] = moved.astype(xs.dtype)
    for b in range(0, blocks, batch):
        pieces = [
            xs[qr, b + qc : b + qc + batch].reshape(batch * count, CH).astype(BF16)
            for qr in range(3)
            for qc in range(3)
        ]
        out = jnp.dot(jnp.concatenate(pieces, axis=1), w_ref[...], preferred_element_type=F32)
        rs[b : b + batch] = out.reshape(batch, count, CH)
    for c in range(chunks):
        for h in range(2):
            cols = [rs[c * GROUPS + g, :, h * LANES : (h + 1) * LANES] for g in range(GROUPS)]
            rows = group_transpose(cols)
            for i in range(GROUPS):
                dst[c, pl.ds(dst_row + GROUPS * h + i, count, stride=B), :] = rows[i]


def weights_kernel(bank_ref, index_ref, coeff_ref, psf_ref, w_ref, pcol_ref, prow_ref):
    kernels = index_ref.shape[1]
    profs, taps = bank_ref.shape
    half = taps // 2
    delta = B - half
    bank = bank_ref[...]
    index = index_ref[0]
    labels = iota((kernels, profs), 1)
    pick_row = (index[:, 0:1] == labels).astype(F32).astype(BF16)
    pick_col = (index[:, 1:2] == labels).astype(F32).astype(BF16)
    diag = iota((kernels, kernels), 0) == iota((kernels, kernels), 1)
    weight = jnp.sum(jnp.where(diag, coeff_ref[...], 0.0), axis=1, keepdims=True)
    rowprof = (weight * jnp.dot(pick_row, bank, preferred_element_type=F32)).astype(BF16)
    colprof = jnp.dot(pick_col, bank, preferred_element_type=F32).astype(BF16)
    span = 3 * B
    total = 4 * B * B
    place = (iota((span, taps), 0) - delta == iota((span, taps), 1)).astype(F32).astype(BF16)
    col_t = lax.dot_general(place, colprof, (((1,), (1,)), ((), ())), preferred_element_type=F32).astype(BF16)
    spread = (span - 1 - iota((taps, total), 1) // B - delta == iota((taps, total), 0)).astype(F32).astype(BF16)
    row_rep = jnp.dot(rowprof, spread, preferred_element_type=F32).astype(BF16)
    z = jnp.dot(col_t, row_rep, preferred_element_type=F32)
    lane = iota((span, total), 1)
    for bit in (1, 2, 4, 8):
        z = jnp.where((lane & bit) != 0, pltpu.roll(z, bit, 0), z)
    z = z.astype(BF16)
    for phase in range(GROUPS):
        zp = z if phase == 0 else pltpu.roll(z, total - phase * B, 1)
        for g in range(span):
            start = span - 1 - g
            if start % GROUPS != phase:
                continue
            at = (start // GROUPS) * LANES
            for qc in range(3):
                row = (g // B) * 3 * CH + qc * CH + (g % B) * B
                w_ref[row : row + B, :] = zp[qc * B : (qc + 1) * B, at : at + CH]
    psf = psf_ref[...].astype(F32)
    size = pcol_ref.shape[0]
    blank = jnp.zeros((LANES, LANES), F32)
    bands = {}
    for off in (-1, 0, 1):
        tap = iota((LANES, LANES), 0) + off * LANES - iota((LANES, LANES), 1) + half
        block = blank
        for t in range(taps):
            block = jnp.where(tap == t, psf[:, t : t + 1], block)
        bands[off] = block.astype(BF16)
    for i in range(size // LANES):
        for j in range(size // LANES):
            pcol_ref[i * LANES : (i + 1) * LANES, j * LANES : (j + 1) * LANES] = bands.get(i - j, blank.astype(BF16))
    shape = prow_ref.shape
    tap = iota(shape, 1) - iota(shape, 0) - delta
    block = jnp.zeros(shape, F32)
    for t in range(taps):
        block = jnp.where(tap == t, psf[:, t : t + 1], block)
    prow_ref[...] = block.astype(BF16)


def to_chunks(dst, dst_row, value):
    value = value.astype(F32)
    rows = value.shape[0]
    for c in range(dst.shape[0]):
        dst[c, dst_row : dst_row + rows, :] = value[:, c * LANES : (c + 1) * LANES]


def own_kernel(t_ref, w_ref, m_ref, src, xs, rs):
    to_chunks(src, 0, t_ref[...])
    conv_blocks(src, t_ref.shape[0] // B, w_ref, xs, rs, m_ref, 0, rs.shape[0] // 2)


def filter_kernel(
    off_ref, live_ref, t_ref, msg_ref, next_ref, sci_ref, m1_ref, w_ref, pcol_ref, prow_ref,
    out_ref, m_ref, src, xs, rs, strip, sa, sb, diff, filt,
):
    rows, cols = t_ref.shape
    ext = rows + 2 * B
    edge = 2 * B
    to_chunks(src, 0, msg_ref[0:edge, :])
    to_chunks(src, edge, t_ref[0:edge, :])
    to_chunks(src, 2 * edge, t_ref[rows - edge : rows, :])
    to_chunks(src, 3 * edge, next_ref[0:edge, :])
    conv_blocks(src, 8, w_ref, xs, rs, strip, 0, rs.shape[0])
    m_ref[:, 0:edge, :] = strip[:, B : B + edge, :]
    m_ref[:, edge : rows, :] = m1_ref[:, B : rows - B, :]
    m_ref[:, rows : rows + edge, :] = strip[:, 5 * B : 5 * B + edge, :]
    to_chunks(sa, rows, sci_ref[...])
    to_chunks(sb, 0, msg_ref[edge : edge + rows, :])
    notes = msg_ref[0:B, 0:LANES].astype(F32)
    off_a = off_ref[0, 0]
    live_a = live_ref[0, 0].astype(F32)
    off_b = (notes[0, 0] * B + notes[0, 1]).astype(jnp.int32)
    live_b = notes[0, 2]
    tile_row = iota((ext, LANES), 0) - B
    in_a = (tile_row >= off_a) & (tile_row < off_a + rows)
    in_b = tile_row < off_b
    for c in range(cols // LANES):
        part = slice(c * LANES, (c + 1) * LANES)
        m = m_ref[c]
        a = sa[c, pl.ds(rows - B - off_a, ext), :]
        b = sb[c, pl.ds(rows - B - off_b, ext), :]
        diff[0, :, part] = jnp.where(in_a, a - m, 0.0).astype(BF16)
        diff[1, :, part] = jnp.where(in_b, b - m, 0.0).astype(BF16)
    for s in range(2):
        filt[s, 0:ext, :] = jnp.dot(diff[s], pcol_ref[...], preferred_element_type=F32).astype(BF16)
        filt[s, ext:, :] = jnp.zeros((filt.shape[1] - ext, cols), BF16)
    share, depth = prow_ref.shape
    prow = prow_ref[...].astype(F32)
    out_row = iota((share, depth), 0)
    lane = iota((B, cols), 1)
    for q in range(out_ref.shape[0]):
        row = out_row + q * share
        left = jnp.where(row >= off_a, prow * live_a, 0.0).astype(BF16)
        right = jnp.where(row < off_b, prow * live_b, 0.0).astype(BF16)
        span = slice(q * share, q * share + depth)
        total = jnp.dot(left, filt[0, span, :], preferred_element_type=F32)
        total += jnp.dot(right, filt[1, span, :], preferred_element_type=F32)
        out_ref[q, 0:share, :] = total.astype(BF16)
        start = jnp.clip(off_a - q * share, 0, share).astype(F32)
        stop = jnp.clip(off_b - q * share, 0, share).astype(F32)
        note = jnp.where(lane == 0, start, jnp.where(lane == 1, live_a, jnp.where(lane == 2, stop, live_b)))
        out_ref[q, share : share + B, :] = note.astype(BF16)


def tile_kernel(off_ref, next_ref, sci_ref, m_ref, w_ref, out_ref, src, xs, rs, big):
    rows, cols = next_ref.shape
    to_chunks(src, 0, next_ref[...])
    conv_blocks(src, rows // B, w_ref, xs, rs, big, rows, rs.shape[0] // 2)
    big[:, 0 : rows + B, :] = m_ref[:, B : rows + 2 * B, :]
    off = off_ref[0, 0]
    for c in range(cols // LANES):
        part = slice(c * LANES, (c + 1) * LANES)
        out_ref[:, part] = (sci_ref[:, part].astype(F32) - big[c, pl.ds(off, rows), :]).astype(BF16)


def coadd_kernel(recv_ref, out_ref):
    count, padded, cols = recv_ref.shape
    share = padded - B
    row = iota((share, LANES), 0).astype(F32)
    accum = jnp.zeros((share, cols), F32)
    cover = jnp.zeros((share, LANES), F32)
    for n in range(count):
        accum += recv_ref[n, 0:share, :].astype(F32)
        note = recv_ref[n, share : share + B, 0:LANES].astype(F32)[0:1, :]
        cover += jnp.where(row >= note[:, 0:1], note[:, 1:2], 0.0)
        cover += jnp.where(row < note[:, 2:3], note[:, 3:4], 0.0)
    scale = lax.rsqrt(jnp.maximum(cover, 1.0))
    for c in range(cols // LANES):
        part = slice(c * LANES, (c + 1) * LANES)
        out_ref[:, part] = accum[:, part] * scale


def call(body, shapes, specs, scratch, flops, name):
    return pl.pallas_call(
        body,
        out_shape=shapes,
        in_specs=specs,
        out_specs=jax.tree.map(lambda _: VM, shapes),
        scratch_shapes=scratch,
        compiler_params=params(),
        cost_estimate=pl.CostEstimate(flops=flops, bytes_accessed=1 << 21, transcendentals=0),
        name=name,
    )


def on_device(template, science, offsets, live_flags, bank, basis_index, coeff, psf_profile):
    rows, cols = template.shape
    sharers = lax.axis_size("visit") * lax.axis_size("band")
    share = rows // sharers
    chunks, blocks = cols // LANES, cols // B
    ext = rows + 2 * B
    edge = 2 * B
    sci = science[:, 0, :]
    off = offsets[0, 0]
    lane = jnp.arange(cols, dtype=jnp.int32)
    note = jnp.where(lane == 0, off // B, jnp.where(lane == 1, off % B, live_flags[0, 0])).astype(BF16)
    msg = jnp.concatenate([note[None], template[rows - edge + 1 :], sci], axis=0)
    msg = shifted(msg, "patch", 1)
    following = shifted(template, "patch", -1)

    sds = jax.ShapeDtypeStruct
    deep = 9 * CH
    depth = -(-(share + edge) // LANES) * LANES
    w, pcol, prow = call(
        weights_kernel,
        (sds((deep, CH), BF16), sds((cols, cols), BF16), sds((share, depth), BF16)),
        [VM] * 4, [], 1 << 26, "weights",
    )(bank, basis_index, coeff, psf_profile[None])
    count = rows // B
    conv_scratch = [
        pltpu.VMEM((chunks, rows, LANES), F32),
        pltpu.VMEM((3, blocks + 2, count, CH), BF16),
        pltpu.VMEM((blocks, count, CH), F32),
    ]
    conv_flops = 2 * rows * cols * deep
    m1 = call(own_kernel, sds((chunks, rows, LANES), F32), [VM] * 2, conv_scratch, conv_flops, "own")(template, w)
    out, m = call(
        filter_kernel,
        (sds((sharers, share + B, cols), BF16), sds((chunks, ext, LANES), F32)),
        [SM, SM] + [VM] * 8,
        [
            pltpu.VMEM((chunks, 8 * B, LANES), F32),
            pltpu.VMEM((3, blocks + 2, 8, CH), F32),
            pltpu.VMEM((blocks, 8, CH), F32),
            pltpu.VMEM((chunks, 8 * B, LANES), F32),
            pltpu.VMEM((chunks, 2 * rows + B, LANES), F32),
            pltpu.VMEM((chunks, 2 * rows + B, LANES), F32),
            pltpu.VMEM((2, ext, cols), BF16),
            pltpu.VMEM((2, rows - share + depth, cols), BF16),
        ],
        1 << 30, "filter",
    )(offsets, live_flags, template, msg, following, sci, m1, w, pcol, prow)
    recv = lax.all_to_all(out, ("visit", "band"), 0, 0, tiled=True)
    difference = call(
        tile_kernel, sds((rows, cols), BF16), [SM] + [VM] * 4,
        conv_scratch + [pltpu.VMEM((chunks, 2 * rows, LANES), F32)], conv_flops, "tile",
    )(offsets, following, sci, m, w)
    detection = call(coadd_kernel, sds((share, cols), F32), [VM], [], 1 << 20, "coadd")(recv)
    return (difference[:, None, :], detection)


def solution(mesh):
    return jax.shard_map(
        on_device,
        mesh=mesh,
        in_specs=(
            P(("group", "patch"), None),
            P(("group", "patch"), ("visit", "band"), None),
            P(("group", "patch"), ("visit", "band")),
            P(("group", "patch"), ("visit", "band")),
            P(),
            P(("group", "visit", "band"), None, None),
            P(("group", "visit", "band"), None),
            P(),
        ),
        out_specs=(
            P(("group", "patch"), ("visit", "band"), None),
            P(("group", "patch", "visit", "band"), None),
        ),
        check_vma=False,
    )
```

```python
import functools

import jax
import jax.numpy as jnp
from jax import lax
from jax.experimental import pallas as pl
from jax.experimental.pallas import tpu as pltpu
from jax.sharding import PartitionSpec as P

B = 16
CH = B * B
LANES = 128
GROUPS = LANES // B
F32 = jnp.float32
BF16 = jnp.bfloat16


def shifted(shard, axis, by):
    devices = lax.axis_size(axis)
    pairs = [(i, i + by) for i in range(devices) if 0 <= i + by < devices]
    return lax.ppermute(shard, axis, pairs)


def iota(shape, dim):
    return lax.broadcasted_iota(jnp.int32, shape, dim)


def params():
    return pltpu.CompilerParams(vmem_limit_bytes=20 * 1024 * 1024)


VM = pl.BlockSpec(memory_space=pltpu.VMEM)
SM = pl.BlockSpec(memory_space=pltpu.SMEM)


def group_transpose(parts):
    parts = list(parts)
    group = iota(parts[0].shape, 1) // B
    for step in (1, 2, 4):
        low = (group & step) == 0
        for m in range(GROUPS):
            if m & step:
                continue
            x, y = parts[m], parts[m + step]
            parts[m] = jnp.where(low, x, pltpu.roll(y, step * B, 1))
            parts[m + step] = jnp.where(low, pltpu.roll(x, LANES - step * B, 1), y)
    return parts


def conv_blocks(src, count, w_ref, xs, rs, dst, dst_row, batch):
    chunks = src.shape[0]
    blocks = chunks * GROUPS
    for q in range(3):
        xs[q, 0] = jnp.zeros((count, CH), xs.dtype)
        xs[q, blocks + 1] = jnp.zeros((count, CH), xs.dtype)
    for c in range(chunks):
        for h in range(2):
            rows = [src[c, pl.ds(GROUPS * h + i, count, stride=B), :] for i in range(GROUPS)]
            cols = group_transpose(rows)
            for g in range(GROUPS):
                for q in range(3):
                    moved = cols[g] if q == 1 else pltpu.roll(cols[g], (1 - q) % count, 0)
                    xs[q, 1 + c * GROUPS + g, :, h * LANES : (h + 1) * LANES] = moved.astype(xs.dtype)
    for b in range(0, blocks, batch):
        pieces = [
            xs[qr, b + qc : b + qc + batch].reshape(batch * count, CH).astype(BF16)
            for qr in range(3)
            for qc in range(3)
        ]
        out = jnp.dot(jnp.concatenate(pieces, axis=1), w_ref[...], preferred_element_type=F32)
        rs[b : b + batch] = out.reshape(batch, count, CH)
    for c in range(chunks):
        for h in range(2):
            cols = [rs[c * GROUPS + g, :, h * LANES : (h + 1) * LANES] for g in range(GROUPS)]
            rows = group_transpose(cols)
            for i in range(GROUPS):
                dst[c, pl.ds(dst_row + GROUPS * h + i, count, stride=B), :] = rows[i]


def weights_kernel(
    off_ref, live_ref, t_ref, bank_ref, index_ref, coeff_ref, psf_ref, w_ref, pcol_ref, prow_ref, msg_ref
):
    edge = 2 * B
    rows, cols = t_ref.shape
    lane = iota((1, cols), 1)
    off = off_ref[0, 0]
    note = jnp.where(lane == 0, off // B, jnp.where(lane == 1, off % B, live_ref[0, 0]))
    tail = t_ref[rows - edge : rows, :].astype(F32)
    msg_ref[...] = jnp.where(iota((edge, cols), 0) == 0, note.astype(F32), tail).astype(BF16)
    kernels = index_ref.shape[1]
    profs, taps = bank_ref.shape
    half = taps // 2
    delta = B - half
    bank = bank_ref[...]
    index = index_ref[0]
    labels = iota((kernels, profs), 1)
    pick_row = (index[:, 0:1] == labels).astype(F32).astype(BF16)
    pick_col = (index[:, 1:2] == labels).astype(F32).astype(BF16)
    diag = iota((kernels, kernels), 0) == iota((kernels, kernels), 1)
    weight = jnp.sum(jnp.where(diag, coeff_ref[...], 0.0), axis=1, keepdims=True)
    rowprof = (weight * jnp.dot(pick_row, bank, preferred_element_type=F32)).astype(BF16)
    colprof = jnp.dot(pick_col, bank, preferred_element_type=F32).astype(BF16)
    span = 3 * B
    total = 4 * B * B
    place = (iota((span, taps), 0) - delta == iota((span, taps), 1)).astype(F32).astype(BF16)
    col_t = lax.dot_general(place, colprof, (((1,), (1,)), ((), ())), preferred_element_type=F32).astype(BF16)
    spread = (span - 1 - iota((taps, total), 1) // B - delta == iota((taps, total), 0)).astype(F32).astype(BF16)
    row_rep = jnp.dot(rowprof, spread, preferred_element_type=F32).astype(BF16)
    z = jnp.dot(col_t, row_rep, preferred_element_type=F32)
    lane = iota((span, total), 1)
    for bit in (1, 2, 4, 8):
        z = jnp.where((lane & bit) != 0, pltpu.roll(z, bit, 0), z)
    z = z.astype(BF16)
    for phase in range(GROUPS):
        zp = z if phase == 0 else pltpu.roll(z, total - phase * B, 1)
        for g in range(span):
            start = span - 1 - g
            if start % GROUPS != phase:
                continue
            at = (start // GROUPS) * LANES
            for qc in range(3):
                row = (g // B) * 3 * CH + qc * CH + (g % B) * B
                w_ref[row : row + B, :] = zp[qc * B : (qc + 1) * B, at : at + CH]
    psf = psf_ref[...].astype(F32)
    size = pcol_ref.shape[0]
    blank = jnp.zeros((LANES, LANES), F32)
    bands = {}
    for off in (-1, 0, 1):
        tap = iota((LANES, LANES), 0) + off * LANES - iota((LANES, LANES), 1) + half
        block = blank
        for t in range(taps):
            block = jnp.where(tap == t, psf[:, t : t + 1], block)
        bands[off] = block.astype(BF16)
    for i in range(size // LANES):
        for j in range(size // LANES):
            pcol_ref[i * LANES : (i + 1) * LANES, j * LANES : (j + 1) * LANES] = bands.get(i - j, blank.astype(BF16))
    shape = prow_ref.shape
    tap = iota(shape, 1) - iota(shape, 0) - delta
    block = jnp.zeros(shape, F32)
    for t in range(taps):
        block = jnp.where(tap == t, psf[:, t : t + 1], block)
    prow_ref[...] = block.astype(BF16)


def to_chunks(dst, dst_row, value):
    value = value.astype(F32)
    rows = value.shape[0]
    for c in range(dst.shape[0]):
        dst[c, dst_row : dst_row + rows, :] = value[:, c * LANES : (c + 1) * LANES]


def tile_diff(sky, m, base, first, last):
    row = iota(m.shape, 0) + (base - B)
    return jnp.where((row >= first) & (row < last), sky - m, 0.0).astype(BF16)


def filter_inner(sci, start, first, last, m_ref, pcol_ref, edge_ref, filt_ref, diff):
    chunks, rows, _ = m_ref.shape
    edge = 2 * B
    for c in range(chunks):
        part = slice(c * LANES, (c + 1) * LANES)
        sky = sci[c, pl.ds(start, rows + edge), :]
        edge_ref[c, 0:edge, :] = sky[0:edge]
        edge_ref[c, edge:, :] = sky[rows:]
        diff[:, part] = tile_diff(sky[edge:rows], m_ref[c, B : rows - B, :], edge, first, last)
    filt_ref[...] = jnp.dot(diff[...], pcol_ref[...], preferred_element_type=F32).astype(BF16)


def own_kernel(off_ref, t_ref, sci_ref, w_ref, pcol_ref, m_ref, edge_ref, filt_ref, src, xs, rs, sci, diff):
    rows = t_ref.shape[0]
    to_chunks(src, 0, t_ref[...])
    conv_blocks(src, rows // B, w_ref, xs, rs, m_ref, 0, rs.shape[0] // 2)
    off = off_ref[0, 0]
    to_chunks(sci, rows, sci_ref[...])
    filter_inner(sci, rows - B - off, off, off + rows, m_ref, pcol_ref, edge_ref, filt_ref, diff)


def read_note(msg_ref):
    note = msg_ref[0:B, 0:LANES].astype(F32)
    return (note[0, 0] * B + note[0, 1]).astype(jnp.int32), note[0, 2]


def before_kernel(msg_ref, sci_ref, m_ref, pcol_ref, edge_ref, filt_ref, sci, diff):
    rows = sci_ref.shape[0]
    off, _ = read_note(msg_ref)
    to_chunks(sci, 0, sci_ref[...])
    filter_inner(sci, rows - B - off, off - rows, off, m_ref, pcol_ref, edge_ref, filt_ref, diff)


def join_kernel(
    off_ref, live_ref, t_ref, msg_ref, next_ref, w_ref, pcol_ref, prow_ref, edge_a, edge_b, filt_a, filt_b,
    out_ref, m_ref, src, xs, rs, strip, diff, sides,
):
    rows, cols = t_ref.shape
    edge = 2 * B
    to_chunks(src, 0, msg_ref[...])
    to_chunks(src, edge, t_ref[0:edge, :])
    to_chunks(src, 2 * edge, t_ref[rows - edge : rows, :])
    to_chunks(src, 3 * edge, next_ref[0:edge, :])
    conv_blocks(src, 8, w_ref, xs, rs, strip, 0, rs.shape[0])
    m_ref[:, 0:edge, :] = strip[:, B : B + edge, :]
    m_ref[:, edge:, :] = strip[:, 5 * B : 5 * B + edge, :]
    off_a = off_ref[0, 0]
    live_a = live_ref[0, 0].astype(F32)
    off_b, live_b = read_note(msg_ref)
    for s, (side, first, last) in enumerate(((edge_a, off_a, off_a + rows), (edge_b, off_b - rows, off_b))):
        for c in range(cols // LANES):
            part = slice(c * LANES, (c + 1) * LANES)
            for k, base in enumerate((0, rows)):
                span = slice(k * edge, (k + 1) * edge)
                at = (2 * s + k) * edge
                diff[at : at + edge, part] = tile_diff(side[c, span, :], m_ref[c, span, :], base, first, last)
    sides[...] = jnp.dot(diff[...], pcol_ref[...], preferred_element_type=F32).astype(BF16)
    inner = (filt_a, filt_b)

    def rows_of(s, low, high):
        pieces = []
        for start, stop, ref, at in (
            (0, edge, sides, 2 * s * edge),
            (edge, rows, inner[s], 0),
            (rows, rows + edge, sides, (2 * s + 1) * edge),
        ):
            a, b = max(low, start), min(high, stop)
            if a < b:
                pieces.append(ref[at + a - start : at + b - start, :])
        if high > rows + edge:
            pieces.append(jnp.zeros((high - max(low, rows + edge), cols), BF16))
        return jnp.concatenate(pieces, axis=0)

    share, depth = prow_ref.shape
    prow = prow_ref[...].astype(F32)
    out_row = iota((share, depth), 0)
    lane = iota((B, cols), 1)
    for q in range(out_ref.shape[0]):
        row = out_row + q * share
        left = jnp.where(row >= off_a, prow * live_a, 0.0).astype(BF16)
        right = jnp.where(row < off_b, prow * live_b, 0.0).astype(BF16)
        total = jnp.dot(left, rows_of(0, q * share, q * share + depth), preferred_element_type=F32)
        total += jnp.dot(right, rows_of(1, q * share, q * share + depth), preferred_element_type=F32)
        out_ref[q, 0:share, :] = total.astype(BF16)
        start = jnp.clip(off_a - q * share, 0, share).astype(F32)
        stop = jnp.clip(off_b - q * share, 0, share).astype(F32)
        note = jnp.where(lane == 0, start, jnp.where(lane == 1, live_a, jnp.where(lane == 2, stop, live_b)))
        out_ref[q, share : share + B, :] = note.astype(BF16)


def tile_kernel(off_ref, next_ref, sci_ref, m1_ref, edge_ref, w_ref, out_ref, src, xs, rs, big):
    rows, cols = next_ref.shape
    to_chunks(src, 0, next_ref[...])
    conv_blocks(src, rows // B, w_ref, xs, rs, big, rows, rs.shape[0] // 2)
    big[:, 0:B, :] = edge_ref[:, B : 2 * B, :]
    big[:, B : rows - B, :] = m1_ref[:, B : rows - B, :]
    big[:, rows - B : rows + B, :] = edge_ref[:, 2 * B : 4 * B, :]
    off = off_ref[0, 0]
    for c in range(cols // LANES):
        part = slice(c * LANES, (c + 1) * LANES)
        out_ref[:, part] = (sci_ref[:, part].astype(F32) - big[c, pl.ds(off, rows), :]).astype(BF16)


def coadd_kernel(recv_ref, out_ref):
    count, padded, cols = recv_ref.shape
    share = padded - B
    row = iota((share, LANES), 0).astype(F32)
    accum = jnp.zeros((share, cols), F32)
    cover = jnp.zeros((share, LANES), F32)
    for n in range(count):
        accum += recv_ref[n, 0:share, :].astype(F32)
        note = recv_ref[n, share : share + B, 0:LANES].astype(F32)[0:1, :]
        cover += jnp.where(row >= note[:, 0:1], note[:, 1:2], 0.0)
        cover += jnp.where(row < note[:, 2:3], note[:, 3:4], 0.0)
    scale = lax.rsqrt(jnp.maximum(cover, 1.0))
    for c in range(cols // LANES):
        part = slice(c * LANES, (c + 1) * LANES)
        out_ref[:, part] = accum[:, part] * scale


def call(body, shapes, specs, scratch, flops, name):
    return pl.pallas_call(
        body,
        out_shape=shapes,
        in_specs=specs,
        out_specs=jax.tree.map(lambda _: VM, shapes),
        scratch_shapes=scratch,
        compiler_params=params(),
        cost_estimate=pl.CostEstimate(flops=flops, bytes_accessed=1 << 21, transcendentals=0),
        name=name,
    )


def on_device(template, science, offsets, live_flags, bank, basis_index, coeff, psf_profile):
    rows, cols = template.shape
    sharers = lax.axis_size("visit") * lax.axis_size("band")
    share = rows // sharers
    chunks, blocks = cols // LANES, cols // B
    edge = 2 * B
    inner = rows - edge
    sci = science[:, 0, :]
    before = shifted(science, "patch", 1)[:, 0, :]
    following = shifted(template, "patch", -1)

    sds = jax.ShapeDtypeStruct
    deep = 9 * CH
    depth = -(-(share + edge) // LANES) * LANES
    w, pcol, prow, msg = call(
        weights_kernel,
        (sds((deep, CH), BF16), sds((cols, cols), BF16), sds((share, depth), BF16), sds((edge, cols), BF16)),
        [SM, SM] + [VM] * 5, [], 1 << 26, "weights",
    )(offsets, live_flags, template, bank, basis_index, coeff, psf_profile[None])
    msg = shifted(msg, "patch", 1)
    count = rows // B
    conv_scratch = [
        pltpu.VMEM((chunks, rows, LANES), F32),
        pltpu.VMEM((3, blocks + 2, count, CH), BF16),
        pltpu.VMEM((blocks, count, CH), F32),
    ]
    conv_flops = 2 * rows * cols * deep
    sky_scratch = [pltpu.VMEM((chunks, 2 * rows + B, LANES), F32), pltpu.VMEM((inner, cols), BF16)]
    sides = (sds((chunks, 2 * edge, LANES), F32), sds((inner, cols), BF16))
    m1, edge_a, filt_a = call(
        own_kernel, (sds((chunks, rows, LANES), F32),) + sides, [SM] + [VM] * 4,
        conv_scratch + sky_scratch, conv_flops, "own",
    )(offsets, template, sci, w, pcol)
    edge_b, filt_b = call(before_kernel, sides, [VM] * 4, sky_scratch, 1 << 28, "before")(msg, before, m1, pcol)
    out, m_edge = call(
        join_kernel,
        (sds((sharers, share + B, cols), BF16), sds((chunks, 2 * edge, LANES), F32)),
        [SM, SM] + [VM] * 10,
        [
            pltpu.VMEM((chunks, 8 * B, LANES), F32),
            pltpu.VMEM((3, blocks + 2, 8, CH), F32),
            pltpu.VMEM((blocks, 8, CH), F32),
            pltpu.VMEM((chunks, 8 * B, LANES), F32),
            pltpu.VMEM((4 * edge, cols), BF16),
            pltpu.VMEM((4 * edge, cols), BF16),
        ],
        1 << 29, "join",
    )(offsets, live_flags, template, msg, following, w, pcol, prow, edge_a, edge_b, filt_a, filt_b)
    recv = lax.all_to_all(out, ("visit", "band"), 0, 0, tiled=True)
    difference = call(
        tile_kernel, sds((rows, cols), BF16), [SM] + [VM] * 5,
        conv_scratch + [pltpu.VMEM((chunks, 2 * rows, LANES), F32)], conv_flops, "tile",
    )(offsets, following, sci, m1, m_edge, w)
    detection = call(coadd_kernel, sds((share, cols), F32), [VM], [], 1 << 20, "coadd")(recv)
    return (difference[:, None, :], detection)


def solution(mesh):
    return jax.shard_map(
        on_device,
        mesh=mesh,
        in_specs=(
            P(("group", "patch"), None),
            P(("group", "patch"), ("visit", "band"), None),
            P(("group", "patch"), ("visit", "band")),
            P(("group", "patch"), ("visit", "band")),
            P(),
            P(("group", "visit", "band"), None, None),
            P(("group", "visit", "band"), None),
            P(),
        ),
        out_specs=(
            P(("group", "patch"), ("visit", "band"), None),
            P(("group", "patch", "visit", "band"), None),
        ),
        check_vma=False,
    )
```

```python
import functools

import jax
import jax.numpy as jnp
from jax import lax
from jax.experimental import pallas as pl
from jax.experimental.pallas import tpu as pltpu
from jax.sharding import PartitionSpec as P

B = 16
CH = B * B
LANES = 128
GROUPS = LANES // B
F32 = jnp.float32
BF16 = jnp.bfloat16


def shifted(shard, axis, by):
    devices = lax.axis_size(axis)
    pairs = [(i, i + by) for i in range(devices) if 0 <= i + by < devices]
    return lax.ppermute(shard, axis, pairs)


def iota(shape, dim):
    return lax.broadcasted_iota(jnp.int32, shape, dim)


LIMIT = 58
VM = pl.BlockSpec(memory_space=pltpu.VMEM)
HBM = pl.BlockSpec(memory_space=pltpu.HBM)


def group_transpose(parts):
    parts = list(parts)
    group = iota(parts[0].shape, 1) // B
    for step in (1, 2, 4):
        low = (group & step) == 0
        for m in range(GROUPS):
            if m & step:
                continue
            x, y = parts[m], parts[m + step]
            parts[m] = jnp.where(low, x, pltpu.roll(y, step * B, 1))
            parts[m + step] = jnp.where(low, pltpu.roll(x, LANES - step * B, 1), y)
    return parts


def conv_blocks(src, count, w_ref, xs, rs, dst, dst_row, batch):
    chunks = src.shape[0]
    blocks = chunks * GROUPS
    for q in range(3):
        xs[q, 0] = jnp.zeros((count, CH), xs.dtype)
        xs[q, blocks + 1] = jnp.zeros((count, CH), xs.dtype)
    for c in range(chunks):
        for h in range(2):
            rows = [src[c, pl.ds(GROUPS * h + i, count, stride=B), :] for i in range(GROUPS)]
            cols = group_transpose(rows)
            for g in range(GROUPS):
                for q in range(3):
                    moved = cols[g] if q == 1 else pltpu.roll(cols[g], (1 - q) % count, 0)
                    xs[q, 1 + c * GROUPS + g, :, h * LANES : (h + 1) * LANES] = moved.astype(xs.dtype)
    for b in range(0, blocks, batch):
        pieces = [
            xs[qr, b + qc : b + qc + batch].reshape(batch * count, CH).astype(BF16)
            for qr in range(3)
            for qc in range(3)
        ]
        out = jnp.dot(jnp.concatenate(pieces, axis=1), w_ref[...], preferred_element_type=F32)
        rs[b : b + batch] = out.reshape(batch, count, CH)
    for c in range(chunks):
        for h in range(2):
            cols = [rs[c * GROUPS + g, :, h * LANES : (h + 1) * LANES] for g in range(GROUPS)]
            rows = group_transpose(cols)
            for i in range(GROUPS):
                dst[c, pl.ds(dst_row + GROUPS * h + i, count, stride=B), :] = rows[i]


def column(row):
    size = row.shape[1]
    diag = iota((size, size), 0) == iota((size, size), 1)
    return jnp.sum(jnp.where(diag, row, jnp.zeros_like(row)), axis=1, keepdims=True)


def first_kernel(
    off_hbm, live_hbm, t_hbm, sci_hbm, bank_hbm, index_hbm, coeff_hbm, psf_hbm,
    w_ref, pcol_ref, prow_ref, note_ref, ends_ref, m_ref, edge_ref, filt_ref,
    off_ref, live_ref, t_ref, sci_ref, bank_ref, index_ref, coeff_ref, psf_ref, sems,
    src, xs, rs, sci, diff,
):
    pairs = (
        (bank_hbm, bank_ref), (index_hbm, index_ref), (coeff_hbm, coeff_ref), (psf_hbm, psf_ref),
        (off_hbm, off_ref), (live_hbm, live_ref), (t_hbm, t_ref), (sci_hbm, sci_ref),
    )
    copies = [pltpu.make_async_copy(a, b, sems.at[n]) for n, (a, b) in enumerate(pairs)]
    for copy in copies:
        copy.start()
    for copy in copies[:4]:
        copy.wait()
    profs, taps = bank_ref.shape
    half = taps // 2
    delta = B - half
    bank = bank_ref[...]
    index = index_ref[0].astype(F32)
    labels = iota((index.shape[1], profs), 1).astype(F32)
    pick_row = (column(index[0:1]) == labels).astype(F32).astype(BF16)
    pick_col = (column(index[1:2]) == labels).astype(F32).astype(BF16)
    weight = column(coeff_ref[...])
    rowprof = (weight * jnp.dot(pick_row, bank, preferred_element_type=F32)).astype(BF16)
    colprof = jnp.dot(pick_col, bank, preferred_element_type=F32).astype(BF16)
    span = 3 * B
    total = 4 * B * B
    place = (iota((span, taps), 0) - delta == iota((span, taps), 1)).astype(F32).astype(BF16)
    col_t = lax.dot_general(place, colprof, (((1,), (1,)), ((), ())), preferred_element_type=F32).astype(BF16)
    spread = (span - 1 - iota((taps, total), 1) // B - delta == iota((taps, total), 0)).astype(F32).astype(BF16)
    row_rep = jnp.dot(rowprof, spread, preferred_element_type=F32).astype(BF16)
    z = jnp.dot(col_t, row_rep, preferred_element_type=F32)
    lane = iota((span, total), 1)
    for bit in (1, 2, 4, 8):
        z = jnp.where((lane & bit) != 0, pltpu.roll(z, bit, 0), z)
    z = z.astype(BF16)
    for phase in range(GROUPS):
        zp = z if phase == 0 else pltpu.roll(z, total - phase * B, 1)
        for g in range(span):
            start = span - 1 - g
            if start % GROUPS != phase:
                continue
            at = (start // GROUPS) * LANES
            for qc in range(3):
                row = (g // B) * 3 * CH + qc * CH + (g % B) * B
                w_ref[row : row + B, :] = zp[qc * B : (qc + 1) * B, at : at + CH]
    psf = psf_ref[...].astype(F32)
    size = pcol_ref.shape[0]
    blank = jnp.zeros((LANES, LANES), F32)
    bands = {}
    for off in (-1, 0, 1):
        tap = iota((LANES, LANES), 0) + off * LANES - iota((LANES, LANES), 1) + half
        block = blank
        for t in range(taps):
            block = jnp.where(tap == t, psf[:, t : t + 1], block)
        bands[off] = block.astype(BF16)
    for i in range(size // LANES):
        for j in range(size // LANES):
            pcol_ref[i * LANES : (i + 1) * LANES, j * LANES : (j + 1) * LANES] = bands.get(i - j, blank.astype(BF16))
    shape = prow_ref.shape
    tap = iota(shape, 1) - iota(shape, 0) - delta
    block = jnp.zeros(shape, F32)
    for t in range(taps):
        block = jnp.where(tap == t, psf[:, t : t + 1], block)
    prow_ref[...] = block.astype(BF16)
    for copy in copies[4:]:
        copy.wait()
    edge = 2 * B
    rows, cols = t_ref.shape
    lane = iota((1, cols), 1)
    off = off_ref[0, 0]
    note = jnp.where(lane == 0, off // B, jnp.where(lane == 1, off % B, live_ref[0, 0]))
    tail = t_ref[rows - edge : rows, :].astype(F32)
    note_ref[...] = jnp.where(iota((edge, cols), 0) == 0, note.astype(F32), tail).astype(BF16)
    ends_ref[0:edge, :] = t_ref[0:edge, :]
    ends_ref[edge:, :] = t_ref[rows - edge : rows, :]
    to_chunks(src, 0, t_ref[...])
    conv_blocks(src, rows // B, w_ref, xs, rs, m_ref, 0, rs.shape[0] // 2)
    to_chunks(sci, rows, sci_ref[...])
    filter_inner(sci, rows - B - off, off, off + rows, m_ref, pcol_ref, edge_ref, filt_ref, diff)


def to_chunks(dst, dst_row, value):
    value = value.astype(F32)
    rows = value.shape[0]
    for c in range(dst.shape[0]):
        dst[c, dst_row : dst_row + rows, :] = value[:, c * LANES : (c + 1) * LANES]


def tile_diff(sky, m, base, first, last):
    row = iota(m.shape, 0) + (base - B)
    return jnp.where((row >= first) & (row < last), sky - m, 0.0).astype(BF16)


def filter_inner(sci, start, first, last, m_ref, pcol_ref, edge_ref, filt_ref, diff):
    chunks, rows, _ = m_ref.shape
    edge = 2 * B
    for c in range(chunks):
        part = slice(c * LANES, (c + 1) * LANES)
        sky = sci[c, pl.ds(start, rows + edge), :]
        edge_ref[c, 0:edge, :] = sky[0:edge]
        edge_ref[c, edge:, :] = sky[rows:]
        diff[:, part] = tile_diff(sky[edge:rows], m_ref[c, B : rows - B, :], edge, first, last)
    filt_ref[...] = jnp.dot(diff[...], pcol_ref[...], preferred_element_type=F32).astype(BF16)


def read_note(msg_ref):
    note = msg_ref[0:B, 0:LANES].astype(F32)
    return (note[0, 0] * B + note[0, 1]).astype(jnp.int32), note[0, 2]


def before_kernel(msg_ref, sci_ref, m_ref, pcol_ref, edge_ref, filt_ref, sci, diff):
    rows = sci_ref.shape[0]
    off, _ = read_note(msg_ref)
    to_chunks(sci, 0, sci_ref[...])
    filter_inner(sci, rows - B - off, off - rows, off, m_ref, pcol_ref, edge_ref, filt_ref, diff)


def join_kernel(
    note_ref, ends_ref, msg_ref, next_ref, w_ref, pcol_ref, prow_ref, edge_a, edge_b, filt_a, filt_b,
    out_ref, m_ref, src, xs, rs, strip, diff, sides,
):
    rows, cols = next_ref.shape
    edge = 2 * B
    to_chunks(src, 0, msg_ref[...])
    to_chunks(src, edge, ends_ref[...])
    to_chunks(src, 3 * edge, next_ref[0:edge, :])
    conv_blocks(src, 8, w_ref, xs, rs, strip, 0, rs.shape[0])
    m_ref[:, 0:edge, :] = strip[:, B : B + edge, :]
    m_ref[:, edge:, :] = strip[:, 5 * B : 5 * B + edge, :]
    off_a, live_a = read_note(note_ref)
    off_b, live_b = read_note(msg_ref)
    for s, (side, first, last) in enumerate(((edge_a, off_a, off_a + rows), (edge_b, off_b - rows, off_b))):
        for c in range(cols // LANES):
            part = slice(c * LANES, (c + 1) * LANES)
            for k, base in enumerate((0, rows)):
                span = slice(k * edge, (k + 1) * edge)
                at = (2 * s + k) * edge
                diff[at : at + edge, part] = tile_diff(side[c, span, :], m_ref[c, span, :], base, first, last)
    sides[...] = jnp.dot(diff[...], pcol_ref[...], preferred_element_type=F32).astype(BF16)
    inner = (filt_a, filt_b)

    def rows_of(s, low, high):
        pieces = []
        for start, stop, ref, at in (
            (0, edge, sides, 2 * s * edge),
            (edge, rows, inner[s], 0),
            (rows, rows + edge, sides, (2 * s + 1) * edge),
        ):
            a, b = max(low, start), min(high, stop)
            if a < b:
                pieces.append(ref[at + a - start : at + b - start, :])
        if high > rows + edge:
            pieces.append(jnp.zeros((high - max(low, rows + edge), cols), BF16))
        return jnp.concatenate(pieces, axis=0)

    share, depth = prow_ref.shape
    prow = prow_ref[...].astype(F32)
    out_row = iota((share, depth), 0)
    lane = iota((B, cols), 1)
    for q in range(out_ref.shape[0]):
        row = out_row + q * share
        left = jnp.where(row >= off_a, prow * live_a, 0.0).astype(BF16)
        right = jnp.where(row < off_b, prow * live_b, 0.0).astype(BF16)
        total = jnp.dot(left, rows_of(0, q * share, q * share + depth), preferred_element_type=F32)
        total += jnp.dot(right, rows_of(1, q * share, q * share + depth), preferred_element_type=F32)
        out_ref[q, 0:share, :] = total.astype(BF16)
        start = jnp.clip(off_a - q * share, 0, share).astype(F32)
        stop = jnp.clip(off_b - q * share, 0, share).astype(F32)
        note = jnp.where(lane == 0, start, jnp.where(lane == 1, live_a, jnp.where(lane == 2, stop, live_b)))
        out_ref[q, share : share + B, :] = note.astype(BF16)


def tile_kernel(note_ref, next_ref, sci_ref, m1_ref, edge_ref, w_ref, out_ref, src, xs, rs, big):
    rows, cols = next_ref.shape
    to_chunks(src, 0, next_ref[...])
    conv_blocks(src, rows // B, w_ref, xs, rs, big, rows, rs.shape[0] // 2)
    big[:, 0:B, :] = edge_ref[:, B : 2 * B, :]
    big[:, B : rows - B, :] = m1_ref[:, B : rows - B, :]
    big[:, rows - B : rows + B, :] = edge_ref[:, 2 * B : 4 * B, :]
    off, _ = read_note(note_ref)
    for c in range(cols // LANES):
        part = slice(c * LANES, (c + 1) * LANES)
        out_ref[:, part] = (sci_ref[:, part].astype(F32) - big[c, pl.ds(off, rows), :]).astype(BF16)


def coadd_kernel(recv_ref, out_ref):
    count, padded, cols = recv_ref.shape
    share = padded - B
    row = iota((share, LANES), 0).astype(F32)
    accum = jnp.zeros((share, cols), F32)
    cover = jnp.zeros((share, LANES), F32)
    for n in range(count):
        accum += recv_ref[n, 0:share, :].astype(F32)
        note = recv_ref[n, share : share + B, 0:LANES].astype(F32)[0:1, :]
        cover += jnp.where(row >= note[:, 0:1], note[:, 1:2], 0.0)
        cover += jnp.where(row < note[:, 2:3], note[:, 3:4], 0.0)
    scale = lax.rsqrt(jnp.maximum(cover, 1.0))
    for c in range(cols // LANES):
        part = slice(c * LANES, (c + 1) * LANES)
        out_ref[:, part] = accum[:, part] * scale


def call(body, shapes, specs, scratch, flops, name, limit=20):
    return pl.pallas_call(
        body,
        out_shape=shapes,
        in_specs=specs,
        out_specs=jax.tree.map(lambda _: VM, shapes),
        scratch_shapes=scratch,
        compiler_params=pltpu.CompilerParams(vmem_limit_bytes=limit * 1024 * 1024),
        cost_estimate=pl.CostEstimate(flops=flops, bytes_accessed=1 << 21, transcendentals=0),
        name=name,
    )


def on_device(template, science, offsets, live_flags, bank, basis_index, coeff, psf_profile):
    rows, cols = template.shape
    sharers = lax.axis_size("visit") * lax.axis_size("band")
    share = rows // sharers
    chunks, blocks = cols // LANES, cols // B
    edge = 2 * B
    inner = rows - edge
    before = shifted(science, "patch", 1)[:, 0, :]
    following = shifted(template, "patch", -1)

    sds = jax.ShapeDtypeStruct
    deep = 9 * CH
    depth = -(-(share + edge) // LANES) * LANES
    sci = science[:, 0, :]
    taps = psf_profile.shape[0]
    index = jnp.swapaxes(basis_index, 1, 2)
    count = rows // B
    conv_scratch = [
        pltpu.VMEM((chunks, rows, LANES), F32),
        pltpu.VMEM((3, blocks + 2, count, CH), BF16),
        pltpu.VMEM((blocks, count, CH), F32),
    ]
    conv_flops = 2 * rows * cols * deep
    sky_scratch = [pltpu.VMEM((chunks, 2 * rows + B, LANES), F32), pltpu.VMEM((inner, cols), BF16)]
    sides = (sds((chunks, 2 * edge, LANES), F32), sds((inner, cols), BF16))
    w, pcol, prow, note, ends, m1, edge_a, filt_a = call(
        first_kernel,
        (
            sds((deep, CH), BF16), sds((cols, cols), BF16), sds((share, depth), BF16), sds((edge, cols), BF16),
            sds((2 * edge, cols), BF16), sds((chunks, rows, LANES), F32),
        ) + sides,
        [HBM] * 8,
        [
            pltpu.SMEM((1, 1), jnp.int32), pltpu.SMEM((1, 1), jnp.int32), pltpu.VMEM((rows, cols), BF16),
            pltpu.VMEM((rows, cols), BF16), pltpu.VMEM(bank.shape, BF16), pltpu.VMEM(index.shape, jnp.int32),
            pltpu.VMEM(coeff.shape, F32), pltpu.VMEM((1, taps), BF16), pltpu.SemaphoreType.DMA((8,)),
        ] + conv_scratch + sky_scratch,
        conv_flops, "first", LIMIT,
    )(offsets, live_flags, template, sci, bank, index, coeff, psf_profile[None])
    msg = shifted(note, "patch", 1)
    edge_b, filt_b = call(before_kernel, sides, [VM] * 4, sky_scratch, 1 << 28, "before")(msg, before, m1, pcol)
    out, m_edge = call(
        join_kernel,
        (sds((sharers, share + B, cols), BF16), sds((chunks, 2 * edge, LANES), F32)),
        [VM] * 11,
        [
            pltpu.VMEM((chunks, 8 * B, LANES), F32),
            pltpu.VMEM((3, blocks + 2, 8, CH), F32),
            pltpu.VMEM((blocks, 8, CH), F32),
            pltpu.VMEM((chunks, 8 * B, LANES), F32),
            pltpu.VMEM((4 * edge, cols), BF16),
            pltpu.VMEM((4 * edge, cols), BF16),
        ],
        1 << 29, "join",
    )(note, ends, msg, following, w, pcol, prow, edge_a, edge_b, filt_a, filt_b)
    recv = lax.all_to_all(out, ("visit", "band"), 0, 0, tiled=True)
    difference = call(
        tile_kernel, sds((rows, cols), BF16), [VM] * 6,
        conv_scratch + [pltpu.VMEM((chunks, 2 * rows, LANES), F32)], conv_flops, "tile",
    )(note, following, sci, m1, m_edge, w)
    detection = call(coadd_kernel, sds((share, cols), F32), [VM], [], 1 << 20, "coadd")(recv)
    return (difference[:, None, :], detection)


def solution(mesh):
    return jax.shard_map(
        on_device,
        mesh=mesh,
        in_specs=(
            P(("group", "patch"), None),
            P(("group", "patch"), ("visit", "band"), None),
            P(("group", "patch"), ("visit", "band")),
            P(("group", "patch"), ("visit", "band")),
            P(),
            P(("group", "visit", "band"), None, None),
            P(("group", "visit", "band"), None),
            P(),
        ),
        out_specs=(
            P(("group", "patch"), ("visit", "band"), None),
            P(("group", "patch", "visit", "band"), None),
        ),
        check_vma=False,
    )
```

```python
import functools

import jax
import jax.numpy as jnp
from jax import lax
from jax.experimental import pallas as pl
from jax.experimental.pallas import tpu as pltpu
from jax.sharding import PartitionSpec as P

B = 16
CH = B * B
LANES = 128
GROUPS = LANES // B
F32 = jnp.float32
BF16 = jnp.bfloat16


def shifted(shard, axis, by):
    devices = lax.axis_size(axis)
    pairs = [(i, i + by) for i in range(devices) if 0 <= i + by < devices]
    return lax.ppermute(shard, axis, pairs)


def iota(shape, dim):
    return lax.broadcasted_iota(jnp.int32, shape, dim)


LIMIT = 20
VM = pl.BlockSpec(memory_space=pltpu.VMEM)
HBM = pl.BlockSpec(memory_space=pltpu.HBM)


def group_transpose(parts):
    parts = list(parts)
    group = iota(parts[0].shape, 1) // B
    for step in (1, 2, 4):
        low = (group & step) == 0
        for m in range(GROUPS):
            if m & step:
                continue
            x, y = parts[m], parts[m + step]
            parts[m] = jnp.where(low, x, pltpu.roll(y, step * B, 1))
            parts[m + step] = jnp.where(low, pltpu.roll(x, LANES - step * B, 1), y)
    return parts


def conv_blocks(src, count, w_ref, xs, rs, dst, dst_row, batch):
    chunks = src.shape[0]
    blocks = chunks * GROUPS
    for q in range(3):
        xs[q, 0] = jnp.zeros((count, CH), xs.dtype)
        xs[q, blocks + 1] = jnp.zeros((count, CH), xs.dtype)
    for c in range(chunks):
        for h in range(2):
            rows = [src[c, pl.ds(GROUPS * h + i, count, stride=B), :] for i in range(GROUPS)]
            cols = group_transpose(rows)
            for g in range(GROUPS):
                for q in range(3):
                    moved = cols[g] if q == 1 else pltpu.roll(cols[g], (1 - q) % count, 0)
                    xs[q, 1 + c * GROUPS + g, :, h * LANES : (h + 1) * LANES] = moved.astype(xs.dtype)
    for b in range(0, blocks, batch):
        pieces = [
            xs[qr, b + qc : b + qc + batch].reshape(batch * count, CH).astype(BF16)
            for qr in range(3)
            for qc in range(3)
        ]
        out = jnp.dot(jnp.concatenate(pieces, axis=1), w_ref[...], preferred_element_type=F32)
        rs[b : b + batch] = out.reshape(batch, count, CH)
    for c in range(chunks):
        for h in range(2):
            cols = [rs[c * GROUPS + g, :, h * LANES : (h + 1) * LANES] for g in range(GROUPS)]
            rows = group_transpose(cols)
            for i in range(GROUPS):
                dst[c, pl.ds(dst_row + GROUPS * h + i, count, stride=B), :] = rows[i]


def column(row):
    size = row.shape[1]
    diag = iota((size, size), 0) == iota((size, size), 1)
    return jnp.sum(jnp.where(diag, row, jnp.zeros_like(row)), axis=1, keepdims=True)


def first_kernel(
    off_hbm, live_hbm, t_hbm, sci_hbm, bank_hbm, index_hbm, coeff_hbm, psf_hbm,
    w_ref, pcol_ref, prow_ref, note_ref, ends_ref, m_ref, edge_ref, filt_ref,
    off_ref, live_ref, t_ref, sci_ref, bank_ref, index_ref, coeff_ref, psf_ref, sems,
    src, xs, rs, sci, diff,
):
    pairs = (
        (bank_hbm, bank_ref), (index_hbm, index_ref), (coeff_hbm, coeff_ref), (psf_hbm, psf_ref),
        (off_hbm, off_ref), (live_hbm, live_ref), (t_hbm, t_ref), (sci_hbm, sci_ref),
    )
    copies = [pltpu.make_async_copy(a, b, sems.at[n]) for n, (a, b) in enumerate(pairs)]
    for copy in copies:
        copy.start()
    for copy in copies[:4]:
        copy.wait()
    profs, taps = bank_ref.shape
    half = taps // 2
    delta = B - half
    bank = bank_ref[...]
    index = index_ref[0].astype(F32)
    labels = iota((index.shape[1], profs), 1).astype(F32)
    pick_row = (column(index[0:1]) == labels).astype(F32).astype(BF16)
    pick_col = (column(index[1:2]) == labels).astype(F32).astype(BF16)
    weight = column(coeff_ref[...])
    rowprof = (weight * jnp.dot(pick_row, bank, preferred_element_type=F32)).astype(BF16)
    colprof = jnp.dot(pick_col, bank, preferred_element_type=F32).astype(BF16)
    span = 3 * B
    total = 4 * B * B
    place = (iota((span, taps), 0) - delta == iota((span, taps), 1)).astype(F32).astype(BF16)
    col_t = lax.dot_general(place, colprof, (((1,), (1,)), ((), ())), preferred_element_type=F32).astype(BF16)
    spread = (span - 1 - iota((taps, total), 1) // B - delta == iota((taps, total), 0)).astype(F32).astype(BF16)
    row_rep = jnp.dot(rowprof, spread, preferred_element_type=F32).astype(BF16)
    z = jnp.dot(col_t, row_rep, preferred_element_type=F32)
    lane = iota((span, total), 1)
    for bit in (1, 2, 4, 8):
        z = jnp.where((lane & bit) != 0, pltpu.roll(z, bit, 0), z)
    z = z.astype(BF16)
    for phase in range(GROUPS):
        zp = z if phase == 0 else pltpu.roll(z, total - phase * B, 1)
        for g in range(span):
            start = span - 1 - g
            if start % GROUPS != phase:
                continue
            at = (start // GROUPS) * LANES
            for qc in range(3):
                row = (g // B) * 3 * CH + qc * CH + (g % B) * B
                w_ref[row : row + B, :] = zp[qc * B : (qc + 1) * B, at : at + CH]
    psf = psf_ref[...].astype(F32)
    size = pcol_ref.shape[0]
    blank = jnp.zeros((LANES, LANES), F32)
    bands = {}
    for off in (-1, 0, 1):
        tap = iota((LANES, LANES), 0) + off * LANES - iota((LANES, LANES), 1) + half
        block = blank
        for t in range(taps):
            block = jnp.where(tap == t, psf[:, t : t + 1], block)
        bands[off] = block.astype(BF16)
    for i in range(size // LANES):
        for j in range(size // LANES):
            pcol_ref[i * LANES : (i + 1) * LANES, j * LANES : (j + 1) * LANES] = bands.get(i - j, blank.astype(BF16))
    shape = prow_ref.shape
    tap = iota(shape, 1) - iota(shape, 0) - delta
    block = jnp.zeros(shape, F32)
    for t in range(taps):
        block = jnp.where(tap == t, psf[:, t : t + 1], block)
    prow_ref[...] = block.astype(BF16)
    for copy in copies[4:]:
        copy.wait()
    edge = 2 * B
    rows, cols = t_ref.shape
    lane = iota((1, cols), 1)
    off = off_ref[0, 0]
    note = jnp.where(lane == 0, off // B, jnp.where(lane == 1, off % B, live_ref[0, 0]))
    tail = t_ref[rows - edge : rows, :].astype(F32)
    note_ref[...] = jnp.where(iota((edge, cols), 0) == 0, note.astype(F32), tail).astype(BF16)
    ends_ref[0:edge, :] = t_ref[0:edge, :]
    ends_ref[edge:, :] = t_ref[rows - edge : rows, :]
    to_chunks(src, 0, t_ref[...])
    conv_blocks(src, rows // B, w_ref, xs, rs, m_ref, 0, rs.shape[0] // 2)
    to_chunks(sci, rows, sci_ref[...])
    filter_inner(sci, rows - B - off, off, off + rows, m_ref, pcol_ref, edge_ref, filt_ref, diff)


def to_chunks(dst, dst_row, value):
    value = value.astype(F32)
    rows = value.shape[0]
    for c in range(dst.shape[0]):
        dst[c, dst_row : dst_row + rows, :] = value[:, c * LANES : (c + 1) * LANES]


def tile_diff(sky, m, base, first, last):
    row = iota(m.shape, 0) + (base - B)
    return jnp.where((row >= first) & (row < last), sky - m, 0.0).astype(BF16)


def filter_inner(sci, start, first, last, m_ref, pcol_ref, edge_ref, filt_ref, diff):
    chunks, rows, _ = m_ref.shape
    edge = 2 * B
    for c in range(chunks):
        part = slice(c * LANES, (c + 1) * LANES)
        sky = sci[c, pl.ds(start, rows + edge), :]
        edge_ref[c, 0:edge, :] = sky[0:edge]
        edge_ref[c, edge:, :] = sky[rows:]
        diff[:, part] = tile_diff(sky[edge:rows], m_ref[c, B : rows - B, :], edge, first, last)
    filt_ref[...] = jnp.dot(diff[...], pcol_ref[...], preferred_element_type=F32).astype(BF16)


def read_note(msg_ref):
    note = msg_ref[0:B, 0:LANES].astype(F32)
    return (note[0, 0] * B + note[0, 1]).astype(jnp.int32), note[0, 2]


def before_kernel(msg_ref, sci_ref, m_ref, pcol_ref, edge_ref, filt_ref, sci, diff):
    rows = sci_ref.shape[0]
    off, _ = read_note(msg_ref)
    to_chunks(sci, 0, sci_ref[...])
    filter_inner(sci, rows - B - off, off - rows, off, m_ref, pcol_ref, edge_ref, filt_ref, diff)


def join_kernel(
    note_ref, ends_ref, msg_ref, next_ref, w_ref, pcol_ref, prow_ref, edge_a, edge_b, filt_a, filt_b,
    out_ref, m_ref, src, xs, rs, strip, diff, sides,
):
    rows, cols = next_ref.shape
    edge = 2 * B
    to_chunks(src, 0, msg_ref[...])
    to_chunks(src, edge, ends_ref[...])
    to_chunks(src, 3 * edge, next_ref[0:edge, :])
    conv_blocks(src, 8, w_ref, xs, rs, strip, 0, rs.shape[0])
    m_ref[:, 0:edge, :] = strip[:, B : B + edge, :]
    m_ref[:, edge:, :] = strip[:, 5 * B : 5 * B + edge, :]
    off_a, live_a = read_note(note_ref)
    off_b, live_b = read_note(msg_ref)
    for s, (side, first, last) in enumerate(((edge_a, off_a, off_a + rows), (edge_b, off_b - rows, off_b))):
        for c in range(cols // LANES):
            part = slice(c * LANES, (c + 1) * LANES)
            for k, base in enumerate((0, rows)):
                span = slice(k * edge, (k + 1) * edge)
                at = (2 * s + k) * edge
                diff[at : at + edge, part] = tile_diff(side[c, span, :], m_ref[c, span, :], base, first, last)
    sides[...] = jnp.dot(diff[...], pcol_ref[...], preferred_element_type=F32).astype(BF16)
    inner = (filt_a, filt_b)

    def rows_of(s, low, high):
        pieces = []
        for start, stop, ref, at in (
            (0, edge, sides, 2 * s * edge),
            (edge, rows, inner[s], 0),
            (rows, rows + edge, sides, (2 * s + 1) * edge),
        ):
            a, b = max(low, start), min(high, stop)
            if a < b:
                pieces.append(ref[at + a - start : at + b - start, :])
        if high > rows + edge:
            pieces.append(jnp.zeros((high - max(low, rows + edge), cols), BF16))
        return jnp.concatenate(pieces, axis=0)

    share, depth = prow_ref.shape
    prow = prow_ref[...].astype(F32)
    out_row = iota((share, depth), 0)
    lane = iota((B, cols), 1)
    for q in range(out_ref.shape[0]):
        row = out_row + q * share
        left = jnp.where(row >= off_a, prow * live_a, 0.0).astype(BF16)
        right = jnp.where(row < off_b, prow * live_b, 0.0).astype(BF16)
        total = jnp.dot(left, rows_of(0, q * share, q * share + depth), preferred_element_type=F32)
        total += jnp.dot(right, rows_of(1, q * share, q * share + depth), preferred_element_type=F32)
        out_ref[q, 0:share, :] = total.astype(BF16)
        start = jnp.clip(off_a - q * share, 0, share).astype(F32)
        stop = jnp.clip(off_b - q * share, 0, share).astype(F32)
        note = jnp.where(lane == 0, start, jnp.where(lane == 1, live_a, jnp.where(lane == 2, stop, live_b)))
        out_ref[q, share : share + B, :] = note.astype(BF16)


def tile_kernel(sci_hbm, note_ref, next_ref, m1_ref, edge_ref, w_ref, out_ref, src, xs, rs, big, sci_ref, sem):
    rows, cols = next_ref.shape
    copy = pltpu.make_async_copy(sci_hbm, sci_ref, sem)
    copy.start()
    to_chunks(src, 0, next_ref[...])
    conv_blocks(src, rows // B, w_ref, xs, rs, big, rows, rs.shape[0] // 2)
    big[:, 0:B, :] = edge_ref[:, B : 2 * B, :]
    big[:, B : rows - B, :] = m1_ref[:, B : rows - B, :]
    big[:, rows - B : rows + B, :] = edge_ref[:, 2 * B : 4 * B, :]
    copy.wait()
    off, _ = read_note(note_ref)
    for c in range(cols // LANES):
        part = slice(c * LANES, (c + 1) * LANES)
        out_ref[:, part] = (sci_ref[:, part].astype(F32) - big[c, pl.ds(off, rows), :]).astype(BF16)


def coadd_kernel(recv_ref, out_ref):
    count, padded, cols = recv_ref.shape
    share = padded - B
    row = iota((share, LANES), 0).astype(F32)
    accum = jnp.zeros((share, cols), F32)
    cover = jnp.zeros((share, LANES), F32)
    for n in range(count):
        accum += recv_ref[n, 0:share, :].astype(F32)
        note = recv_ref[n, share : share + B, 0:LANES].astype(F32)[0:1, :]
        cover += jnp.where(row >= note[:, 0:1], note[:, 1:2], 0.0)
        cover += jnp.where(row < note[:, 2:3], note[:, 3:4], 0.0)
    scale = lax.rsqrt(jnp.maximum(cover, 1.0))
    for c in range(cols // LANES):
        part = slice(c * LANES, (c + 1) * LANES)
        out_ref[:, part] = accum[:, part] * scale


def in_hbm(*arrays):
    return [pltpu.with_memory_space_constraint(x, pltpu.HBM) for x in arrays]


def call(body, shapes, specs, scratch, flops, name, limit=LIMIT):
    return pl.pallas_call(
        body,
        out_shape=shapes,
        in_specs=specs,
        out_specs=jax.tree.map(lambda _: VM, shapes),
        scratch_shapes=scratch,
        compiler_params=pltpu.CompilerParams(vmem_limit_bytes=limit * 1024 * 1024),
        cost_estimate=pl.CostEstimate(flops=flops, bytes_accessed=1 << 21, transcendentals=0),
        name=name,
    )


def on_device(template, science, offsets, live_flags, bank, basis_index, coeff, psf_profile):
    rows, cols = template.shape
    sharers = lax.axis_size("visit") * lax.axis_size("band")
    share = rows // sharers
    chunks, blocks = cols // LANES, cols // B
    edge = 2 * B
    inner = rows - edge
    before = shifted(science, "patch", 1)[:, 0, :]
    following = shifted(template, "patch", -1)

    sds = jax.ShapeDtypeStruct
    deep = 9 * CH
    depth = -(-(share + edge) // LANES) * LANES
    sci = science[:, 0, :]
    taps = psf_profile.shape[0]
    index = jnp.swapaxes(basis_index, 1, 2)
    count = rows // B
    conv_scratch = [
        pltpu.VMEM((chunks, rows, LANES), F32),
        pltpu.VMEM((3, blocks + 2, count, CH), BF16),
        pltpu.VMEM((blocks, count, CH), F32),
    ]
    conv_flops = 2 * rows * cols * deep
    sky_scratch = [pltpu.VMEM((chunks, 2 * rows + B, LANES), F32), pltpu.VMEM((inner, cols), BF16)]
    sides = (sds((chunks, 2 * edge, LANES), F32), sds((inner, cols), BF16))
    w, pcol, prow, note, ends, m1, edge_a, filt_a = call(
        first_kernel,
        (
            sds((deep, CH), BF16), sds((cols, cols), BF16), sds((share, depth), BF16), sds((edge, cols), BF16),
            sds((2 * edge, cols), BF16), sds((chunks, rows, LANES), F32),
        ) + sides,
        [HBM] * 8,
        [
            pltpu.SMEM((1, 1), jnp.int32), pltpu.SMEM((1, 1), jnp.int32), pltpu.VMEM((rows, cols), BF16),
            pltpu.VMEM((rows, cols), BF16), pltpu.VMEM(bank.shape, BF16), pltpu.VMEM(index.shape, jnp.int32),
            pltpu.VMEM(coeff.shape, F32), pltpu.VMEM((1, taps), BF16), pltpu.SemaphoreType.DMA((8,)),
        ] + conv_scratch + sky_scratch,
        conv_flops, "first",
    )(offsets, live_flags, *in_hbm(template, sci, bank, index, coeff, psf_profile[None]))
    msg = shifted(note, "patch", 1)
    edge_b, filt_b = call(before_kernel, sides, [VM] * 4, sky_scratch, 1 << 28, "before")(msg, before, m1, pcol)
    out, m_edge = call(
        join_kernel,
        (sds((sharers, share + B, cols), BF16), sds((chunks, 2 * edge, LANES), F32)),
        [VM] * 11,
        [
            pltpu.VMEM((chunks, 8 * B, LANES), F32),
            pltpu.VMEM((3, blocks + 2, 8, CH), F32),
            pltpu.VMEM((blocks, 8, CH), F32),
            pltpu.VMEM((chunks, 8 * B, LANES), F32),
            pltpu.VMEM((4 * edge, cols), BF16),
            pltpu.VMEM((4 * edge, cols), BF16),
        ],
        1 << 29, "join",
    )(note, ends, msg, following, w, pcol, prow, edge_a, edge_b, filt_a, filt_b)
    recv = lax.all_to_all(out, ("visit", "band"), 0, 0, tiled=True)
    difference = call(
        tile_kernel, sds((rows, cols), BF16), [HBM] + [VM] * 5,
        conv_scratch + [
            pltpu.VMEM((chunks, 2 * rows, LANES), F32), pltpu.VMEM((rows, cols), BF16), pltpu.SemaphoreType.DMA,
        ],
        conv_flops, "tile",
    )(*in_hbm(sci), note, following, m1, m_edge, w)
    detection = call(coadd_kernel, sds((share, cols), F32), [VM], [], 1 << 20, "coadd")(recv)
    return (difference[:, None, :], detection)


def solution(mesh):
    return jax.shard_map(
        on_device,
        mesh=mesh,
        in_specs=(
            P(("group", "patch"), None),
            P(("group", "patch"), ("visit", "band"), None),
            P(("group", "patch"), ("visit", "band")),
            P(("group", "patch"), ("visit", "band")),
            P(),
            P(("group", "visit", "band"), None, None),
            P(("group", "visit", "band"), None),
            P(),
        ),
        out_specs=(
            P(("group", "patch"), ("visit", "band"), None),
            P(("group", "patch", "visit", "band"), None),
        ),
        check_vma=False,
    )
```

```python
import functools

import jax
import jax.numpy as jnp
from jax import lax
from jax.experimental import pallas as pl
from jax.experimental.pallas import tpu as pltpu
from jax.sharding import PartitionSpec as P

B = 16
CH = B * B
LANES = 128
GROUPS = LANES // B
F32 = jnp.float32
BF16 = jnp.bfloat16


def shifted(shard, axis, by):
    devices = lax.axis_size(axis)
    pairs = [(i, i + by) for i in range(devices) if 0 <= i + by < devices]
    return lax.ppermute(shard, axis, pairs)


def iota(shape, dim):
    return lax.broadcasted_iota(jnp.int32, shape, dim)


LIMIT = 20
VM = pl.BlockSpec(memory_space=pltpu.VMEM)
HBM = pl.BlockSpec(memory_space=pltpu.HBM)


def group_transpose(parts):
    parts = list(parts)
    group = iota(parts[0].shape, 1) // B
    for step in (1, 2, 4):
        low = (group & step) == 0
        for m in range(GROUPS):
            if m & step:
                continue
            x, y = parts[m], parts[m + step]
            parts[m] = jnp.where(low, x, pltpu.roll(y, step * B, 1))
            parts[m + step] = jnp.where(low, pltpu.roll(x, LANES - step * B, 1), y)
    return parts


def conv_blocks(src, count, w_ref, xs, dst, dst_row):
    chunks = src.shape[0]
    blocks = chunks * GROUPS
    wide = count // 8

    def load(c):
        for h in range(2):
            rows = [
                jnp.concatenate(
                    [src[c, pl.ds(B * v + GROUPS * h + i, 8, stride=B * wide), :] for v in range(wide)], axis=0
                )
                for i in range(GROUPS)
            ]
            part = slice(h * LANES, (h + 1) * LANES)
            for g, here in enumerate(group_transpose(rows)):
                at = 1 + c * GROUPS + g
                after = pltpu.roll(here[0:8], 7, 0)
                prior = pltpu.roll(here[count - 8 :], 1, 0)
                if wide > 1:
                    after = jnp.concatenate([here[8:], after], axis=0)
                    prior = jnp.concatenate([prior, here[: count - 8]], axis=0)
                xs[0, at, :, part] = prior.astype(xs.dtype)
                xs[1, at, :, part] = here.astype(xs.dtype)
                xs[2, at, :, part] = after.astype(xs.dtype)

    def solve(c):
        b = c * GROUPS
        pieces = [
            xs[qr, b + qc : b + qc + GROUPS].reshape(GROUPS * count, CH).astype(BF16)
            for qr in range(3)
            for qc in range(3)
        ]
        out = jnp.dot(jnp.concatenate(pieces, axis=1), w_ref[...], preferred_element_type=F32)
        for h in range(2):
            part = slice(h * LANES, (h + 1) * LANES)
            rows = group_transpose([out[g * count : (g + 1) * count, part] for g in range(GROUPS)])
            for i in range(GROUPS):
                for v in range(wide):
                    dst[c, pl.ds(dst_row + B * v + GROUPS * h + i, 8, stride=B * wide), :] = rows[i][8 * v : 8 * v + 8]

    for q in range(3):
        xs[q, 0] = jnp.zeros((count, CH), xs.dtype)
        xs[q, blocks + 1] = jnp.zeros((count, CH), xs.dtype)
    load(0)
    for c in range(chunks):
        if c + 1 < chunks:
            load(c + 1)
        solve(c)


def column(row):
    size = row.shape[1]
    diag = iota((size, size), 0) == iota((size, size), 1)
    return jnp.sum(jnp.where(diag, row, jnp.zeros_like(row)), axis=1, keepdims=True)


def first_kernel(
    off_hbm, live_hbm, t_hbm, sci_hbm, bank_hbm, index_hbm, coeff_hbm, psf_hbm,
    w_ref, pcol_ref, prow_ref, note_ref, ends_ref, sci_ref, m_ref, edge_ref, filt_ref,
    off_ref, live_ref, t_ref, bank_ref, index_ref, coeff_ref, psf_ref, sems,
    src, xs, sci, diff,
):
    pairs = (
        (bank_hbm, bank_ref), (index_hbm, index_ref), (coeff_hbm, coeff_ref), (psf_hbm, psf_ref),
        (off_hbm, off_ref), (live_hbm, live_ref), (t_hbm, t_ref), (sci_hbm, sci_ref),
    )
    copies = [pltpu.make_async_copy(a, b, sems.at[n]) for n, (a, b) in enumerate(pairs)]
    for copy in copies:
        copy.start()
    for copy in copies[:4]:
        copy.wait()
    profs, taps = bank_ref.shape
    half = taps // 2
    delta = B - half
    bank = bank_ref[...]
    index = index_ref[0].astype(F32)
    labels = iota((index.shape[1], profs), 1).astype(F32)
    pick_row = (column(index[0:1]) == labels).astype(F32).astype(BF16)
    pick_col = (column(index[1:2]) == labels).astype(F32).astype(BF16)
    weight = column(coeff_ref[...])
    rowprof = (weight * jnp.dot(pick_row, bank, preferred_element_type=F32)).astype(BF16)
    colprof = jnp.dot(pick_col, bank, preferred_element_type=F32).astype(BF16)
    span = 3 * B
    total = 4 * B * B
    place = (iota((span, taps), 0) - delta == iota((span, taps), 1)).astype(F32).astype(BF16)
    col_t = lax.dot_general(place, colprof, (((1,), (1,)), ((), ())), preferred_element_type=F32).astype(BF16)
    spread = (span - 1 - iota((taps, total), 1) // B - delta == iota((taps, total), 0)).astype(F32).astype(BF16)
    row_rep = jnp.dot(rowprof, spread, preferred_element_type=F32).astype(BF16)
    z = jnp.dot(col_t, row_rep, preferred_element_type=F32)
    lane = iota((span, total), 1)
    for bit in (1, 2, 4, 8):
        z = jnp.where((lane & bit) != 0, pltpu.roll(z, bit, 0), z)
    z = z.astype(BF16)
    for phase in range(GROUPS):
        zp = z if phase == 0 else pltpu.roll(z, total - phase * B, 1)
        for g in range(span):
            start = span - 1 - g
            if start % GROUPS != phase:
                continue
            at = (start // GROUPS) * LANES
            for qc in range(3):
                row = (g // B) * 3 * CH + qc * CH + (g % B) * B
                w_ref[row : row + B, :] = zp[qc * B : (qc + 1) * B, at : at + CH]
    psf = psf_ref[...].astype(F32)
    size = pcol_ref.shape[0]
    blank = jnp.zeros((LANES, LANES), F32)
    bands = {}
    for off in (-1, 0, 1):
        tap = iota((LANES, LANES), 0) + off * LANES - iota((LANES, LANES), 1) + half
        block = blank
        for t in range(taps):
            block = jnp.where(tap == t, psf[:, t : t + 1], block)
        bands[off] = block.astype(BF16)
    for i in range(size // LANES):
        for j in range(size // LANES):
            pcol_ref[i * LANES : (i + 1) * LANES, j * LANES : (j + 1) * LANES] = bands.get(i - j, blank.astype(BF16))
    shape = prow_ref.shape
    tap = iota(shape, 1) - iota(shape, 0) - delta
    block = jnp.zeros(shape, F32)
    for t in range(taps):
        block = jnp.where(tap == t, psf[:, t : t + 1], block)
    prow_ref[...] = block.astype(BF16)
    for copy in copies[4:]:
        copy.wait()
    edge = 2 * B
    rows, cols = t_ref.shape
    lane = iota((1, cols), 1)
    off = off_ref[0, 0]
    note = jnp.where(lane == 0, off // B, jnp.where(lane == 1, off % B, live_ref[0, 0]))
    tail = t_ref[rows - edge : rows, :].astype(F32)
    note_ref[...] = jnp.where(iota((edge, cols), 0) == 0, note.astype(F32), tail).astype(BF16)
    ends_ref[0:edge, :] = t_ref[0:edge, :]
    ends_ref[edge:, :] = t_ref[rows - edge : rows, :]
    to_chunks(src, 0, t_ref[...])
    conv_blocks(src, rows // B, w_ref, xs, m_ref, 0)
    to_chunks(sci, rows, sci_ref[...])
    filter_inner(sci, rows - B - off, off, off + rows, m_ref, pcol_ref, edge_ref, filt_ref, diff)


def to_chunks(dst, dst_row, value):
    value = value.astype(F32)
    rows = value.shape[0]
    for c in range(dst.shape[0]):
        dst[c, dst_row : dst_row + rows, :] = value[:, c * LANES : (c + 1) * LANES]


def tile_diff(sky, m, base, first, last):
    row = iota(m.shape, 0) + (base - B)
    return jnp.where((row >= first) & (row < last), sky - m, 0.0).astype(BF16)


def filter_inner(sci, start, first, last, m_ref, pcol_ref, edge_ref, filt_ref, diff):
    chunks, rows, _ = m_ref.shape
    edge = 2 * B
    for c in range(chunks):
        part = slice(c * LANES, (c + 1) * LANES)
        sky = sci[c, pl.ds(start, rows + edge), :]
        edge_ref[c, 0:edge, :] = sky[0:edge]
        edge_ref[c, edge:, :] = sky[rows:]
        diff[:, part] = tile_diff(sky[edge:rows], m_ref[c, B : rows - B, :], edge, first, last)
    filt_ref[...] = jnp.dot(diff[...], pcol_ref[...], preferred_element_type=F32).astype(BF16)


def read_note(msg_ref):
    note = msg_ref[0:B, 0:LANES].astype(F32)
    return (note[0, 0] * B + note[0, 1]).astype(jnp.int32), note[0, 2]


def before_kernel(msg_ref, sci_ref, m_ref, pcol_ref, edge_ref, filt_ref, sci, diff):
    rows = sci_ref.shape[0]
    off, _ = read_note(msg_ref)
    to_chunks(sci, 0, sci_ref[...])
    filter_inner(sci, rows - B - off, off - rows, off, m_ref, pcol_ref, edge_ref, filt_ref, diff)


def join_kernel(
    note_ref, ends_ref, msg_ref, next_ref, w_ref, pcol_ref, prow_ref, edge_a, edge_b, filt_a, filt_b,
    out_ref, m_ref, src, xs, strip, diff, sides,
):
    rows, cols = next_ref.shape
    edge = 2 * B
    to_chunks(src, 0, msg_ref[...])
    to_chunks(src, edge, ends_ref[...])
    to_chunks(src, 3 * edge, next_ref[0:edge, :])
    conv_blocks(src, 8, w_ref, xs, strip, 0)
    m_ref[:, 0:edge, :] = strip[:, B : B + edge, :]
    m_ref[:, edge:, :] = strip[:, 5 * B : 5 * B + edge, :]
    off_a, live_a = read_note(note_ref)
    off_b, live_b = read_note(msg_ref)
    for s, (side, first, last) in enumerate(((edge_a, off_a, off_a + rows), (edge_b, off_b - rows, off_b))):
        for c in range(cols // LANES):
            part = slice(c * LANES, (c + 1) * LANES)
            for k, base in enumerate((0, rows)):
                span = slice(k * edge, (k + 1) * edge)
                at = (2 * s + k) * edge
                diff[at : at + edge, part] = tile_diff(side[c, span, :], m_ref[c, span, :], base, first, last)
    sides[...] = jnp.dot(diff[...], pcol_ref[...], preferred_element_type=F32).astype(BF16)
    inner = (filt_a, filt_b)

    def rows_of(s, low, high):
        pieces = []
        for start, stop, ref, at in (
            (0, edge, sides, 2 * s * edge),
            (edge, rows, inner[s], 0),
            (rows, rows + edge, sides, (2 * s + 1) * edge),
        ):
            a, b = max(low, start), min(high, stop)
            if a < b:
                pieces.append(ref[at + a - start : at + b - start, :])
        if high > rows + edge:
            pieces.append(jnp.zeros((high - max(low, rows + edge), cols), BF16))
        return jnp.concatenate(pieces, axis=0)

    share, depth = prow_ref.shape
    prow = prow_ref[...].astype(F32)
    out_row = iota((share, depth), 0)
    lane = iota((B, cols), 1)
    for q in range(out_ref.shape[0]):
        row = out_row + q * share
        left = jnp.where(row >= off_a, prow * live_a, 0.0).astype(BF16)
        right = jnp.where(row < off_b, prow * live_b, 0.0).astype(BF16)
        total = jnp.dot(left, rows_of(0, q * share, q * share + depth), preferred_element_type=F32)
        total += jnp.dot(right, rows_of(1, q * share, q * share + depth), preferred_element_type=F32)
        out_ref[q, 0:share, :] = total.astype(BF16)
        start = jnp.clip(off_a - q * share, 0, share).astype(F32)
        stop = jnp.clip(off_b - q * share, 0, share).astype(F32)
        note = jnp.where(lane == 0, start, jnp.where(lane == 1, live_a, jnp.where(lane == 2, stop, live_b)))
        out_ref[q, share : share + B, :] = note.astype(BF16)


def tile_kernel(sci_ref, note_ref, next_ref, m1_ref, edge_ref, w_ref, out_ref, src, xs, big):
    rows, cols = next_ref.shape
    to_chunks(src, 0, next_ref[...])
    conv_blocks(src, rows // B, w_ref, xs, big, rows)
    big[:, 0:B, :] = edge_ref[:, B : 2 * B, :]
    big[:, B : rows - B, :] = m1_ref[:, B : rows - B, :]
    big[:, rows - B : rows + B, :] = edge_ref[:, 2 * B : 4 * B, :]
    off, _ = read_note(note_ref)
    for c in range(cols // LANES):
        part = slice(c * LANES, (c + 1) * LANES)
        out_ref[:, part] = (sci_ref[:, part].astype(F32) - big[c, pl.ds(off, rows), :]).astype(BF16)


def coadd_kernel(recv_ref, out_ref):
    count, padded, cols = recv_ref.shape
    share = padded - B
    row = iota((share, LANES), 0).astype(F32)
    accum = jnp.zeros((share, cols), F32)
    cover = jnp.zeros((share, LANES), F32)
    for n in range(count):
        accum += recv_ref[n, 0:share, :].astype(F32)
        note = recv_ref[n, share : share + B, 0:LANES].astype(F32)[0:1, :]
        cover += jnp.where(row >= note[:, 0:1], note[:, 1:2], 0.0)
        cover += jnp.where(row < note[:, 2:3], note[:, 3:4], 0.0)
    scale = lax.rsqrt(jnp.maximum(cover, 1.0))
    for c in range(cols // LANES):
        part = slice(c * LANES, (c + 1) * LANES)
        out_ref[:, part] = accum[:, part] * scale


def in_hbm(*arrays):
    return [pltpu.with_memory_space_constraint(x, pltpu.HBM) for x in arrays]


def call(body, shapes, specs, scratch, flops, name, limit=LIMIT):
    return pl.pallas_call(
        body,
        out_shape=shapes,
        in_specs=specs,
        out_specs=jax.tree.map(lambda _: VM, shapes),
        scratch_shapes=scratch,
        compiler_params=pltpu.CompilerParams(vmem_limit_bytes=limit * 1024 * 1024),
        cost_estimate=pl.CostEstimate(flops=flops, bytes_accessed=1 << 21, transcendentals=0),
        name=name,
    )


def on_device(template, science, offsets, live_flags, bank, basis_index, coeff, psf_profile):
    rows, cols = template.shape
    sharers = lax.axis_size("visit") * lax.axis_size("band")
    share = rows // sharers
    chunks, blocks = cols // LANES, cols // B
    edge = 2 * B
    inner = rows - edge
    before = shifted(science, "patch", 1)[:, 0, :]
    following = shifted(template, "patch", -1)

    sds = jax.ShapeDtypeStruct
    deep = 9 * CH
    depth = -(-(share + edge) // LANES) * LANES
    sci = science[:, 0, :]
    taps = psf_profile.shape[0]
    index = jnp.swapaxes(basis_index, 1, 2)
    count = rows // B
    conv_scratch = [
        pltpu.VMEM((chunks, rows, LANES), F32),
        pltpu.VMEM((3, blocks + 2, count, CH), BF16),
    ]
    conv_flops = 2 * rows * cols * deep
    sky_scratch = [pltpu.VMEM((chunks, 2 * rows + B, LANES), F32), pltpu.VMEM((inner, cols), BF16)]
    sides = (sds((chunks, 2 * edge, LANES), F32), sds((inner, cols), BF16))
    w, pcol, prow, note, ends, tile, m1, edge_a, filt_a = call(
        first_kernel,
        (
            sds((deep, CH), BF16), sds((cols, cols), BF16), sds((share, depth), BF16), sds((edge, cols), BF16),
            sds((2 * edge, cols), BF16), sds((rows, cols), BF16), sds((chunks, rows, LANES), F32),
        ) + sides,
        [HBM] * 8,
        [
            pltpu.SMEM((1, 1), jnp.int32), pltpu.SMEM((1, 1), jnp.int32), pltpu.VMEM((rows, cols), BF16),
            pltpu.VMEM(bank.shape, BF16), pltpu.VMEM(index.shape, jnp.int32),
            pltpu.VMEM(coeff.shape, F32), pltpu.VMEM((1, taps), BF16), pltpu.SemaphoreType.DMA((8,)),
        ] + conv_scratch + sky_scratch,
        conv_flops, "first",
    )(offsets, live_flags, *in_hbm(template, sci, bank, index, coeff, psf_profile[None]))
    msg = shifted(note, "patch", 1)
    edge_b, filt_b = call(before_kernel, sides, [VM] * 4, sky_scratch, 1 << 28, "before")(msg, before, m1, pcol)
    out, m_edge = call(
        join_kernel,
        (sds((sharers, share + B, cols), BF16), sds((chunks, 2 * edge, LANES), F32)),
        [VM] * 11,
        [
            pltpu.VMEM((chunks, 8 * B, LANES), F32),
            pltpu.VMEM((3, blocks + 2, 8, CH), F32),
            pltpu.VMEM((chunks, 8 * B, LANES), F32),
            pltpu.VMEM((4 * edge, cols), BF16),
            pltpu.VMEM((4 * edge, cols), BF16),
        ],
        1 << 29, "join",
    )(note, ends, msg, following, w, pcol, prow, edge_a, edge_b, filt_a, filt_b)
    recv = lax.all_to_all(out, ("visit", "band"), 0, 0, tiled=True)
    difference = call(
        tile_kernel, sds((rows, cols), BF16), [VM] * 6,
        conv_scratch + [pltpu.VMEM((chunks, 2 * rows, LANES), F32)], conv_flops, "tile",
    )(tile, note, following, m1, m_edge, w)
    detection = call(coadd_kernel, sds((share, cols), F32), [VM], [], 1 << 20, "coadd")(recv)
    return (difference[:, None, :], detection)


def solution(mesh):
    return jax.shard_map(
        on_device,
        mesh=mesh,
        in_specs=(
            P(("group", "patch"), None),
            P(("group", "patch"), ("visit", "band"), None),
            P(("group", "patch"), ("visit", "band")),
            P(("group", "patch"), ("visit", "band")),
            P(),
            P(("group", "visit", "band"), None, None),
            P(("group", "visit", "band"), None),
            P(),
        ),
        out_specs=(
            P(("group", "patch"), ("visit", "band"), None),
            P(("group", "patch", "visit", "band"), None),
        ),
        check_vma=False,
    )
```

```python
import functools

import jax
import jax.numpy as jnp
from jax import lax
from jax.experimental import pallas as pl
from jax.experimental.pallas import tpu as pltpu
from jax.sharding import PartitionSpec as P

B = 16
CH = B * B
LANES = 128
GROUPS = LANES // B
F32 = jnp.float32
BF16 = jnp.bfloat16


def shifted(shard, axis, by):
    devices = lax.axis_size(axis)
    pairs = [(i, i + by) for i in range(devices) if 0 <= i + by < devices]
    return lax.ppermute(shard, axis, pairs)


def partner(me, k, count):
    return me ^ k if count & (count - 1) == 0 else (me + k) % count


def iota(shape, dim):
    return lax.broadcasted_iota(jnp.int32, shape, dim)


LIMIT = 10
VM = pl.BlockSpec(memory_space=pltpu.VMEM)
HBM = pl.BlockSpec(memory_space=pltpu.HBM)


def group_transpose(parts):
    parts = list(parts)
    group = iota(parts[0].shape, 1) // B
    for step in (1, 2, 4):
        low = (group & step) == 0
        for m in range(GROUPS):
            if m & step:
                continue
            x, y = parts[m], parts[m + step]
            parts[m] = jnp.where(low, x, pltpu.roll(y, step * B, 1))
            parts[m + step] = jnp.where(low, pltpu.roll(x, LANES - step * B, 1), y)
    return parts


def conv_blocks(src, count, w_ref, xs, dst, dst_row):
    chunks = src.shape[0]
    blocks = chunks * GROUPS
    wide = count // 8

    def load(c):
        for h in range(2):
            rows = [
                jnp.concatenate(
                    [src[c, pl.ds(B * v + GROUPS * h + i, 8, stride=B * wide), :] for v in range(wide)], axis=0
                )
                for i in range(GROUPS)
            ]
            part = slice(h * LANES, (h + 1) * LANES)
            for g, here in enumerate(group_transpose(rows)):
                at = 1 + c * GROUPS + g
                after = pltpu.roll(here[0:8], 7, 0)
                prior = pltpu.roll(here[count - 8 :], 1, 0)
                if wide > 1:
                    after = jnp.concatenate([here[8:], after], axis=0)
                    prior = jnp.concatenate([prior, here[: count - 8]], axis=0)
                xs[0, at, :, part] = prior.astype(xs.dtype)
                xs[1, at, :, part] = here.astype(xs.dtype)
                xs[2, at, :, part] = after.astype(xs.dtype)

    def solve(c):
        b = c * GROUPS
        pieces = [
            xs[qr, b + qc : b + qc + GROUPS].reshape(GROUPS * count, CH).astype(BF16)
            for qr in range(3)
            for qc in range(3)
        ]
        out = jnp.dot(jnp.concatenate(pieces, axis=1), w_ref[...], preferred_element_type=F32)
        for h in range(2):
            part = slice(h * LANES, (h + 1) * LANES)
            rows = group_transpose([out[g * count : (g + 1) * count, part] for g in range(GROUPS)])
            for i in range(GROUPS):
                for v in range(wide):
                    dst[c, pl.ds(dst_row + B * v + GROUPS * h + i, 8, stride=B * wide), :] = rows[i][8 * v : 8 * v + 8]

    for q in range(3):
        xs[q, 0] = jnp.zeros((count, CH), xs.dtype)
        xs[q, blocks + 1] = jnp.zeros((count, CH), xs.dtype)
    load(0)
    for c in range(chunks):
        if c + 1 < chunks:
            load(c + 1)
        solve(c)


def column(row):
    size = row.shape[1]
    diag = iota((size, size), 0) == iota((size, size), 1)
    return jnp.sum(jnp.where(diag, row, jnp.zeros_like(row)), axis=1, keepdims=True)


def first_kernel(
    off_hbm, live_hbm, t_hbm, sci_hbm, bank_hbm, index_hbm, coeff_hbm, psf_hbm,
    w_ref, pcol_ref, prow_ref, note_ref, ends_ref, sci_ref, m_ref, edge_ref, filt_ref,
    off_ref, live_ref, t_ref, bank_ref, index_ref, coeff_ref, psf_ref, sems,
    src, xs, sci, diff,
):
    pairs = (
        (bank_hbm, bank_ref), (index_hbm, index_ref), (coeff_hbm, coeff_ref), (psf_hbm, psf_ref),
        (off_hbm, off_ref), (live_hbm, live_ref), (t_hbm, t_ref), (sci_hbm, sci_ref),
    )
    copies = [pltpu.make_async_copy(a, b, sems.at[n]) for n, (a, b) in enumerate(pairs)]
    for copy in copies:
        copy.start()
    for copy in copies[:4]:
        copy.wait()
    profs, taps = bank_ref.shape
    half = taps // 2
    delta = B - half
    bank = bank_ref[...]
    index = index_ref[0].astype(F32)
    labels = iota((index.shape[1], profs), 1).astype(F32)
    pick_row = (column(index[0:1]) == labels).astype(F32).astype(BF16)
    pick_col = (column(index[1:2]) == labels).astype(F32).astype(BF16)
    weight = column(coeff_ref[...])
    rowprof = (weight * jnp.dot(pick_row, bank, preferred_element_type=F32)).astype(BF16)
    colprof = jnp.dot(pick_col, bank, preferred_element_type=F32).astype(BF16)
    span = 3 * B
    total = 4 * B * B
    place = (iota((span, taps), 0) - delta == iota((span, taps), 1)).astype(F32).astype(BF16)
    col_t = lax.dot_general(place, colprof, (((1,), (1,)), ((), ())), preferred_element_type=F32).astype(BF16)
    spread = (span - 1 - iota((taps, total), 1) // B - delta == iota((taps, total), 0)).astype(F32).astype(BF16)
    row_rep = jnp.dot(rowprof, spread, preferred_element_type=F32).astype(BF16)
    z = jnp.dot(col_t, row_rep, preferred_element_type=F32)
    lane = iota((span, total), 1)
    for bit in (1, 2, 4, 8):
        z = jnp.where((lane & bit) != 0, pltpu.roll(z, bit, 0), z)
    z = z.astype(BF16)
    for phase in range(GROUPS):
        zp = z if phase == 0 else pltpu.roll(z, total - phase * B, 1)
        for g in range(span):
            start = span - 1 - g
            if start % GROUPS != phase:
                continue
            at = (start // GROUPS) * LANES
            for qc in range(3):
                row = (g // B) * 3 * CH + qc * CH + (g % B) * B
                w_ref[row : row + B, :] = zp[qc * B : (qc + 1) * B, at : at + CH]
    psf = psf_ref[...].astype(F32)
    size = pcol_ref.shape[0]
    blank = jnp.zeros((LANES, LANES), F32)
    bands = {}
    for off in (-1, 0, 1):
        tap = iota((LANES, LANES), 0) + off * LANES - iota((LANES, LANES), 1) + half
        block = blank
        for t in range(taps):
            block = jnp.where(tap == t, psf[:, t : t + 1], block)
        bands[off] = block.astype(BF16)
    for i in range(size // LANES):
        for j in range(size // LANES):
            pcol_ref[i * LANES : (i + 1) * LANES, j * LANES : (j + 1) * LANES] = bands.get(i - j, blank.astype(BF16))
    shape = prow_ref.shape
    tap = iota(shape, 1) - iota(shape, 0) - delta
    block = jnp.zeros(shape, F32)
    for t in range(taps):
        block = jnp.where(tap == t, psf[:, t : t + 1], block)
    prow_ref[...] = block.astype(BF16)
    for copy in copies[4:]:
        copy.wait()
    edge = 2 * B
    rows, cols = t_ref.shape
    lane = iota((1, cols), 1)
    off = off_ref[0, 0]
    note = jnp.where(lane == 0, off // B, jnp.where(lane == 1, off % B, live_ref[0, 0]))
    tail = t_ref[rows - edge : rows, :].astype(F32)
    note_ref[...] = jnp.where(iota((edge, cols), 0) == 0, note.astype(F32), tail).astype(BF16)
    ends_ref[0:edge, :] = t_ref[0:edge, :]
    ends_ref[edge:, :] = t_ref[rows - edge : rows, :]
    to_chunks(src, 0, t_ref[...])
    conv_blocks(src, rows // B, w_ref, xs, m_ref, 0)
    to_chunks(sci, rows, sci_ref[...])
    filter_inner(sci, rows - B - off, off, off + rows, m_ref, pcol_ref, edge_ref, filt_ref, diff)


def to_chunks(dst, dst_row, value):
    value = value.astype(F32)
    rows = value.shape[0]
    for c in range(dst.shape[0]):
        dst[c, dst_row : dst_row + rows, :] = value[:, c * LANES : (c + 1) * LANES]


def tile_diff(sky, m, base, first, last):
    row = iota(m.shape, 0) + (base - B)
    return jnp.where((row >= first) & (row < last), sky - m, 0.0).astype(BF16)


def filter_inner(sci, start, first, last, m_ref, pcol_ref, edge_ref, filt_ref, diff):
    chunks, rows, _ = m_ref.shape
    edge = 2 * B
    for c in range(chunks):
        part = slice(c * LANES, (c + 1) * LANES)
        sky = sci[c, pl.ds(start, rows + edge), :]
        edge_ref[c, 0:edge, :] = sky[0:edge]
        edge_ref[c, edge:, :] = sky[rows:]
        diff[:, part] = tile_diff(sky[edge:rows], m_ref[c, B : rows - B, :], edge, first, last)
    filt_ref[...] = jnp.dot(diff[...], pcol_ref[...], preferred_element_type=F32).astype(BF16)


def read_note(msg_ref):
    note = msg_ref[0:B, 0:LANES].astype(F32)
    return (note[0, 0] * B + note[0, 1]).astype(jnp.int32), note[0, 2]


def before_kernel(msg_ref, sci_ref, m_ref, pcol_ref, edge_ref, filt_ref, sci, diff):
    rows = sci_ref.shape[0]
    off, _ = read_note(msg_ref)
    to_chunks(sci, 0, sci_ref[...])
    filter_inner(sci, rows - B - off, off - rows, off, m_ref, pcol_ref, edge_ref, filt_ref, diff)


def join_kernel(
    note_ref, ends_ref, msg_ref, next_ref, w_ref, pcol_ref, prow_ref, edge_a, edge_b, filt_a, filt_b,
    *rest,
):
    *outs, m_ref, src, xs, strip, diff, filt = rest
    rows, cols = next_ref.shape
    edge = 2 * B
    to_chunks(src, 0, msg_ref[...])
    to_chunks(src, edge, ends_ref[...])
    to_chunks(src, 3 * edge, next_ref[0:edge, :])
    conv_blocks(src, 8, w_ref, xs, strip, 0)
    m_ref[:, 0:edge, :] = strip[:, B : B + edge, :]
    m_ref[:, edge:, :] = strip[:, 5 * B : 5 * B + edge, :]
    off_a, live_a = read_note(note_ref)
    off_b, live_b = read_note(msg_ref)
    for s, (side, first, last) in enumerate(((edge_a, off_a, off_a + rows), (edge_b, off_b - rows, off_b))):
        for c in range(cols // LANES):
            part = slice(c * LANES, (c + 1) * LANES)
            for k, base in enumerate((0, rows)):
                span = slice(k * edge, (k + 1) * edge)
                at = (2 * s + k) * edge
                diff[at : at + edge, part] = tile_diff(side[c, span, :], m_ref[c, span, :], base, first, last)
    sides = jnp.dot(diff[...], pcol_ref[...], preferred_element_type=F32).astype(BF16)
    for s, inner in enumerate((filt_a, filt_b)):
        filt[s, 0:edge, :] = sides[2 * s * edge : (2 * s + 1) * edge]
        filt[s, edge:rows, :] = inner[...]
        filt[s, rows : rows + edge, :] = sides[(2 * s + 1) * edge : (2 * s + 2) * edge]
        filt[s, rows + edge :, :] = jnp.zeros((filt.shape[1] - rows - edge, cols), BF16)
    share, depth = prow_ref.shape
    prow = prow_ref[...].astype(F32)
    out_row = iota((share, depth), 0)
    lane = iota((B, cols), 1)
    me = lax.axis_index("visit") * lax.axis_size("band") + lax.axis_index("band")
    for k, out_ref in enumerate(outs):
        base = partner(me, k, len(outs)) * share
        row = out_row + base
        left = jnp.where(row >= off_a, prow * live_a, 0.0).astype(BF16)
        right = jnp.where(row < off_b, prow * live_b, 0.0).astype(BF16)
        span = pl.ds(pl.multiple_of(base, B), depth)
        total = jnp.dot(left, filt[0, span, :], preferred_element_type=F32)
        total += jnp.dot(right, filt[1, span, :], preferred_element_type=F32)
        out_ref[0:share, :] = total.astype(BF16)
        start = jnp.clip(off_a - base, 0, share).astype(F32)
        stop = jnp.clip(off_b - base, 0, share).astype(F32)
        note = jnp.where(lane == 0, start, jnp.where(lane == 1, live_a, jnp.where(lane == 2, stop, live_b)))
        out_ref[share : share + B, :] = note.astype(BF16)


def tile_kernel(sci_ref, note_ref, next_ref, m1_ref, edge_ref, w_ref, out_ref, src, xs, big):
    rows, cols = next_ref.shape
    to_chunks(src, 0, next_ref[...])
    conv_blocks(src, rows // B, w_ref, xs, big, rows)
    big[:, 0:B, :] = edge_ref[:, B : 2 * B, :]
    big[:, B : rows - B, :] = m1_ref[:, B : rows - B, :]
    big[:, rows - B : rows + B, :] = edge_ref[:, 2 * B : 4 * B, :]
    off, _ = read_note(note_ref)
    for c in range(cols // LANES):
        part = slice(c * LANES, (c + 1) * LANES)
        out_ref[:, part] = (sci_ref[:, part].astype(F32) - big[c, pl.ds(off, rows), :]).astype(BF16)


def coadd_kernel(*refs):
    *parts, out_ref = refs
    share, cols = out_ref.shape
    row = iota((share, LANES), 0).astype(F32)
    accum = jnp.zeros((share, cols), F32)
    cover = jnp.zeros((share, LANES), F32)
    for part in parts:
        accum += part[0:share, :].astype(F32)
        note = part[share : share + B, 0:LANES].astype(F32)[0:1, :]
        cover += jnp.where(row >= note[:, 0:1], note[:, 1:2], 0.0)
        cover += jnp.where(row < note[:, 2:3], note[:, 3:4], 0.0)
    scale = lax.rsqrt(jnp.maximum(cover, 1.0))
    for c in range(cols // LANES):
        part = slice(c * LANES, (c + 1) * LANES)
        out_ref[:, part] = accum[:, part] * scale


def in_hbm(*arrays):
    return [pltpu.with_memory_space_constraint(x, pltpu.HBM) for x in arrays]


def call(body, shapes, specs, scratch, flops, name, limit=LIMIT):
    return pl.pallas_call(
        body,
        out_shape=shapes,
        in_specs=specs,
        out_specs=jax.tree.map(lambda _: VM, shapes),
        scratch_shapes=scratch,
        compiler_params=pltpu.CompilerParams(vmem_limit_bytes=limit * 1024 * 1024),
        cost_estimate=pl.CostEstimate(flops=flops, bytes_accessed=1 << 21, transcendentals=0),
        name=name,
    )


def on_device(template, science, offsets, live_flags, bank, basis_index, coeff, psf_profile):
    rows, cols = template.shape
    sharers = lax.axis_size("visit") * lax.axis_size("band")
    share = rows // sharers
    chunks, blocks = cols // LANES, cols // B
    edge = 2 * B
    inner = rows - edge
    before = shifted(science, "patch", 1)[:, 0, :]
    following = shifted(template, "patch", -1)

    sds = jax.ShapeDtypeStruct
    deep = 9 * CH
    depth = -(-(share + edge) // LANES) * LANES
    sci = science[:, 0, :]
    taps = psf_profile.shape[0]
    index = jnp.swapaxes(basis_index, 1, 2)
    count = rows // B
    conv_scratch = [
        pltpu.VMEM((chunks, rows, LANES), F32),
        pltpu.VMEM((3, blocks + 2, count, CH), BF16),
    ]
    conv_flops = 2 * rows * cols * deep
    sky_scratch = [pltpu.VMEM((chunks, 2 * rows + B, LANES), F32), pltpu.VMEM((inner, cols), BF16)]
    sides = (sds((chunks, 2 * edge, LANES), F32), sds((inner, cols), BF16))
    w, pcol, prow, note, ends, tile, m1, edge_a, filt_a = call(
        first_kernel,
        (
            sds((deep, CH), BF16), sds((cols, cols), BF16), sds((share, depth), BF16), sds((edge, cols), BF16),
            sds((2 * edge, cols), BF16), sds((rows, cols), BF16), sds((chunks, rows, LANES), F32),
        ) + sides,
        [HBM] * 8,
        [
            pltpu.SMEM((1, 1), jnp.int32), pltpu.SMEM((1, 1), jnp.int32), pltpu.VMEM((rows, cols), BF16),
            pltpu.VMEM(bank.shape, BF16), pltpu.VMEM(index.shape, jnp.int32),
            pltpu.VMEM(coeff.shape, F32), pltpu.VMEM((1, taps), BF16), pltpu.SemaphoreType.DMA((8,)),
        ] + conv_scratch + sky_scratch,
        conv_flops, "first",
    )(offsets, live_flags, *in_hbm(template, sci, bank, index, coeff, psf_profile[None]))
    msg = shifted(note, "patch", 1)
    edge_b, filt_b = call(before_kernel, sides, [VM] * 4, sky_scratch, 1 << 28, "before")(msg, before, m1, pcol)
    *parts, m_edge = call(
        join_kernel,
        (sds((share + B, cols), BF16),) * sharers + (sds((chunks, 2 * edge, LANES), F32),),
        [VM] * 11,
        [
            pltpu.VMEM((chunks, 8 * B, LANES), F32),
            pltpu.VMEM((3, blocks + 2, 8, CH), F32),
            pltpu.VMEM((chunks, 8 * B, LANES), F32),
            pltpu.VMEM((4 * edge, cols), BF16),
            pltpu.VMEM((2, rows - share + depth, cols), BF16),
        ],
        1 << 29, "join",
    )(note, ends, msg, following, w, pcol, prow, edge_a, edge_b, filt_a, filt_b)
    for k in reversed(range(1, sharers)):
        pairs = [(i, partner(i, k, sharers)) for i in range(sharers)]
        parts[k] = lax.ppermute(parts[k], ("visit", "band"), pairs)
    difference = call(
        tile_kernel, sds((rows, cols), BF16), [VM] * 6,
        conv_scratch + [pltpu.VMEM((chunks, 2 * rows, LANES), F32)], conv_flops, "tile",
    )(tile, note, following, m1, m_edge, w)
    detection = call(coadd_kernel, sds((share, cols), F32), [VM] * sharers, [], 1 << 20, "coadd")(parts[0], *parts[:0:-1])
    return (difference[:, None, :], detection)


def solution(mesh):
    return jax.shard_map(
        on_device,
        mesh=mesh,
        in_specs=(
            P(("group", "patch"), None),
            P(("group", "patch"), ("visit", "band"), None),
            P(("group", "patch"), ("visit", "band")),
            P(("group", "patch"), ("visit", "band")),
            P(),
            P(("group", "visit", "band"), None, None),
            P(("group", "visit", "band"), None),
            P(),
        ),
        out_specs=(
            P(("group", "patch"), ("visit", "band"), None),
            P(("group", "patch", "visit", "band"), None),
        ),
        check_vma=False,
    )
```

```python
import functools

import jax
import jax.numpy as jnp
from jax import lax
from jax.experimental import pallas as pl
from jax.experimental.pallas import tpu as pltpu
from jax.sharding import PartitionSpec as P

B = 16
CH = B * B
LANES = 128
GROUPS = LANES // B
F32 = jnp.float32
BF16 = jnp.bfloat16


def swap_partner(p, parity, count):
    other = p + 1 if p % 2 == parity else p - 1
    return other if 0 <= other < count else p


def place():
    p = lax.axis_index("patch")
    return p % 2 == 0, p > 0, p < lax.axis_size("patch") - 1


def pick(flag, valid, yes, no):
    value = jnp.where(flag, yes.astype(F32), no.astype(F32))
    return jnp.where(valid, value, 0.0)


def partner(me, k, count):
    return me ^ k if count & (count - 1) == 0 else (me + k) % count


def iota(shape, dim):
    return lax.broadcasted_iota(jnp.int32, shape, dim)


LIMIT = 10
VM = pl.BlockSpec(memory_space=pltpu.VMEM)
HBM = pl.BlockSpec(memory_space=pltpu.HBM)


def group_transpose(parts):
    parts = list(parts)
    group = iota(parts[0].shape, 1) // B
    for step in (1, 2, 4):
        low = (group & step) == 0
        for m in range(GROUPS):
            if m & step:
                continue
            x, y = parts[m], parts[m + step]
            parts[m] = jnp.where(low, x, pltpu.roll(y, step * B, 1))
            parts[m + step] = jnp.where(low, pltpu.roll(x, LANES - step * B, 1), y)
    return parts


def conv_blocks(src, count, w_ref, xs, dst, dst_row):
    chunks = src.shape[0]
    blocks = chunks * GROUPS
    wide = count // 8

    def load(c):
        for h in range(2):
            rows = [
                jnp.concatenate(
                    [src[c, pl.ds(B * v + GROUPS * h + i, 8, stride=B * wide), :] for v in range(wide)], axis=0
                )
                for i in range(GROUPS)
            ]
            part = slice(h * LANES, (h + 1) * LANES)
            for g, here in enumerate(group_transpose(rows)):
                at = 1 + c * GROUPS + g
                after = pltpu.roll(here[0:8], 7, 0)
                prior = pltpu.roll(here[count - 8 :], 1, 0)
                if wide > 1:
                    after = jnp.concatenate([here[8:], after], axis=0)
                    prior = jnp.concatenate([prior, here[: count - 8]], axis=0)
                xs[0, at, :, part] = prior.astype(xs.dtype)
                xs[1, at, :, part] = here.astype(xs.dtype)
                xs[2, at, :, part] = after.astype(xs.dtype)

    def solve(c):
        b = c * GROUPS
        pieces = [
            xs[qr, b + qc : b + qc + GROUPS].reshape(GROUPS * count, CH).astype(BF16)
            for qr in range(3)
            for qc in range(3)
        ]
        out = jnp.dot(jnp.concatenate(pieces, axis=1), w_ref[...], preferred_element_type=F32)
        for h in range(2):
            part = slice(h * LANES, (h + 1) * LANES)
            rows = group_transpose([out[g * count : (g + 1) * count, part] for g in range(GROUPS)])
            for i in range(GROUPS):
                for v in range(wide):
                    dst[c, pl.ds(dst_row + B * v + GROUPS * h + i, 8, stride=B * wide), :] = rows[i][8 * v : 8 * v + 8]

    for q in range(3):
        xs[q, 0] = jnp.zeros((count, CH), xs.dtype)
        xs[q, blocks + 1] = jnp.zeros((count, CH), xs.dtype)
    load(0)
    for c in range(chunks):
        if c + 1 < chunks:
            load(c + 1)
        solve(c)


def column(row):
    size = row.shape[1]
    diag = iota((size, size), 0) == iota((size, size), 1)
    return jnp.sum(jnp.where(diag, row, jnp.zeros_like(row)), axis=1, keepdims=True)


def pack_kernel(
    off_hbm, live_hbm, t_hbm, sci_hbm, msg1_ref, msg2_ref, note_ref, off_ref, live_ref, tail_ref, sems
):
    rows, cols = t_hbm.shape
    edge = 2 * B
    even, _, _ = place()

    def send(one, two):
        pltpu.make_async_copy(one, msg1_ref.at[pl.ds(edge, rows)], sems.at[0]).start()
        pltpu.make_async_copy(two, msg2_ref.at[pl.ds(edge, rows)], sems.at[1]).start()

    def finish(one, two):
        pltpu.make_async_copy(one, msg1_ref.at[pl.ds(edge, rows)], sems.at[0]).wait()
        pltpu.make_async_copy(two, msg2_ref.at[pl.ds(edge, rows)], sems.at[1]).wait()

    small = [
        pltpu.make_async_copy(off_hbm, off_ref, sems.at[2]),
        pltpu.make_async_copy(live_hbm, live_ref, sems.at[3]),
        pltpu.make_async_copy(t_hbm.at[pl.ds(rows - edge, edge)], tail_ref, sems.at[4]),
    ]
    for copy in small:
        copy.start()
    pl.when(even)(lambda: send(sci_hbm, t_hbm))
    pl.when(jnp.logical_not(even))(lambda: send(t_hbm, sci_hbm))
    for copy in small:
        copy.wait()
    lane = iota((1, cols), 1)
    off = off_ref[0, 0]
    note = jnp.where(lane == 0, off // B, jnp.where(lane == 1, off % B, live_ref[0, 0]))
    head = jnp.where(iota((edge, cols), 0) == 0, note.astype(F32), tail_ref[...].astype(F32)).astype(BF16)
    note_ref[...] = head
    msg1_ref[0:edge, :] = head
    msg2_ref[0:edge, :] = head
    pl.when(even)(lambda: finish(sci_hbm, t_hbm))
    pl.when(jnp.logical_not(even))(lambda: finish(t_hbm, sci_hbm))


def first_kernel(
    note_ref, t_hbm, sci_hbm, bank_hbm, index_hbm, coeff_hbm, psf_hbm,
    w_ref, pcol_ref, prow_ref, ends_ref, sci_ref, m_ref, edge_ref, filt_ref,
    t_ref, bank_ref, index_ref, coeff_ref, psf_ref, sems,
    src, xs, sci, diff,
):
    pairs = (
        (bank_hbm, bank_ref), (index_hbm, index_ref), (coeff_hbm, coeff_ref), (psf_hbm, psf_ref),
        (t_hbm, t_ref), (sci_hbm, sci_ref),
    )
    copies = [pltpu.make_async_copy(a, b, sems.at[n]) for n, (a, b) in enumerate(pairs)]
    for copy in copies:
        copy.start()
    for copy in copies[:4]:
        copy.wait()
    profs, taps = bank_ref.shape
    half = taps // 2
    delta = B - half
    bank = bank_ref[...]
    index = index_ref[0].astype(F32)
    labels = iota((index.shape[1], profs), 1).astype(F32)
    pick_row = (column(index[0:1]) == labels).astype(F32).astype(BF16)
    pick_col = (column(index[1:2]) == labels).astype(F32).astype(BF16)
    weight = column(coeff_ref[...])
    rowprof = (weight * jnp.dot(pick_row, bank, preferred_element_type=F32)).astype(BF16)
    colprof = jnp.dot(pick_col, bank, preferred_element_type=F32).astype(BF16)
    span = 3 * B
    total = 4 * B * B
    place = (iota((span, taps), 0) - delta == iota((span, taps), 1)).astype(F32).astype(BF16)
    col_t = lax.dot_general(place, colprof, (((1,), (1,)), ((), ())), preferred_element_type=F32).astype(BF16)
    spread = (span - 1 - iota((taps, total), 1) // B - delta == iota((taps, total), 0)).astype(F32).astype(BF16)
    row_rep = jnp.dot(rowprof, spread, preferred_element_type=F32).astype(BF16)
    z = jnp.dot(col_t, row_rep, preferred_element_type=F32)
    lane = iota((span, total), 1)
    for bit in (1, 2, 4, 8):
        z = jnp.where((lane & bit) != 0, pltpu.roll(z, bit, 0), z)
    z = z.astype(BF16)
    for phase in range(GROUPS):
        zp = z if phase == 0 else pltpu.roll(z, total - phase * B, 1)
        for g in range(span):
            start = span - 1 - g
            if start % GROUPS != phase:
                continue
            at = (start // GROUPS) * LANES
            for qc in range(3):
                row = (g // B) * 3 * CH + qc * CH + (g % B) * B
                w_ref[row : row + B, :] = zp[qc * B : (qc + 1) * B, at : at + CH]
    psf = psf_ref[...].astype(F32)
    size = pcol_ref.shape[0]
    blank = jnp.zeros((LANES, LANES), F32)
    bands = {}
    for off in (-1, 0, 1):
        tap = iota((LANES, LANES), 0) + off * LANES - iota((LANES, LANES), 1) + half
        block = blank
        for t in range(taps):
            block = jnp.where(tap == t, psf[:, t : t + 1], block)
        bands[off] = block.astype(BF16)
    for i in range(size // LANES):
        for j in range(size // LANES):
            pcol_ref[i * LANES : (i + 1) * LANES, j * LANES : (j + 1) * LANES] = bands.get(i - j, blank.astype(BF16))
    shape = prow_ref.shape
    tap = iota(shape, 1) - iota(shape, 0) - delta
    block = jnp.zeros(shape, F32)
    for t in range(taps):
        block = jnp.where(tap == t, psf[:, t : t + 1], block)
    prow_ref[...] = block.astype(BF16)
    for copy in copies[4:]:
        copy.wait()
    edge = 2 * B
    rows, cols = t_ref.shape
    off, _ = read_note(note_ref)
    ends_ref[0:edge, :] = t_ref[0:edge, :]
    ends_ref[edge:, :] = t_ref[rows - edge : rows, :]
    to_chunks(src, 0, t_ref[...])
    conv_blocks(src, rows // B, w_ref, xs, m_ref, 0)
    to_chunks(sci, rows, sci_ref[...])
    filter_inner(sci, rows - B - off, off, off + rows, m_ref, pcol_ref, edge_ref, filt_ref, diff)


def to_chunks(dst, dst_row, value):
    value = value.astype(F32)
    rows = value.shape[0]
    for c in range(dst.shape[0]):
        dst[c, dst_row : dst_row + rows, :] = value[:, c * LANES : (c + 1) * LANES]


def tile_diff(sky, m, base, first, last):
    row = iota(m.shape, 0) + (base - B)
    return jnp.where((row >= first) & (row < last), sky - m, 0.0).astype(BF16)


def filter_inner(sci, start, first, last, m_ref, pcol_ref, edge_ref, filt_ref, diff):
    chunks, rows, _ = m_ref.shape
    edge = 2 * B
    for c in range(chunks):
        part = slice(c * LANES, (c + 1) * LANES)
        sky = sci[c, pl.ds(start, rows + edge), :]
        edge_ref[c, 0:edge, :] = sky[0:edge]
        edge_ref[c, edge:, :] = sky[rows:]
        diff[:, part] = tile_diff(sky[edge:rows], m_ref[c, B : rows - B, :], edge, first, last)
    filt_ref[...] = jnp.dot(diff[...], pcol_ref[...], preferred_element_type=F32).astype(BF16)


def read_note(msg_ref):
    return decode(msg_ref[0:B, 0:LANES].astype(F32))


def decode(note):
    return (note[0, 0] * B + note[0, 1]).astype(jnp.int32), note[0, 2]


def note_before(got1_ref, got2_ref):
    even, has_before, _ = place()
    return decode(pick(even, has_before, got2_ref[0:B, 0:LANES], got1_ref[0:B, 0:LANES]))


def before_kernel(got1_ref, got2_ref, m_ref, pcol_ref, edge_ref, filt_ref, sci, diff):
    edge = 2 * B
    rows = got1_ref.shape[0] - edge
    even, has_before, _ = place()
    off, _ = note_before(got1_ref, got2_ref)
    to_chunks(sci, 0, pick(even, has_before, got2_ref[edge:, :], got1_ref[edge:, :]))
    filter_inner(sci, rows - B - off, off - rows, off, m_ref, pcol_ref, edge_ref, filt_ref, diff)


def join_kernel(
    note_ref, ends_ref, got1_ref, got2_ref, w_ref, pcol_ref, prow_ref, edge_a, edge_b, filt_a, filt_b,
    *rest,
):
    *outs, m_ref, src, xs, strip, diff, filt = rest
    edge = 2 * B
    rows, cols = got1_ref.shape[0] - edge, got1_ref.shape[1]
    even, has_before, has_next = place()
    to_chunks(src, 0, pick(even, has_before, got2_ref[0:edge, :], got1_ref[0:edge, :]))
    to_chunks(src, edge, ends_ref[...])
    to_chunks(src, 3 * edge, pick(even, has_next, got1_ref[edge : 2 * edge, :], got2_ref[edge : 2 * edge, :]))
    conv_blocks(src, 8, w_ref, xs, strip, 0)
    m_ref[:, 0:edge, :] = strip[:, B : B + edge, :]
    m_ref[:, edge:, :] = strip[:, 5 * B : 5 * B + edge, :]
    off_a, live_a = read_note(note_ref)
    off_b, live_b = note_before(got1_ref, got2_ref)
    for s, (side, first, last) in enumerate(((edge_a, off_a, off_a + rows), (edge_b, off_b - rows, off_b))):
        for c in range(cols // LANES):
            part = slice(c * LANES, (c + 1) * LANES)
            for k, base in enumerate((0, rows)):
                span = slice(k * edge, (k + 1) * edge)
                at = (2 * s + k) * edge
                diff[at : at + edge, part] = tile_diff(side[c, span, :], m_ref[c, span, :], base, first, last)
    sides = jnp.dot(diff[...], pcol_ref[...], preferred_element_type=F32).astype(BF16)
    for s, inner in enumerate((filt_a, filt_b)):
        filt[s, 0:edge, :] = sides[2 * s * edge : (2 * s + 1) * edge]
        filt[s, edge:rows, :] = inner[...]
        filt[s, rows : rows + edge, :] = sides[(2 * s + 1) * edge : (2 * s + 2) * edge]
        filt[s, rows + edge :, :] = jnp.zeros((filt.shape[1] - rows - edge, cols), BF16)
    share, depth = prow_ref.shape
    prow = prow_ref[...].astype(F32)
    out_row = iota((share, depth), 0)
    lane = iota((B, cols), 1)
    me = lax.axis_index("visit") * lax.axis_size("band") + lax.axis_index("band")
    for k, out_ref in enumerate(outs):
        base = partner(me, k, len(outs)) * share
        row = out_row + base
        left = jnp.where(row >= off_a, prow * live_a, 0.0).astype(BF16)
        right = jnp.where(row < off_b, prow * live_b, 0.0).astype(BF16)
        span = pl.ds(pl.multiple_of(base, B), depth)
        total = jnp.dot(left, filt[0, span, :], preferred_element_type=F32)
        total += jnp.dot(right, filt[1, span, :], preferred_element_type=F32)
        out_ref[0:share, :] = total.astype(BF16)
        start = jnp.clip(off_a - base, 0, share).astype(F32)
        stop = jnp.clip(off_b - base, 0, share).astype(F32)
        note = jnp.where(lane == 0, start, jnp.where(lane == 1, live_a, jnp.where(lane == 2, stop, live_b)))
        out_ref[share : share + B, :] = note.astype(BF16)


def tile_kernel(sci_ref, note_ref, got1_ref, got2_ref, m1_ref, edge_ref, w_ref, out_ref, src, xs, big):
    rows, cols = sci_ref.shape
    even, _, has_next = place()
    to_chunks(src, 0, pick(even, has_next, got1_ref[2 * B :, :], got2_ref[2 * B :, :]))
    conv_blocks(src, rows // B, w_ref, xs, big, rows)
    big[:, 0:B, :] = edge_ref[:, B : 2 * B, :]
    big[:, B : rows - B, :] = m1_ref[:, B : rows - B, :]
    big[:, rows - B : rows + B, :] = edge_ref[:, 2 * B : 4 * B, :]
    off, _ = read_note(note_ref)
    for c in range(cols // LANES):
        part = slice(c * LANES, (c + 1) * LANES)
        out_ref[:, part] = (sci_ref[:, part].astype(F32) - big[c, pl.ds(off, rows), :]).astype(BF16)


def coadd_kernel(*refs):
    *parts, out_ref = refs
    share, cols = out_ref.shape
    row = iota((share, LANES), 0).astype(F32)
    accum = jnp.zeros((share, cols), F32)
    cover = jnp.zeros((share, LANES), F32)
    for part in parts:
        accum += part[0:share, :].astype(F32)
        note = part[share : share + B, 0:LANES].astype(F32)[0:1, :]
        cover += jnp.where(row >= note[:, 0:1], note[:, 1:2], 0.0)
        cover += jnp.where(row < note[:, 2:3], note[:, 3:4], 0.0)
    scale = lax.rsqrt(jnp.maximum(cover, 1.0))
    for c in range(cols // LANES):
        part = slice(c * LANES, (c + 1) * LANES)
        out_ref[:, part] = accum[:, part] * scale


def in_hbm(*arrays):
    return [pltpu.with_memory_space_constraint(x, pltpu.HBM) for x in arrays]


def call(body, shapes, specs, scratch, flops, name, limit=LIMIT):
    return pl.pallas_call(
        body,
        out_shape=shapes,
        in_specs=specs,
        out_specs=jax.tree.map(lambda _: VM, shapes),
        scratch_shapes=scratch,
        compiler_params=pltpu.CompilerParams(vmem_limit_bytes=limit * 1024 * 1024),
        cost_estimate=pl.CostEstimate(flops=flops, bytes_accessed=1 << 21, transcendentals=0),
        name=name,
    )


def on_device(template, science, offsets, live_flags, bank, basis_index, coeff, psf_profile):
    rows, cols = template.shape
    sharers = lax.axis_size("visit") * lax.axis_size("band")
    share = rows // sharers
    chunks, blocks = cols // LANES, cols // B
    edge = 2 * B
    inner = rows - edge
    sds = jax.ShapeDtypeStruct
    deep = 9 * CH
    depth = -(-(share + edge) // LANES) * LANES
    sci = science[:, 0, :]
    taps = psf_profile.shape[0]
    held = in_hbm(template, sci)
    msg1, msg2, note = call(
        pack_kernel,
        (sds((edge + rows, cols), BF16), sds((edge + rows, cols), BF16), sds((edge, cols), BF16)),
        [HBM] * 4,
        [
            pltpu.SMEM((1, 1), jnp.int32), pltpu.SMEM((1, 1), jnp.int32), pltpu.VMEM((edge, cols), BF16),
            pltpu.SemaphoreType.DMA((5,)),
        ],
        1 << 20, "pack",
    )(offsets, live_flags, *held)
    panels = lax.axis_size("patch")
    got1, got2 = (
        lax.ppermute(msg, "patch", [(p, swap_partner(p, parity, panels)) for p in range(panels)])
        for parity, msg in enumerate((msg1, msg2))
    )
    index = jnp.swapaxes(basis_index, 1, 2)
    count = rows // B
    conv_scratch = [
        pltpu.VMEM((chunks, rows, LANES), F32),
        pltpu.VMEM((3, blocks + 2, count, CH), BF16),
    ]
    conv_flops = 2 * rows * cols * deep
    sky_scratch = [pltpu.VMEM((chunks, 2 * rows + B, LANES), F32), pltpu.VMEM((inner, cols), BF16)]
    sides = (sds((chunks, 2 * edge, LANES), F32), sds((inner, cols), BF16))
    w, pcol, prow, ends, tile, m1, edge_a, filt_a = call(
        first_kernel,
        (
            sds((deep, CH), BF16), sds((cols, cols), BF16), sds((share, depth), BF16), sds((2 * edge, cols), BF16),
             sds((rows, cols), BF16), sds((chunks, rows, LANES), F32),
        ) + sides,
        [VM] + [HBM] * 6,
        [
            pltpu.VMEM((rows, cols), BF16), pltpu.VMEM(bank.shape, BF16), pltpu.VMEM(index.shape, jnp.int32),
            pltpu.VMEM(coeff.shape, F32), pltpu.VMEM((1, taps), BF16), pltpu.SemaphoreType.DMA((6,)),
        ] + conv_scratch + sky_scratch,
        conv_flops, "first",
    )(note, *held, *in_hbm(bank, index, coeff, psf_profile[None]))
    edge_b, filt_b = call(before_kernel, sides, [VM] * 4, sky_scratch, 1 << 28, "before")(got1, got2, m1, pcol)
    *parts, m_edge = call(
        join_kernel,
        (sds((share + B, cols), BF16),) * sharers + (sds((chunks, 2 * edge, LANES), F32),),
        [VM] * 11,
        [
            pltpu.VMEM((chunks, 8 * B, LANES), F32),
            pltpu.VMEM((3, blocks + 2, 8, CH), F32),
            pltpu.VMEM((chunks, 8 * B, LANES), F32),
            pltpu.VMEM((4 * edge, cols), BF16),
            pltpu.VMEM((2, rows - share + depth, cols), BF16),
        ],
        1 << 29, "join",
    )(note, ends, got1, got2, w, pcol, prow, edge_a, edge_b, filt_a, filt_b)
    for k in reversed(range(1, sharers)):
        pairs = [(i, partner(i, k, sharers)) for i in range(sharers)]
        parts[k] = lax.ppermute(parts[k], ("visit", "band"), pairs)
    difference = call(
        tile_kernel, sds((rows, cols), BF16), [VM] * 7,
        conv_scratch + [pltpu.VMEM((chunks, 2 * rows, LANES), F32)], conv_flops, "tile",
    )(tile, note, got1, got2, m1, m_edge, w)
    detection = call(coadd_kernel, sds((share, cols), F32), [VM] * sharers, [], 1 << 20, "coadd")(parts[0], *parts[:0:-1])
    return (difference[:, None, :], detection)


def solution(mesh):
    return jax.shard_map(
        on_device,
        mesh=mesh,
        in_specs=(
            P(("group", "patch"), None),
            P(("group", "patch"), ("visit", "band"), None),
            P(("group", "patch"), ("visit", "band")),
            P(("group", "patch"), ("visit", "band")),
            P(),
            P(("group", "visit", "band"), None, None),
            P(("group", "visit", "band"), None),
            P(),
        ),
        out_specs=(
            P(("group", "patch"), ("visit", "band"), None),
            P(("group", "patch", "visit", "band"), None),
        ),
        check_vma=False,
    )
```

```python
import functools

import jax
import jax.numpy as jnp
from jax import lax
from jax.experimental import pallas as pl
from jax.experimental.pallas import tpu as pltpu
from jax.sharding import PartitionSpec as P

B = 16
CH = B * B
LANES = 128
GROUPS = LANES // B
PITCH = B + 1
F32 = jnp.float32
BF16 = jnp.bfloat16


def shifted(shard, axis, by):
    devices = lax.axis_size(axis)
    pairs = [(i, i + by) for i in range(devices) if 0 <= i + by < devices]
    return lax.ppermute(shard, axis, pairs)


def swap_partner(p, parity, count):
    other = p + 1 if p % 2 == parity else p - 1
    return other if 0 <= other < count else p


def place():
    p = lax.axis_index("patch")
    return p % 2 == 0, p > 0, p < lax.axis_size("patch") - 1


def pick(flag, valid, yes, no):
    value = jnp.where(flag, yes.astype(F32), no.astype(F32))
    return jnp.where(valid, value, 0.0)


def partner(me, k, count):
    return me ^ k if count & (count - 1) == 0 else (me + k) % count


def iota(shape, dim):
    return lax.broadcasted_iota(jnp.int32, shape, dim)


LIMIT = 10
VM = pl.BlockSpec(memory_space=pltpu.VMEM)
HBM = pl.BlockSpec(memory_space=pltpu.HBM)


def group_transpose(parts):
    parts = list(parts)
    group = iota(parts[0].shape, 1) // B
    for step in (1, 2, 4):
        low = (group & step) == 0
        for m in range(GROUPS):
            if m & step:
                continue
            x, y = parts[m], parts[m + step]
            parts[m] = jnp.where(low, x, pltpu.roll(y, step * B, 1))
            parts[m + step] = jnp.where(low, pltpu.roll(x, LANES - step * B, 1), y)
    return parts


def to_blocks(dst, block, value):
    value = value.astype(F32)
    for a in range(value.shape[0] // B):
        at = (block + a) * PITCH
        for c in range(dst.shape[0]):
            dst[c, at : at + B, :] = value[a * B : (a + 1) * B, c * LANES : (c + 1) * LANES]


def conv_blocks(src, count, w_ref, xs, dst):
    chunks = src.shape[0]
    blocks = chunks * GROUPS

    def load(c):
        for h in range(2):
            rows = [src[c, pl.ds(GROUPS * h + i, count, stride=PITCH), :] for i in range(GROUPS)]
            part = slice(h * LANES, (h + 1) * LANES)
            for g, here in enumerate(group_transpose(rows)):
                at = 1 + c * GROUPS + g
                xs[0, at, :, part] = pltpu.roll(here, 1, 0).astype(xs.dtype)
                xs[1, at, :, part] = here.astype(xs.dtype)
                xs[2, at, :, part] = pltpu.roll(here, count - 1, 0).astype(xs.dtype)

    def solve(c):
        b = c * GROUPS
        pieces = [
            xs[qr, b + qc : b + qc + GROUPS].reshape(GROUPS * count, CH).astype(BF16)
            for qr in range(3)
            for qc in range(3)
        ]
        out = jnp.dot(jnp.concatenate(pieces, axis=1), w_ref[...], preferred_element_type=F32)
        for h in range(2):
            part = slice(h * LANES, (h + 1) * LANES)
            rows = group_transpose([out[g * count : (g + 1) * count, part] for g in range(GROUPS)])
            for i in range(GROUPS):
                dst[c, pl.ds(GROUPS * h + i, count, stride=PITCH), :] = rows[i]

    for q in range(3):
        xs[q, 0] = jnp.zeros((count, CH), xs.dtype)
        xs[q, blocks + 1] = jnp.zeros((count, CH), xs.dtype)
    load(0)
    for c in range(chunks):
        if c + 1 < chunks:
            load(c + 1)
        solve(c)


def column(row):
    size = row.shape[1]
    diag = iota((size, size), 0) == iota((size, size), 1)
    return jnp.sum(jnp.where(diag, row, jnp.zeros_like(row)), axis=1, keepdims=True)


def pack_kernel(off_hbm, live_hbm, t_hbm, msg_ref, off_ref, live_ref, sems):
    rows, cols = t_hbm.shape
    edge = 2 * B
    copies = [
        pltpu.make_async_copy(t_hbm.at[pl.ds(rows - edge, edge)], msg_ref.at[pl.ds(0, edge)], sems.at[0]),
        pltpu.make_async_copy(t_hbm.at[pl.ds(0, edge)], msg_ref.at[pl.ds(edge, edge)], sems.at[1]),
        pltpu.make_async_copy(off_hbm, off_ref, sems.at[2]),
        pltpu.make_async_copy(live_hbm, live_ref, sems.at[3]),
    ]
    for copy in copies:
        copy.start()
    for copy in copies:
        copy.wait()
    lane = iota((1, cols), 1)
    off = off_ref[0, 0]
    note = jnp.where(lane == 0, off // B, jnp.where(lane == 1, off % B, live_ref[0, 0])).astype(F32)
    block = msg_ref[0:B, :].astype(F32)
    msg_ref[0:B, :] = jnp.where(iota((B, cols), 0) == 0, note, block).astype(BF16)


def first_kernel(
    note_ref, t_hbm, sci_hbm, bank_hbm, index_hbm, coeff_hbm, psf_hbm,
    w_ref, pcol_ref, prow_ref, sci_ref, m_ref, edge_ref, filt_ref,
    t_ref, bank_ref, index_ref, coeff_ref, psf_ref, sems,
    src, xs, res, sci, diff,
):
    pairs = (
        (bank_hbm, bank_ref), (index_hbm, index_ref), (coeff_hbm, coeff_ref), (psf_hbm, psf_ref),
        (t_hbm, t_ref), (sci_hbm, sci_ref),
    )
    copies = [pltpu.make_async_copy(a, b, sems.at[n]) for n, (a, b) in enumerate(pairs)]
    for copy in copies:
        copy.start()
    for copy in copies[:4]:
        copy.wait()
    profs, taps = bank_ref.shape
    half = taps // 2
    delta = B - half
    bank = bank_ref[...]
    index = index_ref[0].astype(F32)
    labels = iota((index.shape[1], profs), 1).astype(F32)
    pick_row = (column(index[0:1]) == labels).astype(F32).astype(BF16)
    pick_col = (column(index[1:2]) == labels).astype(F32).astype(BF16)
    weight = column(coeff_ref[...])
    rowprof = (weight * jnp.dot(pick_row, bank, preferred_element_type=F32)).astype(BF16)
    colprof = jnp.dot(pick_col, bank, preferred_element_type=F32).astype(BF16)
    span = 3 * B
    total = 4 * B * B
    place = (iota((span, taps), 0) - delta == iota((span, taps), 1)).astype(F32).astype(BF16)
    col_t = lax.dot_general(place, colprof, (((1,), (1,)), ((), ())), preferred_element_type=F32).astype(BF16)
    spread = (span - 1 - iota((taps, total), 1) // B - delta == iota((taps, total), 0)).astype(F32).astype(BF16)
    row_rep = jnp.dot(rowprof, spread, preferred_element_type=F32).astype(BF16)
    z = jnp.dot(col_t, row_rep, preferred_element_type=F32)
    lane = iota((span, total), 1)
    for bit in (1, 2, 4, 8):
        z = jnp.where((lane & bit) != 0, pltpu.roll(z, bit, 0), z)
    z = z.astype(BF16)
    for phase in range(GROUPS):
        zp = z if phase == 0 else pltpu.roll(z, total - phase * B, 1)
        for g in range(span):
            start = span - 1 - g
            if start % GROUPS != phase:
                continue
            at = (start // GROUPS) * LANES
            for qc in range(3):
                row = (g // B) * 3 * CH + qc * CH + (g % B) * B
                w_ref[row : row + B, :] = zp[qc * B : (qc + 1) * B, at : at + CH]
    psf = psf_ref[...].astype(F32)
    size = pcol_ref.shape[0]
    blank = jnp.zeros((LANES, LANES), F32)
    bands = {}
    for off in (-1, 0, 1):
        tap = iota((LANES, LANES), 0) + off * LANES - iota((LANES, LANES), 1) + half
        block = blank
        for t in range(taps):
            block = jnp.where(tap == t, psf[:, t : t + 1], block)
        bands[off] = block.astype(BF16)
    for i in range(size // LANES):
        for j in range(size // LANES):
            pcol_ref[i * LANES : (i + 1) * LANES, j * LANES : (j + 1) * LANES] = bands.get(i - j, blank.astype(BF16))
    shape = prow_ref.shape
    tap = iota(shape, 1) - iota(shape, 0) - delta
    block = jnp.zeros(shape, F32)
    for t in range(taps):
        block = jnp.where(tap == t, psf[:, t : t + 1], block)
    prow_ref[...] = block.astype(BF16)
    for copy in copies[4:]:
        copy.wait()
    edge = 2 * B
    rows, cols = t_ref.shape
    off, _ = read_note(note_ref)
    to_blocks(src, 0, t_ref[...])
    conv_blocks(src, rows // B, w_ref, xs, res)
    for a in range(1, rows // B - 1):
        m_ref[:, B * a : B * (a + 1), :] = res[:, PITCH * a : PITCH * a + B, :]
    to_chunks(sci, rows, sci_ref[...])
    filter_inner(sci, rows - B - off, off, off + rows, m_ref, pcol_ref, edge_ref, filt_ref, diff)


def to_chunks(dst, dst_row, value):
    value = value.astype(F32)
    rows = value.shape[0]
    for c in range(dst.shape[0]):
        dst[c, dst_row : dst_row + rows, :] = value[:, c * LANES : (c + 1) * LANES]


def tile_diff(sky, m, base, first, last):
    row = iota(m.shape, 0) + (base - B)
    return jnp.where((row >= first) & (row < last), sky - m, 0.0).astype(BF16)


def filter_inner(sci, start, first, last, m_ref, pcol_ref, edge_ref, filt_ref, diff):
    chunks, rows, _ = m_ref.shape
    edge = 2 * B
    for c in range(chunks):
        part = slice(c * LANES, (c + 1) * LANES)
        sky = sci[c, pl.ds(start, rows + edge), :]
        edge_ref[c, 0:edge, :] = sky[0:edge]
        edge_ref[c, edge:, :] = sky[rows:]
        diff[:, part] = tile_diff(sky[edge:rows], m_ref[c, B : rows - B, :], edge, first, last)
    filt_ref[...] = jnp.dot(diff[...], pcol_ref[...], preferred_element_type=F32).astype(BF16)


def read_note(msg_ref):
    return decode(msg_ref[0:B, 0:LANES].astype(F32))


def decode(note):
    return (note[0, 0] * B + note[0, 1]).astype(jnp.int32), note[0, 2]


def note_before(got1_ref, got2_ref):
    even, has_before, _ = place()
    return decode(pick(even, has_before, got2_ref[0:B, 0:LANES], got1_ref[0:B, 0:LANES]))


def before_kernel(got1_ref, got2_ref, sci_ref, m_ref, pcol_ref, edge_ref, filt_ref, sci, diff):
    rows = sci_ref.shape[0]
    off, _ = note_before(got1_ref, got2_ref)
    to_chunks(sci, 0, sci_ref[...])
    filter_inner(sci, rows - B - off, off - rows, off, m_ref, pcol_ref, edge_ref, filt_ref, diff)


def join_kernel(
    note_ref, got1_ref, got2_ref, w_ref, pcol_ref, prow_ref, edge_a, edge_b, filt_a, filt_b,
    *rest,
):
    *outs, m_ref, src, xs, strip, diff, filt = rest
    edge = 2 * B
    rows, cols = filt_a.shape[0] + edge, filt_a.shape[1]
    even, has_before, has_next = place()
    to_blocks(src, 0, pick(even, has_before, got2_ref[0:edge, :], got1_ref[0:edge, :]))
    to_blocks(src, 2, note_ref[edge:, :])
    to_blocks(src, 4, note_ref[0:edge, :])
    to_blocks(src, 6, pick(even, has_next, got1_ref[edge:, :], got2_ref[edge:, :]))
    conv_blocks(src, 8, w_ref, xs, strip)
    for n, a in enumerate((1, 2, 5, 6)):
        m_ref[:, B * n : B * (n + 1), :] = strip[:, PITCH * a : PITCH * a + B, :]
    off_a, live_a = read_note(note_ref)
    off_b, live_b = note_before(got1_ref, got2_ref)
    for s, (side, first, last) in enumerate(((edge_a, off_a, off_a + rows), (edge_b, off_b - rows, off_b))):
        for c in range(cols // LANES):
            part = slice(c * LANES, (c + 1) * LANES)
            for k, base in enumerate((0, rows)):
                span = slice(k * edge, (k + 1) * edge)
                at = (2 * s + k) * edge
                diff[at : at + edge, part] = tile_diff(side[c, span, :], m_ref[c, span, :], base, first, last)
    sides = jnp.dot(diff[...], pcol_ref[...], preferred_element_type=F32).astype(BF16)
    for s, inner in enumerate((filt_a, filt_b)):
        filt[s, 0:edge, :] = sides[2 * s * edge : (2 * s + 1) * edge]
        filt[s, edge:rows, :] = inner[...]
        filt[s, rows : rows + edge, :] = sides[(2 * s + 1) * edge : (2 * s + 2) * edge]
        filt[s, rows + edge :, :] = jnp.zeros((filt.shape[1] - rows - edge, cols), BF16)
    share, depth = prow_ref.shape
    prow = prow_ref[...].astype(F32)
    out_row = iota((share, depth), 0)
    lane = iota((B, cols), 1)
    me = lax.axis_index("visit") * lax.axis_size("band") + lax.axis_index("band")
    for k, out_ref in enumerate(outs):
        base = partner(me, k, len(outs)) * share
        row = out_row + base
        left = jnp.where(row >= off_a, prow * live_a, 0.0).astype(BF16)
        right = jnp.where(row < off_b, prow * live_b, 0.0).astype(BF16)
        span = pl.ds(pl.multiple_of(base, B), depth)
        total = jnp.dot(left, filt[0, span, :], preferred_element_type=F32)
        total += jnp.dot(right, filt[1, span, :], preferred_element_type=F32)
        out_ref[0:share, :] = total.astype(BF16)
        start = jnp.clip(off_a - base, 0, share).astype(F32)
        stop = jnp.clip(off_b - base, 0, share).astype(F32)
        note = jnp.where(lane == 0, start, jnp.where(lane == 1, live_a, jnp.where(lane == 2, stop, live_b)))
        out_ref[share : share + B, :] = note.astype(BF16)


def tile_kernel(sci_ref, note_ref, next_ref, m1_ref, edge_ref, w_ref, out_ref, src, xs, res, big):
    rows, cols = sci_ref.shape
    to_blocks(src, 0, next_ref[...])
    conv_blocks(src, rows // B, w_ref, xs, res)
    for a in range(1, rows // B):
        big[:, rows + B * a : rows + B * (a + 1), :] = res[:, PITCH * a : PITCH * a + B, :]
    big[:, 0:B, :] = edge_ref[:, B : 2 * B, :]
    big[:, B : rows - B, :] = m1_ref[:, B : rows - B, :]
    big[:, rows - B : rows + B, :] = edge_ref[:, 2 * B : 4 * B, :]
    off, _ = read_note(note_ref)
    for c in range(cols // LANES):
        part = slice(c * LANES, (c + 1) * LANES)
        out_ref[:, part] = (sci_ref[:, part].astype(F32) - big[c, pl.ds(off, rows), :]).astype(BF16)


def coadd_kernel(*refs):
    *parts, out_ref = refs
    share, cols = out_ref.shape
    row = iota((share, LANES), 0).astype(F32)
    accum = jnp.zeros((share, cols), F32)
    cover = jnp.zeros((share, LANES), F32)
    for part in parts:
        accum += part[0:share, :].astype(F32)
        note = part[share : share + B, 0:LANES].astype(F32)[0:1, :]
        cover += jnp.where(row >= note[:, 0:1], note[:, 1:2], 0.0)
        cover += jnp.where(row < note[:, 2:3], note[:, 3:4], 0.0)
    scale = lax.rsqrt(jnp.maximum(cover, 1.0))
    for c in range(cols // LANES):
        part = slice(c * LANES, (c + 1) * LANES)
        out_ref[:, part] = accum[:, part] * scale


def in_hbm(*arrays):
    return [pltpu.with_memory_space_constraint(x, pltpu.HBM) for x in arrays]


def call(body, shapes, specs, scratch, flops, name, limit=LIMIT):
    return pl.pallas_call(
        body,
        out_shape=shapes,
        in_specs=specs,
        out_specs=jax.tree.map(lambda _: VM, shapes),
        scratch_shapes=scratch,
        compiler_params=pltpu.CompilerParams(vmem_limit_bytes=limit * 1024 * 1024),
        cost_estimate=pl.CostEstimate(flops=flops, bytes_accessed=1 << 21, transcendentals=0),
        name=name,
    )


def on_device(template, science, offsets, live_flags, bank, basis_index, coeff, psf_profile):
    rows, cols = template.shape
    sharers = lax.axis_size("visit") * lax.axis_size("band")
    share = rows // sharers
    chunks, blocks = cols // LANES, cols // B
    edge = 2 * B
    inner = rows - edge
    sds = jax.ShapeDtypeStruct
    deep = 9 * CH
    depth = -(-(share + edge) // LANES) * LANES
    sci = science[:, 0, :]
    taps = psf_profile.shape[0]
    held = in_hbm(template, sci)
    index = jnp.swapaxes(basis_index, 1, 2)
    before = shifted(science, "patch", 1)[:, 0, :]
    following = shifted(template, "patch", -1)
    note = call(
        pack_kernel, sds((2 * edge, cols), BF16), [HBM] * 3,
        [pltpu.SMEM((1, 1), jnp.int32), pltpu.SMEM((1, 1), jnp.int32), pltpu.SemaphoreType.DMA((4,))],
        1 << 20, "pack",
    )(offsets, live_flags, held[0])
    panels = lax.axis_size("patch")
    got1, got2 = (
        lax.ppermute(note, "patch", [(p, swap_partner(p, parity, panels)) for p in range(panels)])
        for parity in range(2)
    )
    count = rows // B
    conv_scratch = [
        pltpu.VMEM((chunks, count * PITCH, LANES), F32),
        pltpu.VMEM((3, blocks + 2, count, CH), BF16),
        pltpu.VMEM((chunks, count * PITCH, LANES), F32),
    ]
    conv_flops = 2 * rows * cols * deep
    sky_scratch = [pltpu.VMEM((chunks, 2 * rows + B, LANES), F32), pltpu.VMEM((inner, cols), BF16)]
    sides = (sds((chunks, 2 * edge, LANES), F32), sds((inner, cols), BF16))
    w, pcol, prow, tile, m1, edge_a, filt_a = call(
        first_kernel,
        (
            sds((deep, CH), BF16), sds((cols, cols), BF16), sds((share, depth), BF16),
            sds((rows, cols), BF16), sds((chunks, rows, LANES), F32),
        ) + sides,
        [VM] + [HBM] * 6,
        [
            pltpu.VMEM((rows, cols), BF16), pltpu.VMEM(bank.shape, BF16), pltpu.VMEM(index.shape, jnp.int32),
            pltpu.VMEM(coeff.shape, F32), pltpu.VMEM((1, taps), BF16), pltpu.SemaphoreType.DMA((6,)),
        ] + conv_scratch + sky_scratch,
        conv_flops, "first",
    )(note, *held, *in_hbm(bank, index, coeff, psf_profile[None]))
    edge_b, filt_b = call(before_kernel, sides, [VM] * 5, sky_scratch, 1 << 28, "before")(got1, got2, before, m1, pcol)
    *parts, m_edge = call(
        join_kernel,
        (sds((share + B, cols), BF16),) * sharers + (sds((chunks, 2 * edge, LANES), F32),),
        [VM] * 10,
        [
            pltpu.VMEM((chunks, 8 * PITCH, LANES), F32),
            pltpu.VMEM((3, blocks + 2, 8, CH), F32),
            pltpu.VMEM((chunks, 8 * PITCH, LANES), F32),
            pltpu.VMEM((4 * edge, cols), BF16),
            pltpu.VMEM((2, rows - share + depth, cols), BF16),
        ],
        1 << 29, "join",
    )(note, got1, got2, w, pcol, prow, edge_a, edge_b, filt_a, filt_b)
    for k in reversed(range(1, sharers)):
        pairs = [(i, partner(i, k, sharers)) for i in range(sharers)]
        parts[k] = lax.ppermute(parts[k], ("visit", "band"), pairs)
    difference = call(
        tile_kernel, sds((rows, cols), BF16), [VM] * 6,
        conv_scratch + [pltpu.VMEM((chunks, 2 * rows, LANES), F32)], conv_flops, "tile",
    )(tile, note, following, m1, m_edge, w)
    detection = call(coadd_kernel, sds((share, cols), F32), [VM] * sharers, [], 1 << 20, "coadd")(parts[0], *parts[:0:-1])
    return (difference[:, None, :], detection)


def solution(mesh):
    return jax.shard_map(
        on_device,
        mesh=mesh,
        in_specs=(
            P(("group", "patch"), None),
            P(("group", "patch"), ("visit", "band"), None),
            P(("group", "patch"), ("visit", "band")),
            P(("group", "patch"), ("visit", "band")),
            P(),
            P(("group", "visit", "band"), None, None),
            P(("group", "visit", "band"), None),
            P(),
        ),
        out_specs=(
            P(("group", "patch"), ("visit", "band"), None),
            P(("group", "patch", "visit", "band"), None),
        ),
        check_vma=False,
    )
```

```python
import functools

import jax
import jax.numpy as jnp
from jax import lax
from jax.experimental import pallas as pl
from jax.experimental.pallas import tpu as pltpu
from jax.sharding import PartitionSpec as P

B = 16
CH = B * B
LANES = 128
GROUPS = LANES // B
PITCH = B + 1
F32 = jnp.float32
BF16 = jnp.bfloat16


def shifted(shard, axis, by):
    devices = lax.axis_size(axis)
    pairs = [(i, i + by) for i in range(devices) if 0 <= i + by < devices]
    return lax.ppermute(shard, axis, pairs)


def partner(me, k, count):
    return me ^ k if count & (count - 1) == 0 else (me + k) % count


def swapped(shard, axis, k):
    devices = lax.axis_size(axis)
    return lax.ppermute(shard, axis, [(i, partner(i, k, devices)) for i in range(devices)])


def iota(shape, dim):
    return lax.broadcasted_iota(jnp.int32, shape, dim)


LIMIT = 10
VM = pl.BlockSpec(memory_space=pltpu.VMEM)
HBM = pl.BlockSpec(memory_space=pltpu.HBM)


def group_transpose(parts):
    parts = list(parts)
    group = iota(parts[0].shape, 1) // B
    for step in (1, 2, 4):
        low = (group & step) == 0
        for m in range(GROUPS):
            if m & step:
                continue
            x, y = parts[m], parts[m + step]
            parts[m] = jnp.where(low, x, pltpu.roll(y, step * B, 1))
            parts[m + step] = jnp.where(low, pltpu.roll(x, LANES - step * B, 1), y)
    return parts


def to_blocks(dst, block, value):
    value = value.astype(F32)
    for a in range(value.shape[0] // B):
        at = (block + a) * PITCH
        for c in range(dst.shape[0]):
            dst[c, at : at + B, :] = value[a * B : (a + 1) * B, c * LANES : (c + 1) * LANES]


def conv_blocks(src, count, w_ref, xs, dst):
    chunks = src.shape[0]
    blocks = chunks * GROUPS

    def load(c):
        for h in range(2):
            rows = [src[c, pl.ds(GROUPS * h + i, count, stride=PITCH), :] for i in range(GROUPS)]
            part = slice(h * LANES, (h + 1) * LANES)
            for g, here in enumerate(group_transpose(rows)):
                at = 1 + c * GROUPS + g
                xs[0, at, :, part] = pltpu.roll(here, 1, 0).astype(xs.dtype)
                xs[1, at, :, part] = here.astype(xs.dtype)
                xs[2, at, :, part] = pltpu.roll(here, count - 1, 0).astype(xs.dtype)

    def solve(c):
        b = c * GROUPS
        pieces = [
            xs[qr, b + qc : b + qc + GROUPS].reshape(GROUPS * count, CH).astype(BF16)
            for qr in range(3)
            for qc in range(3)
        ]
        out = jnp.dot(jnp.concatenate(pieces, axis=1), w_ref[...], preferred_element_type=F32)
        for h in range(2):
            part = slice(h * LANES, (h + 1) * LANES)
            rows = group_transpose([out[g * count : (g + 1) * count, part] for g in range(GROUPS)])
            for i in range(GROUPS):
                dst[c, pl.ds(GROUPS * h + i, count, stride=PITCH), :] = rows[i]

    for q in range(3):
        xs[q, 0] = jnp.zeros((count, CH), xs.dtype)
        xs[q, blocks + 1] = jnp.zeros((count, CH), xs.dtype)
    load(0)
    for c in range(chunks):
        if c + 1 < chunks:
            load(c + 1)
        solve(c)


def column(row):
    size = row.shape[1]
    diag = iota((size, size), 0) == iota((size, size), 1)
    return jnp.sum(jnp.where(diag, row, jnp.zeros_like(row)), axis=1, keepdims=True)


def pack_kernel(off_hbm, live_hbm, t_hbm, msg_ref, out_ref, off_ref, live_ref, sems):
    rows, cols = t_hbm.shape
    edge = 2 * B
    copies = [
        pltpu.make_async_copy(t_hbm.at[pl.ds(rows - edge, edge)], msg_ref.at[pl.ds(0, edge)], sems.at[0]),
        pltpu.make_async_copy(t_hbm.at[pl.ds(0, edge)], msg_ref.at[pl.ds(edge, edge)], sems.at[1]),
        pltpu.make_async_copy(off_hbm, off_ref, sems.at[2]),
        pltpu.make_async_copy(live_hbm, live_ref, sems.at[3]),
    ]
    for copy in copies:
        copy.start()
    for copy in copies:
        copy.wait()
    lane = iota((1, cols), 1)
    off = off_ref[0, 0]
    note = jnp.where(lane == 0, off // B, jnp.where(lane == 1, off % B, live_ref[0, 0])).astype(F32)
    block = msg_ref[0:B, :].astype(F32)
    msg_ref[0:B, :] = jnp.where(iota((B, cols), 0) == 0, note, block).astype(BF16)
    out_ref[...] = msg_ref[0:edge, :]


def first_kernel(
    note_ref, t_hbm, sci_hbm, bank_hbm, index_hbm, coeff_hbm, psf_hbm,
    w_ref, pcol_ref, prow_ref, sci_ref, m_ref, edge_ref, filt_ref,
    t_ref, bank_ref, index_ref, coeff_ref, psf_ref, sems,
    src, xs, res, sci, diff,
):
    pairs = (
        (bank_hbm, bank_ref), (index_hbm, index_ref), (coeff_hbm, coeff_ref), (psf_hbm, psf_ref),
        (t_hbm, t_ref), (sci_hbm, sci_ref),
    )
    copies = [pltpu.make_async_copy(a, b, sems.at[n]) for n, (a, b) in enumerate(pairs)]
    for copy in copies:
        copy.start()
    for copy in copies[:4]:
        copy.wait()
    profs, taps = bank_ref.shape
    half = taps // 2
    delta = B - half
    bank = bank_ref[...]
    index = index_ref[0].astype(F32)
    labels = iota((index.shape[1], profs), 1).astype(F32)
    pick_row = (column(index[0:1]) == labels).astype(F32).astype(BF16)
    pick_col = (column(index[1:2]) == labels).astype(F32).astype(BF16)
    weight = column(coeff_ref[...])
    rowprof = (weight * jnp.dot(pick_row, bank, preferred_element_type=F32)).astype(BF16)
    colprof = jnp.dot(pick_col, bank, preferred_element_type=F32).astype(BF16)
    span = 3 * B
    total = 4 * B * B
    place = (iota((span, taps), 0) - delta == iota((span, taps), 1)).astype(F32).astype(BF16)
    col_t = lax.dot_general(place, colprof, (((1,), (1,)), ((), ())), preferred_element_type=F32).astype(BF16)
    spread = (span - 1 - iota((taps, total), 1) // B - delta == iota((taps, total), 0)).astype(F32).astype(BF16)
    row_rep = jnp.dot(rowprof, spread, preferred_element_type=F32).astype(BF16)
    z = jnp.dot(col_t, row_rep, preferred_element_type=F32)
    lane = iota((span, total), 1)
    for bit in (1, 2, 4, 8):
        z = jnp.where((lane & bit) != 0, pltpu.roll(z, bit, 0), z)
    z = z.astype(BF16)
    for phase in range(GROUPS):
        zp = z if phase == 0 else pltpu.roll(z, total - phase * B, 1)
        for g in range(span):
            start = span - 1 - g
            if start % GROUPS != phase:
                continue
            at = (start // GROUPS) * LANES
            for qc in range(3):
                row = (g // B) * 3 * CH + qc * CH + (g % B) * B
                w_ref[row : row + B, :] = zp[qc * B : (qc + 1) * B, at : at + CH]
    psf = psf_ref[...].astype(F32)
    size = pcol_ref.shape[0]
    blank = jnp.zeros((LANES, LANES), F32)
    bands = {}
    for off in (-1, 0, 1):
        tap = iota((LANES, LANES), 0) + off * LANES - iota((LANES, LANES), 1) + half
        block = blank
        for t in range(taps):
            block = jnp.where(tap == t, psf[:, t : t + 1], block)
        bands[off] = block.astype(BF16)
    for i in range(size // LANES):
        for j in range(size // LANES):
            pcol_ref[i * LANES : (i + 1) * LANES, j * LANES : (j + 1) * LANES] = bands.get(i - j, blank.astype(BF16))
    shape = prow_ref.shape
    tap = iota(shape, 1) - iota(shape, 0) - delta
    block = jnp.zeros(shape, F32)
    for t in range(taps):
        block = jnp.where(tap == t, psf[:, t : t + 1], block)
    prow_ref[...] = block.astype(BF16)
    for copy in copies[4:]:
        copy.wait()
    edge = 2 * B
    rows, cols = t_ref.shape
    off, _ = read_note(note_ref)
    to_blocks(src, 0, t_ref[...])
    conv_blocks(src, rows // B, w_ref, xs, res)
    for a in range(1, rows // B - 1):
        m_ref[:, B * a : B * (a + 1), :] = res[:, PITCH * a : PITCH * a + B, :]
    to_chunks(sci, rows, sci_ref[...])
    filter_inner(sci, rows - B - off, off, off + rows, m_ref, pcol_ref, edge_ref, filt_ref, diff)


def to_chunks(dst, dst_row, value):
    value = value.astype(F32)
    rows = value.shape[0]
    for c in range(dst.shape[0]):
        dst[c, dst_row : dst_row + rows, :] = value[:, c * LANES : (c + 1) * LANES]


def tile_diff(sky, m, base, first, last):
    row = iota(m.shape, 0) + (base - B)
    return jnp.where((row >= first) & (row < last), sky - m, 0.0).astype(BF16)


def filter_inner(sci, start, first, last, m_ref, pcol_ref, edge_ref, filt_ref, diff):
    chunks, rows, _ = m_ref.shape
    edge = 2 * B
    for c in range(chunks):
        part = slice(c * LANES, (c + 1) * LANES)
        sky = sci[c, pl.ds(start, rows + edge), :]
        edge_ref[c, 0:edge, :] = sky[0:edge]
        edge_ref[c, edge:, :] = sky[rows:]
        diff[:, part] = tile_diff(sky[edge:rows], m_ref[c, B : rows - B, :], edge, first, last)
    filt_ref[...] = jnp.dot(diff[...], pcol_ref[...], preferred_element_type=F32).astype(BF16)


def read_note(msg_ref):
    note = msg_ref[0:B, 0:LANES].astype(F32)
    return (note[0, 0] * B + note[0, 1]).astype(jnp.int32), note[0, 2]


def before_kernel(msg_ref, sci_ref, m_ref, pcol_ref, edge_ref, filt_ref, sci, diff):
    rows = sci_ref.shape[0]
    off, _ = read_note(msg_ref)
    to_chunks(sci, 0, sci_ref[...])
    filter_inner(sci, rows - B - off, off - rows, off, m_ref, pcol_ref, edge_ref, filt_ref, diff)


def join_kernel(
    note_ref, msg_ref, next_ref, w_ref, pcol_ref, prow_ref, edge_a, edge_b, filt_a, filt_b,
    *rest,
):
    *outs, mark_ref, m_ref, src, xs, strip, diff, filt = rest
    edge = 2 * B
    rows, cols = filt_a.shape[0] + edge, filt_a.shape[1]
    to_blocks(src, 0, msg_ref[...])
    to_blocks(src, 2, note_ref[edge:, :])
    to_blocks(src, 4, note_ref[0:edge, :])
    to_blocks(src, 6, next_ref[0:edge, :])
    conv_blocks(src, 8, w_ref, xs, strip)
    for n, a in enumerate((1, 2, 5, 6)):
        m_ref[:, B * n : B * (n + 1), :] = strip[:, PITCH * a : PITCH * a + B, :]
    off_a, live_a = read_note(note_ref)
    off_b, live_b = read_note(msg_ref)
    for s, (side, first, last) in enumerate(((edge_a, off_a, off_a + rows), (edge_b, off_b - rows, off_b))):
        for c in range(cols // LANES):
            part = slice(c * LANES, (c + 1) * LANES)
            for k, base in enumerate((0, rows)):
                span = slice(k * edge, (k + 1) * edge)
                at = (2 * s + k) * edge
                diff[at : at + edge, part] = tile_diff(side[c, span, :], m_ref[c, span, :], base, first, last)
    sides = jnp.dot(diff[...], pcol_ref[...], preferred_element_type=F32).astype(BF16)
    for s, inner in enumerate((filt_a, filt_b)):
        filt[s, 0:edge, :] = sides[2 * s * edge : (2 * s + 1) * edge]
        filt[s, edge:rows, :] = inner[...]
        filt[s, rows : rows + edge, :] = sides[(2 * s + 1) * edge : (2 * s + 2) * edge]
        filt[s, rows + edge :, :] = jnp.zeros((filt.shape[1] - rows - edge, cols), BF16)
    share, depth = prow_ref.shape
    prow = prow_ref[...].astype(F32)
    out_row = iota((share, depth), 0)
    lane = iota((B, cols), 1)
    visits, bands = lax.axis_size("visit"), lax.axis_size("band")
    hi, lo = off_b // B, off_b % B
    marks = note_ref[0:B, 0:LANES].astype(F32)
    marks = jnp.where(iota(marks.shape, 1) == 3, hi.astype(F32), marks)
    marks = jnp.where(iota(marks.shape, 1) == 4, lo.astype(F32), marks)
    marks = jnp.where(iota(marks.shape, 1) == 5, live_b, marks)
    mark_ref[...] = marks.astype(BF16)
    for j, out_ref in enumerate(outs):
        for k in range(visits):
            to_visit = partner(lax.axis_index("visit"), k, visits)
            base = (to_visit * bands + partner(lax.axis_index("band"), j, bands)) * share
            row = out_row + base
            left = jnp.where(row >= off_a, prow * live_a, 0.0).astype(BF16)
            right = jnp.where(row < off_b, prow * live_b, 0.0).astype(BF16)
            span = pl.ds(pl.multiple_of(base, B), depth)
            total = jnp.dot(left, filt[0, span, :], preferred_element_type=F32)
            total += jnp.dot(right, filt[1, span, :], preferred_element_type=F32)
            out_ref[k * share : (k + 1) * share, :] = total.astype(out_ref.dtype)
        if j:
            out_ref[visits * share :, 0:LANES] = marks.astype(BF16)
            out_ref[visits * share :, LANES:] = jnp.zeros((B, cols - LANES), BF16)


def pair_kernel(*refs):
    bands = lax.axis_size("band")
    visits = lax.axis_size("visit")
    mark_ref, keep_ref, *got = refs[: bands + 1]
    *outs, own_mark_ref = refs[bands + 1 :]
    share, cols = outs[0].shape
    rowid = iota((B, LANES), 0)
    marks = jnp.where(rowid == 0, mark_ref[...].astype(F32), 0.0)
    for n, ref in enumerate(got):
        other = ref[visits * share :, 0:LANES].astype(F32)
        marks = jnp.where(rowid == n + 1, other[0:1, :], marks)
    own_mark_ref[...] = marks.astype(BF16)
    for k, out_ref in enumerate(outs):
        span = slice(k * share, (k + 1) * share)
        total = keep_ref[span, :]
        for ref in got:
            total += ref[span, :].astype(F32)
        out_ref[0:share, :] = total.astype(out_ref.dtype)
        if k:
            out_ref[share:, 0:LANES] = marks.astype(BF16)
            out_ref[share:, LANES:] = jnp.zeros((B, cols - LANES), BF16)


def tile_kernel(mark_ref, sci_ref, note_ref, next_ref, m1_ref, edge_ref, w_ref, out_ref, src, xs, res, big):
    rows, cols = sci_ref.shape
    to_blocks(src, 0, next_ref[...])
    conv_blocks(src, rows // B, w_ref, xs, res)
    for a in range(1, rows // B):
        big[:, rows + B * a : rows + B * (a + 1), :] = res[:, PITCH * a : PITCH * a + B, :]
    big[:, 0:B, :] = edge_ref[:, B : 2 * B, :]
    big[:, B : rows - B, :] = m1_ref[:, B : rows - B, :]
    big[:, rows - B : rows + B, :] = edge_ref[:, 2 * B : 4 * B, :]
    off, _ = read_note(note_ref)
    for c in range(cols // LANES):
        part = slice(c * LANES, (c + 1) * LANES)
        out_ref[:, part] = (sci_ref[:, part].astype(F32) - big[c, pl.ds(off, rows), :]).astype(BF16)


def coadd_kernel(mark_ref, *refs):
    *parts, out_ref = refs
    share, cols = out_ref.shape
    bands = lax.axis_size("band")
    base = (lax.axis_index("visit") * bands + lax.axis_index("band")) * share
    row = (iota((share, LANES), 0) + base).astype(F32)
    accum = parts[0][...]
    cover = jnp.zeros((share, LANES), F32)
    for n, part in enumerate(parts):
        if n:
            accum += part[0:share, :].astype(F32)
        marks = (part[share : share + B, 0:LANES] if n else mark_ref[...]).astype(F32)
        for m in range(bands):
            mark = marks[m : m + 1, :]
            cover += jnp.where(row >= mark[:, 0:1] * B + mark[:, 1:2], mark[:, 2:3], 0.0)
            cover += jnp.where(row < mark[:, 3:4] * B + mark[:, 4:5], mark[:, 5:6], 0.0)
    scale = lax.rsqrt(jnp.maximum(cover, 1.0))
    for c in range(cols // LANES):
        part = slice(c * LANES, (c + 1) * LANES)
        out_ref[:, part] = accum[:, part] * scale


def in_hbm(*arrays):
    return [pltpu.with_memory_space_constraint(x, pltpu.HBM) for x in arrays]


def call(body, shapes, specs, scratch, flops, name, limit=LIMIT):
    return pl.pallas_call(
        body,
        out_shape=shapes,
        in_specs=specs,
        out_specs=jax.tree.map(lambda _: VM, shapes),
        scratch_shapes=scratch,
        compiler_params=pltpu.CompilerParams(vmem_limit_bytes=limit * 1024 * 1024),
        cost_estimate=pl.CostEstimate(flops=flops, bytes_accessed=1 << 21, transcendentals=0),
        name=name,
    )


def on_device(template, science, offsets, live_flags, bank, basis_index, coeff, psf_profile):
    rows, cols = template.shape
    sharers = lax.axis_size("visit") * lax.axis_size("band")
    share = rows // sharers
    chunks, blocks = cols // LANES, cols // B
    edge = 2 * B
    inner = rows - edge
    sds = jax.ShapeDtypeStruct
    deep = 9 * CH
    depth = -(-(share + edge) // LANES) * LANES
    sci = science[:, 0, :]
    taps = psf_profile.shape[0]
    held = in_hbm(template, sci)
    index = jnp.swapaxes(basis_index, 1, 2)
    before = shifted(science, "patch", 1)[:, 0, :]
    following = shifted(template, "patch", -1)
    note, msg = call(
        pack_kernel, (sds((2 * edge, cols), BF16), sds((edge, cols), BF16)), [HBM] * 3,
        [pltpu.SMEM((1, 1), jnp.int32), pltpu.SMEM((1, 1), jnp.int32), pltpu.SemaphoreType.DMA((4,))],
        1 << 20, "pack",
    )(offsets, live_flags, held[0])
    msg = shifted(msg, "patch", 1)
    count = rows // B
    conv_scratch = [
        pltpu.VMEM((chunks, count * PITCH, LANES), F32),
        pltpu.VMEM((3, blocks + 2, count, CH), BF16),
        pltpu.VMEM((chunks, count * PITCH, LANES), F32),
    ]
    conv_flops = 2 * rows * cols * deep
    sky_scratch = [pltpu.VMEM((chunks, 2 * rows + B, LANES), F32), pltpu.VMEM((inner, cols), BF16)]
    sides = (sds((chunks, 2 * edge, LANES), F32), sds((inner, cols), BF16))
    w, pcol, prow, tile, m1, edge_a, filt_a = call(
        first_kernel,
        (
            sds((deep, CH), BF16), sds((cols, cols), BF16), sds((share, depth), BF16),
            sds((rows, cols), BF16), sds((chunks, rows, LANES), F32),
        ) + sides,
        [VM] + [HBM] * 6,
        [
            pltpu.VMEM((rows, cols), BF16), pltpu.VMEM(bank.shape, BF16), pltpu.VMEM(index.shape, jnp.int32),
            pltpu.VMEM(coeff.shape, F32), pltpu.VMEM((1, taps), BF16), pltpu.SemaphoreType.DMA((6,)),
        ] + conv_scratch + sky_scratch,
        conv_flops, "first",
    )(note, *held, *in_hbm(bank, index, coeff, psf_profile[None]))
    edge_b, filt_b = call(before_kernel, sides, [VM] * 4, sky_scratch, 1 << 28, "before")(msg, before, m1, pcol)
    bands, visits = lax.axis_size("band"), lax.axis_size("visit")
    whole = visits * share
    keep, *sent, mark, m_edge = call(
        join_kernel,
        (sds((whole, cols), F32),) + (sds((whole + B, cols), BF16),) * (bands - 1)
        + (sds((B, LANES), BF16), sds((chunks, 2 * edge, LANES), F32)),
        [VM] * 10,
        [
            pltpu.VMEM((chunks, 8 * PITCH, LANES), F32),
            pltpu.VMEM((3, blocks + 2, 8, CH), F32),
            pltpu.VMEM((chunks, 8 * PITCH, LANES), F32),
            pltpu.VMEM((4 * edge, cols), BF16),
            pltpu.VMEM((2, rows - share + depth, cols), BF16),
        ],
        1 << 29, "join",
    )(note, msg, following, w, pcol, prow, edge_a, edge_b, filt_a, filt_b)
    got = [swapped(part, "band", k + 1) for k, part in enumerate(sent)]
    own, *sent, mark = call(
        pair_kernel,
        (sds((share, cols), F32),) + (sds((share + B, cols), BF16),) * (visits - 1) + (sds((B, LANES), BF16),),
        [VM] * (1 + bands), [], 1 << 20, "pair",
    )(mark, keep, *got)
    got = [swapped(part, "visit", k + 1) for k, part in enumerate(sent)]
    difference = call(
        tile_kernel, sds((rows, cols), BF16), [VM] * 7,
        conv_scratch + [pltpu.VMEM((chunks, 2 * rows, LANES), F32)], conv_flops, "tile",
    )(mark, tile, note, following, m1, m_edge, w)
    detection = call(
        coadd_kernel, sds((share, cols), F32), [VM] * (1 + visits), [], 1 << 20, "coadd"
    )(mark, own, *got)
    return (difference[:, None, :], detection)


def solution(mesh):
    return jax.shard_map(
        on_device,
        mesh=mesh,
        in_specs=(
            P(("group", "patch"), None),
            P(("group", "patch"), ("visit", "band"), None),
            P(("group", "patch"), ("visit", "band")),
            P(("group", "patch"), ("visit", "band")),
            P(),
            P(("group", "visit", "band"), None, None),
            P(("group", "visit", "band"), None),
            P(),
        ),
        out_specs=(
            P(("group", "patch"), ("visit", "band"), None),
            P(("group", "patch", "visit", "band"), None),
        ),
        check_vma=False,
    )
```

```python
import functools

import jax
import jax.numpy as jnp
from jax import lax
from jax.experimental import pallas as pl
from jax.experimental.pallas import tpu as pltpu
from jax.sharding import PartitionSpec as P

B = 16
CH = B * B
LANES = 128
GROUPS = LANES // B
PITCH = B + 1
F32 = jnp.float32
BF16 = jnp.bfloat16


def shifted(shard, axis, by):
    devices = lax.axis_size(axis)
    pairs = [(i, i + by) for i in range(devices) if 0 <= i + by < devices]
    return lax.ppermute(shard, axis, pairs)


def partner(me, k, count):
    return me ^ k if count & (count - 1) == 0 else (me + k) % count


def swapped(shard, axis, k):
    devices = lax.axis_size(axis)
    return lax.ppermute(shard, axis, [(i, partner(i, k, devices)) for i in range(devices)])


def iota(shape, dim):
    return lax.broadcasted_iota(jnp.int32, shape, dim)


LIMIT = 10
VM = pl.BlockSpec(memory_space=pltpu.VMEM)
HBM = pl.BlockSpec(memory_space=pltpu.HBM)


def group_transpose(parts):
    parts = list(parts)
    group = iota(parts[0].shape, 1) // B
    for step in (1, 2, 4):
        low = (group & step) == 0
        for m in range(GROUPS):
            if m & step:
                continue
            x, y = parts[m], parts[m + step]
            parts[m] = jnp.where(low, x, pltpu.roll(y, step * B, 1))
            parts[m + step] = jnp.where(low, pltpu.roll(x, LANES - step * B, 1), y)
    return parts


def to_blocks(dst, block, value):
    value = value.astype(F32)
    for a in range(value.shape[0] // B):
        at = (block + a) * PITCH
        for c in range(dst.shape[0]):
            dst[c, at : at + B, :] = value[a * B : (a + 1) * B, c * LANES : (c + 1) * LANES]


def conv_blocks(src, count, w_ref, xs, dst):
    chunks = src.shape[0]
    blocks = chunks * GROUPS

    def load(c):
        for h in range(2):
            rows = [src[c, pl.ds(GROUPS * h + i, count, stride=PITCH), :] for i in range(GROUPS)]
            part = slice(h * LANES, (h + 1) * LANES)
            for g, here in enumerate(group_transpose(rows)):
                at = 1 + c * GROUPS + g
                xs[0, at, :, part] = pltpu.roll(here, 1, 0).astype(xs.dtype)
                xs[1, at, :, part] = here.astype(xs.dtype)
                xs[2, at, :, part] = pltpu.roll(here, count - 1, 0).astype(xs.dtype)

    def solve(c):
        b = c * GROUPS
        pieces = [
            xs[qr, b + qc : b + qc + GROUPS].reshape(GROUPS * count, CH).astype(BF16)
            for qr in range(3)
            for qc in range(3)
        ]
        out = jnp.dot(jnp.concatenate(pieces, axis=1), w_ref[...], preferred_element_type=F32)
        for h in range(2):
            part = slice(h * LANES, (h + 1) * LANES)
            rows = group_transpose([out[g * count : (g + 1) * count, part] for g in range(GROUPS)])
            for i in range(GROUPS):
                dst[c, pl.ds(GROUPS * h + i, count, stride=PITCH), :] = rows[i]

    for q in range(3):
        xs[q, 0] = jnp.zeros((count, CH), xs.dtype)
        xs[q, blocks + 1] = jnp.zeros((count, CH), xs.dtype)
    load(0)
    for c in range(chunks):
        if c + 1 < chunks:
            load(c + 1)
        solve(c)


def column(row):
    size = row.shape[1]
    diag = iota((size, size), 0) == iota((size, size), 1)
    return jnp.sum(jnp.where(diag, row, jnp.zeros_like(row)), axis=1, keepdims=True)


def pack_kernel(
    off_hbm, live_hbm, t_hbm, bank_hbm, index_hbm, coeff_hbm, psf_hbm,
    note_ref, msg_ref, half_ref, bank_ref, index_ref, coeff_ref, psf_ref, off_ref, live_ref, sems,
):
    rows, cols = t_hbm.shape
    edge = 2 * B
    piece = half_ref.shape[0] - edge
    begin = pl.multiple_of(lax.axis_index("band") * piece, B)
    copies = [
        pltpu.make_async_copy(a, b, sems.at[n])
        for n, (a, b) in enumerate((
            (off_hbm, off_ref), (live_hbm, live_ref),
            (t_hbm.at[pl.ds(rows - edge, edge)], note_ref.at[pl.ds(0, edge)]),
            (t_hbm.at[pl.ds(0, edge)], note_ref.at[pl.ds(edge, edge)]),
            (t_hbm.at[pl.ds(0, edge)], half_ref.at[pl.ds(0, edge)]),
            (t_hbm.at[pl.ds(begin, piece)], half_ref.at[pl.ds(edge, piece)]),
            (bank_hbm, bank_ref), (index_hbm, index_ref), (coeff_hbm, coeff_ref), (psf_hbm, psf_ref),
        ))
    ]
    for copy in copies:
        copy.start()
    for copy in copies:
        copy.wait()
    lane = iota((1, cols), 1)
    off = off_ref[0, 0]
    note = jnp.where(lane == 0, off // B, jnp.where(lane == 1, off % B, live_ref[0, 0])).astype(F32)
    block = note_ref[0:B, :].astype(F32)
    note_ref[0:B, :] = jnp.where(iota((B, cols), 0) == 0, note, block).astype(BF16)
    msg_ref[...] = note_ref[0:edge, :]


def first_kernel(
    note_ref, t_hbm, sci_hbm, bank_ref, index_ref, coeff_ref, psf_ref,
    w_ref, pcol_ref, prow_ref, sci_ref, m_ref, edge_ref, filt_ref,
    t_ref, sems, src, xs, res, sci, diff,
):
    copies = [
        pltpu.make_async_copy(t_hbm, t_ref, sems.at[0]), pltpu.make_async_copy(sci_hbm, sci_ref, sems.at[1])
    ]
    for copy in copies:
        copy.start()
    profs, taps = bank_ref.shape
    half = taps // 2
    delta = B - half
    bank = bank_ref[...]
    index = index_ref[0].astype(F32)
    labels = iota((index.shape[1], profs), 1).astype(F32)
    pick_row = (column(index[0:1]) == labels).astype(F32).astype(BF16)
    pick_col = (column(index[1:2]) == labels).astype(F32).astype(BF16)
    weight = column(coeff_ref[...])
    rowprof = (weight * jnp.dot(pick_row, bank, preferred_element_type=F32)).astype(BF16)
    colprof = jnp.dot(pick_col, bank, preferred_element_type=F32).astype(BF16)
    span = 3 * B
    total = 4 * B * B
    place = (iota((span, taps), 0) - delta == iota((span, taps), 1)).astype(F32).astype(BF16)
    col_t = lax.dot_general(place, colprof, (((1,), (1,)), ((), ())), preferred_element_type=F32).astype(BF16)
    spread = (span - 1 - iota((taps, total), 1) // B - delta == iota((taps, total), 0)).astype(F32).astype(BF16)
    row_rep = jnp.dot(rowprof, spread, preferred_element_type=F32).astype(BF16)
    z = jnp.dot(col_t, row_rep, preferred_element_type=F32)
    lane = iota((span, total), 1)
    for bit in (1, 2, 4, 8):
        z = jnp.where((lane & bit) != 0, pltpu.roll(z, bit, 0), z)
    z = z.astype(BF16)
    for phase in range(GROUPS):
        zp = z if phase == 0 else pltpu.roll(z, total - phase * B, 1)
        for g in range(span):
            start = span - 1 - g
            if start % GROUPS != phase:
                continue
            at = (start // GROUPS) * LANES
            for qc in range(3):
                row = (g // B) * 3 * CH + qc * CH + (g % B) * B
                w_ref[row : row + B, :] = zp[qc * B : (qc + 1) * B, at : at + CH]
    psf = psf_ref[...].astype(F32)
    size = pcol_ref.shape[0]
    blank = jnp.zeros((LANES, LANES), F32)
    bands = {}
    for off in (-1, 0, 1):
        tap = iota((LANES, LANES), 0) + off * LANES - iota((LANES, LANES), 1) + half
        block = blank
        for t in range(taps):
            block = jnp.where(tap == t, psf[:, t : t + 1], block)
        bands[off] = block.astype(BF16)
    for i in range(size // LANES):
        for j in range(size // LANES):
            pcol_ref[i * LANES : (i + 1) * LANES, j * LANES : (j + 1) * LANES] = bands.get(i - j, blank.astype(BF16))
    shape = prow_ref.shape
    tap = iota(shape, 1) - iota(shape, 0) - delta
    block = jnp.zeros(shape, F32)
    for t in range(taps):
        block = jnp.where(tap == t, psf[:, t : t + 1], block)
    prow_ref[...] = block.astype(BF16)
    for copy in copies:
        copy.wait()
    edge = 2 * B
    rows, cols = t_ref.shape
    off, _ = read_note(note_ref)
    to_blocks(src, 0, t_ref[...])
    conv_blocks(src, rows // B, w_ref, xs, res)
    for a in range(1, rows // B - 1):
        m_ref[:, B * a : B * (a + 1), :] = res[:, PITCH * a : PITCH * a + B, :]
    to_chunks(sci, rows, sci_ref[...])
    filter_inner(sci, rows - B - off, off, off + rows, m_ref, pcol_ref, edge_ref, filt_ref, diff)


def to_chunks(dst, dst_row, value):
    value = value.astype(F32)
    rows = value.shape[0]
    for c in range(dst.shape[0]):
        dst[c, dst_row : dst_row + rows, :] = value[:, c * LANES : (c + 1) * LANES]


def tile_diff(sky, m, base, first, last):
    row = iota(m.shape, 0) + (base - B)
    return jnp.where((row >= first) & (row < last), sky - m, 0.0).astype(BF16)


def filter_inner(sci, start, first, last, m_ref, pcol_ref, edge_ref, filt_ref, diff):
    chunks, rows, _ = m_ref.shape
    edge = 2 * B
    for c in range(chunks):
        part = slice(c * LANES, (c + 1) * LANES)
        sky = sci[c, pl.ds(start, rows + edge), :]
        edge_ref[c, 0:edge, :] = sky[0:edge]
        edge_ref[c, edge:, :] = sky[rows:]
        diff[:, part] = tile_diff(sky[edge:rows], m_ref[c, B : rows - B, :], edge, first, last)
    filt_ref[...] = jnp.dot(diff[...], pcol_ref[...], preferred_element_type=F32).astype(BF16)


def read_note(msg_ref):
    note = msg_ref[0:B, 0:LANES].astype(F32)
    return (note[0, 0] * B + note[0, 1]).astype(jnp.int32), note[0, 2]


def before_kernel(msg_ref, sci_ref, m_ref, pcol_ref, edge_ref, filt_ref, sci, diff):
    rows = sci_ref.shape[0]
    off, _ = read_note(msg_ref)
    to_chunks(sci, 0, sci_ref[...])
    filter_inner(sci, rows - B - off, off - rows, off, m_ref, pcol_ref, edge_ref, filt_ref, diff)


def join_kernel(
    note_ref, msg_ref, next_ref, w_ref, pcol_ref, prow_ref, edge_a, edge_b, filt_a, filt_b,
    *rest,
):
    *outs, mark_ref, m_ref, src, xs, strip, diff, filt = rest
    edge = 2 * B
    rows, cols = filt_a.shape[0] + edge, filt_a.shape[1]
    to_blocks(src, 0, msg_ref[...])
    to_blocks(src, 2, note_ref[edge:, :])
    to_blocks(src, 4, note_ref[0:edge, :])
    to_blocks(src, 6, next_ref[0:edge, :])
    conv_blocks(src, 8, w_ref, xs, strip)
    for n, a in enumerate((1, 2, 5, 6)):
        m_ref[:, B * n : B * (n + 1), :] = strip[:, PITCH * a : PITCH * a + B, :]
    off_a, live_a = read_note(note_ref)
    off_b, live_b = read_note(msg_ref)
    for s, (side, first, last) in enumerate(((edge_a, off_a, off_a + rows), (edge_b, off_b - rows, off_b))):
        for c in range(cols // LANES):
            part = slice(c * LANES, (c + 1) * LANES)
            for k, base in enumerate((0, rows)):
                span = slice(k * edge, (k + 1) * edge)
                at = (2 * s + k) * edge
                diff[at : at + edge, part] = tile_diff(side[c, span, :], m_ref[c, span, :], base, first, last)
    sides = jnp.dot(diff[...], pcol_ref[...], preferred_element_type=F32).astype(BF16)
    for s, inner in enumerate((filt_a, filt_b)):
        filt[s, 0:edge, :] = sides[2 * s * edge : (2 * s + 1) * edge]
        filt[s, edge:rows, :] = inner[...]
        filt[s, rows : rows + edge, :] = sides[(2 * s + 1) * edge : (2 * s + 2) * edge]
        filt[s, rows + edge :, :] = jnp.zeros((filt.shape[1] - rows - edge, cols), BF16)
    share, depth = prow_ref.shape
    prow = prow_ref[...].astype(F32)
    out_row = iota((share, depth), 0)
    lane = iota((B, cols), 1)
    visits, bands = lax.axis_size("visit"), lax.axis_size("band")
    hi, lo = off_b // B, off_b % B
    marks = note_ref[0:B, 0:LANES].astype(F32)
    marks = jnp.where(iota(marks.shape, 1) == 3, hi.astype(F32), marks)
    marks = jnp.where(iota(marks.shape, 1) == 4, lo.astype(F32), marks)
    marks = jnp.where(iota(marks.shape, 1) == 5, live_b, marks)
    mark_ref[...] = marks.astype(BF16)
    for j, out_ref in enumerate(outs):
        for k in range(visits):
            to_visit = partner(lax.axis_index("visit"), k, visits)
            base = (to_visit * bands + partner(lax.axis_index("band"), j, bands)) * share
            row = out_row + base
            left = jnp.where(row >= off_a, prow * live_a, 0.0).astype(BF16)
            right = jnp.where(row < off_b, prow * live_b, 0.0).astype(BF16)
            span = pl.ds(pl.multiple_of(base, B), depth)
            total = jnp.dot(left, filt[0, span, :], preferred_element_type=F32)
            total += jnp.dot(right, filt[1, span, :], preferred_element_type=F32)
            out_ref[k * share : (k + 1) * share, :] = total.astype(out_ref.dtype)
        if j:
            out_ref[visits * share :, 0:LANES] = marks.astype(BF16)
            out_ref[visits * share :, LANES:] = jnp.zeros((B, cols - LANES), BF16)


def pair_kernel(*refs):
    bands = lax.axis_size("band")
    visits = lax.axis_size("visit")
    mark_ref, keep_ref, *got = refs[: bands + 1]
    *outs, own_mark_ref = refs[bands + 1 :]
    share, cols = outs[0].shape
    rowid = iota((B, LANES), 0)
    marks = jnp.where(rowid == 0, mark_ref[...].astype(F32), 0.0)
    for n, ref in enumerate(got):
        other = ref[visits * share :, 0:LANES].astype(F32)
        marks = jnp.where(rowid == n + 1, other[0:1, :], marks)
    own_mark_ref[...] = marks.astype(BF16)
    for k, out_ref in enumerate(outs):
        span = slice(k * share, (k + 1) * share)
        total = keep_ref[span, :]
        for ref in got:
            total += ref[span, :].astype(F32)
        out_ref[0:share, :] = total.astype(out_ref.dtype)
        if k:
            out_ref[share:, 0:LANES] = marks.astype(BF16)
            out_ref[share:, LANES:] = jnp.zeros((B, cols - LANES), BF16)


def tile_kernel(mark_ref, sci_ref, note_ref, m1_ref, edge_ref, w_ref, *rest):
    rows, cols = sci_ref.shape
    *halves, out_ref, src, xs, res, big = rest
    bands = len(halves)
    blocks = rows // B // bands
    band = lax.axis_index("band")
    for j in range(bands):
        piece = halves[0][2 * B :, :].astype(F32)
        for k in range(1, bands):
            piece = jnp.where(partner(band, k, bands) == j, halves[k][2 * B :, :].astype(F32), piece)
        to_blocks(src, j * blocks, piece)
    conv_blocks(src, rows // B, w_ref, xs, res)
    for a in range(1, rows // B):
        big[:, rows + B * a : rows + B * (a + 1), :] = res[:, PITCH * a : PITCH * a + B, :]
    big[:, 0:B, :] = edge_ref[:, B : 2 * B, :]
    big[:, B : rows - B, :] = m1_ref[:, B : rows - B, :]
    big[:, rows - B : rows + B, :] = edge_ref[:, 2 * B : 4 * B, :]
    off, _ = read_note(note_ref)
    for c in range(cols // LANES):
        part = slice(c * LANES, (c + 1) * LANES)
        out_ref[:, part] = (sci_ref[:, part].astype(F32) - big[c, pl.ds(off, rows), :]).astype(BF16)


def coadd_kernel(mark_ref, *refs):
    *parts, out_ref = refs
    share, cols = out_ref.shape
    bands = lax.axis_size("band")
    base = (lax.axis_index("visit") * bands + lax.axis_index("band")) * share
    row = (iota((share, LANES), 0) + base).astype(F32)
    accum = parts[0][...]
    cover = jnp.zeros((share, LANES), F32)
    for n, part in enumerate(parts):
        if n:
            accum += part[0:share, :].astype(F32)
        marks = (part[share : share + B, 0:LANES] if n else mark_ref[...]).astype(F32)
        for m in range(bands):
            mark = marks[m : m + 1, :]
            cover += jnp.where(row >= mark[:, 0:1] * B + mark[:, 1:2], mark[:, 2:3], 0.0)
            cover += jnp.where(row < mark[:, 3:4] * B + mark[:, 4:5], mark[:, 5:6], 0.0)
    scale = lax.rsqrt(jnp.maximum(cover, 1.0))
    for c in range(cols // LANES):
        part = slice(c * LANES, (c + 1) * LANES)
        out_ref[:, part] = accum[:, part] * scale


def in_hbm(*arrays):
    return [pltpu.with_memory_space_constraint(x, pltpu.HBM) for x in arrays]


def call(body, shapes, specs, scratch, flops, name, limit=LIMIT):
    return pl.pallas_call(
        body,
        out_shape=shapes,
        in_specs=specs,
        out_specs=jax.tree.map(lambda _: VM, shapes),
        scratch_shapes=scratch,
        compiler_params=pltpu.CompilerParams(vmem_limit_bytes=limit * 1024 * 1024),
        cost_estimate=pl.CostEstimate(flops=flops, bytes_accessed=1 << 21, transcendentals=0),
        name=name,
    )


def on_device(template, science, offsets, live_flags, bank, basis_index, coeff, psf_profile):
    rows, cols = template.shape
    sharers = lax.axis_size("visit") * lax.axis_size("band")
    share = rows // sharers
    chunks, blocks = cols // LANES, cols // B
    edge = 2 * B
    inner = rows - edge
    sds = jax.ShapeDtypeStruct
    deep = 9 * CH
    depth = -(-(share + edge) // LANES) * LANES
    sci = science[:, 0, :]
    held = in_hbm(template, sci)
    index = jnp.swapaxes(basis_index, 1, 2)
    before = shifted(science, "patch", 1)[:, 0, :]
    bands, visits = lax.axis_size("band"), lax.axis_size("visit")
    psf = psf_profile[None]
    note, msg, half, *small = call(
        pack_kernel,
        (
            sds((2 * edge, cols), BF16), sds((edge, cols), BF16), sds((edge + rows // bands, cols), BF16),
            *(sds(x.shape, x.dtype) for x in (bank, index, coeff, psf)),
        ),
        [HBM] * 7,
        [pltpu.SMEM((1, 1), jnp.int32), pltpu.SMEM((1, 1), jnp.int32), pltpu.SemaphoreType.DMA((10,))],
        1 << 20, "pack",
    )(offsets, live_flags, held[0], *in_hbm(bank, index, coeff, psf))
    half = shifted(half, "patch", -1)
    msg = shifted(msg, "patch", 1)
    count = rows // B
    conv_scratch = [
        pltpu.VMEM((chunks, count * PITCH, LANES), F32),
        pltpu.VMEM((3, blocks + 2, count, CH), BF16),
        pltpu.VMEM((chunks, count * PITCH, LANES), F32),
    ]
    conv_flops = 2 * rows * cols * deep
    sky_scratch = [pltpu.VMEM((chunks, 2 * rows + B, LANES), F32), pltpu.VMEM((inner, cols), BF16)]
    sides = (sds((chunks, 2 * edge, LANES), F32), sds((inner, cols), BF16))
    w, pcol, prow, tile, m1, edge_a, filt_a = call(
        first_kernel,
        (
            sds((deep, CH), BF16), sds((cols, cols), BF16), sds((share, depth), BF16),
            sds((rows, cols), BF16), sds((chunks, rows, LANES), F32),
        ) + sides,
        [VM, HBM, HBM] + [VM] * 4,
        [pltpu.VMEM((rows, cols), BF16), pltpu.SemaphoreType.DMA((2,))] + conv_scratch + sky_scratch,
        conv_flops, "first",
    )(note, *held, *small)
    edge_b, filt_b = call(before_kernel, sides, [VM] * 4, sky_scratch, 1 << 28, "before")(msg, before, m1, pcol)
    whole = visits * share
    keep, *sent, mark, m_edge = call(
        join_kernel,
        (sds((whole, cols), F32),) + (sds((whole + B, cols), BF16),) * (bands - 1)
        + (sds((B, LANES), BF16), sds((chunks, 2 * edge, LANES), F32)),
        [VM] * 10,
        [
            pltpu.VMEM((chunks, 8 * PITCH, LANES), F32),
            pltpu.VMEM((3, blocks + 2, 8, CH), F32),
            pltpu.VMEM((chunks, 8 * PITCH, LANES), F32),
            pltpu.VMEM((4 * edge, cols), BF16),
            pltpu.VMEM((2, rows - share + depth, cols), BF16),
        ],
        1 << 29, "join",
    )(note, msg, half, w, pcol, prow, edge_a, edge_b, filt_a, filt_b)
    got = [swapped(part, "band", k + 1) for k, part in enumerate(sent)]
    halves = [half] + [swapped(half, "band", k) for k in range(1, bands)]
    own, *sent, mark = call(
        pair_kernel,
        (sds((share, cols), F32),) + (sds((share + B, cols), BF16),) * (visits - 1) + (sds((B, LANES), BF16),),
        [VM] * (1 + bands), [], 1 << 20, "pair",
    )(mark, keep, *got)
    got = [swapped(part, "visit", k + 1) for k, part in enumerate(sent)]
    difference = call(
        tile_kernel, sds((rows, cols), BF16), [VM] * (6 + bands),
        conv_scratch + [pltpu.VMEM((chunks, 2 * rows, LANES), F32)], conv_flops, "tile",
    )(mark, tile, note, m1, m_edge, w, *halves)
    detection = call(
        coadd_kernel, sds((share, cols), F32), [VM] * (1 + visits), [], 1 << 20, "coadd"
    )(mark, own, *got)
    return (difference[:, None, :], detection)


def solution(mesh):
    return jax.shard_map(
        on_device,
        mesh=mesh,
        in_specs=(
            P(("group", "patch"), None),
            P(("group", "patch"), ("visit", "band"), None),
            P(("group", "patch"), ("visit", "band")),
            P(("group", "patch"), ("visit", "band")),
            P(),
            P(("group", "visit", "band"), None, None),
            P(("group", "visit", "band"), None),
            P(),
        ),
        out_specs=(
            P(("group", "patch"), ("visit", "band"), None),
            P(("group", "patch", "visit", "band"), None),
        ),
        check_vma=False,
    )
```

```python
import functools

import jax
import jax.numpy as jnp
from jax import lax
from jax.experimental import pallas as pl
from jax.experimental.pallas import tpu as pltpu
from jax.sharding import PartitionSpec as P

B = 16
CH = B * B
LANES = 128
GROUPS = LANES // B
PITCH = B + 1
F32 = jnp.float32
BF16 = jnp.bfloat16


def shifted(shard, axis, by):
    devices = lax.axis_size(axis)
    pairs = [(i, i + by) for i in range(devices) if 0 <= i + by < devices]
    return lax.ppermute(shard, axis, pairs)


def partner(me, k, count):
    return me ^ k if count & (count - 1) == 0 else (me + k) % count


def swapped(shard, axis, k):
    devices = lax.axis_size(axis)
    return lax.ppermute(shard, axis, [(i, partner(i, k, devices)) for i in range(devices)])


def iota(shape, dim):
    return lax.broadcasted_iota(jnp.int32, shape, dim)


LIMIT = 10
VM = pl.BlockSpec(memory_space=pltpu.VMEM)
HBM = pl.BlockSpec(memory_space=pltpu.HBM)


def group_transpose(parts):
    parts = list(parts)
    group = iota(parts[0].shape, 1) // B
    for step in (1, 2, 4):
        low = (group & step) == 0
        for m in range(GROUPS):
            if m & step:
                continue
            x, y = parts[m], parts[m + step]
            parts[m] = jnp.where(low, x, pltpu.roll(y, step * B, 1))
            parts[m + step] = jnp.where(low, pltpu.roll(x, LANES - step * B, 1), y)
    return parts


def to_blocks(dst, block, value):
    value = value.astype(F32)
    for a in range(value.shape[0] // B):
        at = (block + a) * PITCH
        for c in range(dst.shape[0]):
            dst[c, at : at + B, :] = value[a * B : (a + 1) * B, c * LANES : (c + 1) * LANES]


def conv_blocks(src, count, w_ref, xs, dst):
    chunks = src.shape[0]
    blocks = chunks * GROUPS

    def load(c):
        for h in range(2):
            rows = [src[c, pl.ds(GROUPS * h + i, count, stride=PITCH), :] for i in range(GROUPS)]
            part = slice(h * LANES, (h + 1) * LANES)
            for g, here in enumerate(group_transpose(rows)):
                at = 1 + c * GROUPS + g
                xs[0, at, :, part] = pltpu.roll(here, 1, 0).astype(xs.dtype)
                xs[1, at, :, part] = here.astype(xs.dtype)
                xs[2, at, :, part] = pltpu.roll(here, count - 1, 0).astype(xs.dtype)

    def solve(first, last):
        b, many = first * GROUPS, (last - first) * GROUPS
        pieces = [
            xs[qr, b + qc : b + qc + many].reshape(many * count, CH).astype(BF16)
            for qr in range(3)
            for qc in range(3)
        ]
        out = jnp.dot(jnp.concatenate(pieces, axis=1), w_ref[...], preferred_element_type=F32)
        for c in range(first, last):
            at = (c - first) * GROUPS
            for h in range(2):
                part = slice(h * LANES, (h + 1) * LANES)
                rows = group_transpose([out[(at + g) * count : (at + g + 1) * count, part] for g in range(GROUPS)])
                for i in range(GROUPS):
                    dst[c, pl.ds(GROUPS * h + i, count, stride=PITCH), :] = rows[i]

    for q in range(3):
        xs[q, 0] = jnp.zeros((count, CH), xs.dtype)
        xs[q, blocks + 1] = jnp.zeros((count, CH), xs.dtype)
    group = max(1, 32 // count)
    done = 0
    for c in range(chunks):
        load(c)
        while done + group < c + 1:
            solve(done, done + group)
            done += group
    while done < chunks:
        solve(done, min(done + group, chunks))
        done += group


def column(row):
    size = row.shape[1]
    diag = iota((size, size), 0) == iota((size, size), 1)
    return jnp.sum(jnp.where(diag, row, jnp.zeros_like(row)), axis=1, keepdims=True)


def pack_kernel(
    off_hbm, live_hbm, t_hbm, bank_hbm, index_hbm, coeff_hbm, psf_hbm,
    note_ref, msg_ref, half_ref, bank_ref, index_ref, coeff_ref, psf_ref, off_ref, live_ref, sems,
):
    rows, cols = t_hbm.shape
    edge = 2 * B
    piece = half_ref.shape[0] - edge
    begin = pl.multiple_of(lax.axis_index("band") * piece, B)
    copies = [
        pltpu.make_async_copy(a, b, sems.at[n])
        for n, (a, b) in enumerate((
            (off_hbm, off_ref), (live_hbm, live_ref),
            (t_hbm.at[pl.ds(rows - edge, edge)], note_ref.at[pl.ds(0, edge)]),
            (t_hbm.at[pl.ds(0, edge)], note_ref.at[pl.ds(edge, edge)]),
            (t_hbm.at[pl.ds(0, edge)], half_ref.at[pl.ds(0, edge)]),
            (t_hbm.at[pl.ds(begin, piece)], half_ref.at[pl.ds(edge, piece)]),
            (bank_hbm, bank_ref), (index_hbm, index_ref), (coeff_hbm, coeff_ref), (psf_hbm, psf_ref),
        ))
    ]
    for copy in copies:
        copy.start()
    for copy in copies:
        copy.wait()
    lane = iota((1, cols), 1)
    off = off_ref[0, 0]
    note = jnp.where(lane == 0, off // B, jnp.where(lane == 1, off % B, live_ref[0, 0])).astype(F32)
    block = note_ref[0:B, :].astype(F32)
    note_ref[0:B, :] = jnp.where(iota((B, cols), 0) == 0, note, block).astype(BF16)
    msg_ref[...] = note_ref[0:edge, :]


def first_kernel(
    note_ref, t_hbm, sci_hbm, bank_ref, index_ref, coeff_ref, psf_ref,
    w_ref, pcol_ref, prow_ref, sci_ref, m_ref, edge_ref, filt_ref,
    t_ref, sems, src, xs, res, sci, diff,
):
    copies = [
        pltpu.make_async_copy(t_hbm, t_ref, sems.at[0]), pltpu.make_async_copy(sci_hbm, sci_ref, sems.at[1])
    ]
    for copy in copies:
        copy.start()
    profs, taps = bank_ref.shape
    half = taps // 2
    delta = B - half
    bank = bank_ref[...]
    index = index_ref[0].astype(F32)
    labels = iota((index.shape[1], profs), 1).astype(F32)
    pick_row = (column(index[0:1]) == labels).astype(F32).astype(BF16)
    pick_col = (column(index[1:2]) == labels).astype(F32).astype(BF16)
    weight = column(coeff_ref[...])
    rowprof = (weight * jnp.dot(pick_row, bank, preferred_element_type=F32)).astype(BF16)
    colprof = jnp.dot(pick_col, bank, preferred_element_type=F32).astype(BF16)
    span = 3 * B
    total = 4 * B * B
    place = (iota((span, taps), 0) - delta == iota((span, taps), 1)).astype(F32).astype(BF16)
    col_t = lax.dot_general(place, colprof, (((1,), (1,)), ((), ())), preferred_element_type=F32).astype(BF16)
    spread = (span - 1 - iota((taps, total), 1) // B - delta == iota((taps, total), 0)).astype(F32).astype(BF16)
    row_rep = jnp.dot(rowprof, spread, preferred_element_type=F32).astype(BF16)
    z = jnp.dot(col_t, row_rep, preferred_element_type=F32)
    lane = iota((span, total), 1)
    for bit in (1, 2, 4, 8):
        z = jnp.where((lane & bit) != 0, pltpu.roll(z, bit, 0), z)
    z = z.astype(BF16)
    for phase in range(GROUPS):
        zp = z if phase == 0 else pltpu.roll(z, total - phase * B, 1)
        for g in range(span):
            start = span - 1 - g
            if start % GROUPS != phase:
                continue
            at = (start // GROUPS) * LANES
            for qc in range(3):
                row = (g // B) * 3 * CH + qc * CH + (g % B) * B
                w_ref[row : row + B, :] = zp[qc * B : (qc + 1) * B, at : at + CH]
    psf = psf_ref[...].astype(F32)
    size = pcol_ref.shape[0]
    blank = jnp.zeros((LANES, LANES), F32)
    bands = {}
    for off in (-1, 0, 1):
        tap = iota((LANES, LANES), 0) + off * LANES - iota((LANES, LANES), 1) + half
        block = blank
        for t in range(taps):
            block = jnp.where(tap == t, psf[:, t : t + 1], block)
        bands[off] = block.astype(BF16)
    for i in range(size // LANES):
        for j in range(size // LANES):
            pcol_ref[i * LANES : (i + 1) * LANES, j * LANES : (j + 1) * LANES] = bands.get(i - j, blank.astype(BF16))
    shape = prow_ref.shape
    tap = iota(shape, 1) - iota(shape, 0) - delta
    block = jnp.zeros(shape, F32)
    for t in range(taps):
        block = jnp.where(tap == t, psf[:, t : t + 1], block)
    prow_ref[...] = block.astype(BF16)
    for copy in copies:
        copy.wait()
    edge = 2 * B
    rows, cols = t_ref.shape
    off, _ = read_note(note_ref)
    to_blocks(src, 0, t_ref[...])
    conv_blocks(src, rows // B, w_ref, xs, res)
    for a in range(1, rows // B - 1):
        m_ref[:, B * a : B * (a + 1), :] = res[:, PITCH * a : PITCH * a + B, :]
    to_chunks(sci, rows, sci_ref[...])
    filter_inner(sci, rows - B - off, off, off + rows, m_ref, pcol_ref, edge_ref, filt_ref, diff)


def to_chunks(dst, dst_row, value):
    value = value.astype(F32)
    rows = value.shape[0]
    for c in range(dst.shape[0]):
        dst[c, dst_row : dst_row + rows, :] = value[:, c * LANES : (c + 1) * LANES]


def tile_diff(sky, m, base, first, last):
    row = iota(m.shape, 0) + (base - B)
    return jnp.where((row >= first) & (row < last), sky - m, 0.0).astype(BF16)


def filter_inner(sci, start, first, last, m_ref, pcol_ref, edge_ref, filt_ref, diff):
    chunks, rows, _ = m_ref.shape
    edge = 2 * B
    for c in range(chunks):
        part = slice(c * LANES, (c + 1) * LANES)
        sky = sci[c, pl.ds(start, rows + edge), :]
        edge_ref[c, 0:edge, :] = sky[0:edge]
        edge_ref[c, edge:, :] = sky[rows:]
        diff[:, part] = tile_diff(sky[edge:rows], m_ref[c, B : rows - B, :], edge, first, last)
    filt_ref[...] = jnp.dot(diff[...], pcol_ref[...], preferred_element_type=F32).astype(BF16)


def read_note(msg_ref):
    note = msg_ref[0:B, 0:LANES].astype(F32)
    return (note[0, 0] * B + note[0, 1]).astype(jnp.int32), note[0, 2]


def read_before(msg_ref):
    valid = lax.axis_index("patch") > 0
    off, live = read_note(msg_ref)
    return jnp.where(valid, off, 0), jnp.where(valid, live, 0.0), valid


def before_kernel(msg_ref, sci_ref, m_ref, pcol_ref, edge_ref, filt_ref, sci, diff):
    rows = sci_ref.shape[0]
    off, _, _ = read_before(msg_ref)
    to_chunks(sci, 0, sci_ref[...])
    filter_inner(sci, rows - B - off, off - rows, off, m_ref, pcol_ref, edge_ref, filt_ref, diff)


def join_kernel(
    note_ref, msg_ref, next_ref, w_ref, pcol_ref, prow_ref, edge_a, edge_b, filt_a, filt_b,
    *rest,
):
    *outs, mark_ref, m_ref, src, xs, strip, diff, filt = rest
    edge = 2 * B
    rows, cols = filt_a.shape[0] + edge, filt_a.shape[1]
    off_b, live_b, valid = read_before(msg_ref)
    to_blocks(src, 0, jnp.where(valid, msg_ref[...].astype(F32), 0.0))
    to_blocks(src, 2, note_ref[edge:, :])
    to_blocks(src, 4, note_ref[0:edge, :])
    to_blocks(src, 6, next_ref[0:edge, :])
    conv_blocks(src, 8, w_ref, xs, strip)
    for n, a in enumerate((1, 2, 5, 6)):
        m_ref[:, B * n : B * (n + 1), :] = strip[:, PITCH * a : PITCH * a + B, :]
    off_a, live_a = read_note(note_ref)
    for s, (side, first, last) in enumerate(((edge_a, off_a, off_a + rows), (edge_b, off_b - rows, off_b))):
        for c in range(cols // LANES):
            part = slice(c * LANES, (c + 1) * LANES)
            for k, base in enumerate((0, rows)):
                span = slice(k * edge, (k + 1) * edge)
                at = (2 * s + k) * edge
                diff[at : at + edge, part] = tile_diff(side[c, span, :], m_ref[c, span, :], base, first, last)
    sides = jnp.dot(diff[...], pcol_ref[...], preferred_element_type=F32).astype(BF16)
    for s, inner in enumerate((filt_a, filt_b)):
        filt[s, 0:edge, :] = sides[2 * s * edge : (2 * s + 1) * edge]
        filt[s, edge:rows, :] = inner[...]
        filt[s, rows : rows + edge, :] = sides[(2 * s + 1) * edge : (2 * s + 2) * edge]
        filt[s, rows + edge :, :] = jnp.zeros((filt.shape[1] - rows - edge, cols), BF16)
    share, depth = prow_ref.shape
    prow = prow_ref[...].astype(F32)
    out_row = iota((share, depth), 0)
    lane = iota((B, cols), 1)
    visits, bands = lax.axis_size("visit"), lax.axis_size("band")
    hi, lo = off_b // B, off_b % B
    marks = note_ref[0:B, 0:LANES].astype(F32)
    marks = jnp.where(iota(marks.shape, 1) == 3, hi.astype(F32), marks)
    marks = jnp.where(iota(marks.shape, 1) == 4, lo.astype(F32), marks)
    marks = jnp.where(iota(marks.shape, 1) == 5, live_b, marks)
    mark_ref[...] = marks.astype(BF16)
    for j, out_ref in enumerate(outs):
        for k in range(visits):
            to_visit = partner(lax.axis_index("visit"), k, visits)
            base = (to_visit * bands + partner(lax.axis_index("band"), j, bands)) * share
            row = out_row + base
            left = jnp.where(row >= off_a, prow * live_a, 0.0).astype(BF16)
            right = jnp.where(row < off_b, prow * live_b, 0.0).astype(BF16)
            span = pl.ds(pl.multiple_of(base, B), depth)
            total = jnp.dot(left, filt[0, span, :], preferred_element_type=F32)
            total += jnp.dot(right, filt[1, span, :], preferred_element_type=F32)
            out_ref[k * share : (k + 1) * share, :] = total.astype(out_ref.dtype)
        if j:
            out_ref[visits * share :, 0:LANES] = marks.astype(BF16)
            out_ref[visits * share :, LANES:] = jnp.zeros((B, cols - LANES), BF16)


def pair_kernel(*refs):
    bands = lax.axis_size("band")
    visits = lax.axis_size("visit")
    mark_ref, keep_ref, *got = refs[: bands + 1]
    *outs, own_mark_ref = refs[bands + 1 :]
    share, cols = outs[0].shape
    rowid = iota((B, LANES), 0)
    marks = jnp.where(rowid == 0, mark_ref[...].astype(F32), 0.0)
    for n, ref in enumerate(got):
        other = ref[visits * share :, 0:LANES].astype(F32)
        marks = jnp.where(rowid == n + 1, other[0:1, :], marks)
    own_mark_ref[...] = marks.astype(BF16)
    for k, out_ref in enumerate(outs):
        span = slice(k * share, (k + 1) * share)
        total = keep_ref[span, :]
        for ref in got:
            total += ref[span, :].astype(F32)
        out_ref[0:share, :] = total.astype(out_ref.dtype)
        if k:
            out_ref[share:, 0:LANES] = marks.astype(BF16)
            out_ref[share:, LANES:] = jnp.zeros((B, cols - LANES), BF16)


def tile_kernel(mark_ref, sci_ref, note_ref, m1_ref, edge_ref, w_ref, *rest):
    rows, cols = sci_ref.shape
    *halves, out_ref, src, xs, res, big = rest
    bands = len(halves)
    blocks = rows // B // bands
    band = lax.axis_index("band")
    for j in range(bands):
        piece = halves[0][2 * B :, :].astype(F32)
        for k in range(1, bands):
            piece = jnp.where(partner(band, k, bands) == j, halves[k][2 * B :, :].astype(F32), piece)
        to_blocks(src, j * blocks, piece)
    conv_blocks(src, rows // B, w_ref, xs, res)
    for a in range(1, rows // B):
        big[:, rows + B * a : rows + B * (a + 1), :] = res[:, PITCH * a : PITCH * a + B, :]
    big[:, 0:B, :] = edge_ref[:, B : 2 * B, :]
    big[:, B : rows - B, :] = m1_ref[:, B : rows - B, :]
    big[:, rows - B : rows + B, :] = edge_ref[:, 2 * B : 4 * B, :]
    off, _ = read_note(note_ref)
    for c in range(cols // LANES):
        part = slice(c * LANES, (c + 1) * LANES)
        out_ref[:, part] = (sci_ref[:, part].astype(F32) - big[c, pl.ds(off, rows), :]).astype(BF16)


def coadd_kernel(mark_ref, *refs):
    *parts, out_ref, result, sems = refs
    share, cols = out_ref.shape
    bands = lax.axis_size("band")
    base = (lax.axis_index("visit") * bands + lax.axis_index("band")) * share
    row = (iota((share, LANES), 0) + base).astype(F32)
    cover = jnp.zeros((share, LANES), F32)
    for n, part in enumerate(parts):
        marks = (part[share : share + B, 0:LANES] if n else mark_ref[...]).astype(F32)
        for m in range(bands):
            mark = marks[m : m + 1, :]
            cover += jnp.where(row >= mark[:, 0:1] * B + mark[:, 1:2], mark[:, 2:3], 0.0)
            cover += jnp.where(row < mark[:, 3:4] * B + mark[:, 4:5], mark[:, 5:6], 0.0)
    scale = lax.rsqrt(jnp.maximum(cover, 1.0))
    copies = []
    for c in range(cols // LANES):
        span = slice(c * LANES, (c + 1) * LANES)
        value = parts[0][:, span]
        for part in parts[1:]:
            value += part[0:share, span].astype(F32)
        result[:, span] = value * scale
        there = pl.ds(c * LANES, LANES)
        copies.append(pltpu.make_async_copy(result.at[:, there], out_ref.at[:, there], sems.at[c]))
        copies[-1].start()
    for copy in copies:
        copy.wait()


def in_hbm(*arrays):
    return [pltpu.with_memory_space_constraint(x, pltpu.HBM) for x in arrays]


def call(body, shapes, specs, scratch, flops, name, out=VM):
    return pl.pallas_call(
        body,
        out_shape=shapes,
        in_specs=specs,
        out_specs=jax.tree.map(lambda _: out, shapes),
        scratch_shapes=scratch,
        compiler_params=pltpu.CompilerParams(vmem_limit_bytes=LIMIT * 1024 * 1024),
        cost_estimate=pl.CostEstimate(flops=flops, bytes_accessed=1 << 21, transcendentals=0),
        name=name,
    )


def on_device(template, science, offsets, live_flags, bank, basis_index, coeff, psf_profile):
    rows, cols = template.shape
    sharers = lax.axis_size("visit") * lax.axis_size("band")
    share = rows // sharers
    chunks, blocks = cols // LANES, cols // B
    edge = 2 * B
    inner = rows - edge
    sds = jax.ShapeDtypeStruct
    deep = 9 * CH
    depth = -(-(share + edge) // LANES) * LANES
    sci = science[:, 0, :]
    held = in_hbm(template, sci)
    index = jnp.swapaxes(basis_index, 1, 2)
    before = shifted(science, "patch", 1)[:, 0, :]
    bands, visits = lax.axis_size("band"), lax.axis_size("visit")
    psf = psf_profile[None]
    note, msg, half, *small = call(
        pack_kernel,
        (
            sds((2 * edge, cols), BF16), sds((edge, cols), BF16), sds((edge + rows // bands, cols), BF16),
            *(sds(x.shape, x.dtype) for x in (bank, index, coeff, psf)),
        ),
        [HBM] * 7,
        [pltpu.SMEM((1, 1), jnp.int32), pltpu.SMEM((1, 1), jnp.int32), pltpu.SemaphoreType.DMA((10,))],
        1 << 20, "pack",
    )(offsets, live_flags, held[0], *in_hbm(bank, index, coeff, psf))
    half = shifted(half, "patch", -1)
    panels = lax.axis_size("patch")
    msg = lax.ppermute(msg, "patch", [(i, (i + 1) % panels) for i in range(panels)])
    count = rows // B
    conv_scratch = [
        pltpu.VMEM((chunks, count * PITCH, LANES), F32),
        pltpu.VMEM((3, blocks + 2, count, CH), BF16),
        pltpu.VMEM((chunks, count * PITCH, LANES), F32),
    ]
    conv_flops = 2 * rows * cols * deep
    sky_scratch = [pltpu.VMEM((chunks, 2 * rows + B, LANES), F32), pltpu.VMEM((inner, cols), BF16)]
    sides = (sds((chunks, 2 * edge, LANES), F32), sds((inner, cols), BF16))
    w, pcol, prow, tile, m1, edge_a, filt_a = call(
        first_kernel,
        (
            sds((deep, CH), BF16), sds((cols, cols), BF16), sds((share, depth), BF16),
            sds((rows, cols), BF16), sds((chunks, rows, LANES), F32),
        ) + sides,
        [VM, HBM, HBM] + [VM] * 4,
        [pltpu.VMEM((rows, cols), BF16), pltpu.SemaphoreType.DMA((2,))] + conv_scratch + sky_scratch,
        conv_flops, "first",
    )(note, *held, *small)
    edge_b, filt_b = call(before_kernel, sides, [VM] * 4, sky_scratch, 1 << 28, "before")(msg, before, m1, pcol)
    whole = visits * share
    keep, *sent, mark, m_edge = call(
        join_kernel,
        (sds((whole, cols), F32),) + (sds((whole + B, cols), BF16),) * (bands - 1)
        + (sds((B, LANES), BF16), sds((chunks, 2 * edge, LANES), F32)),
        [VM] * 10,
        [
            pltpu.VMEM((chunks, 8 * PITCH, LANES), F32),
            pltpu.VMEM((3, blocks + 2, 8, CH), F32),
            pltpu.VMEM((chunks, 8 * PITCH, LANES), F32),
            pltpu.VMEM((4 * edge, cols), BF16),
            pltpu.VMEM((2, rows - share + depth, cols), BF16),
        ],
        1 << 29, "join",
    )(note, msg, half, w, pcol, prow, edge_a, edge_b, filt_a, filt_b)
    got = [swapped(part, "band", k + 1) for k, part in enumerate(sent)]
    halves = [half] + [swapped(half, "band", k) for k in range(1, bands)]
    own, *sent, mark = call(
        pair_kernel,
        (sds((share, cols), F32),) + (sds((share + B, cols), BF16),) * (visits - 1) + (sds((B, LANES), BF16),),
        [VM] * (1 + bands), [], 1 << 20, "pair",
    )(mark, keep, *got)
    got = [swapped(part, "visit", k + 1) for k, part in enumerate(sent)]
    difference = call(
        tile_kernel, sds((rows, cols), BF16), [VM] * (6 + bands),
        conv_scratch + [pltpu.VMEM((chunks, 2 * rows, LANES), F32)], conv_flops, "tile",
    )(mark, tile, note, m1, m_edge, w, *halves)
    detection = call(
        coadd_kernel, sds((share, cols), F32), [VM] * (1 + visits),
        [pltpu.VMEM((share, cols), F32), pltpu.SemaphoreType.DMA((chunks,))], 1 << 20, "coadd", HBM,
    )(mark, own, *got)
    return (difference[:, None, :], detection)


def solution(mesh):
    return jax.shard_map(
        on_device,
        mesh=mesh,
        in_specs=(
            P(("group", "patch"), None),
            P(("group", "patch"), ("visit", "band"), None),
            P(("group", "patch"), ("visit", "band")),
            P(("group", "patch"), ("visit", "band")),
            P(),
            P(("group", "visit", "band"), None, None),
            P(("group", "visit", "band"), None),
            P(),
        ),
        out_specs=(
            P(("group", "patch"), ("visit", "band"), None),
            P(("group", "patch", "visit", "band"), None),
        ),
        check_vma=False,
    )
```

```python
import functools

import jax
import jax.numpy as jnp
from jax import lax
from jax.experimental import pallas as pl
from jax.experimental.pallas import tpu as pltpu
from jax.sharding import PartitionSpec as P

B = 16
CH = B * B
LANES = 128
GROUPS = LANES // B
PITCH = B + 1
F32 = jnp.float32
BF16 = jnp.bfloat16


def shifted(shard, axis, by):
    devices = lax.axis_size(axis)
    pairs = [(i, i + by) for i in range(devices) if 0 <= i + by < devices]
    return lax.ppermute(shard, axis, pairs)


def partner(me, k, count):
    return me ^ k if count & (count - 1) == 0 else (me + k) % count


def swapped(shard, axis, k):
    devices = lax.axis_size(axis)
    return lax.ppermute(shard, axis, [(i, partner(i, k, devices)) for i in range(devices)])


def iota(shape, dim):
    return lax.broadcasted_iota(jnp.int32, shape, dim)


LIMIT = 10
VM = pl.BlockSpec(memory_space=pltpu.VMEM)
HBM = pl.BlockSpec(memory_space=pltpu.HBM)


def group_transpose(parts):
    parts = list(parts)
    group = iota(parts[0].shape, 1) // B
    for step in (1, 2, 4):
        low = (group & step) == 0
        for m in range(GROUPS):
            if m & step:
                continue
            x, y = parts[m], parts[m + step]
            parts[m] = jnp.where(low, x, pltpu.roll(y, step * B, 1))
            parts[m + step] = jnp.where(low, pltpu.roll(x, LANES - step * B, 1), y)
    return parts


def to_blocks(dst, block, value):
    value = value.astype(F32)
    for a in range(value.shape[0] // B):
        at = (block + a) * PITCH
        for c in range(dst.shape[0]):
            dst[c, at : at + B, :] = value[a * B : (a + 1) * B, c * LANES : (c + 1) * LANES]


def conv_blocks(src, count, w_ref, xs, dst):
    chunks = src.shape[0]
    blocks = chunks * GROUPS

    def load(c):
        for h in range(2):
            rows = [src[c, pl.ds(GROUPS * h + i, count, stride=PITCH), :] for i in range(GROUPS)]
            part = slice(h * LANES, (h + 1) * LANES)
            for g, here in enumerate(group_transpose(rows)):
                at = 1 + c * GROUPS + g
                xs[0, at, :, part] = pltpu.roll(here, 1, 0).astype(xs.dtype)
                xs[1, at, :, part] = here.astype(xs.dtype)
                xs[2, at, :, part] = pltpu.roll(here, count - 1, 0).astype(xs.dtype)

    def solve(c):
        b = c * GROUPS
        pieces = [
            xs[qr, b + qc : b + qc + GROUPS].reshape(GROUPS * count, CH).astype(BF16)
            for qr in range(3)
            for qc in range(3)
        ]
        out = jnp.dot(jnp.concatenate(pieces, axis=1), w_ref[...], preferred_element_type=F32)
        for h in range(2):
            part = slice(h * LANES, (h + 1) * LANES)
            rows = group_transpose([out[g * count : (g + 1) * count, part] for g in range(GROUPS)])
            for i in range(GROUPS):
                dst[c, pl.ds(GROUPS * h + i, count, stride=PITCH), :] = rows[i]

    for q in range(3):
        xs[q, 0] = jnp.zeros((count, CH), xs.dtype)
        xs[q, blocks + 1] = jnp.zeros((count, CH), xs.dtype)
    load(0)
    for c in range(chunks):
        if c + 1 < chunks:
            load(c + 1)
        solve(c)


def slanted(row, count):
    value = jnp.broadcast_to(row, (count, row.shape[1]))
    index = iota(value.shape, 0)
    bit = 1
    while bit < count:
        value = jnp.where((index & bit) != 0, pltpu.roll(value, bit, 1), value)
        bit *= 2
    return value


def column(row):
    size = row.shape[1]
    diag = iota((size, size), 0) == iota((size, size), 1)
    return jnp.sum(jnp.where(diag, row, jnp.zeros_like(row)), axis=1, keepdims=True)


def pack_kernel(
    off_hbm, live_hbm, t_hbm, bank_hbm, index_hbm, coeff_hbm, psf_hbm,
    note_ref, msg_ref, half_ref, bank_ref, index_ref, coeff_ref, psf_ref, off_ref, live_ref, sems,
):
    rows, cols = t_hbm.shape
    edge = 2 * B
    piece = half_ref.shape[0] - edge
    begin = pl.multiple_of(lax.axis_index("band") * piece, B)
    copies = [
        pltpu.make_async_copy(a, b, sems.at[n])
        for n, (a, b) in enumerate((
            (off_hbm, off_ref), (live_hbm, live_ref),
            (t_hbm.at[pl.ds(rows - edge, edge)], note_ref.at[pl.ds(0, edge)]),
            (t_hbm.at[pl.ds(0, edge)], note_ref.at[pl.ds(edge, edge)]),
            (t_hbm.at[pl.ds(0, edge)], half_ref.at[pl.ds(0, edge)]),
            (t_hbm.at[pl.ds(begin, piece)], half_ref.at[pl.ds(edge, piece)]),
            (bank_hbm, bank_ref), (index_hbm, index_ref), (coeff_hbm, coeff_ref), (psf_hbm, psf_ref),
        ))
    ]
    for copy in copies:
        copy.start()
    for copy in copies:
        copy.wait()
    lane = iota((1, cols), 1)
    off = off_ref[0, 0]
    note = jnp.where(lane == 0, off // B, jnp.where(lane == 1, off % B, live_ref[0, 0])).astype(F32)
    block = note_ref[0:B, :].astype(F32)
    note_ref[0:B, :] = jnp.where(iota((B, cols), 0) == 0, note, block).astype(BF16)
    msg_ref[...] = note_ref[0:edge, :]


def first_kernel(
    note_ref, t_hbm, sci_hbm, bank_ref, index_ref, coeff_ref, psf_ref,
    w_ref, pcol_ref, prow_ref, sci_ref, m_ref, edge_ref, filt_ref,
    t_ref, sems, src, xs, res, sci, diff,
):
    copies = [
        pltpu.make_async_copy(t_hbm, t_ref, sems.at[0]), pltpu.make_async_copy(sci_hbm, sci_ref, sems.at[1])
    ]
    for copy in copies:
        copy.start()
    profs, taps = bank_ref.shape
    half = taps // 2
    delta = B - half
    bank = bank_ref[...]
    index = index_ref[0].astype(F32)
    labels = iota((index.shape[1], profs), 1).astype(F32)
    pick_row = (column(index[0:1]) == labels).astype(F32).astype(BF16)
    pick_col = (column(index[1:2]) == labels).astype(F32).astype(BF16)
    weight = column(coeff_ref[...])
    rowprof = (weight * jnp.dot(pick_row, bank, preferred_element_type=F32)).astype(BF16)
    colprof = jnp.dot(pick_col, bank, preferred_element_type=F32).astype(BF16)
    span = 3 * B
    total = 4 * B * B
    place = (iota((span, taps), 0) - delta == iota((span, taps), 1)).astype(F32).astype(BF16)
    col_t = lax.dot_general(place, colprof, (((1,), (1,)), ((), ())), preferred_element_type=F32).astype(BF16)
    spread = (span - 1 - iota((taps, total), 1) // B - delta == iota((taps, total), 0)).astype(F32).astype(BF16)
    row_rep = jnp.dot(rowprof, spread, preferred_element_type=F32).astype(BF16)
    z = jnp.dot(col_t, row_rep, preferred_element_type=F32)
    lane = iota((span, total), 1)
    for bit in (1, 2, 4, 8):
        z = jnp.where((lane & bit) != 0, pltpu.roll(z, bit, 0), z)
    z = z.astype(BF16)
    for phase in range(GROUPS):
        zp = z if phase == 0 else pltpu.roll(z, total - phase * B, 1)
        for g in range(span):
            start = span - 1 - g
            if start % GROUPS != phase:
                continue
            at = (start // GROUPS) * LANES
            for qc in range(3):
                row = (g // B) * 3 * CH + qc * CH + (g % B) * B
                w_ref[row : row + B, :] = zp[qc * B : (qc + 1) * B, at : at + CH]
    size = pcol_ref.shape[0]
    lanes = iota((taps, 3 * LANES), 1)
    mirror = (lanes - LANES + iota(lanes.shape, 0) == half).astype(F32).astype(BF16)
    bands = slanted(jnp.dot(psf_ref[...], mirror, preferred_element_type=F32), LANES)
    bands = {1 - n: bands[:, n * LANES : (n + 1) * LANES].astype(BF16) for n in range(3)}
    for i in range(size // LANES):
        for j in range(size // LANES):
            block = bands.get(i - j, jnp.zeros((LANES, LANES), BF16))
            pcol_ref[i * LANES : (i + 1) * LANES, j * LANES : (j + 1) * LANES] = block
    share, depth = prow_ref.shape
    lanes = iota((taps, depth), 1)
    ahead = (lanes - iota(lanes.shape, 0) == delta).astype(F32).astype(BF16)
    prow_ref[...] = slanted(jnp.dot(psf_ref[...], ahead, preferred_element_type=F32), share).astype(BF16)
    for copy in copies:
        copy.wait()
    edge = 2 * B
    rows, cols = t_ref.shape
    off, _ = read_note(note_ref)
    to_blocks(src, 0, t_ref[...])
    conv_blocks(src, rows // B, w_ref, xs, res)
    for a in range(1, rows // B - 1):
        m_ref[:, B * a : B * (a + 1), :] = res[:, PITCH * a : PITCH * a + B, :]
    to_chunks(sci, rows, sci_ref[...])
    filter_inner(sci, rows - B - off, off, off + rows, m_ref, pcol_ref, edge_ref, filt_ref, diff)


def to_chunks(dst, dst_row, value):
    value = value.astype(F32)
    rows = value.shape[0]
    for c in range(dst.shape[0]):
        dst[c, dst_row : dst_row + rows, :] = value[:, c * LANES : (c + 1) * LANES]


def tile_diff(sky, m, base, first, last):
    row = iota(m.shape, 0) + (base - B)
    return jnp.where((row >= first) & (row < last), sky - m, 0.0).astype(BF16)


def filter_inner(sci, start, first, last, m_ref, pcol_ref, edge_ref, filt_ref, diff):
    chunks, rows, _ = m_ref.shape
    edge = 2 * B
    for c in range(chunks):
        part = slice(c * LANES, (c + 1) * LANES)
        sky = sci[c, pl.ds(start, rows + edge), :]
        edge_ref[c, 0:edge, :] = sky[0:edge]
        edge_ref[c, edge:, :] = sky[rows:]
        diff[:, part] = tile_diff(sky[edge:rows], m_ref[c, B : rows - B, :], edge, first, last)
    filt_ref[...] = jnp.dot(diff[...], pcol_ref[...], preferred_element_type=F32).astype(BF16)


def read_note(msg_ref):
    note = msg_ref[0:B, 0:LANES].astype(F32)
    return (note[0, 0] * B + note[0, 1]).astype(jnp.int32), note[0, 2]


def read_before(msg_ref):
    valid = lax.axis_index("patch") > 0
    off, live = read_note(msg_ref)
    return jnp.where(valid, off, 0), jnp.where(valid, live, 0.0), valid


def before_kernel(msg_ref, sci_ref, m_ref, pcol_ref, edge_ref, filt_ref, sci, diff):
    rows = sci_ref.shape[0]
    off, _, _ = read_before(msg_ref)
    to_chunks(sci, 0, sci_ref[...])
    filter_inner(sci, rows - B - off, off - rows, off, m_ref, pcol_ref, edge_ref, filt_ref, diff)


def join_kernel(
    note_ref, msg_ref, next_ref, w_ref, pcol_ref, prow_ref, edge_a, edge_b, filt_a, filt_b,
    *rest,
):
    *outs, mark_ref, m_ref, src, xs, strip, diff, filt = rest
    edge = 2 * B
    rows, cols = filt_a.shape[0] + edge, filt_a.shape[1]
    off_b, live_b, valid = read_before(msg_ref)
    to_blocks(src, 0, jnp.where(valid, msg_ref[...].astype(F32), 0.0))
    to_blocks(src, 2, note_ref[edge:, :])
    to_blocks(src, 4, note_ref[0:edge, :])
    to_blocks(src, 6, next_ref[0:edge, :])
    conv_blocks(src, 8, w_ref, xs, strip)
    for n, a in enumerate((1, 2, 5, 6)):
        m_ref[:, B * n : B * (n + 1), :] = strip[:, PITCH * a : PITCH * a + B, :]
    off_a, live_a = read_note(note_ref)
    for s, (side, first, last) in enumerate(((edge_a, off_a, off_a + rows), (edge_b, off_b - rows, off_b))):
        for c in range(cols // LANES):
            part = slice(c * LANES, (c + 1) * LANES)
            for k, base in enumerate((0, rows)):
                span = slice(k * edge, (k + 1) * edge)
                at = (2 * s + k) * edge
                diff[at : at + edge, part] = tile_diff(side[c, span, :], m_ref[c, span, :], base, first, last)
    sides = jnp.dot(diff[...], pcol_ref[...], preferred_element_type=F32).astype(BF16)
    for s, inner in enumerate((filt_a, filt_b)):
        filt[s, 0:edge, :] = sides[2 * s * edge : (2 * s + 1) * edge]
        filt[s, edge:rows, :] = inner[...]
        filt[s, rows : rows + edge, :] = sides[(2 * s + 1) * edge : (2 * s + 2) * edge]
        filt[s, rows + edge :, :] = jnp.zeros((filt.shape[1] - rows - edge, cols), BF16)
    share, depth = prow_ref.shape
    prow = prow_ref[...].astype(F32)
    out_row = iota((share, depth), 0)
    lane = iota((B, cols), 1)
    visits, bands = lax.axis_size("visit"), lax.axis_size("band")
    hi, lo = off_b // B, off_b % B
    marks = note_ref[0:B, 0:LANES].astype(F32)
    marks = jnp.where(iota(marks.shape, 1) == 3, hi.astype(F32), marks)
    marks = jnp.where(iota(marks.shape, 1) == 4, lo.astype(F32), marks)
    marks = jnp.where(iota(marks.shape, 1) == 5, live_b, marks)
    mark_ref[...] = marks.astype(BF16)
    for j, out_ref in enumerate(outs):
        for k in range(visits):
            to_visit = partner(lax.axis_index("visit"), k, visits)
            base = (to_visit * bands + partner(lax.axis_index("band"), j, bands)) * share
            row = out_row + base
            left = jnp.where(row >= off_a, prow * live_a, 0.0).astype(BF16)
            right = jnp.where(row < off_b, prow * live_b, 0.0).astype(BF16)
            span = pl.ds(pl.multiple_of(base, B), depth)
            total = jnp.dot(left, filt[0, span, :], preferred_element_type=F32)
            total += jnp.dot(right, filt[1, span, :], preferred_element_type=F32)
            out_ref[k * share : (k + 1) * share, :] = total.astype(out_ref.dtype)
        if j:
            out_ref[visits * share :, 0:LANES] = marks.astype(BF16)
            out_ref[visits * share :, LANES:] = jnp.zeros((B, cols - LANES), BF16)


def pair_kernel(*refs):
    bands = lax.axis_size("band")
    visits = lax.axis_size("visit")
    mark_ref, keep_ref, *got = refs[: bands + 1]
    *outs, own_mark_ref = refs[bands + 1 :]
    share, cols = outs[0].shape
    rowid = iota((B, LANES), 0)
    marks = jnp.where(rowid == 0, mark_ref[...].astype(F32), 0.0)
    for n, ref in enumerate(got):
        other = ref[visits * share :, 0:LANES].astype(F32)
        marks = jnp.where(rowid == n + 1, other[0:1, :], marks)
    own_mark_ref[...] = marks.astype(BF16)
    for k, out_ref in enumerate(outs):
        span = slice(k * share, (k + 1) * share)
        total = keep_ref[span, :]
        for ref in got:
            total += ref[span, :].astype(F32)
        out_ref[0:share, :] = total.astype(out_ref.dtype)
        if k:
            out_ref[share:, 0:LANES] = marks.astype(BF16)
            out_ref[share:, LANES:] = jnp.zeros((B, cols - LANES), BF16)


def tile_kernel(mark_ref, sci_ref, note_ref, m1_ref, edge_ref, w_ref, *rest):
    rows, cols = sci_ref.shape
    *halves, out_ref, src, xs, res, big = rest
    bands = len(halves)
    blocks = rows // B // bands
    band = lax.axis_index("band")
    for j in range(bands):
        piece = halves[0][2 * B :, :].astype(F32)
        for k in range(1, bands):
            piece = jnp.where(partner(band, k, bands) == j, halves[k][2 * B :, :].astype(F32), piece)
        to_blocks(src, j * blocks, piece)
    conv_blocks(src, rows // B, w_ref, xs, res)
    for a in range(1, rows // B):
        big[:, rows + B * a : rows + B * (a + 1), :] = res[:, PITCH * a : PITCH * a + B, :]
    big[:, 0:B, :] = edge_ref[:, B : 2 * B, :]
    big[:, B : rows - B, :] = m1_ref[:, B : rows - B, :]
    big[:, rows - B : rows + B, :] = edge_ref[:, 2 * B : 4 * B, :]
    off, _ = read_note(note_ref)
    for c in range(cols // LANES):
        part = slice(c * LANES, (c + 1) * LANES)
        out_ref[:, part] = (sci_ref[:, part].astype(F32) - big[c, pl.ds(off, rows), :]).astype(BF16)


def coadd_kernel(mark_ref, *refs):
    *parts, out_ref = refs
    share, cols = out_ref.shape
    bands = lax.axis_size("band")
    base = (lax.axis_index("visit") * bands + lax.axis_index("band")) * share
    row = (iota((share, LANES), 0) + base).astype(F32)
    cover = jnp.zeros((share, LANES), F32)
    for n, part in enumerate(parts):
        marks = (part[share : share + B, 0:LANES] if n else mark_ref[...]).astype(F32)
        for m in range(bands):
            mark = marks[m : m + 1, :]
            cover += jnp.where(row >= mark[:, 0:1] * B + mark[:, 1:2], mark[:, 2:3], 0.0)
            cover += jnp.where(row < mark[:, 3:4] * B + mark[:, 4:5], mark[:, 5:6], 0.0)
    scale = lax.rsqrt(jnp.maximum(cover, 1.0))
    for c in range(cols // LANES):
        span = slice(c * LANES, (c + 1) * LANES)
        value = parts[0][:, span]
        for part in parts[1:]:
            value += part[0:share, span].astype(F32)
        out_ref[:, span] = value * scale


def in_hbm(*arrays):
    return [pltpu.with_memory_space_constraint(x, pltpu.HBM) for x in arrays]


def call(body, shapes, specs, scratch, flops, name):
    return pl.pallas_call(
        body,
        out_shape=shapes,
        in_specs=specs,
        out_specs=jax.tree.map(lambda _: VM, shapes),
        scratch_shapes=scratch,
        compiler_params=pltpu.CompilerParams(vmem_limit_bytes=LIMIT * 1024 * 1024),
        cost_estimate=pl.CostEstimate(flops=flops, bytes_accessed=1 << 21, transcendentals=0),
        name=name,
    )


def on_device(template, science, offsets, live_flags, bank, basis_index, coeff, psf_profile):
    rows, cols = template.shape
    sharers = lax.axis_size("visit") * lax.axis_size("band")
    share = rows // sharers
    chunks, blocks = cols // LANES, cols // B
    edge = 2 * B
    inner = rows - edge
    sds = jax.ShapeDtypeStruct
    deep = 9 * CH
    depth = -(-(share + edge) // LANES) * LANES
    sci = science[:, 0, :]
    held = in_hbm(template, sci)
    index = jnp.swapaxes(basis_index, 1, 2)
    before = shifted(science, "patch", 1)[:, 0, :]
    bands, visits = lax.axis_size("band"), lax.axis_size("visit")
    psf = psf_profile[None]
    note, msg, half, *small = call(
        pack_kernel,
        (
            sds((2 * edge, cols), BF16), sds((edge, cols), BF16), sds((edge + rows // bands, cols), BF16),
            *(sds(x.shape, x.dtype) for x in (bank, index, coeff, psf)),
        ),
        [HBM] * 7,
        [pltpu.SMEM((1, 1), jnp.int32), pltpu.SMEM((1, 1), jnp.int32), pltpu.SemaphoreType.DMA((10,))],
        1 << 20, "pack",
    )(offsets, live_flags, held[0], *in_hbm(bank, index, coeff, psf))
    half = shifted(half, "patch", -1)
    panels = lax.axis_size("patch")
    msg = lax.ppermute(msg, "patch", [(i, (i + 1) % panels) for i in range(panels)])
    count = rows // B
    conv_scratch = [
        pltpu.VMEM((chunks, count * PITCH, LANES), F32),
        pltpu.VMEM((3, blocks + 2, count, CH), BF16),
        pltpu.VMEM((chunks, count * PITCH, LANES), F32),
    ]
    conv_flops = 2 * rows * cols * deep
    sky_scratch = [pltpu.VMEM((chunks, 2 * rows + B, LANES), F32), pltpu.VMEM((inner, cols), BF16)]
    sides = (sds((chunks, 2 * edge, LANES), F32), sds((inner, cols), BF16))
    w, pcol, prow, tile, m1, edge_a, filt_a = call(
        first_kernel,
        (
            sds((deep, CH), BF16), sds((cols, cols), BF16), sds((share, depth), BF16),
            sds((rows, cols), BF16), sds((chunks, rows, LANES), F32),
        ) + sides,
        [VM, HBM, HBM] + [VM] * 4,
        [pltpu.VMEM((rows, cols), BF16), pltpu.SemaphoreType.DMA((2,))] + conv_scratch + sky_scratch,
        conv_flops, "first",
    )(note, *held, *small)
    edge_b, filt_b = call(before_kernel, sides, [VM] * 4, sky_scratch, 1 << 34, "before")(msg, before, m1, pcol)
    whole = visits * share
    keep, *sent, mark, m_edge = call(
        join_kernel,
        (sds((whole, cols), F32),) + (sds((whole + B, cols), BF16),) * (bands - 1)
        + (sds((B, LANES), BF16), sds((chunks, 2 * edge, LANES), F32)),
        [VM] * 10,
        [
            pltpu.VMEM((chunks, 8 * PITCH, LANES), F32),
            pltpu.VMEM((3, blocks + 2, 8, CH), F32),
            pltpu.VMEM((chunks, 8 * PITCH, LANES), F32),
            pltpu.VMEM((4 * edge, cols), BF16),
            pltpu.VMEM((2, rows - share + depth, cols), BF16),
        ],
        1 << 29, "join",
    )(note, msg, half, w, pcol, prow, edge_a, edge_b, filt_a, filt_b)
    got = [swapped(part, "band", k + 1) for k, part in enumerate(sent)]
    halves = [half] + [swapped(half, "band", k) for k in range(1, bands)]
    own, *sent, mark = call(
        pair_kernel,
        (sds((share, cols), F32),) + (sds((share + B, cols), BF16),) * (visits - 1) + (sds((B, LANES), BF16),),
        [VM] * (1 + bands), [], 1 << 20, "pair",
    )(mark, keep, *got)
    got = [swapped(part, "visit", k + 1) for k, part in enumerate(sent)]
    difference = call(
        tile_kernel, sds((rows, cols), BF16), [VM] * (6 + bands),
        conv_scratch + [pltpu.VMEM((chunks, 2 * rows, LANES), F32)], conv_flops, "tile",
    )(mark, tile, note, m1, m_edge, w, *halves)
    detection = call(
        coadd_kernel, sds((share, cols), F32), [VM] * (1 + visits), [], 1 << 20, "coadd"
    )(mark, own, *got)
    return (difference[:, None, :], detection)


def solution(mesh):
    return jax.shard_map(
        on_device,
        mesh=mesh,
        in_specs=(
            P(("group", "patch"), None),
            P(("group", "patch"), ("visit", "band"), None),
            P(("group", "patch"), ("visit", "band")),
            P(("group", "patch"), ("visit", "band")),
            P(),
            P(("group", "visit", "band"), None, None),
            P(("group", "visit", "band"), None),
            P(),
        ),
        out_specs=(
            P(("group", "patch"), ("visit", "band"), None),
            P(("group", "patch", "visit", "band"), None),
        ),
        check_vma=False,
    )
```

```python
import functools

import jax
import jax.numpy as jnp
from jax import lax
from jax.experimental import pallas as pl
from jax.experimental.pallas import tpu as pltpu
from jax.sharding import PartitionSpec as P

B = 16
CH = B * B
LANES = 128
GROUPS = LANES // B
PITCH = B + 1
F32 = jnp.float32
BF16 = jnp.bfloat16


def shifted(shard, axis, by):
    devices = lax.axis_size(axis)
    pairs = [(i, i + by) for i in range(devices) if 0 <= i + by < devices]
    return lax.ppermute(shard, axis, pairs)


def partner(me, k, count):
    return me ^ k if count & (count - 1) == 0 else (me + k) % count


def swapped(shard, axis, k):
    devices = lax.axis_size(axis)
    return lax.ppermute(shard, axis, [(i, partner(i, k, devices)) for i in range(devices)])


def iota(shape, dim):
    return lax.broadcasted_iota(jnp.int32, shape, dim)


LIMIT = 10
VM = pl.BlockSpec(memory_space=pltpu.VMEM)
HBM = pl.BlockSpec(memory_space=pltpu.HBM)


def group_transpose(parts):
    parts = list(parts)
    group = iota(parts[0].shape, 1) // B
    for step in (1, 2, 4):
        low = (group & step) == 0
        for m in range(GROUPS):
            if m & step:
                continue
            x, y = parts[m], parts[m + step]
            parts[m] = jnp.where(low, x, pltpu.roll(y, step * B, 1))
            parts[m + step] = jnp.where(low, pltpu.roll(x, LANES - step * B, 1), y)
    return parts


def to_blocks(dst, block, value):
    value = value.astype(F32)
    for a in range(value.shape[0] // B):
        at = (block + a) * PITCH
        for c in range(dst.shape[0]):
            dst[c, at : at + B, :] = value[a * B : (a + 1) * B, c * LANES : (c + 1) * LANES]


def conv_blocks(src, count, w_ref, xs, dst):
    chunks = src.shape[0]
    blocks = chunks * GROUPS

    def load(c):
        for h in range(2):
            rows = [src[c, pl.ds(GROUPS * h + i, count, stride=PITCH), :] for i in range(GROUPS)]
            part = slice(h * LANES, (h + 1) * LANES)
            for g, here in enumerate(group_transpose(rows)):
                at = 1 + c * GROUPS + g
                xs[0, at, :, part] = pltpu.roll(here, 1, 0).astype(xs.dtype)
                xs[1, at, :, part] = here.astype(xs.dtype)
                xs[2, at, :, part] = pltpu.roll(here, count - 1, 0).astype(xs.dtype)

    def solve(c):
        b = c * GROUPS
        pieces = [
            xs[qr, b + qc : b + qc + GROUPS].reshape(GROUPS * count, CH).astype(BF16)
            for qr in range(3)
            for qc in range(3)
        ]
        out = jnp.dot(jnp.concatenate(pieces, axis=1), w_ref[...], preferred_element_type=F32)
        for h in range(2):
            part = slice(h * LANES, (h + 1) * LANES)
            rows = group_transpose([out[g * count : (g + 1) * count, part] for g in range(GROUPS)])
            for i in range(GROUPS):
                dst[c, pl.ds(GROUPS * h + i, count, stride=PITCH), :] = rows[i]

    for q in range(3):
        xs[q, 0] = jnp.zeros((count, CH), xs.dtype)
        xs[q, blocks + 1] = jnp.zeros((count, CH), xs.dtype)
    load(0)
    for c in range(chunks):
        if c + 1 < chunks:
            load(c + 1)
        solve(c)


def slanted(row, count):
    value = jnp.broadcast_to(row, (count, row.shape[1]))
    index = iota(value.shape, 0)
    bit = 1
    while bit < count:
        value = jnp.where((index & bit) != 0, pltpu.roll(value, bit, 1), value)
        bit *= 2
    return value


def column(row):
    size = row.shape[1]
    diag = iota((size, size), 0) == iota((size, size), 1)
    return jnp.sum(jnp.where(diag, row, jnp.zeros_like(row)), axis=1, keepdims=True)


def pack_kernel(
    off_hbm, live_hbm, t_hbm, bank_hbm, index_hbm, coeff_hbm, psf_hbm,
    note_ref, msg_ref, head_ref, half_ref, bank_ref, index_ref, coeff_ref, psf_ref, off_ref, live_ref, sems,
):
    rows, cols = t_hbm.shape
    edge = 2 * B
    piece = half_ref.shape[0]
    begin = pl.multiple_of(lax.axis_index("band") * piece, B)
    copies = [
        pltpu.make_async_copy(a, b, sems.at[n])
        for n, (a, b) in enumerate((
            (off_hbm, off_ref), (live_hbm, live_ref),
            (t_hbm.at[pl.ds(rows - edge, edge)], note_ref.at[pl.ds(0, edge)]),
            (t_hbm.at[pl.ds(0, edge)], note_ref.at[pl.ds(edge, edge)]),
            (t_hbm.at[pl.ds(0, edge)], head_ref),
            (t_hbm.at[pl.ds(begin, piece)], half_ref),
            (bank_hbm, bank_ref), (index_hbm, index_ref), (coeff_hbm, coeff_ref), (psf_hbm, psf_ref),
        ))
    ]
    for copy in copies:
        copy.start()
    for copy in copies:
        copy.wait()
    lane = iota((1, cols), 1)
    off = off_ref[0, 0]
    note = jnp.where(lane == 0, off // B, jnp.where(lane == 1, off % B, live_ref[0, 0])).astype(F32)
    block = note_ref[0:B, :].astype(F32)
    note_ref[0:B, :] = jnp.where(iota((B, cols), 0) == 0, note, block).astype(BF16)
    msg_ref[...] = note_ref[0:edge, :]


def first_kernel(
    note_ref, t_hbm, sci_hbm, bank_ref, index_ref, coeff_ref, psf_ref,
    w_ref, pcol_ref, prow_ref, sci_ref, m_ref, edge_ref, filt_ref,
    t_ref, sems, src, xs, res, sci, diff,
):
    copies = [
        pltpu.make_async_copy(t_hbm, t_ref, sems.at[0]), pltpu.make_async_copy(sci_hbm, sci_ref, sems.at[1])
    ]
    for copy in copies:
        copy.start()
    profs, taps = bank_ref.shape
    half = taps // 2
    delta = B - half
    bank = bank_ref[...]
    index = index_ref[0].astype(F32)
    labels = iota((index.shape[1], profs), 1).astype(F32)
    pick_row = (column(index[0:1]) == labels).astype(F32).astype(BF16)
    pick_col = (column(index[1:2]) == labels).astype(F32).astype(BF16)
    weight = column(coeff_ref[...])
    rowprof = (weight * jnp.dot(pick_row, bank, preferred_element_type=F32)).astype(BF16)
    colprof = jnp.dot(pick_col, bank, preferred_element_type=F32).astype(BF16)
    span = 3 * B
    total = 4 * B * B
    place = (iota((span, taps), 0) - delta == iota((span, taps), 1)).astype(F32).astype(BF16)
    col_t = lax.dot_general(place, colprof, (((1,), (1,)), ((), ())), preferred_element_type=F32).astype(BF16)
    spread = (span - 1 - iota((taps, total), 1) // B - delta == iota((taps, total), 0)).astype(F32).astype(BF16)
    row_rep = jnp.dot(rowprof, spread, preferred_element_type=F32).astype(BF16)
    z = jnp.dot(col_t, row_rep, preferred_element_type=F32)
    lane = iota((span, total), 1)
    for bit in (1, 2, 4, 8):
        z = jnp.where((lane & bit) != 0, pltpu.roll(z, bit, 0), z)
    z = z.astype(BF16)
    for phase in range(GROUPS):
        zp = z if phase == 0 else pltpu.roll(z, total - phase * B, 1)
        for g in range(span):
            start = span - 1 - g
            if start % GROUPS != phase:
                continue
            at = (start // GROUPS) * LANES
            for qc in range(3):
                row = (g // B) * 3 * CH + qc * CH + (g % B) * B
                w_ref[row : row + B, :] = zp[qc * B : (qc + 1) * B, at : at + CH]
    size = pcol_ref.shape[0]
    lanes = iota((taps, 3 * LANES), 1)
    mirror = (lanes - LANES + iota(lanes.shape, 0) == half).astype(F32).astype(BF16)
    bands = slanted(jnp.dot(psf_ref[...], mirror, preferred_element_type=F32), LANES)
    bands = {1 - n: bands[:, n * LANES : (n + 1) * LANES].astype(BF16) for n in range(3)}
    for i in range(size // LANES):
        for j in range(size // LANES):
            block = bands.get(i - j, jnp.zeros((LANES, LANES), BF16))
            pcol_ref[i * LANES : (i + 1) * LANES, j * LANES : (j + 1) * LANES] = block
    share, depth = prow_ref.shape
    lanes = iota((taps, depth), 1)
    ahead = (lanes - iota(lanes.shape, 0) == delta).astype(F32).astype(BF16)
    prow_ref[...] = slanted(jnp.dot(psf_ref[...], ahead, preferred_element_type=F32), share).astype(BF16)
    for copy in copies:
        copy.wait()
    edge = 2 * B
    rows, cols = t_ref.shape
    off, _ = read_note(note_ref)
    to_blocks(src, 0, t_ref[...])
    conv_blocks(src, rows // B, w_ref, xs, res)
    for a in range(1, rows // B - 1):
        m_ref[:, B * a : B * (a + 1), :] = res[:, PITCH * a : PITCH * a + B, :]
    to_chunks(sci, rows, sci_ref[...])
    filter_inner(sci, rows - B - off, off, off + rows, m_ref, pcol_ref, edge_ref, filt_ref, diff)


def to_chunks(dst, dst_row, value):
    value = value.astype(F32)
    rows = value.shape[0]
    for c in range(dst.shape[0]):
        dst[c, dst_row : dst_row + rows, :] = value[:, c * LANES : (c + 1) * LANES]


def tile_diff(sky, m, base, first, last):
    row = iota(m.shape, 0) + (base - B)
    return jnp.where((row >= first) & (row < last), sky - m, 0.0).astype(BF16)


def filter_inner(sci, start, first, last, m_ref, pcol_ref, edge_ref, filt_ref, diff):
    chunks, rows, _ = m_ref.shape
    edge = 2 * B
    for c in range(chunks):
        part = slice(c * LANES, (c + 1) * LANES)
        sky = sci[c, pl.ds(start, rows + edge), :]
        edge_ref[c, 0:edge, :] = sky[0:edge]
        edge_ref[c, edge:, :] = sky[rows:]
        diff[:, part] = tile_diff(sky[edge:rows], m_ref[c, B : rows - B, :], edge, first, last)
    filt_ref[...] = jnp.dot(diff[...], pcol_ref[...], preferred_element_type=F32).astype(BF16)


def read_note(msg_ref):
    note = msg_ref[0:B, 0:LANES].astype(F32)
    return (note[0, 0] * B + note[0, 1]).astype(jnp.int32), note[0, 2]


def read_before(msg_ref):
    valid = lax.axis_index("patch") > 0
    off, live = read_note(msg_ref)
    return jnp.where(valid, off, 0), jnp.where(valid, live, 0.0), valid


def before_kernel(msg_ref, sci_ref, m_ref, pcol_ref, edge_ref, filt_ref, sci, diff):
    rows = sci_ref.shape[0]
    off, _, _ = read_before(msg_ref)
    to_chunks(sci, 0, sci_ref[...])
    filter_inner(sci, rows - B - off, off - rows, off, m_ref, pcol_ref, edge_ref, filt_ref, diff)


def join_kernel(
    note_ref, msg_ref, head_ref, w_ref, pcol_ref, prow_ref, edge_a, edge_b, filt_a, filt_b,
    *rest,
):
    *outs, mark_ref, m_ref, src, xs, strip, diff, filt = rest
    edge = 2 * B
    rows, cols = filt_a.shape[0] + edge, filt_a.shape[1]
    off_b, live_b, valid = read_before(msg_ref)
    to_blocks(src, 0, jnp.where(valid, msg_ref[...].astype(F32), 0.0))
    to_blocks(src, 2, note_ref[edge:, :])
    to_blocks(src, 4, note_ref[0:edge, :])
    last = lax.axis_index("patch") == lax.axis_size("patch") - 1
    to_blocks(src, 6, jnp.where(last, 0.0, head_ref[...].astype(F32)))
    conv_blocks(src, 8, w_ref, xs, strip)
    for n, a in enumerate((1, 2, 5, 6)):
        m_ref[:, B * n : B * (n + 1), :] = strip[:, PITCH * a : PITCH * a + B, :]
    off_a, live_a = read_note(note_ref)
    for s, (side, first, last) in enumerate(((edge_a, off_a, off_a + rows), (edge_b, off_b - rows, off_b))):
        for c in range(cols // LANES):
            part = slice(c * LANES, (c + 1) * LANES)
            for k, base in enumerate((0, rows)):
                span = slice(k * edge, (k + 1) * edge)
                at = (2 * s + k) * edge
                diff[at : at + edge, part] = tile_diff(side[c, span, :], m_ref[c, span, :], base, first, last)
    sides = jnp.dot(diff[...], pcol_ref[...], preferred_element_type=F32).astype(BF16)
    for s, inner in enumerate((filt_a, filt_b)):
        filt[s, 0:edge, :] = sides[2 * s * edge : (2 * s + 1) * edge]
        filt[s, edge:rows, :] = inner[...]
        filt[s, rows : rows + edge, :] = sides[(2 * s + 1) * edge : (2 * s + 2) * edge]
        filt[s, rows + edge :, :] = jnp.zeros((filt.shape[1] - rows - edge, cols), BF16)
    share, depth = prow_ref.shape
    prow = prow_ref[...].astype(F32)
    out_row = iota((share, depth), 0)
    lane = iota((B, cols), 1)
    visits, bands = lax.axis_size("visit"), lax.axis_size("band")
    hi, lo = off_b // B, off_b % B
    marks = note_ref[0:B, 0:LANES].astype(F32)
    marks = jnp.where(iota(marks.shape, 1) == 3, hi.astype(F32), marks)
    marks = jnp.where(iota(marks.shape, 1) == 4, lo.astype(F32), marks)
    marks = jnp.where(iota(marks.shape, 1) == 5, live_b, marks)
    mark_ref[...] = marks.astype(BF16)
    for j, out_ref in enumerate(outs):
        for k in range(visits):
            to_visit = partner(lax.axis_index("visit"), k, visits)
            base = (to_visit * bands + partner(lax.axis_index("band"), j, bands)) * share
            row = out_row + base
            left = jnp.where(row >= off_a, prow * live_a, 0.0).astype(BF16)
            right = jnp.where(row < off_b, prow * live_b, 0.0).astype(BF16)
            span = pl.ds(pl.multiple_of(base, B), depth)
            total = jnp.dot(left, filt[0, span, :], preferred_element_type=F32)
            total += jnp.dot(right, filt[1, span, :], preferred_element_type=F32)
            out_ref[k * share : (k + 1) * share, :] = total.astype(out_ref.dtype)
        if j:
            out_ref[visits * share :, 0:LANES] = marks.astype(BF16)
            out_ref[visits * share :, LANES:] = jnp.zeros((B, cols - LANES), BF16)


def pair_kernel(*refs):
    bands = lax.axis_size("band")
    visits = lax.axis_size("visit")
    mark_ref, keep_ref, *got = refs[: bands + 1]
    *outs, own_mark_ref = refs[bands + 1 :]
    share, cols = outs[0].shape
    rowid = iota((B, LANES), 0)
    marks = jnp.where(rowid == 0, mark_ref[...].astype(F32), 0.0)
    for n, ref in enumerate(got):
        other = ref[visits * share :, 0:LANES].astype(F32)
        marks = jnp.where(rowid == n + 1, other[0:1, :], marks)
    own_mark_ref[...] = marks.astype(BF16)
    for k, out_ref in enumerate(outs):
        span = slice(k * share, (k + 1) * share)
        total = keep_ref[span, :]
        for ref in got:
            total += ref[span, :].astype(F32)
        out_ref[0:share, :] = total.astype(out_ref.dtype)
        if k:
            out_ref[share:, 0:LANES] = marks.astype(BF16)
            out_ref[share:, LANES:] = jnp.zeros((B, cols - LANES), BF16)


def tile_kernel(mark_ref, sci_ref, note_ref, m1_ref, edge_ref, w_ref, *rest):
    rows, cols = sci_ref.shape
    *halves, out_ref, src, xs, res, big = rest
    bands = len(halves)
    blocks = rows // B // bands
    band = lax.axis_index("band")
    for j in range(bands):
        piece = halves[0][...].astype(F32)
        for k in range(1, bands):
            piece = jnp.where(partner(band, k, bands) == j, halves[k][...].astype(F32), piece)
        to_blocks(src, j * blocks, piece)
    conv_blocks(src, rows // B, w_ref, xs, res)
    for a in range(1, rows // B):
        big[:, rows + B * a : rows + B * (a + 1), :] = res[:, PITCH * a : PITCH * a + B, :]
    big[:, 0:B, :] = edge_ref[:, B : 2 * B, :]
    big[:, B : rows - B, :] = m1_ref[:, B : rows - B, :]
    big[:, rows - B : rows + B, :] = edge_ref[:, 2 * B : 4 * B, :]
    off, _ = read_note(note_ref)
    for c in range(cols // LANES):
        part = slice(c * LANES, (c + 1) * LANES)
        out_ref[:, part] = (sci_ref[:, part].astype(F32) - big[c, pl.ds(off, rows), :]).astype(BF16)


def coadd_kernel(mark_ref, *refs):
    *parts, out_ref = refs
    share, cols = out_ref.shape
    bands = lax.axis_size("band")
    base = (lax.axis_index("visit") * bands + lax.axis_index("band")) * share
    row = (iota((share, LANES), 0) + base).astype(F32)
    cover = jnp.zeros((share, LANES), F32)
    for n, part in enumerate(parts):
        marks = (part[share : share + B, 0:LANES] if n else mark_ref[...]).astype(F32)
        for m in range(bands):
            mark = marks[m : m + 1, :]
            cover += jnp.where(row >= mark[:, 0:1] * B + mark[:, 1:2], mark[:, 2:3], 0.0)
            cover += jnp.where(row < mark[:, 3:4] * B + mark[:, 4:5], mark[:, 5:6], 0.0)
    scale = lax.rsqrt(jnp.maximum(cover, 1.0))
    for c in range(cols // LANES):
        span = slice(c * LANES, (c + 1) * LANES)
        value = parts[0][:, span]
        for part in parts[1:]:
            value += part[0:share, span].astype(F32)
        out_ref[:, span] = value * scale


def in_hbm(*arrays):
    return [pltpu.with_memory_space_constraint(x, pltpu.HBM) for x in arrays]


def call(body, shapes, specs, scratch, flops, name):
    return pl.pallas_call(
        body,
        out_shape=shapes,
        in_specs=specs,
        out_specs=jax.tree.map(lambda _: VM, shapes),
        scratch_shapes=scratch,
        compiler_params=pltpu.CompilerParams(vmem_limit_bytes=LIMIT * 1024 * 1024),
        cost_estimate=pl.CostEstimate(flops=flops, bytes_accessed=1 << 21, transcendentals=0),
        name=name,
    )


def on_device(template, science, offsets, live_flags, bank, basis_index, coeff, psf_profile):
    rows, cols = template.shape
    sharers = lax.axis_size("visit") * lax.axis_size("band")
    share = rows // sharers
    chunks, blocks = cols // LANES, cols // B
    edge = 2 * B
    inner = rows - edge
    sds = jax.ShapeDtypeStruct
    deep = 9 * CH
    depth = -(-(share + edge) // LANES) * LANES
    sci = science[:, 0, :]
    held = in_hbm(template, sci)
    index = jnp.swapaxes(basis_index, 1, 2)
    before = shifted(science, "patch", 1)[:, 0, :]
    bands, visits = lax.axis_size("band"), lax.axis_size("visit")
    psf = psf_profile[None]
    note, msg, head, half, *small = call(
        pack_kernel,
        (
            sds((2 * edge, cols), BF16), sds((edge, cols), BF16), sds((edge, cols), BF16),
            sds((rows // bands, cols), BF16),
            *(sds(x.shape, x.dtype) for x in (bank, index, coeff, psf)),
        ),
        [HBM] * 7,
        [pltpu.SMEM((1, 1), jnp.int32), pltpu.SMEM((1, 1), jnp.int32), pltpu.SemaphoreType.DMA((10,))],
        1 << 20, "pack",
    )(offsets, live_flags, held[0], *in_hbm(bank, index, coeff, psf))
    half = shifted(half, "patch", -1)
    panels = lax.axis_size("patch")
    msg = lax.ppermute(msg, "patch", [(i, (i + 1) % panels) for i in range(panels)])
    head = lax.ppermute(head, "patch", [((i + 1) % panels, i) for i in range(panels)])
    count = rows // B
    conv_scratch = [
        pltpu.VMEM((chunks, count * PITCH, LANES), F32),
        pltpu.VMEM((3, blocks + 2, count, CH), BF16),
        pltpu.VMEM((chunks, count * PITCH, LANES), F32),
    ]
    conv_flops = 2 * rows * cols * deep
    sky_scratch = [pltpu.VMEM((chunks, 2 * rows + B, LANES), F32), pltpu.VMEM((inner, cols), BF16)]
    sides = (sds((chunks, 2 * edge, LANES), F32), sds((inner, cols), BF16))
    w, pcol, prow, tile, m1, edge_a, filt_a = call(
        first_kernel,
        (
            sds((deep, CH), BF16), sds((cols, cols), BF16), sds((share, depth), BF16),
            sds((rows, cols), BF16), sds((chunks, rows, LANES), F32),
        ) + sides,
        [VM, HBM, HBM] + [VM] * 4,
        [pltpu.VMEM((rows, cols), BF16), pltpu.SemaphoreType.DMA((2,))] + conv_scratch + sky_scratch,
        conv_flops, "first",
    )(note, *held, *small)
    edge_b, filt_b = call(before_kernel, sides, [VM] * 4, sky_scratch, 1 << 34, "before")(msg, before, m1, pcol)
    whole = visits * share
    keep, *sent, mark, m_edge = call(
        join_kernel,
        (sds((whole, cols), F32),) + (sds((whole + B, cols), BF16),) * (bands - 1)
        + (sds((B, LANES), BF16), sds((chunks, 2 * edge, LANES), F32)),
        [VM] * 10,
        [
            pltpu.VMEM((chunks, 8 * PITCH, LANES), F32),
            pltpu.VMEM((3, blocks + 2, 8, CH), F32),
            pltpu.VMEM((chunks, 8 * PITCH, LANES), F32),
            pltpu.VMEM((4 * edge, cols), BF16),
            pltpu.VMEM((2, rows - share + depth, cols), BF16),
        ],
        1 << 29, "join",
    )(note, msg, head, w, pcol, prow, edge_a, edge_b, filt_a, filt_b)
    got = [swapped(part, "band", k + 1) for k, part in enumerate(sent)]
    halves = [half] + [swapped(half, "band", k) for k in range(1, bands)]
    own, *sent, mark = call(
        pair_kernel,
        (sds((share, cols), F32),) + (sds((share + B, cols), BF16),) * (visits - 1) + (sds((B, LANES), BF16),),
        [VM] * (1 + bands), [], 1 << 20, "pair",
    )(mark, keep, *got)
    got = [swapped(part, "visit", k + 1) for k, part in enumerate(sent)]
    difference = call(
        tile_kernel, sds((rows, cols), BF16), [VM] * (6 + bands),
        conv_scratch + [pltpu.VMEM((chunks, 2 * rows, LANES), F32)], conv_flops, "tile",
    )(mark, tile, note, m1, m_edge, w, *halves)
    detection = call(
        coadd_kernel, sds((share, cols), F32), [VM] * (1 + visits), [], 1 << 20, "coadd"
    )(mark, own, *got)
    return (difference[:, None, :], detection)


def solution(mesh):
    return jax.shard_map(
        on_device,
        mesh=mesh,
        in_specs=(
            P(("group", "patch"), None),
            P(("group", "patch"), ("visit", "band"), None),
            P(("group", "patch"), ("visit", "band")),
            P(("group", "patch"), ("visit", "band")),
            P(),
            P(("group", "visit", "band"), None, None),
            P(("group", "visit", "band"), None),
            P(),
        ),
        out_specs=(
            P(("group", "patch"), ("visit", "band"), None),
            P(("group", "patch", "visit", "band"), None),
        ),
        check_vma=False,
    )
```

```python
import functools

import jax
import jax.numpy as jnp
from jax import lax
from jax.experimental import pallas as pl
from jax.experimental.pallas import tpu as pltpu
from jax.sharding import PartitionSpec as P

B = 16
CH = B * B
LANES = 128
GROUPS = LANES // B
PITCH = B + 1
F32 = jnp.float32
BF16 = jnp.bfloat16


def shifted(shard, axis, by):
    devices = lax.axis_size(axis)
    pairs = [(i, i + by) for i in range(devices) if 0 <= i + by < devices]
    return lax.ppermute(shard, axis, pairs)


def partner(me, k, count):
    return me ^ k if count & (count - 1) == 0 else (me + k) % count


def swapped(shard, axis, k):
    devices = lax.axis_size(axis)
    return lax.ppermute(shard, axis, [(i, partner(i, k, devices)) for i in range(devices)])


def iota(shape, dim):
    return lax.broadcasted_iota(jnp.int32, shape, dim)


LIMIT = 10
VM = pl.BlockSpec(memory_space=pltpu.VMEM)
HBM = pl.BlockSpec(memory_space=pltpu.HBM)


def group_transpose(parts):
    parts = list(parts)
    group = iota(parts[0].shape, 1) // B
    for step in (1, 2, 4):
        low = (group & step) == 0
        for m in range(GROUPS):
            if m & step:
                continue
            x, y = parts[m], parts[m + step]
            parts[m] = jnp.where(low, x, pltpu.roll(y, step * B, 1))
            parts[m + step] = jnp.where(low, pltpu.roll(x, LANES - step * B, 1), y)
    return parts


def to_blocks(dst, block, value):
    value = value.astype(F32)
    for a in range(value.shape[0] // B):
        at = (block + a) * PITCH
        for c in range(dst.shape[0]):
            dst[c, at : at + B, :] = value[a * B : (a + 1) * B, c * LANES : (c + 1) * LANES]


def conv_blocks(src, count, w_ref, xs, dst):
    chunks = src.shape[0]
    blocks = chunks * GROUPS

    def load(c):
        for h in range(2):
            rows = [src[c, pl.ds(GROUPS * h + i, count, stride=PITCH), :] for i in range(GROUPS)]
            part = slice(h * LANES, (h + 1) * LANES)
            for g, here in enumerate(group_transpose(rows)):
                at = 1 + c * GROUPS + g
                xs[0, at, :, part] = pltpu.roll(here, 1, 0).astype(xs.dtype)
                xs[1, at, :, part] = here.astype(xs.dtype)
                xs[2, at, :, part] = pltpu.roll(here, count - 1, 0).astype(xs.dtype)

    def solve(c):
        b = c * GROUPS
        pieces = [
            xs[qr, b + qc : b + qc + GROUPS].reshape(GROUPS * count, CH).astype(BF16)
            for qr in range(3)
            for qc in range(3)
        ]
        out = jnp.dot(jnp.concatenate(pieces, axis=1), w_ref[...], preferred_element_type=F32)
        for h in range(2):
            part = slice(h * LANES, (h + 1) * LANES)
            rows = group_transpose([out[g * count : (g + 1) * count, part] for g in range(GROUPS)])
            for i in range(GROUPS):
                dst[c, pl.ds(GROUPS * h + i, count, stride=PITCH), :] = rows[i]

    for q in range(3):
        xs[q, 0] = jnp.zeros((count, CH), xs.dtype)
        xs[q, blocks + 1] = jnp.zeros((count, CH), xs.dtype)
    load(0)
    for c in range(chunks):
        if c + 1 < chunks:
            load(c + 1)
        solve(c)


def slanted(row, count):
    value = jnp.broadcast_to(row, (count, row.shape[1]))
    index = iota(value.shape, 0)
    bit = 1
    while bit < count:
        value = jnp.where((index & bit) != 0, pltpu.roll(value, bit, 1), value)
        bit *= 2
    return value


def column(row):
    size = row.shape[1]
    diag = iota((size, size), 0) == iota((size, size), 1)
    return jnp.sum(jnp.where(diag, row, jnp.zeros_like(row)), axis=1, keepdims=True)


def pack_kernel(
    off_hbm, live_hbm, t_hbm, bank_hbm, index_hbm, coeff_hbm, psf_hbm,
    note_ref, msg_ref, head_ref, half_ref, bank_ref, index_ref, coeff_ref, psf_ref, off_ref, live_ref, sems,
):
    rows, cols = t_hbm.shape
    edge = 2 * B
    piece = half_ref.shape[0]
    begin = pl.multiple_of(lax.axis_index("band") * piece, B)
    copies = [
        pltpu.make_async_copy(a, b, sems.at[n])
        for n, (a, b) in enumerate((
            (off_hbm, off_ref), (live_hbm, live_ref),
            (t_hbm.at[pl.ds(rows - edge, edge)], note_ref.at[pl.ds(0, edge)]),
            (t_hbm.at[pl.ds(0, edge)], note_ref.at[pl.ds(edge, edge)]),
            (t_hbm.at[pl.ds(0, edge)], head_ref),
            (t_hbm.at[pl.ds(begin, piece)], half_ref),
            (bank_hbm, bank_ref), (index_hbm, index_ref), (coeff_hbm, coeff_ref), (psf_hbm, psf_ref),
        ))
    ]
    for copy in copies:
        copy.start()
    for copy in copies:
        copy.wait()
    lane = iota((1, cols), 1)
    off = off_ref[0, 0]
    note = jnp.where(lane == 0, off // B, jnp.where(lane == 1, off % B, live_ref[0, 0])).astype(F32)
    block = note_ref[0:B, :].astype(F32)
    note_ref[0:B, :] = jnp.where(iota((B, cols), 0) == 0, note, block).astype(BF16)
    msg_ref[...] = note_ref[0:edge, :]


def first_kernel(
    note_ref, t_hbm, sci_hbm, bank_ref, index_ref, coeff_ref, psf_ref,
    w_ref, pcol_ref, prow_ref, sci_ref, m_ref, edge_ref, filt_ref,
    t_ref, sems, src, xs, res, sci, diff,
):
    copies = [
        pltpu.make_async_copy(t_hbm, t_ref, sems.at[0]), pltpu.make_async_copy(sci_hbm, sci_ref, sems.at[1])
    ]
    for copy in copies:
        copy.start()
    profs, taps = bank_ref.shape
    half = taps // 2
    delta = B - half
    bank = bank_ref[...]
    index = index_ref[0].astype(F32)
    labels = iota((index.shape[1], profs), 1).astype(F32)
    pick_row = (column(index[0:1]) == labels).astype(F32).astype(BF16)
    pick_col = (column(index[1:2]) == labels).astype(F32).astype(BF16)
    weight = column(coeff_ref[...])
    rowprof = (weight * jnp.dot(pick_row, bank, preferred_element_type=F32)).astype(BF16)
    colprof = jnp.dot(pick_col, bank, preferred_element_type=F32).astype(BF16)
    span = 3 * B
    total = 4 * B * B
    place = (iota((span, taps), 0) - delta == iota((span, taps), 1)).astype(F32).astype(BF16)
    col_t = lax.dot_general(place, colprof, (((1,), (1,)), ((), ())), preferred_element_type=F32).astype(BF16)
    spread = (span - 1 - iota((taps, total), 1) // B - delta == iota((taps, total), 0)).astype(F32).astype(BF16)
    row_rep = jnp.dot(rowprof, spread, preferred_element_type=F32).astype(BF16)
    z = jnp.dot(col_t, row_rep, preferred_element_type=F32)
    lane = iota((span, total), 1)
    for bit in (1, 2, 4, 8):
        z = jnp.where((lane & bit) != 0, pltpu.roll(z, bit, 0), z)
    z = z.astype(BF16)
    for phase in range(GROUPS):
        zp = z if phase == 0 else pltpu.roll(z, total - phase * B, 1)
        for g in range(span):
            start = span - 1 - g
            if start % GROUPS != phase:
                continue
            at = (start // GROUPS) * LANES
            for qc in range(3):
                row = (g // B) * 3 * CH + qc * CH + (g % B) * B
                w_ref[row : row + B, :] = zp[qc * B : (qc + 1) * B, at : at + CH]
    size = pcol_ref.shape[0]
    lanes = iota((taps, 3 * LANES), 1)
    mirror = (lanes - LANES + iota(lanes.shape, 0) == half).astype(F32).astype(BF16)
    bands = slanted(jnp.dot(psf_ref[...], mirror, preferred_element_type=F32), LANES)
    bands = {1 - n: bands[:, n * LANES : (n + 1) * LANES].astype(BF16) for n in range(3)}
    for i in range(size // LANES):
        for j in range(size // LANES):
            block = bands.get(i - j, jnp.zeros((LANES, LANES), BF16))
            pcol_ref[i * LANES : (i + 1) * LANES, j * LANES : (j + 1) * LANES] = block
    share, depth = prow_ref.shape
    lanes = iota((taps, depth), 1)
    ahead = (lanes - iota(lanes.shape, 0) == delta).astype(F32).astype(BF16)
    prow_ref[...] = slanted(jnp.dot(psf_ref[...], ahead, preferred_element_type=F32), share).astype(BF16)
    for copy in copies:
        copy.wait()
    edge = 2 * B
    rows, cols = t_ref.shape
    off, _ = read_note(note_ref)
    to_blocks(src, 0, t_ref[...])
    conv_blocks(src, rows // B, w_ref, xs, res)
    for a in range(1, rows // B - 1):
        m_ref[:, B * a : B * (a + 1), :] = res[:, PITCH * a : PITCH * a + B, :]
    to_chunks(sci, rows, sci_ref[...])
    filter_inner(sci, rows - B - off, off, off + rows, m_ref, pcol_ref, edge_ref, filt_ref, diff)


def to_chunks(dst, dst_row, value):
    value = value.astype(F32)
    rows = value.shape[0]
    for c in range(dst.shape[0]):
        dst[c, dst_row : dst_row + rows, :] = value[:, c * LANES : (c + 1) * LANES]


def tile_diff(sky, m, base, first, last):
    row = iota(m.shape, 0) + (base - B)
    return jnp.where((row >= first) & (row < last), sky - m, 0.0).astype(BF16)


def filter_inner(sci, start, first, last, m_ref, pcol_ref, edge_ref, filt_ref, diff):
    chunks, rows, _ = m_ref.shape
    edge = 2 * B
    for c in range(chunks):
        part = slice(c * LANES, (c + 1) * LANES)
        sky = sci[c, pl.ds(start, rows + edge), :]
        edge_ref[c, 0:edge, :] = sky[0:edge]
        edge_ref[c, edge:, :] = sky[rows:]
        diff[:, part] = tile_diff(sky[edge:rows], m_ref[c, B : rows - B, :], edge, first, last)
    filt_ref[...] = jnp.dot(diff[...], pcol_ref[...], preferred_element_type=F32).astype(BF16)


def read_note(msg_ref):
    note = msg_ref[0:B, 0:LANES].astype(F32)
    return (note[0, 0] * B + note[0, 1]).astype(jnp.int32), note[0, 2]


def read_before(msg_ref):
    valid = lax.axis_index("patch") > 0
    off, live = read_note(msg_ref)
    return jnp.where(valid, off, 0), jnp.where(valid, live, 0.0), valid


def join_kernel(
    note_ref, msg_ref, head_ref, sci_ref, m1_ref, w_ref, pcol_ref, prow_ref, edge_a, filt_a,
    *rest,
):
    *outs, mark_ref, m_ref, src, xs, strip, diff, filt, sci, inner, edge_b, filt_b = rest
    edge = 2 * B
    rows, cols = filt_a.shape[0] + edge, filt_a.shape[1]
    off_b, live_b, valid = read_before(msg_ref)
    to_chunks(sci, 0, sci_ref[...])
    to_blocks(src, 0, jnp.where(valid, msg_ref[...].astype(F32), 0.0))
    to_blocks(src, 2, note_ref[edge:, :])
    to_blocks(src, 4, note_ref[0:edge, :])
    last = lax.axis_index("patch") == lax.axis_size("patch") - 1
    to_blocks(src, 6, jnp.where(last, 0.0, head_ref[...].astype(F32)))
    filter_inner(sci, rows - B - off_b, off_b - rows, off_b, m1_ref, pcol_ref, edge_b, filt_b, inner)
    conv_blocks(src, 8, w_ref, xs, strip)
    for n, a in enumerate((1, 2, 5, 6)):
        m_ref[:, B * n : B * (n + 1), :] = strip[:, PITCH * a : PITCH * a + B, :]
    off_a, live_a = read_note(note_ref)
    for s, (side, first, last) in enumerate(((edge_a, off_a, off_a + rows), (edge_b, off_b - rows, off_b))):
        for c in range(cols // LANES):
            part = slice(c * LANES, (c + 1) * LANES)
            for k, base in enumerate((0, rows)):
                span = slice(k * edge, (k + 1) * edge)
                at = (2 * s + k) * edge
                diff[at : at + edge, part] = tile_diff(side[c, span, :], m_ref[c, span, :], base, first, last)
    sides = jnp.dot(diff[...], pcol_ref[...], preferred_element_type=F32).astype(BF16)
    for s, inner in enumerate((filt_a, filt_b)):
        filt[s, 0:edge, :] = sides[2 * s * edge : (2 * s + 1) * edge]
        filt[s, edge:rows, :] = inner[...]
        filt[s, rows : rows + edge, :] = sides[(2 * s + 1) * edge : (2 * s + 2) * edge]
        filt[s, rows + edge :, :] = jnp.zeros((filt.shape[1] - rows - edge, cols), BF16)
    share, depth = prow_ref.shape
    prow = prow_ref[...].astype(F32)
    out_row = iota((share, depth), 0)
    lane = iota((B, cols), 1)
    visits, bands = lax.axis_size("visit"), lax.axis_size("band")
    hi, lo = off_b // B, off_b % B
    marks = note_ref[0:B, 0:LANES].astype(F32)
    marks = jnp.where(iota(marks.shape, 1) == 3, hi.astype(F32), marks)
    marks = jnp.where(iota(marks.shape, 1) == 4, lo.astype(F32), marks)
    marks = jnp.where(iota(marks.shape, 1) == 5, live_b, marks)
    mark_ref[...] = marks.astype(BF16)
    for j, out_ref in enumerate(outs):
        for k in range(visits):
            to_visit = partner(lax.axis_index("visit"), k, visits)
            base = (to_visit * bands + partner(lax.axis_index("band"), j, bands)) * share
            row = out_row + base
            left = jnp.where(row >= off_a, prow * live_a, 0.0).astype(BF16)
            right = jnp.where(row < off_b, prow * live_b, 0.0).astype(BF16)
            span = pl.ds(pl.multiple_of(base, B), depth)
            total = jnp.dot(left, filt[0, span, :], preferred_element_type=F32)
            total += jnp.dot(right, filt[1, span, :], preferred_element_type=F32)
            out_ref[k * share : (k + 1) * share, :] = total.astype(out_ref.dtype)
        if j:
            out_ref[visits * share :, 0:LANES] = marks.astype(BF16)
            out_ref[visits * share :, LANES:] = jnp.zeros((B, cols - LANES), BF16)


def pair_kernel(*refs):
    bands = lax.axis_size("band")
    visits = lax.axis_size("visit")
    mark_ref, keep_ref, *got = refs[: bands + 1]
    *outs, own_mark_ref = refs[bands + 1 :]
    share, cols = outs[0].shape
    rowid = iota((B, LANES), 0)
    marks = jnp.where(rowid == 0, mark_ref[...].astype(F32), 0.0)
    for n, ref in enumerate(got):
        other = ref[visits * share :, 0:LANES].astype(F32)
        marks = jnp.where(rowid == n + 1, other[0:1, :], marks)
    own_mark_ref[...] = marks.astype(BF16)
    for k, out_ref in enumerate(outs):
        span = slice(k * share, (k + 1) * share)
        total = keep_ref[span, :]
        for ref in got:
            total += ref[span, :].astype(F32)
        out_ref[...] = total.astype(out_ref.dtype)


def tile_kernel(mark_ref, sci_ref, note_ref, m1_ref, edge_ref, w_ref, *rest):
    rows, cols = sci_ref.shape
    *halves, out_ref, src, xs, res, big = rest
    bands = len(halves)
    blocks = rows // B // bands
    band = lax.axis_index("band")
    for j in range(bands):
        piece = halves[0][...].astype(F32)
        for k in range(1, bands):
            piece = jnp.where(partner(band, k, bands) == j, halves[k][...].astype(F32), piece)
        to_blocks(src, j * blocks, piece)
    conv_blocks(src, rows // B, w_ref, xs, res)
    for a in range(1, rows // B):
        big[:, rows + B * a : rows + B * (a + 1), :] = res[:, PITCH * a : PITCH * a + B, :]
    big[:, 0:B, :] = edge_ref[:, B : 2 * B, :]
    big[:, B : rows - B, :] = m1_ref[:, B : rows - B, :]
    big[:, rows - B : rows + B, :] = edge_ref[:, 2 * B : 4 * B, :]
    off, _ = read_note(note_ref)
    for c in range(cols // LANES):
        part = slice(c * LANES, (c + 1) * LANES)
        out_ref[:, part] = (sci_ref[:, part].astype(F32) - big[c, pl.ds(off, rows), :]).astype(BF16)


def coadd_kernel(*refs):
    *parts, out_ref = refs
    marks, parts = parts[: len(parts) // 2], parts[len(parts) // 2 :]
    share, cols = out_ref.shape
    bands = lax.axis_size("band")
    base = (lax.axis_index("visit") * bands + lax.axis_index("band")) * share
    row = (iota((share, LANES), 0) + base).astype(F32)
    cover = jnp.zeros((share, LANES), F32)
    for ref in marks:
        for m in range(bands):
            mark = ref[...].astype(F32)[m : m + 1, :]
            cover += jnp.where(row >= mark[:, 0:1] * B + mark[:, 1:2], mark[:, 2:3], 0.0)
            cover += jnp.where(row < mark[:, 3:4] * B + mark[:, 4:5], mark[:, 5:6], 0.0)
    scale = lax.rsqrt(jnp.maximum(cover, 1.0))
    for c in range(cols // LANES):
        span = slice(c * LANES, (c + 1) * LANES)
        value = parts[0][:, span]
        for part in parts[1:]:
            value += part[:, span].astype(F32)
        out_ref[:, span] = value * scale


def in_hbm(*arrays):
    return [pltpu.with_memory_space_constraint(x, pltpu.HBM) for x in arrays]


def call(body, shapes, specs, scratch, flops, name):
    return pl.pallas_call(
        body,
        out_shape=shapes,
        in_specs=specs,
        out_specs=jax.tree.map(lambda _: VM, shapes),
        scratch_shapes=scratch,
        compiler_params=pltpu.CompilerParams(vmem_limit_bytes=LIMIT * 1024 * 1024),
        cost_estimate=pl.CostEstimate(flops=flops, bytes_accessed=1 << 21, transcendentals=0),
        name=name,
    )


def on_device(template, science, offsets, live_flags, bank, basis_index, coeff, psf_profile):
    rows, cols = template.shape
    sharers = lax.axis_size("visit") * lax.axis_size("band")
    share = rows // sharers
    chunks, blocks = cols // LANES, cols // B
    edge = 2 * B
    inner = rows - edge
    sds = jax.ShapeDtypeStruct
    deep = 9 * CH
    depth = -(-(share + edge) // LANES) * LANES
    sci = science[:, 0, :]
    held = in_hbm(template, sci)
    index = jnp.swapaxes(basis_index, 1, 2)
    before = shifted(science, "patch", 1)[:, 0, :]
    bands, visits = lax.axis_size("band"), lax.axis_size("visit")
    psf = psf_profile[None]
    note, msg, head, half, *small = call(
        pack_kernel,
        (
            sds((2 * edge, cols), BF16), sds((edge, cols), BF16), sds((edge, cols), BF16),
            sds((rows // bands, cols), BF16),
            *(sds(x.shape, x.dtype) for x in (bank, index, coeff, psf)),
        ),
        [HBM] * 7,
        [pltpu.SMEM((1, 1), jnp.int32), pltpu.SMEM((1, 1), jnp.int32), pltpu.SemaphoreType.DMA((10,))],
        1 << 20, "pack",
    )(offsets, live_flags, held[0], *in_hbm(bank, index, coeff, psf))
    half = shifted(half, "patch", -1)
    panels = lax.axis_size("patch")
    msg = lax.ppermute(msg, "patch", [(i, (i + 1) % panels) for i in range(panels)])
    head = lax.ppermute(head, "patch", [((i + 1) % panels, i) for i in range(panels)])
    count = rows // B
    conv_scratch = [
        pltpu.VMEM((chunks, count * PITCH, LANES), F32),
        pltpu.VMEM((3, blocks + 2, count, CH), BF16),
        pltpu.VMEM((chunks, count * PITCH, LANES), F32),
    ]
    conv_flops = 2 * rows * cols * deep
    sky_scratch = [pltpu.VMEM((chunks, 2 * rows + B, LANES), F32), pltpu.VMEM((inner, cols), BF16)]
    sides = (sds((chunks, 2 * edge, LANES), F32), sds((inner, cols), BF16))
    w, pcol, prow, tile, m1, edge_a, filt_a = call(
        first_kernel,
        (
            sds((deep, CH), BF16), sds((cols, cols), BF16), sds((share, depth), BF16),
            sds((rows, cols), BF16), sds((chunks, rows, LANES), F32),
        ) + sides,
        [VM, HBM, HBM] + [VM] * 4,
        [pltpu.VMEM((rows, cols), BF16), pltpu.SemaphoreType.DMA((2,))] + conv_scratch + sky_scratch,
        conv_flops, "first",
    )(note, *held, *small)
    whole = visits * share
    keep, *sent, mark, m_edge = call(
        join_kernel,
        (sds((whole, cols), F32),) + (sds((whole + B, cols), BF16),) * (bands - 1)
        + (sds((B, LANES), BF16), sds((chunks, 2 * edge, LANES), F32)),
        [VM] * 10,
        [
            pltpu.VMEM((chunks, 8 * PITCH, LANES), F32),
            pltpu.VMEM((3, blocks + 2, 8, CH), F32),
            pltpu.VMEM((chunks, 8 * PITCH, LANES), F32),
            pltpu.VMEM((4 * edge, cols), BF16),
            pltpu.VMEM((2, rows - share + depth, cols), BF16),
        ] + sky_scratch + [pltpu.VMEM((chunks, 2 * edge, LANES), F32), pltpu.VMEM((inner, cols), BF16)],
        1 << 34, "join",
    )(note, msg, head, before, m1, w, pcol, prow, edge_a, filt_a)
    got = [swapped(part, "band", k + 1) for k, part in enumerate(sent)]
    halves = [half] + [swapped(half, "band", k) for k in range(1, bands)]
    own, *sent, mark = call(
        pair_kernel,
        (sds((share, cols), F32),) + (sds((share, cols), BF16),) * (visits - 1) + (sds((B, LANES), BF16),),
        [VM] * (1 + bands), [], 1 << 20, "pair",
    )(mark, keep, *got)
    got = [swapped(part, "visit", k + 1) for k, part in enumerate(sent)]
    marks = [mark] + [swapped(mark, "visit", k) for k in range(1, visits)]
    difference = call(
        tile_kernel, sds((rows, cols), BF16), [VM] * (6 + bands),
        conv_scratch + [pltpu.VMEM((chunks, 2 * rows, LANES), F32)], conv_flops, "tile",
    )(mark, tile, note, m1, m_edge, w, *halves)
    detection = call(
        coadd_kernel, sds((share, cols), F32), [VM] * (2 * visits), [], 1 << 20, "coadd"
    )(*marks, own, *got)
    return (difference[:, None, :], detection)


def solution(mesh):
    return jax.shard_map(
        on_device,
        mesh=mesh,
        in_specs=(
            P(("group", "patch"), None),
            P(("group", "patch"), ("visit", "band"), None),
            P(("group", "patch"), ("visit", "band")),
            P(("group", "patch"), ("visit", "band")),
            P(),
            P(("group", "visit", "band"), None, None),
            P(("group", "visit", "band"), None),
            P(),
        ),
        out_specs=(
            P(("group", "patch"), ("visit", "band"), None),
            P(("group", "patch", "visit", "band"), None),
        ),
        check_vma=False,
    )
```

```python
import functools

import jax
import jax.numpy as jnp
from jax import lax
from jax.experimental import pallas as pl
from jax.experimental.pallas import tpu as pltpu
from jax.sharding import PartitionSpec as P

B = 16
CH = B * B
LANES = 128
GROUPS = LANES // B
PITCH = B + 1
F32 = jnp.float32
BF16 = jnp.bfloat16


def shifted(shard, axis, by):
    devices = lax.axis_size(axis)
    pairs = [(i, i + by) for i in range(devices) if 0 <= i + by < devices]
    return lax.ppermute(shard, axis, pairs)


def partner(me, k, count):
    return me ^ k if count & (count - 1) == 0 else (me + k) % count


def swapped(shard, axis, k):
    devices = lax.axis_size(axis)
    return lax.ppermute(shard, axis, [(i, partner(i, k, devices)) for i in range(devices)])


def iota(shape, dim):
    return lax.broadcasted_iota(jnp.int32, shape, dim)


LIMIT = 10
VM = pl.BlockSpec(memory_space=pltpu.VMEM)
HBM = pl.BlockSpec(memory_space=pltpu.HBM)


def group_transpose(parts):
    parts = list(parts)
    group = iota(parts[0].shape, 1) // B
    for step in (1, 2, 4):
        low = (group & step) == 0
        for m in range(GROUPS):
            if m & step:
                continue
            x, y = parts[m], parts[m + step]
            parts[m] = jnp.where(low, x, pltpu.roll(y, step * B, 1))
            parts[m + step] = jnp.where(low, pltpu.roll(x, LANES - step * B, 1), y)
    return parts


def to_blocks(dst, block, value):
    value = value.astype(F32)
    for a in range(value.shape[0] // B):
        at = (block + a) * PITCH
        for c in range(dst.shape[0]):
            dst[c, at : at + B, :] = value[a * B : (a + 1) * B, c * LANES : (c + 1) * LANES]


def conv_blocks(src, count, w_ref, xs, dst, after=None):
    chunks = src.shape[0]
    blocks = chunks * GROUPS

    def load(c):
        for h in range(2):
            rows = [src[c, pl.ds(GROUPS * h + i, count, stride=PITCH), :] for i in range(GROUPS)]
            part = slice(h * LANES, (h + 1) * LANES)
            for g, here in enumerate(group_transpose(rows)):
                at = 1 + c * GROUPS + g
                xs[0, at, :, part] = pltpu.roll(here, 1, 0).astype(xs.dtype)
                xs[1, at, :, part] = here.astype(xs.dtype)
                xs[2, at, :, part] = pltpu.roll(here, count - 1, 0).astype(xs.dtype)

    def solve(c):
        b = c * GROUPS
        pieces = [
            xs[qr, b + qc : b + qc + GROUPS].reshape(GROUPS * count, CH).astype(BF16)
            for qr in range(3)
            for qc in range(3)
        ]
        out = jnp.dot(jnp.concatenate(pieces, axis=1), w_ref[...], preferred_element_type=F32)
        for h in range(2):
            part = slice(h * LANES, (h + 1) * LANES)
            rows = group_transpose([out[g * count : (g + 1) * count, part] for g in range(GROUPS)])
            for i in range(GROUPS):
                dst[c, pl.ds(GROUPS * h + i, count, stride=PITCH), :] = rows[i]

    for q in range(3):
        xs[q, 0] = jnp.zeros((count, CH), xs.dtype)
        xs[q, blocks + 1] = jnp.zeros((count, CH), xs.dtype)
    load(0)
    for c in range(chunks):
        if c + 1 < chunks:
            load(c + 1)
        solve(c)
        if after is not None:
            after(c)


def slanted(row, count):
    value = jnp.broadcast_to(row, (count, row.shape[1]))
    index = iota(value.shape, 0)
    bit = 1
    while bit < count:
        value = jnp.where((index & bit) != 0, pltpu.roll(value, bit, 1), value)
        bit *= 2
    return value


def column(row):
    size = row.shape[1]
    diag = iota((size, size), 0) == iota((size, size), 1)
    return jnp.sum(jnp.where(diag, row, jnp.zeros_like(row)), axis=1, keepdims=True)


def pack_kernel(
    off_hbm, live_hbm, t_hbm, bank_hbm, index_hbm, coeff_hbm, psf_hbm,
    note_ref, msg_ref, head_ref, half_ref, bank_ref, index_ref, coeff_ref, psf_ref, off_ref, live_ref, sems,
):
    rows, cols = t_hbm.shape
    edge = 2 * B
    piece = half_ref.shape[0]
    begin = pl.multiple_of(lax.axis_index("band") * piece, B)
    copies = [
        pltpu.make_async_copy(a, b, sems.at[n])
        for n, (a, b) in enumerate((
            (off_hbm, off_ref), (live_hbm, live_ref),
            (t_hbm.at[pl.ds(rows - edge, edge)], note_ref.at[pl.ds(0, edge)]),
            (t_hbm.at[pl.ds(0, edge)], note_ref.at[pl.ds(edge, edge)]),
            (t_hbm.at[pl.ds(0, edge)], head_ref),
            (t_hbm.at[pl.ds(begin, piece)], half_ref),
            (bank_hbm, bank_ref), (index_hbm, index_ref), (coeff_hbm, coeff_ref), (psf_hbm, psf_ref),
        ))
    ]
    for copy in copies:
        copy.start()
    for copy in copies:
        copy.wait()
    lane = iota((1, cols), 1)
    off = off_ref[0, 0]
    note = jnp.where(lane == 0, off // B, jnp.where(lane == 1, off % B, live_ref[0, 0])).astype(F32)
    block = note_ref[0:B, :].astype(F32)
    note_ref[0:B, :] = jnp.where(iota((B, cols), 0) == 0, note, block).astype(BF16)
    msg_ref[...] = note_ref[0:edge, :]


def first_kernel(
    note_ref, t_hbm, sci_hbm, bank_ref, index_ref, coeff_ref, psf_ref,
    w_ref, pcol_ref, prow_ref, sci_ref, m_ref, edge_ref, filt_ref,
    t_ref, sems, src, xs, res, sci, diff,
):
    copies = [
        pltpu.make_async_copy(t_hbm, t_ref, sems.at[0]), pltpu.make_async_copy(sci_hbm, sci_ref, sems.at[1])
    ]
    for copy in copies:
        copy.start()
    profs, taps = bank_ref.shape
    half = taps // 2
    delta = B - half
    bank = bank_ref[...]
    index = index_ref[0].astype(F32)
    labels = iota((index.shape[1], profs), 1).astype(F32)
    pick_row = (column(index[0:1]) == labels).astype(F32).astype(BF16)
    pick_col = (column(index[1:2]) == labels).astype(F32).astype(BF16)
    weight = column(coeff_ref[...])
    rowprof = (weight * jnp.dot(pick_row, bank, preferred_element_type=F32)).astype(BF16)
    colprof = jnp.dot(pick_col, bank, preferred_element_type=F32).astype(BF16)
    span = 3 * B
    total = 4 * B * B
    place = (iota((span, taps), 0) - delta == iota((span, taps), 1)).astype(F32).astype(BF16)
    col_t = lax.dot_general(place, colprof, (((1,), (1,)), ((), ())), preferred_element_type=F32).astype(BF16)
    spread = (span - 1 - iota((taps, total), 1) // B - delta == iota((taps, total), 0)).astype(F32).astype(BF16)
    row_rep = jnp.dot(rowprof, spread, preferred_element_type=F32).astype(BF16)
    z = jnp.dot(col_t, row_rep, preferred_element_type=F32)
    lane = iota((span, total), 1)
    for bit in (1, 2, 4, 8):
        z = jnp.where((lane & bit) != 0, pltpu.roll(z, bit, 0), z)
    z = z.astype(BF16)
    for phase in range(GROUPS):
        zp = z if phase == 0 else pltpu.roll(z, total - phase * B, 1)
        for g in range(span):
            start = span - 1 - g
            if start % GROUPS != phase:
                continue
            at = (start // GROUPS) * LANES
            for qc in range(3):
                row = (g // B) * 3 * CH + qc * CH + (g % B) * B
                w_ref[row : row + B, :] = zp[qc * B : (qc + 1) * B, at : at + CH]
    size = pcol_ref.shape[0]
    lanes = iota((taps, 3 * LANES), 1)
    mirror = (lanes - LANES + iota(lanes.shape, 0) == half).astype(F32).astype(BF16)
    bands = slanted(jnp.dot(psf_ref[...], mirror, preferred_element_type=F32), LANES)
    bands = {1 - n: bands[:, n * LANES : (n + 1) * LANES].astype(BF16) for n in range(3)}
    for i in range(size // LANES):
        for j in range(size // LANES):
            block = bands.get(i - j, jnp.zeros((LANES, LANES), BF16))
            pcol_ref[i * LANES : (i + 1) * LANES, j * LANES : (j + 1) * LANES] = block
    share, depth = prow_ref.shape
    lanes = iota((taps, depth), 1)
    ahead = (lanes - iota(lanes.shape, 0) == delta).astype(F32).astype(BF16)
    prow_ref[...] = slanted(jnp.dot(psf_ref[...], ahead, preferred_element_type=F32), share).astype(BF16)
    for copy in copies:
        copy.wait()
    edge = 2 * B
    rows, cols = t_ref.shape
    off, _ = read_note(note_ref)
    to_blocks(src, 0, t_ref[...])
    conv_blocks(src, rows // B, w_ref, xs, res)
    for a in range(1, rows // B - 1):
        m_ref[:, B * a : B * (a + 1), :] = res[:, PITCH * a : PITCH * a + B, :]
    to_chunks(sci, rows, sci_ref[...])
    filter_inner(sci, rows - B - off, off, off + rows, m_ref, pcol_ref, edge_ref, filt_ref, diff)


def to_chunks(dst, dst_row, value):
    value = value.astype(F32)
    rows = value.shape[0]
    for c in range(dst.shape[0]):
        dst[c, dst_row : dst_row + rows, :] = value[:, c * LANES : (c + 1) * LANES]


def tile_diff(sky, m, base, first, last):
    row = iota(m.shape, 0) + (base - B)
    return jnp.where((row >= first) & (row < last), sky - m, 0.0).astype(BF16)


def filter_inner(sci, start, first, last, m_ref, pcol_ref, edge_ref, filt_ref, diff):
    chunks, rows, _ = m_ref.shape
    edge = 2 * B
    for c in range(chunks):
        part = slice(c * LANES, (c + 1) * LANES)
        sky = sci[c, pl.ds(start, rows + edge), :]
        edge_ref[c, 0:edge, :] = sky[0:edge]
        edge_ref[c, edge:, :] = sky[rows:]
        diff[:, part] = tile_diff(sky[edge:rows], m_ref[c, B : rows - B, :], edge, first, last)
    filt_ref[...] = jnp.dot(diff[...], pcol_ref[...], preferred_element_type=F32).astype(BF16)


def read_note(msg_ref):
    note = msg_ref[0:B, 0:LANES].astype(F32)
    return (note[0, 0] * B + note[0, 1]).astype(jnp.int32), note[0, 2]


def read_before(msg_ref):
    valid = lax.axis_index("patch") > 0
    off, live = read_note(msg_ref)
    return jnp.where(valid, off, 0), jnp.where(valid, live, 0.0), valid


def join_kernel(
    note_ref, msg_ref, head_ref, sci_ref, m1_ref, w_ref, pcol_ref, prow_ref, edge_a, filt_a,
    *rest,
):
    *outs, mark_ref, m_ref, src, xs, strip, diff, filt, sci, inner, edge_b, filt_b = rest
    edge = 2 * B
    rows, cols = filt_a.shape[0] + edge, filt_a.shape[1]
    off_b, live_b, valid = read_before(msg_ref)
    to_chunks(sci, 0, sci_ref[...])
    to_blocks(src, 0, jnp.where(valid, msg_ref[...].astype(F32), 0.0))
    to_blocks(src, 2, note_ref[edge:, :])
    to_blocks(src, 4, note_ref[0:edge, :])
    last = lax.axis_index("patch") == lax.axis_size("patch") - 1
    to_blocks(src, 6, jnp.where(last, 0.0, head_ref[...].astype(F32)))
    filter_inner(sci, rows - B - off_b, off_b - rows, off_b, m1_ref, pcol_ref, edge_b, filt_b, inner)
    conv_blocks(src, 8, w_ref, xs, strip)
    for n, a in enumerate((1, 2, 5, 6)):
        m_ref[:, B * n : B * (n + 1), :] = strip[:, PITCH * a : PITCH * a + B, :]
    off_a, live_a = read_note(note_ref)
    for s, (side, first, last) in enumerate(((edge_a, off_a, off_a + rows), (edge_b, off_b - rows, off_b))):
        for c in range(cols // LANES):
            part = slice(c * LANES, (c + 1) * LANES)
            for k, base in enumerate((0, rows)):
                span = slice(k * edge, (k + 1) * edge)
                at = (2 * s + k) * edge
                diff[at : at + edge, part] = tile_diff(side[c, span, :], m_ref[c, span, :], base, first, last)
    sides = jnp.dot(diff[...], pcol_ref[...], preferred_element_type=F32).astype(BF16)
    for s, inner in enumerate((filt_a, filt_b)):
        filt[s, 0:edge, :] = sides[2 * s * edge : (2 * s + 1) * edge]
        filt[s, edge:rows, :] = inner[...]
        filt[s, rows : rows + edge, :] = sides[(2 * s + 1) * edge : (2 * s + 2) * edge]
        filt[s, rows + edge :, :] = jnp.zeros((filt.shape[1] - rows - edge, cols), BF16)
    share, depth = prow_ref.shape
    prow = prow_ref[...].astype(F32)
    out_row = iota((share, depth), 0)
    lane = iota((B, cols), 1)
    visits, bands = lax.axis_size("visit"), lax.axis_size("band")
    hi, lo = off_b // B, off_b % B
    marks = note_ref[0:B, 0:LANES].astype(F32)
    marks = jnp.where(iota(marks.shape, 1) == 3, hi.astype(F32), marks)
    marks = jnp.where(iota(marks.shape, 1) == 4, lo.astype(F32), marks)
    marks = jnp.where(iota(marks.shape, 1) == 5, live_b, marks)
    mark_ref[...] = marks.astype(BF16)
    for j, out_ref in enumerate(outs):
        for k in range(visits):
            to_visit = partner(lax.axis_index("visit"), k, visits)
            base = (to_visit * bands + partner(lax.axis_index("band"), j, bands)) * share
            row = out_row + base
            left = jnp.where(row >= off_a, prow * live_a, 0.0).astype(BF16)
            right = jnp.where(row < off_b, prow * live_b, 0.0).astype(BF16)
            span = pl.ds(pl.multiple_of(base, B), depth)
            total = jnp.dot(left, filt[0, span, :], preferred_element_type=F32)
            total += jnp.dot(right, filt[1, span, :], preferred_element_type=F32)
            out_ref[k * share : (k + 1) * share, :] = total.astype(out_ref.dtype)
        if j:
            out_ref[visits * share :, 0:LANES] = marks.astype(BF16)
            out_ref[visits * share :, LANES:] = jnp.zeros((B, cols - LANES), BF16)


def pair_kernel(*refs):
    bands = lax.axis_size("band")
    visits = lax.axis_size("visit")
    mark_ref, keep_ref, *got = refs[: bands + 1]
    *outs, own_mark_ref = refs[bands + 1 :]
    share, cols = outs[0].shape
    rowid = iota((B, LANES), 0)
    marks = jnp.where(rowid == 0, mark_ref[...].astype(F32), 0.0)
    for n, ref in enumerate(got):
        other = ref[visits * share :, 0:LANES].astype(F32)
        marks = jnp.where(rowid == n + 1, other[0:1, :], marks)
    own_mark_ref[...] = marks.astype(BF16)
    for k, out_ref in enumerate(outs):
        span = slice(k * share, (k + 1) * share)
        total = keep_ref[span, :]
        for ref in got:
            total += ref[span, :].astype(F32)
        out_ref[...] = total.astype(out_ref.dtype)


def tile_kernel(mark_ref, sci_ref, note_ref, m1_ref, edge_ref, w_ref, *rest):
    rows, cols = sci_ref.shape
    *halves, out_hbm, src, xs, res, big, out, sems = rest
    bands = len(halves)
    blocks = rows // B // bands
    band = lax.axis_index("band")
    for j in range(bands):
        piece = halves[0][...].astype(F32)
        for k in range(1, bands):
            piece = jnp.where(partner(band, k, bands) == j, halves[k][...].astype(F32), piece)
        to_blocks(src, j * blocks, piece)
    off, _ = read_note(note_ref)
    copies = []

    def after(c):
        big[c, 0:B, :] = edge_ref[c, B : 2 * B, :]
        big[c, B : rows - B, :] = m1_ref[c, B : rows - B, :]
        big[c, rows - B : rows + B, :] = edge_ref[c, 2 * B : 4 * B, :]
        for a in range(1, rows // B):
            big[c, rows + B * a : rows + B * (a + 1), :] = res[c, PITCH * a : PITCH * a + B, :]
        part = slice(c * LANES, (c + 1) * LANES)
        out[:, part] = (sci_ref[:, part].astype(F32) - big[c, pl.ds(off, rows), :]).astype(BF16)
        there = pl.ds(c * LANES, LANES)
        copies.append(pltpu.make_async_copy(out.at[:, there], out_hbm.at[:, there], sems.at[c]))
        copies[-1].start()

    conv_blocks(src, rows // B, w_ref, xs, res, after)
    for copy in copies:
        copy.wait()


def coadd_kernel(*refs):
    *parts, out_ref = refs
    marks, parts = parts[: len(parts) // 2], parts[len(parts) // 2 :]
    share, cols = out_ref.shape
    bands = lax.axis_size("band")
    base = (lax.axis_index("visit") * bands + lax.axis_index("band")) * share
    row = (iota((share, LANES), 0) + base).astype(F32)
    cover = jnp.zeros((share, LANES), F32)
    for ref in marks:
        for m in range(bands):
            mark = ref[...].astype(F32)[m : m + 1, :]
            cover += jnp.where(row >= mark[:, 0:1] * B + mark[:, 1:2], mark[:, 2:3], 0.0)
            cover += jnp.where(row < mark[:, 3:4] * B + mark[:, 4:5], mark[:, 5:6], 0.0)
    scale = lax.rsqrt(jnp.maximum(cover, 1.0))
    for c in range(cols // LANES):
        span = slice(c * LANES, (c + 1) * LANES)
        value = parts[0][:, span]
        for part in parts[1:]:
            value += part[:, span].astype(F32)
        out_ref[:, span] = value * scale


def in_hbm(*arrays):
    return [pltpu.with_memory_space_constraint(x, pltpu.HBM) for x in arrays]


def call(body, shapes, specs, scratch, flops, name, out=VM):
    return pl.pallas_call(
        body,
        out_shape=shapes,
        in_specs=specs,
        out_specs=jax.tree.map(lambda _: out, shapes),
        scratch_shapes=scratch,
        compiler_params=pltpu.CompilerParams(vmem_limit_bytes=LIMIT * 1024 * 1024),
        cost_estimate=pl.CostEstimate(flops=flops, bytes_accessed=1 << 21, transcendentals=0),
        name=name,
    )


def on_device(template, science, offsets, live_flags, bank, basis_index, coeff, psf_profile):
    rows, cols = template.shape
    sharers = lax.axis_size("visit") * lax.axis_size("band")
    share = rows // sharers
    chunks, blocks = cols // LANES, cols // B
    edge = 2 * B
    inner = rows - edge
    sds = jax.ShapeDtypeStruct
    deep = 9 * CH
    depth = -(-(share + edge) // LANES) * LANES
    sci = science[:, 0, :]
    held = in_hbm(template, sci)
    index = jnp.swapaxes(basis_index, 1, 2)
    before = shifted(science, "patch", 1)[:, 0, :]
    bands, visits = lax.axis_size("band"), lax.axis_size("visit")
    psf = psf_profile[None]
    note, msg, head, half, *small = call(
        pack_kernel,
        (
            sds((2 * edge, cols), BF16), sds((edge, cols), BF16), sds((edge, cols), BF16),
            sds((rows // bands, cols), BF16),
            *(sds(x.shape, x.dtype) for x in (bank, index, coeff, psf)),
        ),
        [HBM] * 7,
        [pltpu.SMEM((1, 1), jnp.int32), pltpu.SMEM((1, 1), jnp.int32), pltpu.SemaphoreType.DMA((10,))],
        1 << 20, "pack",
    )(offsets, live_flags, held[0], *in_hbm(bank, index, coeff, psf))
    half = shifted(half, "patch", -1)
    panels = lax.axis_size("patch")
    msg = lax.ppermute(msg, "patch", [(i, (i + 1) % panels) for i in range(panels)])
    head = lax.ppermute(head, "patch", [((i + 1) % panels, i) for i in range(panels)])
    count = rows // B
    conv_scratch = [
        pltpu.VMEM((chunks, count * PITCH, LANES), F32),
        pltpu.VMEM((3, blocks + 2, count, CH), BF16),
        pltpu.VMEM((chunks, count * PITCH, LANES), F32),
    ]
    conv_flops = 2 * rows * cols * deep
    sky_scratch = [pltpu.VMEM((chunks, 2 * rows + B, LANES), F32), pltpu.VMEM((inner, cols), BF16)]
    sides = (sds((chunks, 2 * edge, LANES), F32), sds((inner, cols), BF16))
    w, pcol, prow, tile, m1, edge_a, filt_a = call(
        first_kernel,
        (
            sds((deep, CH), BF16), sds((cols, cols), BF16), sds((share, depth), BF16),
            sds((rows, cols), BF16), sds((chunks, rows, LANES), F32),
        ) + sides,
        [VM, HBM, HBM] + [VM] * 4,
        [pltpu.VMEM((rows, cols), BF16), pltpu.SemaphoreType.DMA((2,))] + conv_scratch + sky_scratch,
        conv_flops, "first",
    )(note, *held, *small)
    whole = visits * share
    keep, *sent, mark, m_edge = call(
        join_kernel,
        (sds((whole, cols), F32),) + (sds((whole + B, cols), BF16),) * (bands - 1)
        + (sds((B, LANES), BF16), sds((chunks, 2 * edge, LANES), F32)),
        [VM] * 10,
        [
            pltpu.VMEM((chunks, 8 * PITCH, LANES), F32),
            pltpu.VMEM((3, blocks + 2, 8, CH), F32),
            pltpu.VMEM((chunks, 8 * PITCH, LANES), F32),
            pltpu.VMEM((4 * edge, cols), BF16),
            pltpu.VMEM((2, rows - share + depth, cols), BF16),
        ] + sky_scratch + [pltpu.VMEM((chunks, 2 * edge, LANES), F32), pltpu.VMEM((inner, cols), BF16)],
        1 << 34, "join",
    )(note, msg, head, before, m1, w, pcol, prow, edge_a, filt_a)
    got = [swapped(part, "band", k + 1) for k, part in enumerate(sent)]
    halves = [half] + [swapped(half, "band", k) for k in range(1, bands)]
    own, *sent, mark = call(
        pair_kernel,
        (sds((share, cols), F32),) + (sds((share, cols), BF16),) * (visits - 1) + (sds((B, LANES), BF16),),
        [VM] * (1 + bands), [], 1 << 20, "pair",
    )(mark, keep, *got)
    got = [swapped(part, "visit", k + 1) for k, part in enumerate(sent)]
    marks = [mark] + [swapped(mark, "visit", k) for k in range(1, visits)]
    difference = call(
        tile_kernel, sds((rows, cols), BF16), [VM] * (6 + bands),
        conv_scratch + [
            pltpu.VMEM((chunks, 2 * rows, LANES), F32), pltpu.VMEM((rows, cols), BF16),
            pltpu.SemaphoreType.DMA((chunks,)),
        ],
        conv_flops, "tile", HBM,
    )(mark, tile, note, m1, m_edge, w, *halves)
    detection = call(
        coadd_kernel, sds((share, cols), F32), [VM] * (2 * visits), [], 1 << 20, "coadd"
    )(*marks, own, *got)
    return (difference[:, None, :], detection)


def solution(mesh):
    return jax.shard_map(
        on_device,
        mesh=mesh,
        in_specs=(
            P(("group", "patch"), None),
            P(("group", "patch"), ("visit", "band"), None),
            P(("group", "patch"), ("visit", "band")),
            P(("group", "patch"), ("visit", "band")),
            P(),
            P(("group", "visit", "band"), None, None),
            P(("group", "visit", "band"), None),
            P(),
        ),
        out_specs=(
            P(("group", "patch"), ("visit", "band"), None),
            P(("group", "patch", "visit", "band"), None),
        ),
        check_vma=False,
    )
```

```python
import functools

import jax
import jax.numpy as jnp
from jax import lax
from jax.experimental import pallas as pl
from jax.experimental.pallas import tpu as pltpu
from jax.sharding import PartitionSpec as P

B = 16
CH = B * B
LANES = 128
GROUPS = LANES // B
PITCH = B + 1
F32 = jnp.float32
BF16 = jnp.bfloat16


def shifted(shard, axis, by):
    devices = lax.axis_size(axis)
    pairs = [(i, i + by) for i in range(devices) if 0 <= i + by < devices]
    return lax.ppermute(shard, axis, pairs)


def partner(me, k, count):
    return me ^ k if count & (count - 1) == 0 else (me + k) % count


def swapped(shard, axis, k):
    devices = lax.axis_size(axis)
    return lax.ppermute(shard, axis, [(i, partner(i, k, devices)) for i in range(devices)])


def iota(shape, dim):
    return lax.broadcasted_iota(jnp.int32, shape, dim)


LIMIT = 10
VM = pl.BlockSpec(memory_space=pltpu.VMEM)
HBM = pl.BlockSpec(memory_space=pltpu.HBM)


def group_transpose(parts):
    parts = list(parts)
    group = iota(parts[0].shape, 1) // B
    for step in (1, 2, 4):
        low = (group & step) == 0
        for m in range(GROUPS):
            if m & step:
                continue
            x, y = parts[m], parts[m + step]
            parts[m] = jnp.where(low, x, pltpu.roll(y, step * B, 1))
            parts[m + step] = jnp.where(low, pltpu.roll(x, LANES - step * B, 1), y)
    return parts


def to_blocks(dst, block, value):
    value = value.astype(F32)
    for a in range(value.shape[0] // B):
        at = (block + a) * PITCH
        for c in range(dst.shape[0]):
            dst[c, at : at + B, :] = value[a * B : (a + 1) * B, c * LANES : (c + 1) * LANES]


def conv_blocks(src, count, w_ref, xs, dst, after=None):
    chunks = src.shape[0]
    blocks = chunks * GROUPS

    def load(c):
        for h in range(2):
            rows = [src[c, pl.ds(GROUPS * h + i, count, stride=PITCH), :] for i in range(GROUPS)]
            part = slice(h * LANES, (h + 1) * LANES)
            for g, here in enumerate(group_transpose(rows)):
                at = 1 + c * GROUPS + g
                xs[0, at, :, part] = pltpu.roll(here, 1, 0).astype(xs.dtype)
                xs[1, at, :, part] = here.astype(xs.dtype)
                xs[2, at, :, part] = pltpu.roll(here, count - 1, 0).astype(xs.dtype)

    def solve(c):
        b = c * GROUPS
        pieces = [
            xs[qr, b + qc : b + qc + GROUPS].reshape(GROUPS * count, CH).astype(BF16)
            for qr in range(3)
            for qc in range(3)
        ]
        out = jnp.dot(jnp.concatenate(pieces, axis=1), w_ref[...], preferred_element_type=F32)
        for h in range(2):
            part = slice(h * LANES, (h + 1) * LANES)
            rows = group_transpose([out[g * count : (g + 1) * count, part] for g in range(GROUPS)])
            for i in range(GROUPS):
                dst[c, pl.ds(GROUPS * h + i, count, stride=PITCH), :] = rows[i]

    for q in range(3):
        xs[q, 0] = jnp.zeros((count, CH), xs.dtype)
        xs[q, blocks + 1] = jnp.zeros((count, CH), xs.dtype)
    load(0)
    for c in range(chunks):
        if c + 1 < chunks:
            load(c + 1)
        solve(c)
        if after is not None:
            after(c)


def slanted(row, count):
    value = jnp.broadcast_to(row, (count, row.shape[1]))
    index = iota(value.shape, 0)
    bit = 1
    while bit < count:
        value = jnp.where((index & bit) != 0, pltpu.roll(value, bit, 1), value)
        bit *= 2
    return value


def column(row):
    size = row.shape[1]
    diag = iota((size, size), 0) == iota((size, size), 1)
    return jnp.sum(jnp.where(diag, row, jnp.zeros_like(row)), axis=1, keepdims=True)


def pack_kernel(
    off_hbm, live_hbm, t_hbm, bank_hbm, index_hbm, coeff_hbm, psf_hbm,
    note_ref, msg_ref, bank_ref, index_ref, coeff_ref, psf_ref, off_ref, live_ref, sems,
):
    rows, cols = t_hbm.shape
    edge = 2 * B
    copies = [
        pltpu.make_async_copy(a, b, sems.at[n])
        for n, (a, b) in enumerate((
            (off_hbm, off_ref), (live_hbm, live_ref),
            (t_hbm.at[pl.ds(rows - edge, edge)], note_ref.at[pl.ds(0, edge)]),
            (t_hbm.at[pl.ds(0, edge)], note_ref.at[pl.ds(edge, edge)]),
            (bank_hbm, bank_ref), (index_hbm, index_ref), (coeff_hbm, coeff_ref), (psf_hbm, psf_ref),
        ))
    ]
    for copy in copies:
        copy.start()
    for copy in copies:
        copy.wait()
    lane = iota((1, cols), 1)
    off = off_ref[0, 0]
    note = jnp.where(lane == 0, off // B, jnp.where(lane == 1, off % B, live_ref[0, 0])).astype(F32)
    block = note_ref[0:B, :].astype(F32)
    note_ref[0:B, :] = jnp.where(iota((B, cols), 0) == 0, note, block).astype(BF16)
    msg_ref[...] = note_ref[0:edge, :]


def weights_kernel(
    note_ref, t_hbm, sci_hbm, bank_ref, index_ref, coeff_ref, psf_ref,
    w_ref, pcol_ref, prow_ref, head_ref, half_ref, t_ref, sci_ref, sems,
):
    piece = half_ref.shape[0]
    begin = pl.multiple_of(lax.axis_index("band") * piece, B)
    copies = [
        pltpu.make_async_copy(t_hbm.at[pl.ds(begin, piece)], half_ref, sems.at[0]),
        pltpu.make_async_copy(t_hbm, t_ref, sems.at[1]),
        pltpu.make_async_copy(sci_hbm, sci_ref, sems.at[2]),
    ]
    for copy in copies:
        copy.start()
    head_ref[...] = note_ref[2 * B :, :]
    profs, taps = bank_ref.shape
    half = taps // 2
    delta = B - half
    bank = bank_ref[...]
    index = index_ref[0].astype(F32)
    labels = iota((index.shape[1], profs), 1).astype(F32)
    pick_row = (column(index[0:1]) == labels).astype(F32).astype(BF16)
    pick_col = (column(index[1:2]) == labels).astype(F32).astype(BF16)
    weight = column(coeff_ref[...])
    rowprof = (weight * jnp.dot(pick_row, bank, preferred_element_type=F32)).astype(BF16)
    colprof = jnp.dot(pick_col, bank, preferred_element_type=F32).astype(BF16)
    span = 3 * B
    total = 4 * B * B
    place = (iota((span, taps), 0) - delta == iota((span, taps), 1)).astype(F32).astype(BF16)
    col_t = lax.dot_general(place, colprof, (((1,), (1,)), ((), ())), preferred_element_type=F32).astype(BF16)
    spread = (span - 1 - iota((taps, total), 1) // B - delta == iota((taps, total), 0)).astype(F32).astype(BF16)
    row_rep = jnp.dot(rowprof, spread, preferred_element_type=F32).astype(BF16)
    z = jnp.dot(col_t, row_rep, preferred_element_type=F32)
    lane = iota((span, total), 1)
    for bit in (1, 2, 4, 8):
        z = jnp.where((lane & bit) != 0, pltpu.roll(z, bit, 0), z)
    z = z.astype(BF16)
    for phase in range(GROUPS):
        zp = z if phase == 0 else pltpu.roll(z, total - phase * B, 1)
        for g in range(span):
            start = span - 1 - g
            if start % GROUPS != phase:
                continue
            at = (start // GROUPS) * LANES
            for qc in range(3):
                row = (g // B) * 3 * CH + qc * CH + (g % B) * B
                w_ref[row : row + B, :] = zp[qc * B : (qc + 1) * B, at : at + CH]
    size = pcol_ref.shape[0]
    lanes = iota((taps, 3 * LANES), 1)
    mirror = (lanes - LANES + iota(lanes.shape, 0) == half).astype(F32).astype(BF16)
    bands = slanted(jnp.dot(psf_ref[...], mirror, preferred_element_type=F32), LANES)
    bands = {1 - n: bands[:, n * LANES : (n + 1) * LANES].astype(BF16) for n in range(3)}
    for i in range(size // LANES):
        for j in range(size // LANES):
            block = bands.get(i - j, jnp.zeros((LANES, LANES), BF16))
            pcol_ref[i * LANES : (i + 1) * LANES, j * LANES : (j + 1) * LANES] = block
    share, depth = prow_ref.shape
    lanes = iota((taps, depth), 1)
    ahead = (lanes - iota(lanes.shape, 0) == delta).astype(F32).astype(BF16)
    prow_ref[...] = slanted(jnp.dot(psf_ref[...], ahead, preferred_element_type=F32), share).astype(BF16)
    for copy in copies:
        copy.wait()


def own_kernel(note_ref, t_ref, sci_ref, w_ref, pcol_ref, m_ref, edge_ref, filt_ref, src, xs, res, sci, diff):
    rows = t_ref.shape[0]
    off, _ = read_note(note_ref)
    to_blocks(src, 0, t_ref[...])
    conv_blocks(src, rows // B, w_ref, xs, res)
    for a in range(1, rows // B - 1):
        m_ref[:, B * a : B * (a + 1), :] = res[:, PITCH * a : PITCH * a + B, :]
    to_chunks(sci, rows, sci_ref[...])
    filter_inner(sci, rows - B - off, off, off + rows, m_ref, pcol_ref, edge_ref, filt_ref, diff)


def to_chunks(dst, dst_row, value):
    value = value.astype(F32)
    rows = value.shape[0]
    for c in range(dst.shape[0]):
        dst[c, dst_row : dst_row + rows, :] = value[:, c * LANES : (c + 1) * LANES]


def tile_diff(sky, m, base, first, last):
    row = iota(m.shape, 0) + (base - B)
    return jnp.where((row >= first) & (row < last), sky - m, 0.0).astype(BF16)


def filter_inner(sci, start, first, last, m_ref, pcol_ref, edge_ref, filt_ref, diff):
    chunks, rows, _ = m_ref.shape
    edge = 2 * B
    for c in range(chunks):
        part = slice(c * LANES, (c + 1) * LANES)
        sky = sci[c, pl.ds(start, rows + edge), :]
        edge_ref[c, 0:edge, :] = sky[0:edge]
        edge_ref[c, edge:, :] = sky[rows:]
        diff[:, part] = tile_diff(sky[edge:rows], m_ref[c, B : rows - B, :], edge, first, last)
    filt_ref[...] = jnp.dot(diff[...], pcol_ref[...], preferred_element_type=F32).astype(BF16)


def read_note(msg_ref):
    note = msg_ref[0:B, 0:LANES].astype(F32)
    return (note[0, 0] * B + note[0, 1]).astype(jnp.int32), note[0, 2]


def halo_kernel(msg_ref, out_ref):
    valid = lax.axis_index("patch") > 0
    out_ref[...] = jnp.where(valid, msg_ref[...].astype(F32), 0.0).astype(BF16)


def join_kernel(
    note_ref, msg_ref, head_ref, sci_ref, m1_ref, w_ref, pcol_ref, prow_ref, edge_a, filt_a,
    *rest,
):
    *outs, mark_ref, m_ref, src, xs, strip, diff, filt, sci, inner, edge_b, filt_b = rest
    edge = 2 * B
    rows, cols = filt_a.shape[0] + edge, filt_a.shape[1]
    off_b, live_b = read_note(msg_ref)
    to_chunks(sci, 0, sci_ref[...])
    to_blocks(src, 0, msg_ref[...])
    to_blocks(src, 2, note_ref[edge:, :])
    to_blocks(src, 4, note_ref[0:edge, :])
    last = lax.axis_index("patch") == lax.axis_size("patch") - 1
    to_blocks(src, 6, jnp.where(last, 0.0, head_ref[...].astype(F32)))
    filter_inner(sci, rows - B - off_b, off_b - rows, off_b, m1_ref, pcol_ref, edge_b, filt_b, inner)
    conv_blocks(src, 8, w_ref, xs, strip)
    for n, a in enumerate((1, 2, 5, 6)):
        m_ref[:, B * n : B * (n + 1), :] = strip[:, PITCH * a : PITCH * a + B, :]
    off_a, live_a = read_note(note_ref)
    for s, (side, first, last) in enumerate(((edge_a, off_a, off_a + rows), (edge_b, off_b - rows, off_b))):
        for c in range(cols // LANES):
            part = slice(c * LANES, (c + 1) * LANES)
            for k, base in enumerate((0, rows)):
                span = slice(k * edge, (k + 1) * edge)
                at = (2 * s + k) * edge
                diff[at : at + edge, part] = tile_diff(side[c, span, :], m_ref[c, span, :], base, first, last)
    sides = jnp.dot(diff[...], pcol_ref[...], preferred_element_type=F32).astype(BF16)
    for s, inner in enumerate((filt_a, filt_b)):
        filt[s, 0:edge, :] = sides[2 * s * edge : (2 * s + 1) * edge]
        filt[s, edge:rows, :] = inner[...]
        filt[s, rows : rows + edge, :] = sides[(2 * s + 1) * edge : (2 * s + 2) * edge]
        filt[s, rows + edge :, :] = jnp.zeros((filt.shape[1] - rows - edge, cols), BF16)
    share, depth = prow_ref.shape
    prow = prow_ref[...].astype(F32)
    out_row = iota((share, depth), 0)
    lane = iota((B, cols), 1)
    visits, bands = lax.axis_size("visit"), lax.axis_size("band")
    hi, lo = off_b // B, off_b % B
    marks = note_ref[0:B, 0:LANES].astype(F32)
    marks = jnp.where(iota(marks.shape, 1) == 3, hi.astype(F32), marks)
    marks = jnp.where(iota(marks.shape, 1) == 4, lo.astype(F32), marks)
    marks = jnp.where(iota(marks.shape, 1) == 5, live_b, marks)
    mark_ref[...] = marks.astype(BF16)
    for j, out_ref in enumerate(outs):
        for k in range(visits):
            to_visit = partner(lax.axis_index("visit"), k, visits)
            base = (to_visit * bands + partner(lax.axis_index("band"), j, bands)) * share
            row = out_row + base
            left = jnp.where(row >= off_a, prow * live_a, 0.0).astype(BF16)
            right = jnp.where(row < off_b, prow * live_b, 0.0).astype(BF16)
            span = pl.ds(pl.multiple_of(base, B), depth)
            total = jnp.dot(left, filt[0, span, :], preferred_element_type=F32)
            total += jnp.dot(right, filt[1, span, :], preferred_element_type=F32)
            out_ref[k * share : (k + 1) * share, :] = total.astype(out_ref.dtype)
        if j:
            out_ref[visits * share :, 0:LANES] = marks.astype(BF16)
            out_ref[visits * share :, LANES:] = jnp.zeros((B, cols - LANES), BF16)


def pair_kernel(*refs):
    bands = lax.axis_size("band")
    visits = lax.axis_size("visit")
    mark_ref, keep_ref, *got = refs[: bands + 1]
    *outs, own_mark_ref = refs[bands + 1 :]
    share, cols = outs[0].shape
    rowid = iota((B, LANES), 0)
    marks = jnp.where(rowid == 0, mark_ref[...].astype(F32), 0.0)
    for n, ref in enumerate(got):
        other = ref[visits * share :, 0:LANES].astype(F32)
        marks = jnp.where(rowid == n + 1, other[0:1, :], marks)
    own_mark_ref[...] = marks.astype(BF16)
    for k, out_ref in enumerate(outs):
        span = slice(k * share, (k + 1) * share)
        total = keep_ref[span, :]
        for ref in got:
            total += ref[span, :].astype(F32)
        out_ref[...] = total.astype(out_ref.dtype)


def tile_kernel(mark_ref, sci_ref, note_ref, m1_ref, edge_ref, w_ref, *rest):
    rows, cols = sci_ref.shape
    *halves, out_hbm, src, xs, res, big, out, sems = rest
    bands = len(halves)
    blocks = rows // B // bands
    band = lax.axis_index("band")
    for j in range(bands):
        piece = halves[0][...].astype(F32)
        for k in range(1, bands):
            piece = jnp.where(partner(band, k, bands) == j, halves[k][...].astype(F32), piece)
        to_blocks(src, j * blocks, piece)
    off, _ = read_note(note_ref)
    copies = []

    def after(c):
        big[c, 0:B, :] = edge_ref[c, B : 2 * B, :]
        big[c, B : rows - B, :] = m1_ref[c, B : rows - B, :]
        big[c, rows - B : rows + B, :] = edge_ref[c, 2 * B : 4 * B, :]
        for a in range(1, rows // B):
            big[c, rows + B * a : rows + B * (a + 1), :] = res[c, PITCH * a : PITCH * a + B, :]
        part = slice(c * LANES, (c + 1) * LANES)
        out[:, part] = (sci_ref[:, part].astype(F32) - big[c, pl.ds(off, rows), :]).astype(BF16)
        there = pl.ds(c * LANES, LANES)
        copies.append(pltpu.make_async_copy(out.at[:, there], out_hbm.at[:, there], sems.at[c]))
        copies[-1].start()

    conv_blocks(src, rows // B, w_ref, xs, res, after)
    for copy in copies:
        copy.wait()


def coadd_kernel(*refs):
    *parts, out_ref = refs
    marks, parts = parts[: len(parts) // 2], parts[len(parts) // 2 :]
    share, cols = out_ref.shape
    bands = lax.axis_size("band")
    base = (lax.axis_index("visit") * bands + lax.axis_index("band")) * share
    row = (iota((share, LANES), 0) + base).astype(F32)
    cover = jnp.zeros((share, LANES), F32)
    for ref in marks:
        for m in range(bands):
            mark = ref[...].astype(F32)[m : m + 1, :]
            cover += jnp.where(row >= mark[:, 0:1] * B + mark[:, 1:2], mark[:, 2:3], 0.0)
            cover += jnp.where(row < mark[:, 3:4] * B + mark[:, 4:5], mark[:, 5:6], 0.0)
    scale = lax.rsqrt(jnp.maximum(cover, 1.0))
    for c in range(cols // LANES):
        span = slice(c * LANES, (c + 1) * LANES)
        value = parts[0][:, span]
        for part in parts[1:]:
            value += part[:, span].astype(F32)
        out_ref[:, span] = value * scale


def in_hbm(*arrays):
    return [pltpu.with_memory_space_constraint(x, pltpu.HBM) for x in arrays]


def call(body, shapes, specs, scratch, flops, name, out=VM):
    return pl.pallas_call(
        body,
        out_shape=shapes,
        in_specs=specs,
        out_specs=jax.tree.map(lambda _: out, shapes),
        scratch_shapes=scratch,
        compiler_params=pltpu.CompilerParams(vmem_limit_bytes=LIMIT * 1024 * 1024),
        cost_estimate=pl.CostEstimate(flops=flops, bytes_accessed=1 << 21, transcendentals=0),
        name=name,
    )


def on_device(template, science, offsets, live_flags, bank, basis_index, coeff, psf_profile):
    rows, cols = template.shape
    sharers = lax.axis_size("visit") * lax.axis_size("band")
    share = rows // sharers
    chunks, blocks = cols // LANES, cols // B
    edge = 2 * B
    inner = rows - edge
    sds = jax.ShapeDtypeStruct
    deep = 9 * CH
    depth = -(-(share + edge) // LANES) * LANES
    sci = science[:, 0, :]
    held = in_hbm(template, sci)
    index = jnp.swapaxes(basis_index, 1, 2)
    before = shifted(science, "patch", 1)[:, 0, :]
    bands, visits = lax.axis_size("band"), lax.axis_size("visit")
    psf = psf_profile[None]
    note, msg, *small = call(
        pack_kernel,
        (
            sds((2 * edge, cols), BF16), sds((edge, cols), BF16),
            *(sds(x.shape, x.dtype) for x in (bank, index, coeff, psf)),
        ),
        [HBM] * 7,
        [pltpu.SMEM((1, 1), jnp.int32), pltpu.SMEM((1, 1), jnp.int32), pltpu.SemaphoreType.DMA((8,))],
        1 << 20, "pack",
    )(offsets, live_flags, held[0], *in_hbm(bank, index, coeff, psf))
    panels = lax.axis_size("patch")
    msg = lax.ppermute(msg, "patch", [(i, (i + 1) % panels) for i in range(panels)])
    w, pcol, prow, head, half, panel, tile = call(
        weights_kernel,
        (
            sds((deep, CH), BF16), sds((cols, cols), BF16), sds((share, depth), BF16), sds((edge, cols), BF16),
            sds((rows // bands, cols), BF16), sds((rows, cols), BF16), sds((rows, cols), BF16),
        ),
        [VM, HBM, HBM] + [VM] * 4, [pltpu.SemaphoreType.DMA((3,))], 1 << 28, "weights",
    )(note, *held, *small)
    head = lax.ppermute(head, "patch", [((i + 1) % panels, i) for i in range(panels)])
    half = shifted(half, "patch", -1)
    count = rows // B
    conv_scratch = [
        pltpu.VMEM((chunks, count * PITCH, LANES), F32),
        pltpu.VMEM((3, blocks + 2, count, CH), BF16),
        pltpu.VMEM((chunks, count * PITCH, LANES), F32),
    ]
    conv_flops = 2 * rows * cols * deep
    sky_scratch = [pltpu.VMEM((chunks, 2 * rows + B, LANES), F32), pltpu.VMEM((inner, cols), BF16)]
    sides = (sds((chunks, 2 * edge, LANES), F32), sds((inner, cols), BF16))
    m1, edge_a, filt_a = call(
        own_kernel, (sds((chunks, rows, LANES), F32),) + sides, [VM] * 5,
        conv_scratch + sky_scratch, 1 << 20, "own",
    )(note, panel, tile, w, pcol)
    msg = call(halo_kernel, sds((edge, cols), BF16), [VM], [], 1 << 32, "halo")(msg)
    whole = visits * share
    keep, *sent, mark, m_edge = call(
        join_kernel,
        (sds((whole, cols), F32),) + (sds((whole + B, cols), BF16),) * (bands - 1)
        + (sds((B, LANES), BF16), sds((chunks, 2 * edge, LANES), F32)),
        [VM] * 10,
        [
            pltpu.VMEM((chunks, 8 * PITCH, LANES), F32),
            pltpu.VMEM((3, blocks + 2, 8, CH), F32),
            pltpu.VMEM((chunks, 8 * PITCH, LANES), F32),
            pltpu.VMEM((4 * edge, cols), BF16),
            pltpu.VMEM((2, rows - share + depth, cols), BF16),
        ] + sky_scratch + [pltpu.VMEM((chunks, 2 * edge, LANES), F32), pltpu.VMEM((inner, cols), BF16)],
        1 << 34, "join",
    )(note, msg, head, before, m1, w, pcol, prow, edge_a, filt_a)
    got = [swapped(part, "band", k + 1) for k, part in enumerate(sent)]
    halves = [half] + [swapped(half, "band", k) for k in range(1, bands)]
    own, *sent, mark = call(
        pair_kernel,
        (sds((share, cols), F32),) + (sds((share, cols), BF16),) * (visits - 1) + (sds((B, LANES), BF16),),
        [VM] * (1 + bands), [], 1 << 20, "pair",
    )(mark, keep, *got)
    got = [swapped(part, "visit", k + 1) for k, part in enumerate(sent)]
    marks = [mark] + [swapped(mark, "visit", k) for k in range(1, visits)]
    difference = call(
        tile_kernel, sds((rows, cols), BF16), [VM] * (6 + bands),
        conv_scratch + [
            pltpu.VMEM((chunks, 2 * rows, LANES), F32), pltpu.VMEM((rows, cols), BF16),
            pltpu.SemaphoreType.DMA((chunks,)),
        ],
        conv_flops, "tile", HBM,
    )(mark, tile, note, m1, m_edge, w, *halves)
    detection = call(
        coadd_kernel, sds((share, cols), F32), [VM] * (2 * visits), [], 1 << 20, "coadd"
    )(*marks, own, *got)
    return (difference[:, None, :], detection)


def solution(mesh):
    return jax.shard_map(
        on_device,
        mesh=mesh,
        in_specs=(
            P(("group", "patch"), None),
            P(("group", "patch"), ("visit", "band"), None),
            P(("group", "patch"), ("visit", "band")),
            P(("group", "patch"), ("visit", "band")),
            P(),
            P(("group", "visit", "band"), None, None),
            P(("group", "visit", "band"), None),
            P(),
        ),
        out_specs=(
            P(("group", "patch"), ("visit", "band"), None),
            P(("group", "patch", "visit", "band"), None),
        ),
        check_vma=False,
    )
```

```python
import functools

import jax
import jax.numpy as jnp
from jax import lax
from jax.experimental import pallas as pl
from jax.experimental.pallas import tpu as pltpu
from jax.sharding import PartitionSpec as P

B = 16
CH = B * B
LANES = 128
GROUPS = LANES // B
PITCH = B + 1
F32 = jnp.float32
BF16 = jnp.bfloat16


def shifted(shard, axis, by):
    devices = lax.axis_size(axis)
    pairs = [(i, i + by) for i in range(devices) if 0 <= i + by < devices]
    return lax.ppermute(shard, axis, pairs)


def partner(me, k, count):
    return me ^ k if count & (count - 1) == 0 else (me + k) % count


def swapped(shard, axis, k):
    devices = lax.axis_size(axis)
    return lax.ppermute(shard, axis, [(i, partner(i, k, devices)) for i in range(devices)])


def iota(shape, dim):
    return lax.broadcasted_iota(jnp.int32, shape, dim)


LIMIT = 14
VM = pl.BlockSpec(memory_space=pltpu.VMEM)
HBM = pl.BlockSpec(memory_space=pltpu.HBM)


def group_transpose(parts):
    parts = list(parts)
    group = iota(parts[0].shape, 1) // B
    for step in (1, 2, 4):
        low = (group & step) == 0
        for m in range(GROUPS):
            if m & step:
                continue
            x, y = parts[m], parts[m + step]
            parts[m] = jnp.where(low, x, pltpu.roll(y, step * B, 1))
            parts[m + step] = jnp.where(low, pltpu.roll(x, LANES - step * B, 1), y)
    return parts


def to_blocks(dst, block, value):
    value = value.astype(F32)
    for a in range(value.shape[0] // B):
        at = (block + a) * PITCH
        for c in range(dst.shape[0]):
            dst[c, at : at + B, :] = value[a * B : (a + 1) * B, c * LANES : (c + 1) * LANES]


def conv_blocks(src, count, w_ref, xs, stage, dst, after=None):
    chunks = src.shape[0]
    blocks = chunks * GROUPS

    def load(c):
        for h in range(2):
            rows = [src[c, pl.ds(GROUPS * h + i, count, stride=PITCH), :] for i in range(GROUPS)]
            part = slice(h * LANES, (h + 1) * LANES)
            for g, here in enumerate(group_transpose(rows)):
                at = 1 + c * GROUPS + g
                slot = (c * 2 + h) * GROUPS + g
                stage[slot, 8 : 8 + count, :] = here
                for q in range(3):
                    xs[q, at, :, part] = stage[slot, 7 + q : 7 + q + count, :].astype(xs.dtype)

    def solve(c):
        b = c * GROUPS
        pieces = [
            xs[qr, b + qc : b + qc + GROUPS].reshape(GROUPS * count, CH).astype(BF16)
            for qr in range(3)
            for qc in range(3)
        ]
        out = jnp.dot(jnp.concatenate(pieces, axis=1), w_ref[...], preferred_element_type=F32)
        for h in range(2):
            part = slice(h * LANES, (h + 1) * LANES)
            rows = group_transpose([out[g * count : (g + 1) * count, part] for g in range(GROUPS)])
            for i in range(GROUPS):
                dst[c, pl.ds(GROUPS * h + i, count, stride=PITCH), :] = rows[i]

    for q in range(3):
        xs[q, 0] = jnp.zeros((count, CH), xs.dtype)
        xs[q, blocks + 1] = jnp.zeros((count, CH), xs.dtype)
    load(0)
    for c in range(chunks):
        if c + 1 < chunks:
            load(c + 1)
        solve(c)
        if after is not None:
            after(c)


def slanted(row, count):
    value = jnp.broadcast_to(row, (count, row.shape[1]))
    index = iota(value.shape, 0)
    bit = 1
    while bit < count:
        value = jnp.where((index & bit) != 0, pltpu.roll(value, bit, 1), value)
        bit *= 2
    return value


def column(row):
    size = row.shape[1]
    diag = iota((size, size), 0) == iota((size, size), 1)
    return jnp.sum(jnp.where(diag, row, jnp.zeros_like(row)), axis=1, keepdims=True)


def pack_kernel(
    off_hbm, live_hbm, t_hbm, bank_hbm, index_hbm, coeff_hbm, psf_hbm,
    note_ref, msg_ref, head_ref, half_ref, bank_ref, index_ref, coeff_ref, psf_ref, off_ref, live_ref, sems,
):
    rows, cols = t_hbm.shape
    edge = 2 * B
    piece = half_ref.shape[0]
    begin = pl.multiple_of(lax.axis_index("band") * piece, B)
    copies = [
        pltpu.make_async_copy(a, b, sems.at[n])
        for n, (a, b) in enumerate((
            (off_hbm, off_ref), (live_hbm, live_ref),
            (t_hbm.at[pl.ds(rows - edge, edge)], note_ref.at[pl.ds(0, edge)]),
            (t_hbm.at[pl.ds(0, edge)], note_ref.at[pl.ds(edge, edge)]),
            (t_hbm.at[pl.ds(0, edge)], head_ref),
            (t_hbm.at[pl.ds(begin, piece)], half_ref),
            (bank_hbm, bank_ref), (index_hbm, index_ref), (coeff_hbm, coeff_ref), (psf_hbm, psf_ref),
        ))
    ]
    for copy in copies:
        copy.start()
    for copy in copies:
        copy.wait()
    lane = iota((1, cols), 1)
    off = off_ref[0, 0]
    note = jnp.where(lane == 0, off // B, jnp.where(lane == 1, off % B, live_ref[0, 0])).astype(F32)
    block = note_ref[0:B, :].astype(F32)
    note_ref[0:B, :] = jnp.where(iota((B, cols), 0) == 0, note, block).astype(BF16)
    msg_ref[...] = note_ref[0:edge, :]


def first_kernel(
    note_ref, t_hbm, sci_hbm, bank_ref, index_ref, coeff_ref, psf_ref,
    w_ref, pcol_ref, prow_ref, sci_ref, m_ref, edge_ref, filt_ref,
    t_ref, sems, src, xs, stage, res, sci, diff,
):
    copies = [
        pltpu.make_async_copy(t_hbm, t_ref, sems.at[0]), pltpu.make_async_copy(sci_hbm, sci_ref, sems.at[1])
    ]
    for copy in copies:
        copy.start()
    profs, taps = bank_ref.shape
    half = taps // 2
    delta = B - half
    bank = bank_ref[...]
    index = index_ref[0].astype(F32)
    labels = iota((index.shape[1], profs), 1).astype(F32)
    pick_row = (column(index[0:1]) == labels).astype(F32).astype(BF16)
    pick_col = (column(index[1:2]) == labels).astype(F32).astype(BF16)
    weight = column(coeff_ref[...])
    rowprof = (weight * jnp.dot(pick_row, bank, preferred_element_type=F32)).astype(BF16)
    colprof = jnp.dot(pick_col, bank, preferred_element_type=F32).astype(BF16)
    span = 3 * B
    total = 4 * B * B
    place = (iota((span, taps), 0) - delta == iota((span, taps), 1)).astype(F32).astype(BF16)
    col_t = lax.dot_general(place, colprof, (((1,), (1,)), ((), ())), preferred_element_type=F32).astype(BF16)
    spread = (span - 1 - iota((taps, total), 1) // B - delta == iota((taps, total), 0)).astype(F32).astype(BF16)
    row_rep = jnp.dot(rowprof, spread, preferred_element_type=F32).astype(BF16)
    z = jnp.dot(col_t, row_rep, preferred_element_type=F32)
    lane = iota((span, total), 1)
    for bit in (1, 2, 4, 8):
        z = jnp.where((lane & bit) != 0, pltpu.roll(z, bit, 0), z)
    z = z.astype(BF16)
    for phase in range(GROUPS):
        zp = z if phase == 0 else pltpu.roll(z, total - phase * B, 1)
        for g in range(span):
            start = span - 1 - g
            if start % GROUPS != phase:
                continue
            at = (start // GROUPS) * LANES
            for qc in range(3):
                row = (g // B) * 3 * CH + qc * CH + (g % B) * B
                w_ref[row : row + B, :] = zp[qc * B : (qc + 1) * B, at : at + CH]
    size = pcol_ref.shape[0]
    lanes = iota((taps, 3 * LANES), 1)
    mirror = (lanes - LANES + iota(lanes.shape, 0) == half).astype(F32).astype(BF16)
    bands = slanted(jnp.dot(psf_ref[...], mirror, preferred_element_type=F32), LANES)
    bands = {1 - n: bands[:, n * LANES : (n + 1) * LANES].astype(BF16) for n in range(3)}
    for i in range(size // LANES):
        for j in range(size // LANES):
            block = bands.get(i - j, jnp.zeros((LANES, LANES), BF16))
            pcol_ref[i * LANES : (i + 1) * LANES, j * LANES : (j + 1) * LANES] = block
    share, depth = prow_ref.shape
    lanes = iota((taps, depth), 1)
    ahead = (lanes - iota(lanes.shape, 0) == delta).astype(F32).astype(BF16)
    prow_ref[...] = slanted(jnp.dot(psf_ref[...], ahead, preferred_element_type=F32), share).astype(BF16)
    for copy in copies:
        copy.wait()
    edge = 2 * B
    rows, cols = t_ref.shape
    off, _ = read_note(note_ref)
    to_blocks(src, 0, t_ref[...])
    conv_blocks(src, rows // B, w_ref, xs, stage, res)
    for a in range(1, rows // B - 1):
        m_ref[:, B * a : B * (a + 1), :] = res[:, PITCH * a : PITCH * a + B, :]
    to_chunks(sci, rows, sci_ref[...])
    filter_inner(sci, rows - B - off, off, off + rows, m_ref, pcol_ref, edge_ref, filt_ref, diff)


def to_chunks(dst, dst_row, value):
    value = value.astype(F32)
    rows = value.shape[0]
    for c in range(dst.shape[0]):
        dst[c, dst_row : dst_row + rows, :] = value[:, c * LANES : (c + 1) * LANES]


def tile_diff(sky, m, base, first, last):
    row = iota(m.shape, 0) + (base - B)
    return jnp.where((row >= first) & (row < last), sky - m, 0.0).astype(BF16)


def filter_inner(sci, start, first, last, m_ref, pcol_ref, edge_ref, filt_ref, diff):
    chunks, rows, _ = m_ref.shape
    edge = 2 * B
    for c in range(chunks):
        part = slice(c * LANES, (c + 1) * LANES)
        sky = sci[c, pl.ds(start, rows + edge), :]
        edge_ref[c, 0:edge, :] = sky[0:edge]
        edge_ref[c, edge:, :] = sky[rows:]
        diff[:, part] = tile_diff(sky[edge:rows], m_ref[c, B : rows - B, :], edge, first, last)
    filt_ref[...] = jnp.dot(diff[...], pcol_ref[...], preferred_element_type=F32).astype(BF16)


def read_note(msg_ref):
    note = msg_ref[0:B, 0:LANES].astype(F32)
    return (note[0, 0] * B + note[0, 1]).astype(jnp.int32), note[0, 2]


def read_before(msg_ref):
    valid = lax.axis_index("patch") > 0
    off, live = read_note(msg_ref)
    return jnp.where(valid, off, 0), jnp.where(valid, live, 0.0), valid


def join_kernel(
    note_ref, msg_ref, head_ref, sci_ref, m1_ref, w_ref, pcol_ref, prow_ref, edge_a, filt_a,
    *rest,
):
    *outs, mark_ref, m_ref, src, xs, stage, strip, diff, filt, sci, inner, edge_b, filt_b = rest
    edge = 2 * B
    rows, cols = filt_a.shape[0] + edge, filt_a.shape[1]
    off_b, live_b, valid = read_before(msg_ref)
    to_chunks(sci, 0, sci_ref[...])
    to_blocks(src, 0, jnp.where(valid, msg_ref[...].astype(F32), 0.0))
    to_blocks(src, 2, note_ref[edge:, :])
    to_blocks(src, 4, note_ref[0:edge, :])
    to_blocks(src, 6, head_ref[...])
    filter_inner(sci, rows - B - off_b, off_b - rows, off_b, m1_ref, pcol_ref, edge_b, filt_b, inner)
    conv_blocks(src, 8, w_ref, xs, stage, strip)
    for n, a in enumerate((1, 2, 5, 6)):
        m_ref[:, B * n : B * (n + 1), :] = strip[:, PITCH * a : PITCH * a + B, :]
    off_a, live_a = read_note(note_ref)
    for s, (side, first, last) in enumerate(((edge_a, off_a, off_a + rows), (edge_b, off_b - rows, off_b))):
        for c in range(cols // LANES):
            part = slice(c * LANES, (c + 1) * LANES)
            for k, base in enumerate((0, rows)):
                span = slice(k * edge, (k + 1) * edge)
                at = (2 * s + k) * edge
                diff[at : at + edge, part] = tile_diff(side[c, span, :], m_ref[c, span, :], base, first, last)
    sides = jnp.dot(diff[...], pcol_ref[...], preferred_element_type=F32).astype(BF16)
    for s, inner in enumerate((filt_a, filt_b)):
        filt[s, 0:edge, :] = sides[2 * s * edge : (2 * s + 1) * edge]
        filt[s, edge:rows, :] = inner[...]
        filt[s, rows : rows + edge, :] = sides[(2 * s + 1) * edge : (2 * s + 2) * edge]
        filt[s, rows + edge :, :] = jnp.zeros((filt.shape[1] - rows - edge, cols), BF16)
    share, depth = prow_ref.shape
    prow = prow_ref[...].astype(F32)
    out_row = iota((share, depth), 0)
    lane = iota((B, cols), 1)
    visits, bands = lax.axis_size("visit"), lax.axis_size("band")
    hi, lo = off_b // B, off_b % B
    marks = note_ref[0:B, 0:LANES].astype(F32)
    marks = jnp.where(iota(marks.shape, 1) == 3, hi.astype(F32), marks)
    marks = jnp.where(iota(marks.shape, 1) == 4, lo.astype(F32), marks)
    marks = jnp.where(iota(marks.shape, 1) == 5, live_b, marks)
    mark_ref[...] = marks.astype(BF16)
    for j, out_ref in enumerate(outs):
        for k in range(visits):
            to_visit = partner(lax.axis_index("visit"), k, visits)
            base = (to_visit * bands + partner(lax.axis_index("band"), j, bands)) * share
            row = out_row + base
            left = jnp.where(row >= off_a, prow * live_a, 0.0).astype(BF16)
            right = jnp.where(row < off_b, prow * live_b, 0.0).astype(BF16)
            span = pl.ds(pl.multiple_of(base, B), depth)
            total = jnp.dot(left, filt[0, span, :], preferred_element_type=F32)
            total += jnp.dot(right, filt[1, span, :], preferred_element_type=F32)
            out_ref[k * share : (k + 1) * share, :] = total.astype(out_ref.dtype)
        if j:
            out_ref[visits * share :, 0:LANES] = marks.astype(BF16)
            out_ref[visits * share :, LANES:] = jnp.zeros((B, cols - LANES), BF16)


def pair_kernel(*refs):
    bands = lax.axis_size("band")
    visits = lax.axis_size("visit")
    mark_ref, keep_ref, *got = refs[: bands + 1]
    *outs, own_mark_ref = refs[bands + 1 :]
    share, cols = outs[0].shape
    rowid = iota((B, LANES), 0)
    marks = jnp.where(rowid == 0, mark_ref[...].astype(F32), 0.0)
    for n, ref in enumerate(got):
        other = ref[visits * share :, 0:LANES].astype(F32)
        marks = jnp.where(rowid == n + 1, other[0:1, :], marks)
    own_mark_ref[...] = marks.astype(BF16)
    for k, out_ref in enumerate(outs):
        span = slice(k * share, (k + 1) * share)
        total = keep_ref[span, :]
        for ref in got:
            total += ref[span, :].astype(F32)
        out_ref[...] = total.astype(out_ref.dtype)


def tile_kernel(mark_ref, sci_ref, note_ref, m1_ref, edge_ref, w_ref, *rest):
    rows, cols = sci_ref.shape
    *halves, out_hbm, src, xs, stage, res, big, out, sems = rest
    bands = len(halves)
    blocks = rows // B // bands
    band = lax.axis_index("band")
    for j in range(bands):
        piece = halves[0][...].astype(F32)
        for k in range(1, bands):
            piece = jnp.where(partner(band, k, bands) == j, halves[k][...].astype(F32), piece)
        to_blocks(src, j * blocks, piece)
    off, _ = read_note(note_ref)
    copies = []

    def after(c):
        big[c, 0:B, :] = edge_ref[c, B : 2 * B, :]
        big[c, B : rows - B, :] = m1_ref[c, B : rows - B, :]
        big[c, rows - B : rows + B, :] = edge_ref[c, 2 * B : 4 * B, :]
        for a in range(1, rows // B):
            big[c, rows + B * a : rows + B * (a + 1), :] = res[c, PITCH * a : PITCH * a + B, :]
        part = slice(c * LANES, (c + 1) * LANES)
        out[:, part] = (sci_ref[:, part].astype(F32) - big[c, pl.ds(off, rows), :]).astype(BF16)
        there = pl.ds(c * LANES, LANES)
        copies.append(pltpu.make_async_copy(out.at[:, there], out_hbm.at[:, there], sems.at[c]))
        copies[-1].start()

    conv_blocks(src, rows // B, w_ref, xs, stage, res, after)
    for copy in copies:
        copy.wait()


def coadd_kernel(*refs):
    *parts, out_ref = refs
    marks, parts = parts[: len(parts) // 2], parts[len(parts) // 2 :]
    share, cols = out_ref.shape
    bands = lax.axis_size("band")
    base = (lax.axis_index("visit") * bands + lax.axis_index("band")) * share
    row = (iota((share, LANES), 0) + base).astype(F32)
    cover = jnp.zeros((share, LANES), F32)
    for ref in marks:
        for m in range(bands):
            mark = ref[...].astype(F32)[m : m + 1, :]
            cover += jnp.where(row >= mark[:, 0:1] * B + mark[:, 1:2], mark[:, 2:3], 0.0)
            cover += jnp.where(row < mark[:, 3:4] * B + mark[:, 4:5], mark[:, 5:6], 0.0)
    scale = lax.rsqrt(jnp.maximum(cover, 1.0))
    for c in range(cols // LANES):
        span = slice(c * LANES, (c + 1) * LANES)
        value = parts[0][:, span]
        for part in parts[1:]:
            value += part[:, span].astype(F32)
        out_ref[:, span] = value * scale


def in_hbm(*arrays):
    return [pltpu.with_memory_space_constraint(x, pltpu.HBM) for x in arrays]


def call(body, shapes, specs, scratch, flops, name, out=VM):
    return pl.pallas_call(
        body,
        out_shape=shapes,
        in_specs=specs,
        out_specs=jax.tree.map(lambda _: out, shapes),
        scratch_shapes=scratch,
        compiler_params=pltpu.CompilerParams(vmem_limit_bytes=LIMIT * 1024 * 1024),
        cost_estimate=pl.CostEstimate(flops=flops, bytes_accessed=1 << 21, transcendentals=0),
        name=name,
    )


def on_device(template, science, offsets, live_flags, bank, basis_index, coeff, psf_profile):
    rows, cols = template.shape
    sharers = lax.axis_size("visit") * lax.axis_size("band")
    share = rows // sharers
    chunks, blocks = cols // LANES, cols // B
    edge = 2 * B
    inner = rows - edge
    sds = jax.ShapeDtypeStruct
    deep = 9 * CH
    depth = -(-(share + edge) // LANES) * LANES
    sci = science[:, 0, :]
    held = in_hbm(template, sci)
    index = jnp.swapaxes(basis_index, 1, 2)
    before = shifted(science, "patch", 1)[:, 0, :]
    bands, visits = lax.axis_size("band"), lax.axis_size("visit")
    psf = psf_profile[None]
    note, msg, head, half, *small = call(
        pack_kernel,
        (
            sds((2 * edge, cols), BF16), sds((edge, cols), BF16), sds((edge, cols), BF16),
            sds((rows // bands, cols), BF16),
            *(sds(x.shape, x.dtype) for x in (bank, index, coeff, psf)),
        ),
        [HBM] * 7,
        [pltpu.SMEM((1, 1), jnp.int32), pltpu.SMEM((1, 1), jnp.int32), pltpu.SemaphoreType.DMA((10,))],
        1 << 20, "pack",
    )(offsets, live_flags, held[0], *in_hbm(bank, index, coeff, psf))
    half = shifted(half, "patch", -1)
    panels = lax.axis_size("patch")
    msg = lax.ppermute(msg, "patch", [(i, (i + 1) % panels) for i in range(panels)])
    head = shifted(head, "patch", -1)
    count = rows // B
    conv_scratch = [
        pltpu.VMEM((chunks, count * PITCH, LANES), F32),
        pltpu.VMEM((3, blocks + 2, count, CH), BF16),
        pltpu.VMEM((2 * blocks, count + 16, LANES), F32),
        pltpu.VMEM((chunks, count * PITCH, LANES), F32),
    ]
    conv_flops = 2 * rows * cols * deep
    sky_scratch = [pltpu.VMEM((chunks, 2 * rows + B, LANES), F32), pltpu.VMEM((inner, cols), BF16)]
    sides = (sds((chunks, 2 * edge, LANES), F32), sds((inner, cols), BF16))
    w, pcol, prow, tile, m1, edge_a, filt_a = call(
        first_kernel,
        (
            sds((deep, CH), BF16), sds((cols, cols), BF16), sds((share, depth), BF16),
            sds((rows, cols), BF16), sds((chunks, rows, LANES), F32),
        ) + sides,
        [VM, HBM, HBM] + [VM] * 4,
        [pltpu.VMEM((rows, cols), BF16), pltpu.SemaphoreType.DMA((2,))] + conv_scratch + sky_scratch,
        conv_flops, "first",
    )(note, *held, *small)
    whole = visits * share
    keep, *sent, mark, m_edge = call(
        join_kernel,
        (sds((whole, cols), F32),) + (sds((whole + B, cols), BF16),) * (bands - 1)
        + (sds((B, LANES), BF16), sds((chunks, 2 * edge, LANES), F32)),
        [VM] * 10,
        [
            pltpu.VMEM((chunks, 8 * PITCH, LANES), F32),
            pltpu.VMEM((3, blocks + 2, 8, CH), F32),
            pltpu.VMEM((2 * blocks, 24, LANES), F32),
            pltpu.VMEM((chunks, 8 * PITCH, LANES), F32),
            pltpu.VMEM((4 * edge, cols), BF16),
            pltpu.VMEM((2, rows - share + depth, cols), BF16),
        ] + sky_scratch + [pltpu.VMEM((chunks, 2 * edge, LANES), F32), pltpu.VMEM((inner, cols), BF16)],
        1 << 34, "join",
    )(note, msg, head, before, m1, w, pcol, prow, edge_a, filt_a)
    got = [swapped(part, "band", k + 1) for k, part in enumerate(sent)]
    halves = [half] + [swapped(half, "band", k) for k in range(1, bands)]
    own, *sent, mark = call(
        pair_kernel,
        (sds((share, cols), F32),) + (sds((share, cols), BF16),) * (visits - 1) + (sds((B, LANES), BF16),),
        [VM] * (1 + bands), [], 1 << 20, "pair",
    )(mark, keep, *got)
    got = [swapped(part, "visit", k + 1) for k, part in enumerate(sent)]
    marks = [mark] + [swapped(mark, "visit", k) for k in range(1, visits)]
    difference = call(
        tile_kernel, sds((rows, cols), BF16), [VM] * (6 + bands),
        conv_scratch + [
            pltpu.VMEM((chunks, 2 * rows, LANES), F32), pltpu.VMEM((rows, cols), BF16),
            pltpu.SemaphoreType.DMA((chunks,)),
        ],
        conv_flops, "tile", HBM,
    )(mark, tile, note, m1, m_edge, w, *halves)
    detection = call(
        coadd_kernel, sds((share, cols), F32), [VM] * (2 * visits), [], 1 << 20, "coadd"
    )(*marks, own, *got)
    return (difference[:, None, :], detection)


def solution(mesh):
    return jax.shard_map(
        on_device,
        mesh=mesh,
        in_specs=(
            P(("group", "patch"), None),
            P(("group", "patch"), ("visit", "band"), None),
            P(("group", "patch"), ("visit", "band")),
            P(("group", "patch"), ("visit", "band")),
            P(),
            P(("group", "visit", "band"), None, None),
            P(("group", "visit", "band"), None),
            P(),
        ),
        out_specs=(
            P(("group", "patch"), ("visit", "band"), None),
            P(("group", "patch", "visit", "band"), None),
        ),
        check_vma=False,
    )
```

```python
import functools

import jax
import jax.numpy as jnp
from jax import lax
from jax.experimental import pallas as pl
from jax.experimental.pallas import tpu as pltpu
from jax.sharding import PartitionSpec as P

B = 16
CH = B * B
LANES = 128
GROUPS = LANES // B
PITCH = B + 1
F32 = jnp.float32
BF16 = jnp.bfloat16


def shifted(shard, axis, by):
    devices = lax.axis_size(axis)
    pairs = [(i, i + by) for i in range(devices) if 0 <= i + by < devices]
    return lax.ppermute(shard, axis, pairs)


def partner(me, k, count):
    return me ^ k if count & (count - 1) == 0 else (me + k) % count


def swapped(shard, axis, k):
    devices = lax.axis_size(axis)
    return lax.ppermute(shard, axis, [(i, partner(i, k, devices)) for i in range(devices)])


def iota(shape, dim):
    return lax.broadcasted_iota(jnp.int32, shape, dim)


LIMIT = 14
VM = pl.BlockSpec(memory_space=pltpu.VMEM)
HBM = pl.BlockSpec(memory_space=pltpu.HBM)


def group_transpose(parts):
    parts = list(parts)
    group = iota(parts[0].shape, 1) // B
    for step in (1, 2, 4):
        low = (group & step) == 0
        for m in range(GROUPS):
            if m & step:
                continue
            x, y = parts[m], parts[m + step]
            parts[m] = jnp.where(low, x, pltpu.roll(y, step * B, 1))
            parts[m + step] = jnp.where(low, pltpu.roll(x, LANES - step * B, 1), y)
    return parts


def to_blocks(dst, block, value):
    value = value.astype(F32)
    for a in range(value.shape[0] // B):
        at = (block + a) * PITCH
        for c in range(dst.shape[0]):
            dst[c, at : at + B, :] = value[a * B : (a + 1) * B, c * LANES : (c + 1) * LANES]


def conv_blocks(src, count, w_ref, xs, dst, after=None):
    chunks = src.shape[0]
    blocks = chunks * GROUPS

    def load(c):
        for h in range(2):
            rows = [src[c, pl.ds(GROUPS * h + i, count, stride=PITCH), :] for i in range(GROUPS)]
            part = slice(h * LANES, (h + 1) * LANES)
            for g, here in enumerate(group_transpose(rows)):
                at = 1 + c * GROUPS + g
                xs[0, at, :, part] = pltpu.roll(here, 1, 0).astype(xs.dtype)
                xs[1, at, :, part] = here.astype(xs.dtype)
                xs[2, at, :, part] = pltpu.roll(here, count - 1, 0).astype(xs.dtype)

    def solve(c):
        b = c * GROUPS
        pieces = [
            xs[qr, b + qc : b + qc + GROUPS].reshape(GROUPS * count, CH).astype(BF16)
            for qr in range(3)
            for qc in range(3)
        ]
        out = jnp.dot(jnp.concatenate(pieces, axis=1), w_ref[...], preferred_element_type=F32)
        for h in range(2):
            part = slice(h * LANES, (h + 1) * LANES)
            rows = group_transpose([out[g * count : (g + 1) * count, part] for g in range(GROUPS)])
            for i in range(GROUPS):
                dst[c, pl.ds(GROUPS * h + i, count, stride=PITCH), :] = rows[i]

    for q in range(3):
        xs[q, 0] = jnp.zeros((count, CH), xs.dtype)
        xs[q, blocks + 1] = jnp.zeros((count, CH), xs.dtype)
    load(0)
    for c in range(chunks):
        if c + 1 < chunks:
            load(c + 1)
        solve(c)
        if after is not None:
            after(c)


def slanted(row, count):
    value = jnp.broadcast_to(row, (count, row.shape[1]))
    index = iota(value.shape, 0)
    bit = 1
    while bit < count:
        value = jnp.where((index & bit) != 0, pltpu.roll(value, bit, 1), value)
        bit *= 2
    return value


def column(row):
    size = row.shape[1]
    diag = iota((size, size), 0) == iota((size, size), 1)
    return jnp.sum(jnp.where(diag, row, jnp.zeros_like(row)), axis=1, keepdims=True)


def pack_kernel(
    off_hbm, live_hbm, t_hbm, bank_hbm, index_hbm, coeff_hbm, psf_hbm,
    note_ref, msg_ref, head_ref, half_ref, bank_ref, index_ref, coeff_ref, psf_ref, off_ref, live_ref, sems,
):
    rows, cols = t_hbm.shape
    edge = 2 * B
    piece = half_ref.shape[0]
    begin = pl.multiple_of(lax.axis_index("band") * piece, B)
    copies = [
        pltpu.make_async_copy(a, b, sems.at[n])
        for n, (a, b) in enumerate((
            (off_hbm, off_ref), (live_hbm, live_ref),
            (t_hbm.at[pl.ds(rows - edge, edge)], note_ref.at[pl.ds(0, edge)]),
            (t_hbm.at[pl.ds(0, edge)], note_ref.at[pl.ds(edge, edge)]),
            (t_hbm.at[pl.ds(0, edge)], head_ref),
            (t_hbm.at[pl.ds(begin, piece)], half_ref),
            (bank_hbm, bank_ref), (index_hbm, index_ref), (coeff_hbm, coeff_ref), (psf_hbm, psf_ref),
        ))
    ]
    for copy in copies:
        copy.start()
    for copy in copies:
        copy.wait()
    lane = iota((1, cols), 1)
    off = off_ref[0, 0]
    note = jnp.where(lane == 0, off // B, jnp.where(lane == 1, off % B, live_ref[0, 0])).astype(F32)
    block = note_ref[0:B, :].astype(F32)
    note_ref[0:B, :] = jnp.where(iota((B, cols), 0) == 0, note, block).astype(BF16)
    msg_ref[...] = note_ref[0:edge, :]


def first_kernel(
    note_ref, t_hbm, sci_hbm, bank_ref, index_ref, coeff_ref, psf_ref,
    w_ref, pcol_ref, prow_ref, sci_ref, m_ref, edge_ref, filt_ref,
    t_ref, sems, src, xs, sci, diff,
):
    copies = [
        pltpu.make_async_copy(t_hbm, t_ref, sems.at[0]), pltpu.make_async_copy(sci_hbm, sci_ref, sems.at[1])
    ]
    for copy in copies:
        copy.start()
    profs, taps = bank_ref.shape
    half = taps // 2
    delta = B - half
    bank = bank_ref[...]
    index = index_ref[0].astype(F32)
    labels = iota((index.shape[1], profs), 1).astype(F32)
    pick_row = (column(index[0:1]) == labels).astype(F32).astype(BF16)
    pick_col = (column(index[1:2]) == labels).astype(F32).astype(BF16)
    weight = column(coeff_ref[...])
    rowprof = (weight * jnp.dot(pick_row, bank, preferred_element_type=F32)).astype(BF16)
    colprof = jnp.dot(pick_col, bank, preferred_element_type=F32).astype(BF16)
    span = 3 * B
    total = 4 * B * B
    place = (iota((span, taps), 0) - delta == iota((span, taps), 1)).astype(F32).astype(BF16)
    col_t = lax.dot_general(place, colprof, (((1,), (1,)), ((), ())), preferred_element_type=F32).astype(BF16)
    spread = (span - 1 - iota((taps, total), 1) // B - delta == iota((taps, total), 0)).astype(F32).astype(BF16)
    row_rep = jnp.dot(rowprof, spread, preferred_element_type=F32).astype(BF16)
    z = jnp.dot(col_t, row_rep, preferred_element_type=F32)
    lane = iota((span, total), 1)
    for bit in (1, 2, 4, 8):
        z = jnp.where((lane & bit) != 0, pltpu.roll(z, bit, 0), z)
    z = z.astype(BF16)
    for phase in range(GROUPS):
        zp = z if phase == 0 else pltpu.roll(z, total - phase * B, 1)
        for g in range(span):
            start = span - 1 - g
            if start % GROUPS != phase:
                continue
            at = (start // GROUPS) * LANES
            for qc in range(3):
                row = (g // B) * 3 * CH + qc * CH + (g % B) * B
                w_ref[row : row + B, :] = zp[qc * B : (qc + 1) * B, at : at + CH]
    size = pcol_ref.shape[0]
    lanes = iota((taps, 3 * LANES), 1)
    mirror = (lanes - LANES + iota(lanes.shape, 0) == half).astype(F32).astype(BF16)
    bands = slanted(jnp.dot(psf_ref[...], mirror, preferred_element_type=F32), LANES)
    bands = {1 - n: bands[:, n * LANES : (n + 1) * LANES].astype(BF16) for n in range(3)}
    for i in range(size // LANES):
        for j in range(size // LANES):
            block = bands.get(i - j, jnp.zeros((LANES, LANES), BF16))
            pcol_ref[i * LANES : (i + 1) * LANES, j * LANES : (j + 1) * LANES] = block
    share, depth = prow_ref.shape
    lanes = iota((taps, depth), 1)
    ahead = (lanes - iota(lanes.shape, 0) == delta).astype(F32).astype(BF16)
    prow_ref[...] = slanted(jnp.dot(psf_ref[...], ahead, preferred_element_type=F32), share).astype(BF16)
    for copy in copies:
        copy.wait()
    edge = 2 * B
    rows, cols = t_ref.shape
    off, _ = read_note(note_ref)
    to_blocks(src, 0, t_ref[...])
    conv_blocks(src, rows // B, w_ref, xs, m_ref)
    to_chunks(sci, rows, sci_ref[...])
    filter_inner(sci, rows - B - off, off, off + rows, m_ref, pcol_ref, edge_ref, filt_ref, diff)


def to_chunks(dst, dst_row, value):
    value = value.astype(F32)
    rows = value.shape[0]
    for c in range(dst.shape[0]):
        dst[c, dst_row : dst_row + rows, :] = value[:, c * LANES : (c + 1) * LANES]


def tile_diff(sky, m, base, first, last):
    row = iota(m.shape, 0) + (base - B)
    return jnp.where((row >= first) & (row < last), sky - m, 0.0).astype(BF16)


def filter_inner(sci, start, first, last, m_ref, pcol_ref, edge_ref, filt_ref, diff):
    chunks, blocks = m_ref.shape[0], m_ref.shape[1] // PITCH
    rows, edge = blocks * B, 2 * B
    for c in range(chunks):
        part = slice(c * LANES, (c + 1) * LANES)
        sky = sci[c, pl.ds(start, rows + edge), :]
        inner = jnp.concatenate([m_ref[c, PITCH * a : PITCH * a + B, :] for a in range(1, blocks - 1)], axis=0)
        edge_ref[c, 0:edge, :] = sky[0:edge]
        edge_ref[c, edge:, :] = sky[rows:]
        diff[:, part] = tile_diff(sky[edge:rows], inner, edge, first, last)
    filt_ref[...] = jnp.dot(diff[...], pcol_ref[...], preferred_element_type=F32).astype(BF16)


def read_note(msg_ref):
    note = msg_ref[0:B, 0:LANES].astype(F32)
    return (note[0, 0] * B + note[0, 1]).astype(jnp.int32), note[0, 2]


def read_before(msg_ref):
    valid = lax.axis_index("patch") > 0
    off, live = read_note(msg_ref)
    return jnp.where(valid, off, 0), jnp.where(valid, live, 0.0), valid


def join_kernel(
    note_ref, msg_ref, head_ref, sci_ref, m1_ref, w_ref, pcol_ref, prow_ref, edge_a, filt_a,
    *rest,
):
    *outs, mark_ref, m_ref, src, xs, strip, diff, filt, sci, inner, edge_b, filt_b = rest
    edge = 2 * B
    rows, cols = filt_a.shape[0] + edge, filt_a.shape[1]
    off_b, live_b, valid = read_before(msg_ref)
    to_chunks(sci, 0, sci_ref[...])
    to_blocks(src, 0, jnp.where(valid, msg_ref[...].astype(F32), 0.0))
    to_blocks(src, 2, note_ref[edge:, :])
    to_blocks(src, 4, note_ref[0:edge, :])
    to_blocks(src, 6, head_ref[...])
    filter_inner(sci, rows - B - off_b, off_b - rows, off_b, m1_ref, pcol_ref, edge_b, filt_b, inner)
    conv_blocks(src, 8, w_ref, xs, strip)
    for n, a in enumerate((1, 2, 5, 6)):
        m_ref[:, B * n : B * (n + 1), :] = strip[:, PITCH * a : PITCH * a + B, :]
    off_a, live_a = read_note(note_ref)
    for s, (side, first, last) in enumerate(((edge_a, off_a, off_a + rows), (edge_b, off_b - rows, off_b))):
        for c in range(cols // LANES):
            part = slice(c * LANES, (c + 1) * LANES)
            for k, base in enumerate((0, rows)):
                span = slice(k * edge, (k + 1) * edge)
                at = (2 * s + k) * edge
                diff[at : at + edge, part] = tile_diff(side[c, span, :], m_ref[c, span, :], base, first, last)
    sides = jnp.dot(diff[...], pcol_ref[...], preferred_element_type=F32).astype(BF16)
    for s, inner in enumerate((filt_a, filt_b)):
        filt[s, 0:edge, :] = sides[2 * s * edge : (2 * s + 1) * edge]
        filt[s, edge:rows, :] = inner[...]
        filt[s, rows : rows + edge, :] = sides[(2 * s + 1) * edge : (2 * s + 2) * edge]
        filt[s, rows + edge :, :] = jnp.zeros((filt.shape[1] - rows - edge, cols), BF16)
    share, depth = prow_ref.shape
    prow = prow_ref[...].astype(F32)
    out_row = iota((share, depth), 0)
    lane = iota((B, cols), 1)
    visits, bands = lax.axis_size("visit"), lax.axis_size("band")
    hi, lo = off_b // B, off_b % B
    marks = note_ref[0:B, 0:LANES].astype(F32)
    marks = jnp.where(iota(marks.shape, 1) == 3, hi.astype(F32), marks)
    marks = jnp.where(iota(marks.shape, 1) == 4, lo.astype(F32), marks)
    marks = jnp.where(iota(marks.shape, 1) == 5, live_b, marks)
    mark_ref[...] = marks.astype(BF16)
    for j, out_ref in enumerate(outs):
        for k in range(visits):
            to_visit = partner(lax.axis_index("visit"), k, visits)
            base = (to_visit * bands + partner(lax.axis_index("band"), j, bands)) * share
            row = out_row + base
            left = jnp.where(row >= off_a, prow * live_a, 0.0).astype(BF16)
            right = jnp.where(row < off_b, prow * live_b, 0.0).astype(BF16)
            span = pl.ds(pl.multiple_of(base, B), depth)
            total = jnp.dot(left, filt[0, span, :], preferred_element_type=F32)
            total += jnp.dot(right, filt[1, span, :], preferred_element_type=F32)
            out_ref[k * share : (k + 1) * share, :] = total.astype(out_ref.dtype)
        if j:
            out_ref[visits * share :, 0:LANES] = marks.astype(BF16)
            out_ref[visits * share :, LANES:] = jnp.zeros((B, cols - LANES), BF16)


def pair_kernel(*refs):
    bands = lax.axis_size("band")
    visits = lax.axis_size("visit")
    mark_ref, keep_ref, *got = refs[: bands + 1]
    *outs, own_mark_ref = refs[bands + 1 :]
    share, cols = outs[0].shape
    rowid = iota((B, LANES), 0)
    marks = jnp.where(rowid == 0, mark_ref[...].astype(F32), 0.0)
    for n, ref in enumerate(got):
        other = ref[visits * share :, 0:LANES].astype(F32)
        marks = jnp.where(rowid == n + 1, other[0:1, :], marks)
    own_mark_ref[...] = marks.astype(BF16)
    for k, out_ref in enumerate(outs):
        span = slice(k * share, (k + 1) * share)
        total = keep_ref[span, :]
        for ref in got:
            total += ref[span, :].astype(F32)
        out_ref[...] = total.astype(out_ref.dtype)


def tile_kernel(mark_ref, sci_ref, note_ref, m1_ref, edge_ref, w_ref, *rest):
    rows, cols = sci_ref.shape
    *halves, out_hbm, src, xs, res, big, out, sems = rest
    bands = len(halves)
    blocks = rows // B // bands
    band = lax.axis_index("band")
    for j in range(bands):
        piece = halves[0][...].astype(F32)
        for k in range(1, bands):
            piece = jnp.where(partner(band, k, bands) == j, halves[k][...].astype(F32), piece)
        to_blocks(src, j * blocks, piece)
    off, _ = read_note(note_ref)
    copies = []

    def after(c):
        big[c, 0:B, :] = edge_ref[c, B : 2 * B, :]
        for a in range(1, rows // B - 1):
            big[c, B * a : B * (a + 1), :] = m1_ref[c, PITCH * a : PITCH * a + B, :]
        big[c, rows - B : rows + B, :] = edge_ref[c, 2 * B : 4 * B, :]
        for a in range(1, rows // B):
            big[c, rows + B * a : rows + B * (a + 1), :] = res[c, PITCH * a : PITCH * a + B, :]
        part = slice(c * LANES, (c + 1) * LANES)
        out[:, part] = (sci_ref[:, part].astype(F32) - big[c, pl.ds(off, rows), :]).astype(BF16)
        there = pl.ds(c * LANES, LANES)
        copies.append(pltpu.make_async_copy(out.at[:, there], out_hbm.at[:, there], sems.at[c]))
        copies[-1].start()

    conv_blocks(src, rows // B, w_ref, xs, res, after)
    for copy in copies:
        copy.wait()


def coadd_kernel(*refs):
    *parts, out_ref = refs
    marks, parts = parts[: len(parts) // 2], parts[len(parts) // 2 :]
    share, cols = out_ref.shape
    bands = lax.axis_size("band")
    base = (lax.axis_index("visit") * bands + lax.axis_index("band")) * share
    row = (iota((share, LANES), 0) + base).astype(F32)
    cover = jnp.zeros((share, LANES), F32)
    for ref in marks:
        for m in range(bands):
            mark = ref[...].astype(F32)[m : m + 1, :]
            cover += jnp.where(row >= mark[:, 0:1] * B + mark[:, 1:2], mark[:, 2:3], 0.0)
            cover += jnp.where(row < mark[:, 3:4] * B + mark[:, 4:5], mark[:, 5:6], 0.0)
    scale = lax.rsqrt(jnp.maximum(cover, 1.0))
    for c in range(cols // LANES):
        span = slice(c * LANES, (c + 1) * LANES)
        value = parts[0][:, span]
        for part in parts[1:]:
            value += part[:, span].astype(F32)
        out_ref[:, span] = value * scale


def in_hbm(*arrays):
    return [pltpu.with_memory_space_constraint(x, pltpu.HBM) for x in arrays]


def call(body, shapes, specs, scratch, flops, name, out=VM):
    return pl.pallas_call(
        body,
        out_shape=shapes,
        in_specs=specs,
        out_specs=jax.tree.map(lambda _: out, shapes),
        scratch_shapes=scratch,
        compiler_params=pltpu.CompilerParams(vmem_limit_bytes=LIMIT * 1024 * 1024),
        cost_estimate=pl.CostEstimate(flops=flops, bytes_accessed=1 << 21, transcendentals=0),
        name=name,
    )


def on_device(template, science, offsets, live_flags, bank, basis_index, coeff, psf_profile):
    rows, cols = template.shape
    sharers = lax.axis_size("visit") * lax.axis_size("band")
    share = rows // sharers
    chunks, blocks = cols // LANES, cols // B
    edge = 2 * B
    inner = rows - edge
    sds = jax.ShapeDtypeStruct
    deep = 9 * CH
    depth = -(-(share + edge) // LANES) * LANES
    sci = science[:, 0, :]
    held = in_hbm(template, sci)
    index = jnp.swapaxes(basis_index, 1, 2)
    before = shifted(science, "patch", 1)[:, 0, :]
    bands, visits = lax.axis_size("band"), lax.axis_size("visit")
    psf = psf_profile[None]
    note, msg, head, half, *small = call(
        pack_kernel,
        (
            sds((2 * edge, cols), BF16), sds((edge, cols), BF16), sds((edge, cols), BF16),
            sds((rows // bands, cols), BF16),
            *(sds(x.shape, x.dtype) for x in (bank, index, coeff, psf)),
        ),
        [HBM] * 7,
        [pltpu.SMEM((1, 1), jnp.int32), pltpu.SMEM((1, 1), jnp.int32), pltpu.SemaphoreType.DMA((10,))],
        1 << 20, "pack",
    )(offsets, live_flags, held[0], *in_hbm(bank, index, coeff, psf))
    half = shifted(half, "patch", -1)
    panels = lax.axis_size("patch")
    msg = lax.ppermute(msg, "patch", [(i, (i + 1) % panels) for i in range(panels)])
    head = shifted(head, "patch", -1)
    count = rows // B
    conv_scratch = [
        pltpu.VMEM((chunks, count * PITCH, LANES), F32),
        pltpu.VMEM((3, blocks + 2, count, CH), BF16),
        pltpu.VMEM((chunks, count * PITCH, LANES), F32),
    ]
    conv_flops = 2 * rows * cols * deep
    sky_scratch = [pltpu.VMEM((chunks, 2 * rows + B, LANES), F32), pltpu.VMEM((inner, cols), BF16)]
    sides = (sds((chunks, 2 * edge, LANES), F32), sds((inner, cols), BF16))
    w, pcol, prow, tile, m1, edge_a, filt_a = call(
        first_kernel,
        (
            sds((deep, CH), BF16), sds((cols, cols), BF16), sds((share, depth), BF16),
            sds((rows, cols), BF16), sds((chunks, count * PITCH, LANES), F32),
        ) + sides,
        [VM, HBM, HBM] + [VM] * 4,
        [pltpu.VMEM((rows, cols), BF16), pltpu.SemaphoreType.DMA((2,))] + conv_scratch[:2] + sky_scratch,
        conv_flops, "first",
    )(note, *held, *small)
    whole = visits * share
    keep, *sent, mark, m_edge = call(
        join_kernel,
        (sds((whole, cols), F32),) + (sds((whole + B, cols), BF16),) * (bands - 1)
        + (sds((B, LANES), BF16), sds((chunks, 2 * edge, LANES), F32)),
        [VM] * 10,
        [
            pltpu.VMEM((chunks, 8 * PITCH, LANES), F32),
            pltpu.VMEM((3, blocks + 2, 8, CH), F32),
            pltpu.VMEM((chunks, 8 * PITCH, LANES), F32),
            pltpu.VMEM((4 * edge, cols), BF16),
            pltpu.VMEM((2, rows - share + depth, cols), BF16),
        ] + sky_scratch + [pltpu.VMEM((chunks, 2 * edge, LANES), F32), pltpu.VMEM((inner, cols), BF16)],
        1 << 34, "join",
    )(note, msg, head, before, m1, w, pcol, prow, edge_a, filt_a)
    got = [swapped(part, "band", k + 1) for k, part in enumerate(sent)]
    halves = [half] + [swapped(half, "band", k) for k in range(1, bands)]
    own, *sent, mark = call(
        pair_kernel,
        (sds((share, cols), F32),) + (sds((share, cols), BF16),) * (visits - 1) + (sds((B, LANES), BF16),),
        [VM] * (1 + bands), [], 1 << 20, "pair",
    )(mark, keep, *got)
    got = [swapped(part, "visit", k + 1) for k, part in enumerate(sent)]
    marks = [mark] + [swapped(mark, "visit", k) for k in range(1, visits)]
    difference = call(
        tile_kernel, sds((rows, cols), BF16), [VM] * (6 + bands),
        conv_scratch + [
            pltpu.VMEM((chunks, 2 * rows, LANES), F32), pltpu.VMEM((rows, cols), BF16),
            pltpu.SemaphoreType.DMA((chunks,)),
        ],
        conv_flops, "tile", HBM,
    )(mark, tile, note, m1, m_edge, w, *halves)
    detection = call(
        coadd_kernel, sds((share, cols), F32), [VM] * (2 * visits), [], 1 << 20, "coadd"
    )(*marks, own, *got)
    return (difference[:, None, :], detection)


def solution(mesh):
    return jax.shard_map(
        on_device,
        mesh=mesh,
        in_specs=(
            P(("group", "patch"), None),
            P(("group", "patch"), ("visit", "band"), None),
            P(("group", "patch"), ("visit", "band")),
            P(("group", "patch"), ("visit", "band")),
            P(),
            P(("group", "visit", "band"), None, None),
            P(("group", "visit", "band"), None),
            P(),
        ),
        out_specs=(
            P(("group", "patch"), ("visit", "band"), None),
            P(("group", "patch", "visit", "band"), None),
        ),
        check_vma=False,
    )
```

```python
import functools

import jax
import jax.numpy as jnp
from jax import lax
from jax.experimental import pallas as pl
from jax.experimental.pallas import tpu as pltpu
from jax.sharding import PartitionSpec as P

B = 16
CH = B * B
LANES = 128
GROUPS = LANES // B
PITCH = B + 1
F32 = jnp.float32
BF16 = jnp.bfloat16


def shifted(shard, axis, by):
    devices = lax.axis_size(axis)
    pairs = [(i, i + by) for i in range(devices) if 0 <= i + by < devices]
    return lax.ppermute(shard, axis, pairs)


def partner(me, k, count):
    return me ^ k if count & (count - 1) == 0 else (me + k) % count


def swapped(shard, axis, k):
    devices = lax.axis_size(axis)
    return lax.ppermute(shard, axis, [(i, partner(i, k, devices)) for i in range(devices)])


def iota(shape, dim):
    return lax.broadcasted_iota(jnp.int32, shape, dim)


LIMIT = 14
VM = pl.BlockSpec(memory_space=pltpu.VMEM)
HBM = pl.BlockSpec(memory_space=pltpu.HBM)


def group_transpose(parts):
    parts = list(parts)
    group = iota(parts[0].shape, 1) // B
    for step in (1, 2, 4):
        low = (group & step) == 0
        for m in range(GROUPS):
            if m & step:
                continue
            x, y = parts[m], parts[m + step]
            parts[m] = jnp.where(low, x, pltpu.roll(y, step * B, 1))
            parts[m + step] = jnp.where(low, pltpu.roll(x, LANES - step * B, 1), y)
    return parts


def to_blocks(dst, block, value):
    value = value.astype(F32)
    for a in range(value.shape[0] // B):
        at = (block + a) * PITCH
        for c in range(dst.shape[0]):
            dst[c, at : at + B, :] = value[a * B : (a + 1) * B, c * LANES : (c + 1) * LANES]


def conv_blocks(src, count, w_ref, xs, dst, after=None):
    chunks = src.shape[0]
    blocks = chunks * GROUPS

    def load(c):
        for h in range(2):
            rows = [src[c, pl.ds(GROUPS * h + i, count, stride=PITCH), :] for i in range(GROUPS)]
            part = slice(h * LANES, (h + 1) * LANES)
            for g, here in enumerate(group_transpose(rows)):
                at = 1 + c * GROUPS + g
                xs[0, at, :, part] = pltpu.roll(here, 1, 0).astype(xs.dtype)
                xs[1, at, :, part] = here.astype(xs.dtype)
                xs[2, at, :, part] = pltpu.roll(here, count - 1, 0).astype(xs.dtype)

    def solve(c):
        b = c * GROUPS
        pieces = [
            xs[qr, b + qc : b + qc + GROUPS].reshape(GROUPS * count, CH).astype(BF16)
            for qr in range(3)
            for qc in range(3)
        ]
        out = jnp.dot(jnp.concatenate(pieces, axis=1), w_ref[...], preferred_element_type=F32)
        for h in range(2):
            part = slice(h * LANES, (h + 1) * LANES)
            rows = group_transpose([out[g * count : (g + 1) * count, part] for g in range(GROUPS)])
            for i in range(GROUPS):
                dst[c, pl.ds(GROUPS * h + i, count, stride=PITCH), :] = rows[i]

    for q in range(3):
        xs[q, 0] = jnp.zeros((count, CH), xs.dtype)
        xs[q, blocks + 1] = jnp.zeros((count, CH), xs.dtype)
    load(0)
    for c in range(chunks):
        if c + 1 < chunks:
            load(c + 1)
        solve(c)
        if after is not None:
            after(c)


def slanted(row, count):
    value = jnp.broadcast_to(row, (count, row.shape[1]))
    index = iota(value.shape, 0)
    bit = 1
    while bit < count:
        value = jnp.where((index & bit) != 0, pltpu.roll(value, bit, 1), value)
        bit *= 2
    return value


def column(row):
    size = row.shape[1]
    diag = iota((size, size), 0) == iota((size, size), 1)
    return jnp.sum(jnp.where(diag, row, jnp.zeros_like(row)), axis=1, keepdims=True)


def pack_kernel(
    off_hbm, live_hbm, t_hbm, bank_hbm, index_hbm, coeff_hbm, psf_hbm,
    note_ref, msg_ref, head_ref, half_ref, bank_ref, index_ref, coeff_ref, psf_ref, off_ref, live_ref, sems,
):
    rows, cols = t_hbm.shape
    edge = 2 * B
    piece = half_ref.shape[0]
    begin = pl.multiple_of(lax.axis_index("band") * piece, B)
    copies = [
        pltpu.make_async_copy(a, b, sems.at[n])
        for n, (a, b) in enumerate((
            (off_hbm, off_ref), (live_hbm, live_ref),
            (t_hbm.at[pl.ds(rows - edge, edge)], note_ref.at[pl.ds(0, edge)]),
            (t_hbm.at[pl.ds(0, edge)], note_ref.at[pl.ds(edge, edge)]),
            (t_hbm.at[pl.ds(0, edge)], head_ref),
            (t_hbm.at[pl.ds(begin, piece)], half_ref),
            (bank_hbm, bank_ref), (index_hbm, index_ref), (coeff_hbm, coeff_ref), (psf_hbm, psf_ref),
        ))
    ]
    for copy in copies:
        copy.start()
    for copy in copies:
        copy.wait()
    lane = iota((1, cols), 1)
    off = off_ref[0, 0]
    note = jnp.where(lane == 0, off // B, jnp.where(lane == 1, off % B, live_ref[0, 0])).astype(F32)
    block = note_ref[0:B, :].astype(F32)
    note_ref[0:B, :] = jnp.where(iota((B, cols), 0) == 0, note, block).astype(BF16)
    msg_ref[...] = note_ref[0:edge, :]


def first_kernel(
    note_ref, t_hbm, sci_hbm, bank_ref, index_ref, coeff_ref, psf_ref,
    w_ref, pcol_ref, prow_ref, sci_ref, m_ref, edge_ref, filt_ref,
    t_ref, sems, src, xs, sci, diff,
):
    copies = [
        pltpu.make_async_copy(t_hbm, t_ref, sems.at[0]), pltpu.make_async_copy(sci_hbm, sci_ref, sems.at[1])
    ]
    for copy in copies:
        copy.start()
    profs, taps = bank_ref.shape
    half = taps // 2
    delta = B - half
    bank = bank_ref[...]
    index = index_ref[0].astype(F32)
    labels = iota((index.shape[1], profs), 1).astype(F32)
    pick_row = (column(index[0:1]) == labels).astype(F32).astype(BF16)
    pick_col = (column(index[1:2]) == labels).astype(F32).astype(BF16)
    weight = column(coeff_ref[...])
    rowprof = (weight * jnp.dot(pick_row, bank, preferred_element_type=F32)).astype(BF16)
    colprof = jnp.dot(pick_col, bank, preferred_element_type=F32).astype(BF16)
    span = 3 * B
    total = 4 * B * B
    place = (iota((span, taps), 0) - delta == iota((span, taps), 1)).astype(F32).astype(BF16)
    col_t = lax.dot_general(place, colprof, (((1,), (1,)), ((), ())), preferred_element_type=F32).astype(BF16)
    spread = (span - 1 - iota((taps, total), 1) // B - delta == iota((taps, total), 0)).astype(F32).astype(BF16)
    row_rep = jnp.dot(rowprof, spread, preferred_element_type=F32).astype(BF16)
    z = jnp.dot(col_t, row_rep, preferred_element_type=F32)
    lane = iota((span, total), 1)
    for bit in (1, 2, 4, 8):
        z = jnp.where((lane & bit) != 0, pltpu.roll(z, bit, 0), z)
    z = z.astype(BF16)
    for phase in range(GROUPS):
        zp = z if phase == 0 else pltpu.roll(z, total - phase * B, 1)
        for g in range(span):
            start = span - 1 - g
            if start % GROUPS != phase:
                continue
            at = (start // GROUPS) * LANES
            for qc in range(3):
                row = (g // B) * 3 * CH + qc * CH + (g % B) * B
                w_ref[row : row + B, :] = zp[qc * B : (qc + 1) * B, at : at + CH]
    size = pcol_ref.shape[0]
    lanes = iota((taps, 3 * LANES), 1)
    mirror = (lanes - LANES + iota(lanes.shape, 0) == half).astype(F32).astype(BF16)
    bands = slanted(jnp.dot(psf_ref[...], mirror, preferred_element_type=F32), LANES)
    bands = {1 - n: bands[:, n * LANES : (n + 1) * LANES].astype(BF16) for n in range(3)}
    for i in range(size // LANES):
        for j in range(size // LANES):
            block = bands.get(i - j, jnp.zeros((LANES, LANES), BF16))
            pcol_ref[i * LANES : (i + 1) * LANES, j * LANES : (j + 1) * LANES] = block
    share, depth = prow_ref.shape
    lanes = iota((taps, depth), 1)
    ahead = (lanes - iota(lanes.shape, 0) == delta).astype(F32).astype(BF16)
    prow_ref[...] = slanted(jnp.dot(psf_ref[...], ahead, preferred_element_type=F32), share).astype(BF16)
    copies[0].wait()
    edge = 2 * B
    rows, cols = t_ref.shape
    off, _ = read_note(note_ref)
    to_blocks(src, 0, t_ref[...])
    conv_blocks(src, rows // B, w_ref, xs, m_ref)
    copies[1].wait()
    to_chunks(sci, rows, sci_ref[...])
    filter_inner(sci, rows - B - off, off, off + rows, m_ref, pcol_ref, edge_ref, filt_ref, diff)


def to_chunks(dst, dst_row, value):
    value = value.astype(F32)
    rows = value.shape[0]
    for c in range(dst.shape[0]):
        dst[c, dst_row : dst_row + rows, :] = value[:, c * LANES : (c + 1) * LANES]


def tile_diff(sky, m, base, first, last):
    row = iota(m.shape, 0) + (base - B)
    return jnp.where((row >= first) & (row < last), sky - m, 0.0).astype(BF16)


def filter_inner(sci, start, first, last, m_ref, pcol_ref, edge_ref, filt_ref, diff):
    chunks, blocks = m_ref.shape[0], m_ref.shape[1] // PITCH
    rows, edge = blocks * B, 2 * B
    for c in range(chunks):
        part = slice(c * LANES, (c + 1) * LANES)
        sky = sci[c, pl.ds(start, rows + edge), :]
        inner = jnp.concatenate([m_ref[c, PITCH * a : PITCH * a + B, :] for a in range(1, blocks - 1)], axis=0)
        edge_ref[c, 0:edge, :] = sky[0:edge]
        edge_ref[c, edge:, :] = sky[rows:]
        diff[:, part] = tile_diff(sky[edge:rows], inner, edge, first, last)
    filt_ref[...] = jnp.dot(diff[...], pcol_ref[...], preferred_element_type=F32).astype(BF16)


def read_note(msg_ref):
    note = msg_ref[0:B, 0:LANES].astype(F32)
    return (note[0, 0] * B + note[0, 1]).astype(jnp.int32), note[0, 2]


def read_before(msg_ref):
    valid = lax.axis_index("patch") > 0
    off, live = read_note(msg_ref)
    return jnp.where(valid, off, 0), jnp.where(valid, live, 0.0), valid


def join_kernel(
    note_ref, msg_ref, head_ref, sci_ref, m1_ref, w_ref, pcol_ref, prow_ref, edge_a, filt_a,
    *rest,
):
    *outs, mark_ref, m_ref, src, xs, strip, diff, filt, sci, inner, edge_b, filt_b = rest
    edge = 2 * B
    rows, cols = filt_a.shape[0] + edge, filt_a.shape[1]
    off_b, live_b, valid = read_before(msg_ref)
    to_chunks(sci, 0, sci_ref[...])
    to_blocks(src, 0, jnp.where(valid, msg_ref[...].astype(F32), 0.0))
    to_blocks(src, 2, note_ref[edge:, :])
    to_blocks(src, 4, note_ref[0:edge, :])
    to_blocks(src, 6, head_ref[...])
    filter_inner(sci, rows - B - off_b, off_b - rows, off_b, m1_ref, pcol_ref, edge_b, filt_b, inner)
    conv_blocks(src, 8, w_ref, xs, strip)
    for n, a in enumerate((1, 2, 5, 6)):
        m_ref[:, B * n : B * (n + 1), :] = strip[:, PITCH * a : PITCH * a + B, :]
    off_a, live_a = read_note(note_ref)
    for s, (side, first, last) in enumerate(((edge_a, off_a, off_a + rows), (edge_b, off_b - rows, off_b))):
        for c in range(cols // LANES):
            part = slice(c * LANES, (c + 1) * LANES)
            for k, base in enumerate((0, rows)):
                span = slice(k * edge, (k + 1) * edge)
                at = (2 * s + k) * edge
                diff[at : at + edge, part] = tile_diff(side[c, span, :], m_ref[c, span, :], base, first, last)
    sides = jnp.dot(diff[...], pcol_ref[...], preferred_element_type=F32).astype(BF16)
    for s, inner in enumerate((filt_a, filt_b)):
        filt[s, 0:edge, :] = sides[2 * s * edge : (2 * s + 1) * edge]
        filt[s, edge:rows, :] = inner[...]
        filt[s, rows : rows + edge, :] = sides[(2 * s + 1) * edge : (2 * s + 2) * edge]
        filt[s, rows + edge :, :] = jnp.zeros((filt.shape[1] - rows - edge, cols), BF16)
    share, depth = prow_ref.shape
    prow = prow_ref[...].astype(F32)
    out_row = iota((share, depth), 0)
    lane = iota((B, cols), 1)
    visits, bands = lax.axis_size("visit"), lax.axis_size("band")
    hi, lo = off_b // B, off_b % B
    marks = note_ref[0:B, 0:LANES].astype(F32)
    marks = jnp.where(iota(marks.shape, 1) == 3, hi.astype(F32), marks)
    marks = jnp.where(iota(marks.shape, 1) == 4, lo.astype(F32), marks)
    marks = jnp.where(iota(marks.shape, 1) == 5, live_b, marks)
    mark_ref[...] = marks.astype(BF16)
    for j, out_ref in enumerate(outs):
        for k in range(visits):
            to_visit = partner(lax.axis_index("visit"), k, visits)
            base = (to_visit * bands + partner(lax.axis_index("band"), j, bands)) * share
            row = out_row + base
            left = jnp.where(row >= off_a, prow * live_a, 0.0).astype(BF16)
            right = jnp.where(row < off_b, prow * live_b, 0.0).astype(BF16)
            span = pl.ds(pl.multiple_of(base, B), depth)
            total = jnp.dot(left, filt[0, span, :], preferred_element_type=F32)
            total += jnp.dot(right, filt[1, span, :], preferred_element_type=F32)
            out_ref[k * share : (k + 1) * share, :] = total.astype(out_ref.dtype)
        if j:
            out_ref[visits * share :, 0:LANES] = marks.astype(BF16)
            out_ref[visits * share :, LANES:] = jnp.zeros((B, cols - LANES), BF16)


def pair_kernel(*refs):
    bands = lax.axis_size("band")
    visits = lax.axis_size("visit")
    mark_ref, keep_ref, *got = refs[: bands + 1]
    *outs, own_mark_ref = refs[bands + 1 :]
    share, cols = outs[0].shape
    rowid = iota((B, LANES), 0)
    marks = jnp.where(rowid == 0, mark_ref[...].astype(F32), 0.0)
    for n, ref in enumerate(got):
        other = ref[visits * share :, 0:LANES].astype(F32)
        marks = jnp.where(rowid == n + 1, other[0:1, :], marks)
    own_mark_ref[...] = marks.astype(BF16)
    for k, out_ref in enumerate(outs):
        span = slice(k * share, (k + 1) * share)
        total = keep_ref[span, :]
        for ref in got:
            total += ref[span, :].astype(F32)
        out_ref[0:share, :] = total.astype(out_ref.dtype)
        if k:
            out_ref[share:, 0:LANES] = marks.astype(BF16)
            out_ref[share:, LANES:] = jnp.zeros((B, cols - LANES), BF16)


def tile_kernel(mark_ref, sci_ref, note_ref, m1_ref, edge_ref, w_ref, *rest):
    rows, cols = sci_ref.shape
    *halves, out_hbm, src, xs, res, big, out, sems = rest
    bands = len(halves)
    blocks = rows // B // bands
    band = lax.axis_index("band")
    for j in range(bands):
        piece = halves[0][...].astype(F32)
        for k in range(1, bands):
            piece = jnp.where(partner(band, k, bands) == j, halves[k][...].astype(F32), piece)
        to_blocks(src, j * blocks, piece)
    off, _ = read_note(note_ref)
    copies = []

    def after(c):
        big[c, 0:B, :] = edge_ref[c, B : 2 * B, :]
        for a in range(1, rows // B - 1):
            big[c, B * a : B * (a + 1), :] = m1_ref[c, PITCH * a : PITCH * a + B, :]
        big[c, rows - B : rows + B, :] = edge_ref[c, 2 * B : 4 * B, :]
        for a in range(1, rows // B):
            big[c, rows + B * a : rows + B * (a + 1), :] = res[c, PITCH * a : PITCH * a + B, :]
        part = slice(c * LANES, (c + 1) * LANES)
        out[:, part] = (sci_ref[:, part].astype(F32) - big[c, pl.ds(off, rows), :]).astype(BF16)
        there = pl.ds(c * LANES, LANES)
        copies.append(pltpu.make_async_copy(out.at[:, there], out_hbm.at[:, there], sems.at[c]))
        copies[-1].start()

    conv_blocks(src, rows // B, w_ref, xs, res, after)
    for copy in copies:
        copy.wait()


def coadd_kernel(mark_ref, *refs):
    *parts, out_ref = refs
    share, cols = out_ref.shape
    bands = lax.axis_size("band")
    base = (lax.axis_index("visit") * bands + lax.axis_index("band")) * share
    row = (iota((share, LANES), 0) + base).astype(F32)
    cover = jnp.zeros((share, LANES), F32)
    for n, part in enumerate(parts):
        marks = (part[share : share + B, 0:LANES] if n else mark_ref[...]).astype(F32)
        for m in range(bands):
            mark = marks[m : m + 1, :]
            cover += jnp.where(row >= mark[:, 0:1] * B + mark[:, 1:2], mark[:, 2:3], 0.0)
            cover += jnp.where(row < mark[:, 3:4] * B + mark[:, 4:5], mark[:, 5:6], 0.0)
    scale = lax.rsqrt(jnp.maximum(cover, 1.0))
    for c in range(cols // LANES):
        span = slice(c * LANES, (c + 1) * LANES)
        value = parts[0][:, span]
        for part in parts[1:]:
            value += part[0:share, span].astype(F32)
        out_ref[:, span] = value * scale


def in_hbm(*arrays):
    return [pltpu.with_memory_space_constraint(x, pltpu.HBM) for x in arrays]


def call(body, shapes, specs, scratch, flops, name, out=VM):
    return pl.pallas_call(
        body,
        out_shape=shapes,
        in_specs=specs,
        out_specs=jax.tree.map(lambda _: out, shapes),
        scratch_shapes=scratch,
        compiler_params=pltpu.CompilerParams(vmem_limit_bytes=LIMIT * 1024 * 1024),
        cost_estimate=pl.CostEstimate(flops=flops, bytes_accessed=1 << 21, transcendentals=0),
        name=name,
    )


def on_device(template, science, offsets, live_flags, bank, basis_index, coeff, psf_profile):
    rows, cols = template.shape
    sharers = lax.axis_size("visit") * lax.axis_size("band")
    share = rows // sharers
    chunks, blocks = cols // LANES, cols // B
    edge = 2 * B
    inner = rows - edge
    sds = jax.ShapeDtypeStruct
    deep = 9 * CH
    depth = -(-(share + edge) // LANES) * LANES
    sci = science[:, 0, :]
    held = in_hbm(template, sci)
    index = jnp.swapaxes(basis_index, 1, 2)
    before = shifted(science, "patch", 1)[:, 0, :]
    bands, visits = lax.axis_size("band"), lax.axis_size("visit")
    psf = psf_profile[None]
    note, msg, head, half, *small = call(
        pack_kernel,
        (
            sds((2 * edge, cols), BF16), sds((edge, cols), BF16), sds((edge, cols), BF16),
            sds((rows // bands, cols), BF16),
            *(sds(x.shape, x.dtype) for x in (bank, index, coeff, psf)),
        ),
        [HBM] * 7,
        [pltpu.SMEM((1, 1), jnp.int32), pltpu.SMEM((1, 1), jnp.int32), pltpu.SemaphoreType.DMA((10,))],
        1 << 20, "pack",
    )(offsets, live_flags, held[0], *in_hbm(bank, index, coeff, psf))
    half = shifted(half, "patch", -1)
    panels = lax.axis_size("patch")
    msg = lax.ppermute(msg, "patch", [(i, (i + 1) % panels) for i in range(panels)])
    head = shifted(head, "patch", -1)
    count = rows // B
    conv_scratch = [
        pltpu.VMEM((chunks, count * PITCH, LANES), F32),
        pltpu.VMEM((3, blocks + 2, count, CH), BF16),
        pltpu.VMEM((chunks, count * PITCH, LANES), F32),
    ]
    conv_flops = 2 * rows * cols * deep
    sky_scratch = [pltpu.VMEM((chunks, 2 * rows + B, LANES), F32), pltpu.VMEM((inner, cols), BF16)]
    sides = (sds((chunks, 2 * edge, LANES), F32), sds((inner, cols), BF16))
    w, pcol, prow, tile, m1, edge_a, filt_a = call(
        first_kernel,
        (
            sds((deep, CH), BF16), sds((cols, cols), BF16), sds((share, depth), BF16),
            sds((rows, cols), BF16), sds((chunks, count * PITCH, LANES), F32),
        ) + sides,
        [VM, HBM, HBM] + [VM] * 4,
        [pltpu.VMEM((rows, cols), BF16), pltpu.SemaphoreType.DMA((2,))] + conv_scratch[:2] + sky_scratch,
        conv_flops, "first",
    )(note, *held, *small)
    whole = visits * share
    keep, *sent, mark, m_edge = call(
        join_kernel,
        (sds((whole, cols), F32),) + (sds((whole + B, cols), BF16),) * (bands - 1)
        + (sds((B, LANES), BF16), sds((chunks, 2 * edge, LANES), F32)),
        [VM] * 10,
        [
            pltpu.VMEM((chunks, 8 * PITCH, LANES), F32),
            pltpu.VMEM((3, blocks + 2, 8, CH), F32),
            pltpu.VMEM((chunks, 8 * PITCH, LANES), F32),
            pltpu.VMEM((4 * edge, cols), BF16),
            pltpu.VMEM((2, rows - share + depth, cols), BF16),
        ] + sky_scratch + [pltpu.VMEM((chunks, 2 * edge, LANES), F32), pltpu.VMEM((inner, cols), BF16)],
        1 << 34, "join",
    )(note, msg, head, before, m1, w, pcol, prow, edge_a, filt_a)
    got = [swapped(part, "band", k + 1) for k, part in enumerate(sent)]
    halves = [half] + [swapped(half, "band", k) for k in range(1, bands)]
    own, *sent, mark = call(
        pair_kernel,
        (sds((share, cols), F32),) + (sds((share + B, cols), BF16),) * (visits - 1) + (sds((B, LANES), BF16),),
        [VM] * (1 + bands), [], 1 << 20, "pair",
    )(mark, keep, *got)
    got = [swapped(part, "visit", k + 1) for k, part in enumerate(sent)]
    difference = call(
        tile_kernel, sds((rows, cols), BF16), [VM] * (6 + bands),
        conv_scratch + [
            pltpu.VMEM((chunks, 2 * rows, LANES), F32), pltpu.VMEM((rows, cols), BF16),
            pltpu.SemaphoreType.DMA((chunks,)),
        ],
        conv_flops, "tile", HBM,
    )(mark, tile, note, m1, m_edge, w, *halves)
    detection = call(
        coadd_kernel, sds((share, cols), F32), [VM] * (1 + visits), [], 1 << 20, "coadd"
    )(mark, own, *got)
    return (difference[:, None, :], detection)


def solution(mesh):
    return jax.shard_map(
        on_device,
        mesh=mesh,
        in_specs=(
            P(("group", "patch"), None),
            P(("group", "patch"), ("visit", "band"), None),
            P(("group", "patch"), ("visit", "band")),
            P(("group", "patch"), ("visit", "band")),
            P(),
            P(("group", "visit", "band"), None, None),
            P(("group", "visit", "band"), None),
            P(),
        ),
        out_specs=(
            P(("group", "patch"), ("visit", "band"), None),
            P(("group", "patch", "visit", "band"), None),
        ),
        check_vma=False,
    )
```

```python
import functools

import jax
import jax.numpy as jnp
from jax import lax
from jax.experimental import pallas as pl
from jax.experimental.pallas import tpu as pltpu
from jax.sharding import PartitionSpec as P

B = 16
CH = B * B
LANES = 128
GROUPS = LANES // B
PITCH = B + 1
F32 = jnp.float32
BF16 = jnp.bfloat16


def shifted(shard, axis, by):
    devices = lax.axis_size(axis)
    pairs = [(i, i + by) for i in range(devices) if 0 <= i + by < devices]
    return lax.ppermute(shard, axis, pairs)


def partner(me, k, count):
    return me ^ k if count & (count - 1) == 0 else (me + k) % count


def swapped(shard, axis, k):
    devices = lax.axis_size(axis)
    return lax.ppermute(shard, axis, [(i, partner(i, k, devices)) for i in range(devices)])


def iota(shape, dim):
    return lax.broadcasted_iota(jnp.int32, shape, dim)


LIMIT = 14
VM = pl.BlockSpec(memory_space=pltpu.VMEM)
HBM = pl.BlockSpec(memory_space=pltpu.HBM)


def group_transpose(parts):
    parts = list(parts)
    group = iota(parts[0].shape, 1) // B
    for step in (1, 2, 4):
        low = (group & step) == 0
        for m in range(GROUPS):
            if m & step:
                continue
            x, y = parts[m], parts[m + step]
            parts[m] = jnp.where(low, x, pltpu.roll(y, step * B, 1))
            parts[m + step] = jnp.where(low, pltpu.roll(x, LANES - step * B, 1), y)
    return parts


def to_blocks(dst, block, value):
    value = value.astype(F32)
    for a in range(value.shape[0] // B):
        at = (block + a) * PITCH
        for c in range(dst.shape[0]):
            dst[c, at : at + B, :] = value[a * B : (a + 1) * B, c * LANES : (c + 1) * LANES]


def conv_blocks(src, count, w_ref, xs, dst, after=None):
    chunks = src.shape[0]
    blocks = chunks * GROUPS

    def load(c):
        for h in range(2):
            rows = [src[c, pl.ds(GROUPS * h + i, count, stride=PITCH), :] for i in range(GROUPS)]
            part = slice(h * LANES, (h + 1) * LANES)
            for g, here in enumerate(group_transpose(rows)):
                at = 1 + c * GROUPS + g
                xs[0, at, :, part] = pltpu.roll(here, 1, 0).astype(xs.dtype)
                xs[1, at, :, part] = here.astype(xs.dtype)
                xs[2, at, :, part] = pltpu.roll(here, count - 1, 0).astype(xs.dtype)

    def solve(c):
        b = c * GROUPS
        pieces = [
            xs[qr, b + qc : b + qc + GROUPS].reshape(GROUPS * count, CH).astype(BF16)
            for qr in range(3)
            for qc in range(3)
        ]
        out = jnp.dot(jnp.concatenate(pieces, axis=1), w_ref[...], preferred_element_type=F32)
        for h in range(2):
            part = slice(h * LANES, (h + 1) * LANES)
            rows = group_transpose([out[g * count : (g + 1) * count, part] for g in range(GROUPS)])
            for i in range(GROUPS):
                dst[c, pl.ds(GROUPS * h + i, count, stride=PITCH), :] = rows[i]

    for q in range(3):
        xs[q, 0] = jnp.zeros((count, CH), xs.dtype)
        xs[q, blocks + 1] = jnp.zeros((count, CH), xs.dtype)
    load(0)
    for c in range(chunks):
        if c + 1 < chunks:
            load(c + 1)
        solve(c)
        if after is not None:
            after(c)


def slanted(row, count):
    value = jnp.broadcast_to(row, (count, row.shape[1]))
    index = iota(value.shape, 0)
    bit = 1
    while bit < count:
        value = jnp.where((index & bit) != 0, pltpu.roll(value, bit, 1), value)
        bit *= 2
    return value


def column(row):
    size = row.shape[1]
    diag = iota((size, size), 0) == iota((size, size), 1)
    return jnp.sum(jnp.where(diag, row, jnp.zeros_like(row)), axis=1, keepdims=True)


def pack_kernel(
    off_hbm, live_hbm, t_hbm, bank_hbm, index_hbm, coeff_hbm, psf_hbm,
    note_ref, msg_ref, head_ref, half_ref, bank_ref, index_ref, coeff_ref, psf_ref, off_ref, live_ref, sems,
):
    rows, cols = t_hbm.shape
    edge = 2 * B
    piece = half_ref.shape[0]
    begin = pl.multiple_of(lax.axis_index("band") * piece, B)
    copies = [
        pltpu.make_async_copy(a, b, sems.at[n])
        for n, (a, b) in enumerate((
            (off_hbm, off_ref), (live_hbm, live_ref),
            (t_hbm.at[pl.ds(rows - edge, edge)], note_ref.at[pl.ds(0, edge)]),
            (t_hbm.at[pl.ds(0, edge)], note_ref.at[pl.ds(edge, edge)]),
            (t_hbm.at[pl.ds(0, edge)], head_ref),
            (t_hbm.at[pl.ds(begin, piece)], half_ref),
            (bank_hbm, bank_ref), (index_hbm, index_ref), (coeff_hbm, coeff_ref), (psf_hbm, psf_ref),
        ))
    ]
    for copy in copies:
        copy.start()
    for copy in copies:
        copy.wait()
    lane = iota((1, cols), 1)
    off = off_ref[0, 0]
    note = jnp.where(lane == 0, off // B, jnp.where(lane == 1, off % B, live_ref[0, 0])).astype(F32)
    block = note_ref[0:B, :].astype(F32)
    note_ref[0:B, :] = jnp.where(iota((B, cols), 0) == 0, note, block).astype(BF16)
    msg_ref[...] = note_ref[0:edge, :]


def first_kernel(
    note_ref, t_hbm, sci_hbm, bank_ref, index_ref, coeff_ref, psf_ref,
    w_ref, pcol_ref, prow_ref, sci_ref, m_ref, edge_ref, filt_ref,
    t_ref, sems, src, xs, sci, diff,
):
    copies = [
        pltpu.make_async_copy(t_hbm, t_ref, sems.at[0]), pltpu.make_async_copy(sci_hbm, sci_ref, sems.at[1])
    ]
    for copy in copies:
        copy.start()
    profs, taps = bank_ref.shape
    half = taps // 2
    delta = B - half
    bank = bank_ref[...]
    index = index_ref[0].astype(F32)
    labels = iota((index.shape[1], profs), 1).astype(F32)
    pick_row = (column(index[0:1]) == labels).astype(F32).astype(BF16)
    pick_col = (column(index[1:2]) == labels).astype(F32).astype(BF16)
    weight = column(coeff_ref[...])
    rowprof = (weight * jnp.dot(pick_row, bank, preferred_element_type=F32)).astype(BF16)
    colprof = jnp.dot(pick_col, bank, preferred_element_type=F32).astype(BF16)
    span = 3 * B
    total = 4 * B * B
    place = (iota((span, taps), 0) - delta == iota((span, taps), 1)).astype(F32).astype(BF16)
    col_t = lax.dot_general(place, colprof, (((1,), (1,)), ((), ())), preferred_element_type=F32).astype(BF16)
    spread = (span - 1 - iota((taps, total), 1) // B - delta == iota((taps, total), 0)).astype(F32).astype(BF16)
    row_rep = jnp.dot(rowprof, spread, preferred_element_type=F32).astype(BF16)
    z = jnp.dot(col_t, row_rep, preferred_element_type=F32)
    lane = iota((span, total), 1)
    for bit in (1, 2, 4, 8):
        z = jnp.where((lane & bit) != 0, pltpu.roll(z, bit, 0), z)
    z = z.astype(BF16)
    for phase in range(GROUPS):
        zp = z if phase == 0 else pltpu.roll(z, total - phase * B, 1)
        for g in range(span):
            start = span - 1 - g
            if start % GROUPS != phase:
                continue
            at = (start // GROUPS) * LANES
            for qc in range(3):
                row = (g // B) * 3 * CH + qc * CH + (g % B) * B
                w_ref[row : row + B, :] = zp[qc * B : (qc + 1) * B, at : at + CH]
    size = pcol_ref.shape[0]
    lanes = iota((taps, 3 * LANES), 1)
    mirror = (lanes - LANES + iota(lanes.shape, 0) == half).astype(F32).astype(BF16)
    bands = slanted(jnp.dot(psf_ref[...], mirror, preferred_element_type=F32), LANES)
    bands = {1 - n: bands[:, n * LANES : (n + 1) * LANES].astype(BF16) for n in range(3)}
    for i in range(size // LANES):
        for j in range(size // LANES):
            block = bands.get(i - j, jnp.zeros((LANES, LANES), BF16))
            pcol_ref[i * LANES : (i + 1) * LANES, j * LANES : (j + 1) * LANES] = block
    share, depth = prow_ref.shape
    lanes = iota((taps, depth), 1)
    ahead = (lanes - iota(lanes.shape, 0) == delta).astype(F32).astype(BF16)
    prow_ref[...] = slanted(jnp.dot(psf_ref[...], ahead, preferred_element_type=F32), share).astype(BF16)
    copies[0].wait()
    edge = 2 * B
    rows, cols = t_ref.shape
    off, _ = read_note(note_ref)
    to_blocks(src, 0, t_ref[...])
    conv_blocks(src, rows // B, w_ref, xs, m_ref)
    copies[1].wait()
    to_chunks(sci, rows, sci_ref[...])
    filter_inner(sci, rows - B - off, off, off + rows, m_ref, pcol_ref, edge_ref, filt_ref, diff)


def to_chunks(dst, dst_row, value):
    value = value.astype(F32)
    rows = value.shape[0]
    for c in range(dst.shape[0]):
        dst[c, dst_row : dst_row + rows, :] = value[:, c * LANES : (c + 1) * LANES]


def tile_diff(sky, m, base, first, last):
    row = iota(m.shape, 0) + (base - B)
    return jnp.where((row >= first) & (row < last), sky - m, 0.0).astype(BF16)


def filter_inner(sci, start, first, last, m_ref, pcol_ref, edge_ref, filt_ref, diff):
    chunks, blocks = m_ref.shape[0], m_ref.shape[1] // PITCH
    rows, edge = blocks * B, 2 * B
    for c in range(chunks):
        part = slice(c * LANES, (c + 1) * LANES)
        sky = sci[c, pl.ds(start, rows + edge), :]
        inner = jnp.concatenate([m_ref[c, PITCH * a : PITCH * a + B, :] for a in range(1, blocks - 1)], axis=0)
        edge_ref[c, 0:edge, :] = sky[0:edge]
        edge_ref[c, edge:, :] = sky[rows:]
        diff[:, part] = tile_diff(sky[edge:rows], inner, edge, first, last)
    filt_ref[...] = jnp.dot(diff[...], pcol_ref[...], preferred_element_type=F32).astype(BF16)


def read_note(msg_ref):
    note = msg_ref[0:B, 0:LANES].astype(F32)
    return (note[0, 0] * B + note[0, 1]).astype(jnp.int32), note[0, 2]


def read_before(msg_ref):
    valid = lax.axis_index("patch") > 0
    off, live = read_note(msg_ref)
    return jnp.where(valid, off, 0), jnp.where(valid, live, 0.0), valid


def join_kernel(
    note_ref, msg_ref, head_ref, sci_ref, m1_ref, w_ref, pcol_ref, prow_ref, edge_a, filt_a,
    *rest,
):
    *outs, mark_ref, m_ref, src, xs, strip, diff, filt, sci, inner, edge_b, filt_b = rest
    edge = 2 * B
    rows, cols = filt_a.shape[0] + edge, filt_a.shape[1]
    off_b, live_b, valid = read_before(msg_ref)
    to_chunks(sci, 0, sci_ref[...])
    to_blocks(src, 0, jnp.where(valid, msg_ref[...].astype(F32), 0.0))
    to_blocks(src, 2, note_ref[edge:, :])
    to_blocks(src, 4, note_ref[0:edge, :])
    to_blocks(src, 6, head_ref[...])
    filter_inner(sci, rows - B - off_b, off_b - rows, off_b, m1_ref, pcol_ref, edge_b, filt_b, inner)
    conv_blocks(src, 8, w_ref, xs, strip)
    for n, a in enumerate((1, 2, 5, 6)):
        m_ref[:, B * n : B * (n + 1), :] = strip[:, PITCH * a : PITCH * a + B, :]
    off_a, live_a = read_note(note_ref)
    for s, (side, first, last) in enumerate(((edge_a, off_a, off_a + rows), (edge_b, off_b - rows, off_b))):
        for c in range(cols // LANES):
            part = slice(c * LANES, (c + 1) * LANES)
            for k, base in enumerate((0, rows)):
                span = slice(k * edge, (k + 1) * edge)
                at = (2 * s + k) * edge
                diff[at : at + edge, part] = tile_diff(side[c, span, :], m_ref[c, span, :], base, first, last)
    sides = jnp.dot(diff[...], pcol_ref[...], preferred_element_type=F32).astype(BF16)
    for s, inner in enumerate((filt_a, filt_b)):
        filt[s, 0:edge, :] = sides[2 * s * edge : (2 * s + 1) * edge]
        filt[s, edge:rows, :] = inner[...]
        filt[s, rows : rows + edge, :] = sides[(2 * s + 1) * edge : (2 * s + 2) * edge]
        filt[s, rows + edge :, :] = jnp.zeros((filt.shape[1] - rows - edge, cols), BF16)
    share, depth = prow_ref.shape
    prow = prow_ref[...].astype(F32)
    out_row = iota((share, depth), 0)
    lane = iota((B, cols), 1)
    visits, bands = lax.axis_size("visit"), lax.axis_size("band")
    hi, lo = off_b // B, off_b % B
    marks = note_ref[0:B, 0:LANES].astype(F32)
    marks = jnp.where(iota(marks.shape, 1) == 3, hi.astype(F32), marks)
    marks = jnp.where(iota(marks.shape, 1) == 4, lo.astype(F32), marks)
    marks = jnp.where(iota(marks.shape, 1) == 5, live_b, marks)
    mark_ref[...] = marks.astype(BF16)
    for j, out_ref in enumerate(outs):
        for k in range(visits):
            to_visit = partner(lax.axis_index("visit"), k, visits)
            base = (to_visit * bands + partner(lax.axis_index("band"), j, bands)) * share
            row = out_row + base
            left = jnp.where(row >= off_a, prow * live_a, 0.0).astype(BF16)
            right = jnp.where(row < off_b, prow * live_b, 0.0).astype(BF16)
            span = pl.ds(pl.multiple_of(base, B), depth)
            total = jnp.dot(left, filt[0, span, :], preferred_element_type=F32)
            total += jnp.dot(right, filt[1, span, :], preferred_element_type=F32)
            out_ref[k * share : (k + 1) * share, :] = total.astype(out_ref.dtype)
        if j:
            out_ref[visits * share :, 0:LANES] = marks.astype(BF16)
            out_ref[visits * share :, LANES:] = jnp.zeros((B, cols - LANES), BF16)


def pair_kernel(*refs):
    bands = lax.axis_size("band")
    visits = lax.axis_size("visit")
    mark_ref, keep_ref, *got = refs[: bands + 1]
    *outs, own_mark_ref = refs[bands + 1 :]
    share, cols = outs[0].shape
    rowid = iota((B, LANES), 0)
    marks = jnp.where(rowid == 0, mark_ref[...].astype(F32), 0.0)
    for n, ref in enumerate(got):
        other = ref[visits * share :, 0:LANES].astype(F32)
        marks = jnp.where(rowid == n + 1, other[0:1, :], marks)
    own_mark_ref[...] = marks.astype(BF16)
    for k, out_ref in enumerate(outs):
        span = slice(k * share, (k + 1) * share)
        total = keep_ref[span, :]
        for ref in got:
            total += ref[span, :].astype(F32)
        out_ref[...] = total.astype(out_ref.dtype)


def tile_kernel(mark_ref, sci_ref, note_ref, m1_ref, edge_ref, w_ref, *rest):
    rows, cols = sci_ref.shape
    *halves, out_hbm, src, xs, res, big, out, sems = rest
    bands = len(halves)
    blocks = rows // B // bands
    band = lax.axis_index("band")
    for j in range(bands):
        piece = halves[0][...].astype(F32)
        for k in range(1, bands):
            piece = jnp.where(partner(band, k, bands) == j, halves[k][...].astype(F32), piece)
        to_blocks(src, j * blocks, piece)
    off, _ = read_note(note_ref)
    copies = []

    def after(c):
        big[c, 0:B, :] = edge_ref[c, B : 2 * B, :]
        for a in range(1, rows // B - 1):
            big[c, B * a : B * (a + 1), :] = m1_ref[c, PITCH * a : PITCH * a + B, :]
        big[c, rows - B : rows + B, :] = edge_ref[c, 2 * B : 4 * B, :]
        for a in range(1, rows // B):
            big[c, rows + B * a : rows + B * (a + 1), :] = res[c, PITCH * a : PITCH * a + B, :]
        part = slice(c * LANES, (c + 1) * LANES)
        out[:, part] = (sci_ref[:, part].astype(F32) - big[c, pl.ds(off, rows), :]).astype(BF16)
        there = pl.ds(c * LANES, LANES)
        copies.append(pltpu.make_async_copy(out.at[:, there], out_hbm.at[:, there], sems.at[c]))
        copies[-1].start()

    conv_blocks(src, rows // B, w_ref, xs, res, after)
    for copy in copies:
        copy.wait()


def coadd_kernel(*refs):
    *parts, out_ref = refs
    marks, parts = parts[: len(parts) // 2], parts[len(parts) // 2 :]
    share, cols = out_ref.shape
    bands = lax.axis_size("band")
    base = (lax.axis_index("visit") * bands + lax.axis_index("band")) * share
    row = (iota((share, LANES), 0) + base).astype(F32)
    cover = jnp.zeros((share, LANES), F32)
    for ref in marks:
        for m in range(bands):
            mark = ref[...].astype(F32)[m : m + 1, :]
            cover += jnp.where(row >= mark[:, 0:1] * B + mark[:, 1:2], mark[:, 2:3], 0.0)
            cover += jnp.where(row < mark[:, 3:4] * B + mark[:, 4:5], mark[:, 5:6], 0.0)
    scale = lax.rsqrt(jnp.maximum(cover, 1.0))
    for c in range(cols // LANES):
        span = slice(c * LANES, (c + 1) * LANES)
        value = parts[0][:, span]
        for part in parts[1:]:
            value += part[:, span].astype(F32)
        out_ref[:, span] = value * scale


def in_hbm(*arrays):
    return [pltpu.with_memory_space_constraint(x, pltpu.HBM) for x in arrays]


def call(body, shapes, specs, scratch, flops, name, out=VM):
    return pl.pallas_call(
        body,
        out_shape=shapes,
        in_specs=specs,
        out_specs=jax.tree.map(lambda _: out, shapes),
        scratch_shapes=scratch,
        compiler_params=pltpu.CompilerParams(vmem_limit_bytes=LIMIT * 1024 * 1024),
        cost_estimate=pl.CostEstimate(flops=flops, bytes_accessed=1 << 21, transcendentals=0),
        name=name,
    )


def on_device(template, science, offsets, live_flags, bank, basis_index, coeff, psf_profile):
    rows, cols = template.shape
    sharers = lax.axis_size("visit") * lax.axis_size("band")
    share = rows // sharers
    chunks, blocks = cols // LANES, cols // B
    edge = 2 * B
    inner = rows - edge
    sds = jax.ShapeDtypeStruct
    deep = 9 * CH
    depth = -(-(share + edge) // LANES) * LANES
    sci = science[:, 0, :]
    held = in_hbm(template, sci)
    index = jnp.swapaxes(basis_index, 1, 2)
    before = shifted(science, "patch", 1)[:, 0, :]
    bands, visits = lax.axis_size("band"), lax.axis_size("visit")
    psf = psf_profile[None]
    note, msg, head, half, *small = call(
        pack_kernel,
        (
            sds((2 * edge, cols), BF16), sds((edge, cols), BF16), sds((edge, cols), BF16),
            sds((rows // bands, cols), BF16),
            *(sds(x.shape, x.dtype) for x in (bank, index, coeff, psf)),
        ),
        [HBM] * 7,
        [pltpu.SMEM((1, 1), jnp.int32), pltpu.SMEM((1, 1), jnp.int32), pltpu.SemaphoreType.DMA((10,))],
        1 << 20, "pack",
    )(offsets, live_flags, held[0], *in_hbm(bank, index, coeff, psf))
    half = shifted(half, "patch", -1)
    panels = lax.axis_size("patch")
    msg = lax.ppermute(msg, "patch", [(i, (i + 1) % panels) for i in range(panels)])
    head = shifted(head, "patch", -1)
    count = rows // B
    conv_scratch = [
        pltpu.VMEM((chunks, count * PITCH, LANES), F32),
        pltpu.VMEM((3, blocks + 2, count, CH), BF16),
        pltpu.VMEM((chunks, count * PITCH, LANES), F32),
    ]
    conv_flops = 2 * rows * cols * deep
    sky_scratch = [pltpu.VMEM((chunks, 2 * rows + B, LANES), F32), pltpu.VMEM((inner, cols), BF16)]
    sides = (sds((chunks, 2 * edge, LANES), F32), sds((inner, cols), BF16))
    w, pcol, prow, tile, m1, edge_a, filt_a = call(
        first_kernel,
        (
            sds((deep, CH), BF16), sds((cols, cols), BF16), sds((share, depth), BF16),
            sds((rows, cols), BF16), sds((chunks, count * PITCH, LANES), F32),
        ) + sides,
        [VM, HBM, HBM] + [VM] * 4,
        [pltpu.VMEM((rows, cols), BF16), pltpu.SemaphoreType.DMA((2,))] + conv_scratch[:2] + sky_scratch,
        conv_flops, "first",
    )(note, *held, *small)
    whole = visits * share
    keep, *sent, mark, m_edge = call(
        join_kernel,
        (sds((whole, cols), F32),) + (sds((whole + B, cols), BF16),) * (bands - 1)
        + (sds((B, LANES), BF16), sds((chunks, 2 * edge, LANES), F32)),
        [VM] * 10,
        [
            pltpu.VMEM((chunks, 8 * PITCH, LANES), F32),
            pltpu.VMEM((3, blocks + 2, 8, CH), F32),
            pltpu.VMEM((chunks, 8 * PITCH, LANES), F32),
            pltpu.VMEM((4 * edge, cols), BF16),
            pltpu.VMEM((2, rows - share + depth, cols), BF16),
        ] + sky_scratch + [pltpu.VMEM((chunks, 2 * edge, LANES), F32), pltpu.VMEM((inner, cols), BF16)],
        1 << 34, "join",
    )(note, msg, head, before, m1, w, pcol, prow, edge_a, filt_a)
    got = [swapped(part, "band", k + 1) for k, part in enumerate(sent)]
    halves = [half] + [swapped(half, "band", k) for k in range(1, bands)]
    own, *sent, mark = call(
        pair_kernel,
        (sds((share, cols), F32),) + (sds((share, cols), BF16),) * (visits - 1) + (sds((B, LANES), BF16),),
        [VM] * (1 + bands), [], 1 << 20, "pair",
    )(mark, keep, *got)
    got = [swapped(part, "visit", k + 1) for k, part in enumerate(sent)]
    marks = [mark] + [swapped(mark, "visit", k) for k in range(1, visits)]
    difference = call(
        tile_kernel, sds((rows, cols), BF16), [VM] * (6 + bands),
        conv_scratch + [
            pltpu.VMEM((chunks, 2 * rows, LANES), F32), pltpu.VMEM((rows, cols), BF16),
            pltpu.SemaphoreType.DMA((chunks,)),
        ],
        conv_flops, "tile", HBM,
    )(mark, tile, note, m1, m_edge, w, *halves)
    detection = call(
        coadd_kernel, sds((share, cols), F32), [VM] * (2 * visits), [], 1 << 20, "coadd"
    )(*marks, own, *got)
    return (difference[:, None, :], detection)


def solution(mesh):
    return jax.shard_map(
        on_device,
        mesh=mesh,
        in_specs=(
            P(("group", "patch"), None),
            P(("group", "patch"), ("visit", "band"), None),
            P(("group", "patch"), ("visit", "band")),
            P(("group", "patch"), ("visit", "band")),
            P(),
            P(("group", "visit", "band"), None, None),
            P(("group", "visit", "band"), None),
            P(),
        ),
        out_specs=(
            P(("group", "patch"), ("visit", "band"), None),
            P(("group", "patch", "visit", "band"), None),
        ),
        check_vma=False,
    )
```

```python
import functools

import jax
import jax.numpy as jnp
from jax import lax
from jax.experimental import pallas as pl
from jax.experimental.pallas import tpu as pltpu
from jax.sharding import PartitionSpec as P

B = 16
CH = B * B
LANES = 128
GROUPS = LANES // B
PITCH = B + 1
F32 = jnp.float32
BF16 = jnp.bfloat16


def shifted(shard, axis, by):
    devices = lax.axis_size(axis)
    pairs = [(i, i + by) for i in range(devices) if 0 <= i + by < devices]
    return lax.ppermute(shard, axis, pairs)


def partner(me, k, count):
    return me ^ k if count & (count - 1) == 0 else (me + k) % count


def swapped(shard, axis, k):
    devices = lax.axis_size(axis)
    return lax.ppermute(shard, axis, [(i, partner(i, k, devices)) for i in range(devices)])


def iota(shape, dim):
    return lax.broadcasted_iota(jnp.int32, shape, dim)


LIMIT = 14
VM = pl.BlockSpec(memory_space=pltpu.VMEM)
HBM = pl.BlockSpec(memory_space=pltpu.HBM)


def group_transpose(parts):
    parts = list(parts)
    group = iota(parts[0].shape, 1) // B
    for step in (1, 2, 4):
        low = (group & step) == 0
        for m in range(GROUPS):
            if m & step:
                continue
            x, y = parts[m], parts[m + step]
            parts[m] = jnp.where(low, x, pltpu.roll(y, step * B, 1))
            parts[m + step] = jnp.where(low, pltpu.roll(x, LANES - step * B, 1), y)
    return parts


def to_blocks(dst, block, value):
    value = value.astype(F32)
    for a in range(value.shape[0] // B):
        at = (block + a) * PITCH
        for c in range(dst.shape[0]):
            dst[c, at : at + B, :] = value[a * B : (a + 1) * B, c * LANES : (c + 1) * LANES]


def conv_blocks(src, count, w_ref, xs, dst, after=None):
    chunks = src.shape[0]
    blocks = chunks * GROUPS

    def load(c):
        for h in range(2):
            rows = [src[c, pl.ds(GROUPS * h + i, count, stride=PITCH), :] for i in range(GROUPS)]
            part = slice(h * LANES, (h + 1) * LANES)
            for g, here in enumerate(group_transpose(rows)):
                at = 1 + c * GROUPS + g
                xs[0, at, :, part] = pltpu.roll(here, 1, 0).astype(xs.dtype)
                xs[1, at, :, part] = here.astype(xs.dtype)
                xs[2, at, :, part] = pltpu.roll(here, count - 1, 0).astype(xs.dtype)

    def solve(c):
        b = c * GROUPS
        pieces = [
            xs[qr, b + qc : b + qc + GROUPS].reshape(GROUPS * count, CH).astype(BF16)
            for qr in range(3)
            for qc in range(3)
        ]
        out = jnp.dot(jnp.concatenate(pieces, axis=1), w_ref[...], preferred_element_type=F32)
        for h in range(2):
            part = slice(h * LANES, (h + 1) * LANES)
            rows = group_transpose([out[g * count : (g + 1) * count, part] for g in range(GROUPS)])
            for i in range(GROUPS):
                dst[c, pl.ds(GROUPS * h + i, count, stride=PITCH), :] = rows[i]

    for q in range(3):
        xs[q, 0] = jnp.zeros((count, CH), xs.dtype)
        xs[q, blocks + 1] = jnp.zeros((count, CH), xs.dtype)
    load(0)
    for c in range(chunks):
        if c + 1 < chunks:
            load(c + 1)
        solve(c)
        if after is not None:
            after(c)


def slanted(row, count):
    value = jnp.broadcast_to(row, (count, row.shape[1]))
    index = iota(value.shape, 0)
    bit = 1
    while bit < count:
        value = jnp.where((index & bit) != 0, pltpu.roll(value, bit, 1), value)
        bit *= 2
    return value


def column(row):
    size = row.shape[1]
    diag = iota((size, size), 0) == iota((size, size), 1)
    return jnp.sum(jnp.where(diag, row, jnp.zeros_like(row)), axis=1, keepdims=True)


def pack_kernel(
    off_hbm, live_hbm, t_hbm, bank_hbm, index_hbm, coeff_hbm, psf_hbm,
    note_ref, msg_ref, head_ref, half_ref, bank_ref, index_ref, coeff_ref, psf_ref, off_ref, live_ref, sems,
):
    rows, cols = t_hbm.shape
    edge = 2 * B
    piece = half_ref.shape[0]
    begin = pl.multiple_of(lax.axis_index("band") * piece, B)
    copies = [
        pltpu.make_async_copy(a, b, sems.at[n])
        for n, (a, b) in enumerate((
            (off_hbm, off_ref), (live_hbm, live_ref),
            (t_hbm.at[pl.ds(rows - edge, edge)], note_ref.at[pl.ds(0, edge)]),
            (t_hbm.at[pl.ds(0, edge)], note_ref.at[pl.ds(edge, edge)]),
            (t_hbm.at[pl.ds(0, edge)], head_ref),
            (t_hbm.at[pl.ds(begin, piece)], half_ref),
            (bank_hbm, bank_ref), (index_hbm, index_ref), (coeff_hbm, coeff_ref), (psf_hbm, psf_ref),
        ))
    ]
    for copy in copies:
        copy.start()
    for copy in copies:
        copy.wait()
    lane = iota((1, cols), 1)
    off = off_ref[0, 0]
    note = jnp.where(lane == 0, off // B, jnp.where(lane == 1, off % B, live_ref[0, 0])).astype(F32)
    block = note_ref[0:B, :].astype(F32)
    note_ref[0:B, :] = jnp.where(iota((B, cols), 0) == 0, note, block).astype(BF16)
    msg_ref[...] = note_ref[0:edge, :]


def first_kernel(
    note_ref, t_hbm, sci_hbm, bank_ref, index_ref, coeff_ref, psf_ref,
    w_ref, pcol_ref, prow_ref, sci_ref, m_ref, edge_ref, filt_ref,
    t_ref, sems, src, xs, sci, diff,
):
    copies = [
        pltpu.make_async_copy(t_hbm, t_ref, sems.at[0]), pltpu.make_async_copy(sci_hbm, sci_ref, sems.at[1])
    ]
    for copy in copies:
        copy.start()
    profs, taps = bank_ref.shape
    half = taps // 2
    delta = B - half
    bank = bank_ref[...]
    index = index_ref[0].astype(F32)
    labels = iota((index.shape[1], profs), 1).astype(F32)
    pick_row = (column(index[0:1]) == labels).astype(F32).astype(BF16)
    pick_col = (column(index[1:2]) == labels).astype(F32).astype(BF16)
    weight = column(coeff_ref[...])
    rowprof = (weight * jnp.dot(pick_row, bank, preferred_element_type=F32)).astype(BF16)
    colprof = jnp.dot(pick_col, bank, preferred_element_type=F32).astype(BF16)
    span = 3 * B
    total = 4 * B * B
    place = (iota((span, taps), 0) - delta == iota((span, taps), 1)).astype(F32).astype(BF16)
    col_t = lax.dot_general(place, colprof, (((1,), (1,)), ((), ())), preferred_element_type=F32).astype(BF16)
    spread = (span - 1 - iota((taps, total), 1) // B - delta == iota((taps, total), 0)).astype(F32).astype(BF16)
    row_rep = jnp.dot(rowprof, spread, preferred_element_type=F32).astype(BF16)
    z = jnp.dot(col_t, row_rep, preferred_element_type=F32)
    lane = iota((span, total), 1)
    for bit in (1, 2, 4, 8):
        z = jnp.where((lane & bit) != 0, pltpu.roll(z, bit, 0), z)
    z = z.astype(BF16)
    for phase in range(GROUPS):
        zp = z if phase == 0 else pltpu.roll(z, total - phase * B, 1)
        for g in range(span):
            start = span - 1 - g
            if start % GROUPS != phase:
                continue
            at = (start // GROUPS) * LANES
            for qc in range(3):
                row = (g // B) * 3 * CH + qc * CH + (g % B) * B
                w_ref[row : row + B, :] = zp[qc * B : (qc + 1) * B, at : at + CH]
    size = pcol_ref.shape[0]
    lanes = iota((taps, 3 * LANES), 1)
    mirror = (lanes - LANES + iota(lanes.shape, 0) == half).astype(F32).astype(BF16)
    bands = slanted(jnp.dot(psf_ref[...], mirror, preferred_element_type=F32), LANES)
    bands = {1 - n: bands[:, n * LANES : (n + 1) * LANES].astype(BF16) for n in range(3)}
    for i in range(size // LANES):
        for j in range(size // LANES):
            block = bands.get(i - j, jnp.zeros((LANES, LANES), BF16))
            pcol_ref[i * LANES : (i + 1) * LANES, j * LANES : (j + 1) * LANES] = block
    share, depth = prow_ref.shape
    lanes = iota((taps, depth), 1)
    ahead = (lanes - iota(lanes.shape, 0) == delta).astype(F32).astype(BF16)
    prow_ref[...] = slanted(jnp.dot(psf_ref[...], ahead, preferred_element_type=F32), share).astype(BF16)
    copies[0].wait()
    edge = 2 * B
    rows, cols = t_ref.shape
    off, _ = read_note(note_ref)
    to_blocks(src, 0, t_ref[...])
    conv_blocks(src, rows // B, w_ref, xs, m_ref)
    copies[1].wait()
    to_chunks(sci, rows, sci_ref[...])
    filter_inner(sci, rows - B - off, off, off + rows, m_ref, pcol_ref, edge_ref, filt_ref, diff)


def to_chunks(dst, dst_row, value):
    value = value.astype(F32)
    rows = value.shape[0]
    for c in range(dst.shape[0]):
        dst[c, dst_row : dst_row + rows, :] = value[:, c * LANES : (c + 1) * LANES]


def tile_diff(sky, m, base, first, last):
    row = iota(m.shape, 0) + (base - B)
    return jnp.where((row >= first) & (row < last), sky - m, 0.0).astype(BF16)


def filter_inner(sci, start, first, last, m_ref, pcol_ref, edge_ref, filt_ref, diff):
    chunks, blocks = m_ref.shape[0], m_ref.shape[1] // PITCH
    rows, edge = blocks * B, 2 * B
    for c in range(chunks):
        part = slice(c * LANES, (c + 1) * LANES)
        sky = sci[c, pl.ds(start, rows + edge), :]
        inner = jnp.concatenate([m_ref[c, PITCH * a : PITCH * a + B, :] for a in range(1, blocks - 1)], axis=0)
        edge_ref[c, 0:edge, :] = sky[0:edge]
        edge_ref[c, edge:, :] = sky[rows:]
        diff[:, part] = tile_diff(sky[edge:rows], inner, edge, first, last)
    filt_ref[...] = jnp.dot(diff[...], pcol_ref[...], preferred_element_type=F32).astype(BF16)


def read_note(msg_ref):
    note = msg_ref[0:B, 0:LANES].astype(F32)
    return (note[0, 0] * B + note[0, 1]).astype(jnp.int32), note[0, 2]


def read_before(msg_ref):
    valid = lax.axis_index("patch") > 0
    off, live = read_note(msg_ref)
    return jnp.where(valid, off, 0), jnp.where(valid, live, 0.0), valid


def join_kernel(
    note_ref, msg_ref, head_ref, sci_ref, m1_ref, w_ref, pcol_ref, prow_ref, edge_a, filt_a,
    *rest,
):
    *outs, mark_ref, m_ref, src, xs, strip, diff, filt, sci, inner, edge_b, filt_b = rest
    edge = 2 * B
    rows, cols = filt_a.shape[0] + edge, filt_a.shape[1]
    off_b, live_b, valid = read_before(msg_ref)
    to_chunks(sci, 0, sci_ref[...])
    to_blocks(src, 0, jnp.where(valid, msg_ref[...].astype(F32), 0.0))
    to_blocks(src, 2, note_ref[edge:, :])
    to_blocks(src, 4, note_ref[0:edge, :])
    to_blocks(src, 6, head_ref[...])
    filter_inner(sci, rows - B - off_b, off_b - rows, off_b, m1_ref, pcol_ref, edge_b, filt_b, inner)
    conv_blocks(src, 8, w_ref, xs, strip)
    for n, a in enumerate((1, 2, 5, 6)):
        m_ref[:, B * n : B * (n + 1), :] = strip[:, PITCH * a : PITCH * a + B, :]
    off_a, live_a = read_note(note_ref)
    for s, (side, first, last) in enumerate(((edge_a, off_a, off_a + rows), (edge_b, off_b - rows, off_b))):
        for c in range(cols // LANES):
            part = slice(c * LANES, (c + 1) * LANES)
            for k, base in enumerate((0, rows)):
                span = slice(k * edge, (k + 1) * edge)
                at = (2 * s + k) * edge
                diff[at : at + edge, part] = tile_diff(side[c, span, :], m_ref[c, span, :], base, first, last)
    sides = jnp.dot(diff[...], pcol_ref[...], preferred_element_type=F32).astype(BF16)
    for s, inner in enumerate((filt_a, filt_b)):
        filt[s, 0:edge, :] = sides[2 * s * edge : (2 * s + 1) * edge]
        filt[s, edge:rows, :] = inner[...]
        filt[s, rows : rows + edge, :] = sides[(2 * s + 1) * edge : (2 * s + 2) * edge]
        filt[s, rows + edge :, :] = jnp.zeros((filt.shape[1] - rows - edge, cols), BF16)
    share, depth = prow_ref.shape
    prow = prow_ref[...].astype(F32)
    out_row = iota((share, depth), 0)
    lane = iota((B, cols), 1)
    visits, bands = lax.axis_size("visit"), lax.axis_size("band")
    hi, lo = off_b // B, off_b % B
    marks = note_ref[0:B, 0:LANES].astype(F32)
    marks = jnp.where(iota(marks.shape, 1) == 3, hi.astype(F32), marks)
    marks = jnp.where(iota(marks.shape, 1) == 4, lo.astype(F32), marks)
    marks = jnp.where(iota(marks.shape, 1) == 5, live_b, marks)
    mark_ref[...] = marks.astype(BF16)
    for j, out_ref in enumerate(outs):
        for k in range(visits):
            to_visit = partner(lax.axis_index("visit"), k, visits)
            base = (to_visit * bands + partner(lax.axis_index("band"), j, bands)) * share
            row = out_row + base
            left = jnp.where(row >= off_a, prow * live_a, 0.0).astype(BF16)
            right = jnp.where(row < off_b, prow * live_b, 0.0).astype(BF16)
            span = pl.ds(pl.multiple_of(base, B), depth)
            total = jnp.dot(left, filt[0, span, :], preferred_element_type=F32)
            total += jnp.dot(right, filt[1, span, :], preferred_element_type=F32)
            out_ref[k * share : (k + 1) * share, :] = total.astype(out_ref.dtype)
        if j:
            out_ref[visits * share :, 0:LANES] = marks.astype(BF16)
            out_ref[visits * share :, LANES:] = jnp.zeros((B, cols - LANES), BF16)


def pair_kernel(*refs):
    bands = lax.axis_size("band")
    visits = lax.axis_size("visit")
    mark_ref, keep_ref, *got = refs[: bands + 1]
    *outs, own_mark_ref = refs[bands + 1 :]
    share, cols = outs[0].shape
    rowid = iota((B, LANES), 0)
    marks = jnp.where(rowid == 0, mark_ref[...].astype(F32), 0.0)
    for n, ref in enumerate(got):
        other = ref[visits * share :, 0:LANES].astype(F32)
        marks = jnp.where(rowid == n + 1, other[0:1, :], marks)
    own_mark_ref[...] = marks.astype(BF16)
    for k, out_ref in enumerate(outs):
        span = slice(k * share, (k + 1) * share)
        total = keep_ref[span, :]
        for ref in got:
            total += ref[span, :].astype(F32)
        out_ref[...] = total.astype(out_ref.dtype)


def tile_kernel(mark_ref, sci_ref, note_ref, m1_ref, edge_ref, w_ref, *rest):
    rows, cols = sci_ref.shape
    *halves, out_hbm, src, xs, res, big, out, sems = rest
    bands = len(halves)
    blocks = rows // B // bands
    band = lax.axis_index("band")

    def place_halves(own):
        for k in range(bands):
            to_blocks(src, partner(own, k, bands) * blocks, halves[k][...])

    for own in range(bands):
        pl.when(band == own)(functools.partial(place_halves, own))
    off, _ = read_note(note_ref)
    copies = []

    def after(c):
        big[c, 0:B, :] = edge_ref[c, B : 2 * B, :]
        for a in range(1, rows // B - 1):
            big[c, B * a : B * (a + 1), :] = m1_ref[c, PITCH * a : PITCH * a + B, :]
        big[c, rows - B : rows + B, :] = edge_ref[c, 2 * B : 4 * B, :]
        for a in range(1, rows // B):
            big[c, rows + B * a : rows + B * (a + 1), :] = res[c, PITCH * a : PITCH * a + B, :]
        part = slice(c * LANES, (c + 1) * LANES)
        out[:, part] = (sci_ref[:, part].astype(F32) - big[c, pl.ds(off, rows), :]).astype(BF16)
        there = pl.ds(c * LANES, LANES)
        copies.append(pltpu.make_async_copy(out.at[:, there], out_hbm.at[:, there], sems.at[c]))
        copies[-1].start()

    conv_blocks(src, rows // B, w_ref, xs, res, after)
    for copy in copies:
        copy.wait()


def coadd_kernel(*refs):
    *parts, out_ref = refs
    marks, parts = parts[: len(parts) // 2], parts[len(parts) // 2 :]
    share, cols = out_ref.shape
    bands = lax.axis_size("band")
    base = (lax.axis_index("visit") * bands + lax.axis_index("band")) * share
    row = (iota((share, LANES), 0) + base).astype(F32)
    cover = jnp.zeros((share, LANES), F32)
    for ref in marks:
        for m in range(bands):
            mark = ref[...].astype(F32)[m : m + 1, :]
            cover += jnp.where(row >= mark[:, 0:1] * B + mark[:, 1:2], mark[:, 2:3], 0.0)
            cover += jnp.where(row < mark[:, 3:4] * B + mark[:, 4:5], mark[:, 5:6], 0.0)
    scale = lax.rsqrt(jnp.maximum(cover, 1.0))
    for c in range(cols // LANES):
        span = slice(c * LANES, (c + 1) * LANES)
        value = parts[0][:, span]
        for part in parts[1:]:
            value += part[:, span].astype(F32)
        out_ref[:, span] = value * scale


def in_hbm(*arrays):
    return [pltpu.with_memory_space_constraint(x, pltpu.HBM) for x in arrays]


def call(body, shapes, specs, scratch, flops, name, out=VM):
    return pl.pallas_call(
        body,
        out_shape=shapes,
        in_specs=specs,
        out_specs=jax.tree.map(lambda _: out, shapes),
        scratch_shapes=scratch,
        compiler_params=pltpu.CompilerParams(vmem_limit_bytes=LIMIT * 1024 * 1024),
        cost_estimate=pl.CostEstimate(flops=flops, bytes_accessed=1 << 21, transcendentals=0),
        name=name,
    )


def on_device(template, science, offsets, live_flags, bank, basis_index, coeff, psf_profile):
    rows, cols = template.shape
    sharers = lax.axis_size("visit") * lax.axis_size("band")
    share = rows // sharers
    chunks, blocks = cols // LANES, cols // B
    edge = 2 * B
    inner = rows - edge
    sds = jax.ShapeDtypeStruct
    deep = 9 * CH
    depth = -(-(share + edge) // LANES) * LANES
    sci = science[:, 0, :]
    held = in_hbm(template, sci)
    index = jnp.swapaxes(basis_index, 1, 2)
    before = shifted(science, "patch", 1)[:, 0, :]
    bands, visits = lax.axis_size("band"), lax.axis_size("visit")
    psf = psf_profile[None]
    note, msg, head, half, *small = call(
        pack_kernel,
        (
            sds((2 * edge, cols), BF16), sds((edge, cols), BF16), sds((edge, cols), BF16),
            sds((rows // bands, cols), BF16),
            *(sds(x.shape, x.dtype) for x in (bank, index, coeff, psf)),
        ),
        [HBM] * 7,
        [pltpu.SMEM((1, 1), jnp.int32), pltpu.SMEM((1, 1), jnp.int32), pltpu.SemaphoreType.DMA((10,))],
        1 << 20, "pack",
    )(offsets, live_flags, held[0], *in_hbm(bank, index, coeff, psf))
    half = shifted(half, "patch", -1)
    panels = lax.axis_size("patch")
    msg = lax.ppermute(msg, "patch", [(i, (i + 1) % panels) for i in range(panels)])
    head = shifted(head, "patch", -1)
    count = rows // B
    conv_scratch = [
        pltpu.VMEM((chunks, count * PITCH, LANES), F32),
        pltpu.VMEM((3, blocks + 2, count, CH), BF16),
        pltpu.VMEM((chunks, count * PITCH, LANES), F32),
    ]
    conv_flops = 2 * rows * cols * deep
    sky_scratch = [pltpu.VMEM((chunks, 2 * rows + B, LANES), F32), pltpu.VMEM((inner, cols), BF16)]
    sides = (sds((chunks, 2 * edge, LANES), F32), sds((inner, cols), BF16))
    w, pcol, prow, tile, m1, edge_a, filt_a = call(
        first_kernel,
        (
            sds((deep, CH), BF16), sds((cols, cols), BF16), sds((share, depth), BF16),
            sds((rows, cols), BF16), sds((chunks, count * PITCH, LANES), F32),
        ) + sides,
        [VM, HBM, HBM] + [VM] * 4,
        [pltpu.VMEM((rows, cols), BF16), pltpu.SemaphoreType.DMA((2,))] + conv_scratch[:2] + sky_scratch,
        conv_flops, "first",
    )(note, *held, *small)
    whole = visits * share
    keep, *sent, mark, m_edge = call(
        join_kernel,
        (sds((whole, cols), F32),) + (sds((whole + B, cols), BF16),) * (bands - 1)
        + (sds((B, LANES), BF16), sds((chunks, 2 * edge, LANES), F32)),
        [VM] * 10,
        [
            pltpu.VMEM((chunks, 8 * PITCH, LANES), F32),
            pltpu.VMEM((3, blocks + 2, 8, CH), F32),
            pltpu.VMEM((chunks, 8 * PITCH, LANES), F32),
            pltpu.VMEM((4 * edge, cols), BF16),
            pltpu.VMEM((2, rows - share + depth, cols), BF16),
        ] + sky_scratch + [pltpu.VMEM((chunks, 2 * edge, LANES), F32), pltpu.VMEM((inner, cols), BF16)],
        1 << 34, "join",
    )(note, msg, head, before, m1, w, pcol, prow, edge_a, filt_a)
    got = [swapped(part, "band", k + 1) for k, part in enumerate(sent)]
    halves = [half] + [swapped(half, "band", k) for k in range(1, bands)]
    own, *sent, mark = call(
        pair_kernel,
        (sds((share, cols), F32),) + (sds((share, cols), BF16),) * (visits - 1) + (sds((B, LANES), BF16),),
        [VM] * (1 + bands), [], 1 << 20, "pair",
    )(mark, keep, *got)
    got = [swapped(part, "visit", k + 1) for k, part in enumerate(sent)]
    marks = [mark] + [swapped(mark, "visit", k) for k in range(1, visits)]
    difference = call(
        tile_kernel, sds((rows, cols), BF16), [VM] * (6 + bands),
        conv_scratch + [
            pltpu.VMEM((chunks, 2 * rows, LANES), F32), pltpu.VMEM((rows, cols), BF16),
            pltpu.SemaphoreType.DMA((chunks,)),
        ],
        conv_flops, "tile", HBM,
    )(mark, tile, note, m1, m_edge, w, *halves)
    detection = call(
        coadd_kernel, sds((share, cols), F32), [VM] * (2 * visits), [], 1 << 20, "coadd"
    )(*marks, own, *got)
    return (difference[:, None, :], detection)


def solution(mesh):
    return jax.shard_map(
        on_device,
        mesh=mesh,
        in_specs=(
            P(("group", "patch"), None),
            P(("group", "patch"), ("visit", "band"), None),
            P(("group", "patch"), ("visit", "band")),
            P(("group", "patch"), ("visit", "band")),
            P(),
            P(("group", "visit", "band"), None, None),
            P(("group", "visit", "band"), None),
            P(),
        ),
        out_specs=(
            P(("group", "patch"), ("visit", "band"), None),
            P(("group", "patch", "visit", "band"), None),
        ),
        check_vma=False,
    )
```

```python
import functools

import jax
import jax.numpy as jnp
from jax import lax
from jax.experimental import pallas as pl
from jax.experimental.pallas import tpu as pltpu
from jax.sharding import PartitionSpec as P

B = 16
CH = B * B
LANES = 128
GROUPS = LANES // B
PITCH = B + 1
F32 = jnp.float32
BF16 = jnp.bfloat16


def shifted(shard, axis, by):
    devices = lax.axis_size(axis)
    pairs = [(i, i + by) for i in range(devices) if 0 <= i + by < devices]
    return lax.ppermute(shard, axis, pairs)


def partner(me, k, count):
    return me ^ k if count & (count - 1) == 0 else (me + k) % count


def swapped(shard, axis, k):
    devices = lax.axis_size(axis)
    return lax.ppermute(shard, axis, [(i, partner(i, k, devices)) for i in range(devices)])


def iota(shape, dim):
    return lax.broadcasted_iota(jnp.int32, shape, dim)


LIMIT = 14
VM = pl.BlockSpec(memory_space=pltpu.VMEM)
HBM = pl.BlockSpec(memory_space=pltpu.HBM)


def group_transpose(parts):
    parts = list(parts)
    group = iota(parts[0].shape, 1) // B
    for step in (1, 2, 4):
        low = (group & step) == 0
        for m in range(GROUPS):
            if m & step:
                continue
            x, y = parts[m], parts[m + step]
            parts[m] = jnp.where(low, x, pltpu.roll(y, step * B, 1))
            parts[m + step] = jnp.where(low, pltpu.roll(x, LANES - step * B, 1), y)
    return parts


def to_blocks(dst, block, value):
    value = value.astype(F32)
    for a in range(value.shape[0] // B):
        at = (block + a) * PITCH
        for c in range(dst.shape[0]):
            dst[c, at : at + B, :] = value[a * B : (a + 1) * B, c * LANES : (c + 1) * LANES]


def conv_blocks(src, count, w_ref, xs, dst, after=None):
    chunks = src.shape[0]
    blocks = chunks * GROUPS

    def load(c):
        for h in range(2):
            rows = [src[c, pl.ds(GROUPS * h + i, count, stride=PITCH), :] for i in range(GROUPS)]
            part = slice(h * LANES, (h + 1) * LANES)
            for g, here in enumerate(group_transpose(rows)):
                at = 1 + c * GROUPS + g
                xs[0, at, :, part] = pltpu.roll(here, 1, 0).astype(xs.dtype)
                xs[1, at, :, part] = here.astype(xs.dtype)
                xs[2, at, :, part] = pltpu.roll(here, count - 1, 0).astype(xs.dtype)

    def solve(c):
        b = c * GROUPS
        pieces = [
            xs[qr, b + qc : b + qc + GROUPS].reshape(GROUPS * count, CH).astype(BF16)
            for qr in range(3)
            for qc in range(3)
        ]
        out = jnp.dot(jnp.concatenate(pieces, axis=1), w_ref[...], preferred_element_type=F32)
        for h in range(2):
            part = slice(h * LANES, (h + 1) * LANES)
            rows = group_transpose([out[g * count : (g + 1) * count, part] for g in range(GROUPS)])
            for i in range(GROUPS):
                dst[c, pl.ds(GROUPS * h + i, count, stride=PITCH), :] = rows[i]

    for q in range(3):
        xs[q, 0] = jnp.zeros((count, CH), xs.dtype)
        xs[q, blocks + 1] = jnp.zeros((count, CH), xs.dtype)
    load(0)
    for c in range(chunks):
        if c + 1 < chunks:
            load(c + 1)
        solve(c)
        if after is not None:
            after(c)


def slanted(row, count):
    value = jnp.broadcast_to(row, (count, row.shape[1]))
    index = iota(value.shape, 0)
    bit = 1
    while bit < count:
        value = jnp.where((index & bit) != 0, pltpu.roll(value, bit, 1), value)
        bit *= 2
    return value


def column(row):
    size = row.shape[1]
    diag = iota((size, size), 0) == iota((size, size), 1)
    return jnp.sum(jnp.where(diag, row, jnp.zeros_like(row)), axis=1, keepdims=True)


def pack_kernel(
    off_hbm, live_hbm, t_hbm, bank_hbm, index_hbm, coeff_hbm, psf_hbm,
    note_ref, msg_ref, head_ref, bank_ref, index_ref, coeff_ref, psf_ref, off_ref, live_ref, sems,
):
    rows, cols = t_hbm.shape
    edge = 2 * B
    copies = [
        pltpu.make_async_copy(a, b, sems.at[n])
        for n, (a, b) in enumerate((
            (off_hbm, off_ref), (live_hbm, live_ref),
            (t_hbm.at[pl.ds(rows - edge, edge)], note_ref.at[pl.ds(0, edge)]),
            (t_hbm.at[pl.ds(0, edge)], note_ref.at[pl.ds(edge, edge)]),
            (t_hbm.at[pl.ds(0, edge)], head_ref),
            (bank_hbm, bank_ref), (index_hbm, index_ref), (coeff_hbm, coeff_ref), (psf_hbm, psf_ref),
        ))
    ]
    for copy in copies:
        copy.start()
    for copy in copies:
        copy.wait()
    lane = iota((1, cols), 1)
    off = off_ref[0, 0]
    note = jnp.where(lane == 0, off // B, jnp.where(lane == 1, off % B, live_ref[0, 0])).astype(F32)
    block = note_ref[0:B, :].astype(F32)
    note_ref[0:B, :] = jnp.where(iota((B, cols), 0) == 0, note, block).astype(BF16)
    msg_ref[...] = note_ref[0:edge, :]


def cut_kernel(note_ref, t_hbm, half_ref, sem):
    piece = half_ref.shape[0]
    begin = pl.multiple_of(lax.axis_index("band") * piece, B)
    copy = pltpu.make_async_copy(t_hbm.at[pl.ds(begin, piece)], half_ref, sem)
    copy.start()
    copy.wait()


def first_kernel(
    note_ref, t_hbm, sci_hbm, bank_ref, index_ref, coeff_ref, psf_ref,
    w_ref, pcol_ref, prow_ref, sci_ref, m_ref, edge_ref, filt_ref,
    t_ref, sems, src, xs, sci, diff,
):
    copies = [
        pltpu.make_async_copy(t_hbm, t_ref, sems.at[0]), pltpu.make_async_copy(sci_hbm, sci_ref, sems.at[1])
    ]
    for copy in copies:
        copy.start()
    profs, taps = bank_ref.shape
    half = taps // 2
    delta = B - half
    bank = bank_ref[...]
    index = index_ref[0].astype(F32)
    labels = iota((index.shape[1], profs), 1).astype(F32)
    pick_row = (column(index[0:1]) == labels).astype(F32).astype(BF16)
    pick_col = (column(index[1:2]) == labels).astype(F32).astype(BF16)
    weight = column(coeff_ref[...])
    rowprof = (weight * jnp.dot(pick_row, bank, preferred_element_type=F32)).astype(BF16)
    colprof = jnp.dot(pick_col, bank, preferred_element_type=F32).astype(BF16)
    span = 3 * B
    total = 4 * B * B
    place = (iota((span, taps), 0) - delta == iota((span, taps), 1)).astype(F32).astype(BF16)
    col_t = lax.dot_general(place, colprof, (((1,), (1,)), ((), ())), preferred_element_type=F32).astype(BF16)
    spread = (span - 1 - iota((taps, total), 1) // B - delta == iota((taps, total), 0)).astype(F32).astype(BF16)
    row_rep = jnp.dot(rowprof, spread, preferred_element_type=F32).astype(BF16)
    z = jnp.dot(col_t, row_rep, preferred_element_type=F32)
    lane = iota((span, total), 1)
    for bit in (1, 2, 4, 8):
        z = jnp.where((lane & bit) != 0, pltpu.roll(z, bit, 0), z)
    z = z.astype(BF16)
    for phase in range(GROUPS):
        zp = z if phase == 0 else pltpu.roll(z, total - phase * B, 1)
        for g in range(span):
            start = span - 1 - g
            if start % GROUPS != phase:
                continue
            at = (start // GROUPS) * LANES
            for qc in range(3):
                row = (g // B) * 3 * CH + qc * CH + (g % B) * B
                w_ref[row : row + B, :] = zp[qc * B : (qc + 1) * B, at : at + CH]
    size = pcol_ref.shape[0]
    lanes = iota((taps, 3 * LANES), 1)
    mirror = (lanes - LANES + iota(lanes.shape, 0) == half).astype(F32).astype(BF16)
    bands = slanted(jnp.dot(psf_ref[...], mirror, preferred_element_type=F32), LANES)
    bands = {1 - n: bands[:, n * LANES : (n + 1) * LANES].astype(BF16) for n in range(3)}
    for i in range(size // LANES):
        for j in range(size // LANES):
            block = bands.get(i - j, jnp.zeros((LANES, LANES), BF16))
            pcol_ref[i * LANES : (i + 1) * LANES, j * LANES : (j + 1) * LANES] = block
    share, depth = prow_ref.shape
    lanes = iota((taps, depth), 1)
    ahead = (lanes - iota(lanes.shape, 0) == delta).astype(F32).astype(BF16)
    prow_ref[...] = slanted(jnp.dot(psf_ref[...], ahead, preferred_element_type=F32), share).astype(BF16)
    copies[0].wait()
    edge = 2 * B
    rows, cols = t_ref.shape
    off, _ = read_note(note_ref)
    to_blocks(src, 0, t_ref[...])
    conv_blocks(src, rows // B, w_ref, xs, m_ref)
    copies[1].wait()
    to_chunks(sci, rows, sci_ref[...])
    filter_inner(sci, rows - B - off, off, off + rows, m_ref, pcol_ref, edge_ref, filt_ref, diff)


def to_chunks(dst, dst_row, value):
    value = value.astype(F32)
    rows = value.shape[0]
    for c in range(dst.shape[0]):
        dst[c, dst_row : dst_row + rows, :] = value[:, c * LANES : (c + 1) * LANES]


def tile_diff(sky, m, base, first, last):
    row = iota(m.shape, 0) + (base - B)
    return jnp.where((row >= first) & (row < last), sky - m, 0.0).astype(BF16)


def filter_inner(sci, start, first, last, m_ref, pcol_ref, edge_ref, filt_ref, diff):
    chunks, blocks = m_ref.shape[0], m_ref.shape[1] // PITCH
    rows, edge = blocks * B, 2 * B
    for c in range(chunks):
        part = slice(c * LANES, (c + 1) * LANES)
        sky = sci[c, pl.ds(start, rows + edge), :]
        inner = jnp.concatenate([m_ref[c, PITCH * a : PITCH * a + B, :] for a in range(1, blocks - 1)], axis=0)
        edge_ref[c, 0:edge, :] = sky[0:edge]
        edge_ref[c, edge:, :] = sky[rows:]
        diff[:, part] = tile_diff(sky[edge:rows], inner, edge, first, last)
    filt_ref[...] = jnp.dot(diff[...], pcol_ref[...], preferred_element_type=F32).astype(BF16)


def read_note(msg_ref):
    note = msg_ref[0:B, 0:LANES].astype(F32)
    return (note[0, 0] * B + note[0, 1]).astype(jnp.int32), note[0, 2]


def read_before(msg_ref):
    valid = lax.axis_index("patch") > 0
    off, live = read_note(msg_ref)
    return jnp.where(valid, off, 0), jnp.where(valid, live, 0.0), valid


def join_kernel(
    note_ref, msg_ref, head_ref, sci_ref, m1_ref, w_ref, pcol_ref, prow_ref, edge_a, filt_a,
    *rest,
):
    *outs, mark_ref, m_ref, src, xs, strip, diff, filt, sci, inner, edge_b, filt_b = rest
    edge = 2 * B
    rows, cols = filt_a.shape[0] + edge, filt_a.shape[1]
    off_b, live_b, valid = read_before(msg_ref)
    to_chunks(sci, 0, sci_ref[...])
    to_blocks(src, 0, jnp.where(valid, msg_ref[...].astype(F32), 0.0))
    to_blocks(src, 2, note_ref[edge:, :])
    to_blocks(src, 4, note_ref[0:edge, :])
    to_blocks(src, 6, head_ref[...])
    filter_inner(sci, rows - B - off_b, off_b - rows, off_b, m1_ref, pcol_ref, edge_b, filt_b, inner)
    conv_blocks(src, 8, w_ref, xs, strip)
    for n, a in enumerate((1, 2, 5, 6)):
        m_ref[:, B * n : B * (n + 1), :] = strip[:, PITCH * a : PITCH * a + B, :]
    off_a, live_a = read_note(note_ref)
    for s, (side, first, last) in enumerate(((edge_a, off_a, off_a + rows), (edge_b, off_b - rows, off_b))):
        for c in range(cols // LANES):
            part = slice(c * LANES, (c + 1) * LANES)
            for k, base in enumerate((0, rows)):
                span = slice(k * edge, (k + 1) * edge)
                at = (2 * s + k) * edge
                diff[at : at + edge, part] = tile_diff(side[c, span, :], m_ref[c, span, :], base, first, last)
    sides = jnp.dot(diff[...], pcol_ref[...], preferred_element_type=F32).astype(BF16)
    for s, inner in enumerate((filt_a, filt_b)):
        filt[s, 0:edge, :] = sides[2 * s * edge : (2 * s + 1) * edge]
        filt[s, edge:rows, :] = inner[...]
        filt[s, rows : rows + edge, :] = sides[(2 * s + 1) * edge : (2 * s + 2) * edge]
        filt[s, rows + edge :, :] = jnp.zeros((filt.shape[1] - rows - edge, cols), BF16)
    share, depth = prow_ref.shape
    prow = prow_ref[...].astype(F32)
    out_row = iota((share, depth), 0)
    lane = iota((B, cols), 1)
    visits, bands = lax.axis_size("visit"), lax.axis_size("band")
    hi, lo = off_b // B, off_b % B
    marks = note_ref[0:B, 0:LANES].astype(F32)
    marks = jnp.where(iota(marks.shape, 1) == 3, hi.astype(F32), marks)
    marks = jnp.where(iota(marks.shape, 1) == 4, lo.astype(F32), marks)
    marks = jnp.where(iota(marks.shape, 1) == 5, live_b, marks)
    mark_ref[...] = marks.astype(BF16)
    for j, out_ref in enumerate(outs):
        for k in range(visits):
            to_visit = partner(lax.axis_index("visit"), k, visits)
            base = (to_visit * bands + partner(lax.axis_index("band"), j, bands)) * share
            row = out_row + base
            left = jnp.where(row >= off_a, prow * live_a, 0.0).astype(BF16)
            right = jnp.where(row < off_b, prow * live_b, 0.0).astype(BF16)
            span = pl.ds(pl.multiple_of(base, B), depth)
            total = jnp.dot(left, filt[0, span, :], preferred_element_type=F32)
            total += jnp.dot(right, filt[1, span, :], preferred_element_type=F32)
            out_ref[k * share : (k + 1) * share, :] = total.astype(out_ref.dtype)
        if j:
            out_ref[visits * share :, 0:LANES] = marks.astype(BF16)
            out_ref[visits * share :, LANES:] = jnp.zeros((B, cols - LANES), BF16)


def pair_kernel(*refs):
    bands = lax.axis_size("band")
    visits = lax.axis_size("visit")
    mark_ref, keep_ref, *got = refs[: bands + 1]
    *outs, own_mark_ref = refs[bands + 1 :]
    share, cols = outs[0].shape
    rowid = iota((B, LANES), 0)
    marks = jnp.where(rowid == 0, mark_ref[...].astype(F32), 0.0)
    for n, ref in enumerate(got):
        other = ref[visits * share :, 0:LANES].astype(F32)
        marks = jnp.where(rowid == n + 1, other[0:1, :], marks)
    own_mark_ref[...] = marks.astype(BF16)
    for k, out_ref in enumerate(outs):
        span = slice(k * share, (k + 1) * share)
        total = keep_ref[span, :]
        for ref in got:
            total += ref[span, :].astype(F32)
        out_ref[...] = total.astype(out_ref.dtype)


def tile_kernel(mark_ref, sci_ref, note_ref, m1_ref, edge_ref, w_ref, *rest):
    rows, cols = sci_ref.shape
    *halves, out_hbm, src, xs, res, big, out, sems = rest
    bands = len(halves)
    blocks = rows // B // bands
    band = lax.axis_index("band")
    for j in range(bands):
        piece = halves[0][...].astype(F32)
        for k in range(1, bands):
            piece = jnp.where(partner(band, k, bands) == j, halves[k][...].astype(F32), piece)
        to_blocks(src, j * blocks, piece)
    off, _ = read_note(note_ref)
    copies = []

    def after(c):
        big[c, 0:B, :] = edge_ref[c, B : 2 * B, :]
        for a in range(1, rows // B - 1):
            big[c, B * a : B * (a + 1), :] = m1_ref[c, PITCH * a : PITCH * a + B, :]
        big[c, rows - B : rows + B, :] = edge_ref[c, 2 * B : 4 * B, :]
        for a in range(1, rows // B):
            big[c, rows + B * a : rows + B * (a + 1), :] = res[c, PITCH * a : PITCH * a + B, :]
        part = slice(c * LANES, (c + 1) * LANES)
        out[:, part] = (sci_ref[:, part].astype(F32) - big[c, pl.ds(off, rows), :]).astype(BF16)
        there = pl.ds(c * LANES, LANES)
        copies.append(pltpu.make_async_copy(out.at[:, there], out_hbm.at[:, there], sems.at[c]))
        copies[-1].start()

    conv_blocks(src, rows // B, w_ref, xs, res, after)
    for copy in copies:
        copy.wait()


def coadd_kernel(*refs):
    *parts, out_ref = refs
    marks, parts = parts[: len(parts) // 2], parts[len(parts) // 2 :]
    share, cols = out_ref.shape
    bands = lax.axis_size("band")
    base = (lax.axis_index("visit") * bands + lax.axis_index("band")) * share
    row = (iota((share, LANES), 0) + base).astype(F32)
    cover = jnp.zeros((share, LANES), F32)
    for ref in marks:
        for m in range(bands):
            mark = ref[...].astype(F32)[m : m + 1, :]
            cover += jnp.where(row >= mark[:, 0:1] * B + mark[:, 1:2], mark[:, 2:3], 0.0)
            cover += jnp.where(row < mark[:, 3:4] * B + mark[:, 4:5], mark[:, 5:6], 0.0)
    scale = lax.rsqrt(jnp.maximum(cover, 1.0))
    for c in range(cols // LANES):
        span = slice(c * LANES, (c + 1) * LANES)
        value = parts[0][:, span]
        for part in parts[1:]:
            value += part[:, span].astype(F32)
        out_ref[:, span] = value * scale


def in_hbm(*arrays):
    return [pltpu.with_memory_space_constraint(x, pltpu.HBM) for x in arrays]


def call(body, shapes, specs, scratch, flops, name, out=VM):
    return pl.pallas_call(
        body,
        out_shape=shapes,
        in_specs=specs,
        out_specs=jax.tree.map(lambda _: out, shapes),
        scratch_shapes=scratch,
        compiler_params=pltpu.CompilerParams(vmem_limit_bytes=LIMIT * 1024 * 1024),
        cost_estimate=pl.CostEstimate(flops=flops, bytes_accessed=1 << 21, transcendentals=0),
        name=name,
    )


def on_device(template, science, offsets, live_flags, bank, basis_index, coeff, psf_profile):
    rows, cols = template.shape
    sharers = lax.axis_size("visit") * lax.axis_size("band")
    share = rows // sharers
    chunks, blocks = cols // LANES, cols // B
    edge = 2 * B
    inner = rows - edge
    sds = jax.ShapeDtypeStruct
    deep = 9 * CH
    depth = -(-(share + edge) // LANES) * LANES
    sci = science[:, 0, :]
    held = in_hbm(template, sci)
    index = jnp.swapaxes(basis_index, 1, 2)
    before = shifted(science, "patch", 1)[:, 0, :]
    bands, visits = lax.axis_size("band"), lax.axis_size("visit")
    psf = psf_profile[None]
    note, msg, head, *small = call(
        pack_kernel,
        (
            sds((2 * edge, cols), BF16), sds((edge, cols), BF16), sds((edge, cols), BF16),
            *(sds(x.shape, x.dtype) for x in (bank, index, coeff, psf)),
        ),
        [HBM] * 7,
        [pltpu.SMEM((1, 1), jnp.int32), pltpu.SMEM((1, 1), jnp.int32), pltpu.SemaphoreType.DMA((10,))],
        1 << 20, "pack",
    )(offsets, live_flags, held[0], *in_hbm(bank, index, coeff, psf))
    half = call(
        cut_kernel, sds((rows // bands, cols), BF16), [VM, HBM], [pltpu.SemaphoreType.DMA], 1, "cut"
    )(note, held[0])
    half = shifted(half, "patch", -1)
    panels = lax.axis_size("patch")
    msg = lax.ppermute(msg, "patch", [(i, (i + 1) % panels) for i in range(panels)])
    head = shifted(head, "patch", -1)
    count = rows // B
    conv_scratch = [
        pltpu.VMEM((chunks, count * PITCH, LANES), F32),
        pltpu.VMEM((3, blocks + 2, count, CH), BF16),
        pltpu.VMEM((chunks, count * PITCH, LANES), F32),
    ]
    conv_flops = 2 * rows * cols * deep
    sky_scratch = [pltpu.VMEM((chunks, 2 * rows + B, LANES), F32), pltpu.VMEM((inner, cols), BF16)]
    sides = (sds((chunks, 2 * edge, LANES), F32), sds((inner, cols), BF16))
    w, pcol, prow, tile, m1, edge_a, filt_a = call(
        first_kernel,
        (
            sds((deep, CH), BF16), sds((cols, cols), BF16), sds((share, depth), BF16),
            sds((rows, cols), BF16), sds((chunks, count * PITCH, LANES), F32),
        ) + sides,
        [VM, HBM, HBM] + [VM] * 4,
        [pltpu.VMEM((rows, cols), BF16), pltpu.SemaphoreType.DMA((2,))] + conv_scratch[:2] + sky_scratch,
        conv_flops, "first",
    )(note, *held, *small)
    whole = visits * share
    keep, *sent, mark, m_edge = call(
        join_kernel,
        (sds((whole, cols), F32),) + (sds((whole + B, cols), BF16),) * (bands - 1)
        + (sds((B, LANES), BF16), sds((chunks, 2 * edge, LANES), F32)),
        [VM] * 10,
        [
            pltpu.VMEM((chunks, 8 * PITCH, LANES), F32),
            pltpu.VMEM((3, blocks + 2, 8, CH), F32),
            pltpu.VMEM((chunks, 8 * PITCH, LANES), F32),
            pltpu.VMEM((4 * edge, cols), BF16),
            pltpu.VMEM((2, rows - share + depth, cols), BF16),
        ] + sky_scratch + [pltpu.VMEM((chunks, 2 * edge, LANES), F32), pltpu.VMEM((inner, cols), BF16)],
        1 << 34, "join",
    )(note, msg, head, before, m1, w, pcol, prow, edge_a, filt_a)
    got = [swapped(part, "band", k + 1) for k, part in enumerate(sent)]
    halves = [half] + [swapped(half, "band", k) for k in range(1, bands)]
    own, *sent, mark = call(
        pair_kernel,
        (sds((share, cols), F32),) + (sds((share, cols), BF16),) * (visits - 1) + (sds((B, LANES), BF16),),
        [VM] * (1 + bands), [], 1 << 20, "pair",
    )(mark, keep, *got)
    got = [swapped(part, "visit", k + 1) for k, part in enumerate(sent)]
    marks = [mark] + [swapped(mark, "visit", k) for k in range(1, visits)]
    difference = call(
        tile_kernel, sds((rows, cols), BF16), [VM] * (6 + bands),
        conv_scratch + [
            pltpu.VMEM((chunks, 2 * rows, LANES), F32), pltpu.VMEM((rows, cols), BF16),
            pltpu.SemaphoreType.DMA((chunks,)),
        ],
        conv_flops, "tile", HBM,
    )(mark, tile, note, m1, m_edge, w, *halves)
    detection = call(
        coadd_kernel, sds((share, cols), F32), [VM] * (2 * visits), [], 1 << 20, "coadd"
    )(*marks, own, *got)
    return (difference[:, None, :], detection)


def solution(mesh):
    return jax.shard_map(
        on_device,
        mesh=mesh,
        in_specs=(
            P(("group", "patch"), None),
            P(("group", "patch"), ("visit", "band"), None),
            P(("group", "patch"), ("visit", "band")),
            P(("group", "patch"), ("visit", "band")),
            P(),
            P(("group", "visit", "band"), None, None),
            P(("group", "visit", "band"), None),
            P(),
        ),
        out_specs=(
            P(("group", "patch"), ("visit", "band"), None),
            P(("group", "patch", "visit", "band"), None),
        ),
        check_vma=False,
    )
```

```python
import functools

import jax
import jax.numpy as jnp
from jax import lax
from jax.experimental import pallas as pl
from jax.experimental.pallas import tpu as pltpu
from jax.sharding import PartitionSpec as P

B = 16
CH = B * B
LANES = 128
GROUPS = LANES // B
PITCH = B + 1
F32 = jnp.float32
BF16 = jnp.bfloat16


def shifted(shard, axis, by):
    devices = lax.axis_size(axis)
    pairs = [(i, i + by) for i in range(devices) if 0 <= i + by < devices]
    return lax.ppermute(shard, axis, pairs)


def partner(me, k, count):
    return me ^ k if count & (count - 1) == 0 else (me + k) % count


def swapped(shard, axis, k):
    devices = lax.axis_size(axis)
    return lax.ppermute(shard, axis, [(i, partner(i, k, devices)) for i in range(devices)])


def iota(shape, dim):
    return lax.broadcasted_iota(jnp.int32, shape, dim)


LIMIT = 14
VM = pl.BlockSpec(memory_space=pltpu.VMEM)
HBM = pl.BlockSpec(memory_space=pltpu.HBM)


def group_transpose(parts):
    parts = list(parts)
    group = iota(parts[0].shape, 1) // B
    for step in (1, 2, 4):
        low = (group & step) == 0
        for m in range(GROUPS):
            if m & step:
                continue
            x, y = parts[m], parts[m + step]
            parts[m] = jnp.where(low, x, pltpu.roll(y, step * B, 1))
            parts[m + step] = jnp.where(low, pltpu.roll(x, LANES - step * B, 1), y)
    return parts


def to_blocks(dst, block, value):
    value = value.astype(F32)
    for a in range(value.shape[0] // B):
        at = (block + a) * PITCH
        for c in range(dst.shape[0]):
            dst[c, at : at + B, :] = value[a * B : (a + 1) * B, c * LANES : (c + 1) * LANES]


def conv_blocks(src, count, w_ref, xs, dst, after=None):
    chunks = src.shape[0]
    blocks = chunks * GROUPS

    def load(c):
        for h in range(2):
            rows = [src[c, pl.ds(GROUPS * h + i, count, stride=PITCH), :] for i in range(GROUPS)]
            part = slice(h * LANES, (h + 1) * LANES)
            for g, here in enumerate(group_transpose(rows)):
                at = 1 + c * GROUPS + g
                xs[0, at, :, part] = pltpu.roll(here, 1, 0).astype(xs.dtype)
                xs[1, at, :, part] = here.astype(xs.dtype)
                xs[2, at, :, part] = pltpu.roll(here, count - 1, 0).astype(xs.dtype)

    def solve(c):
        b = c * GROUPS
        pieces = [
            xs[qr, b + qc : b + qc + GROUPS].reshape(GROUPS * count, CH).astype(BF16)
            for qr in range(3)
            for qc in range(3)
        ]
        out = jnp.dot(jnp.concatenate(pieces, axis=1), w_ref[...], preferred_element_type=F32)
        for h in range(2):
            part = slice(h * LANES, (h + 1) * LANES)
            rows = group_transpose([out[g * count : (g + 1) * count, part] for g in range(GROUPS)])
            for i in range(GROUPS):
                dst[c, pl.ds(GROUPS * h + i, count, stride=PITCH), :] = rows[i]

    for q in range(3):
        xs[q, 0] = jnp.zeros((count, CH), xs.dtype)
        xs[q, blocks + 1] = jnp.zeros((count, CH), xs.dtype)
    load(0)
    for c in range(chunks):
        if c + 1 < chunks:
            load(c + 1)
        solve(c)
        if after is not None:
            after(c)


def slanted(row, count):
    value = jnp.broadcast_to(row, (count, row.shape[1]))
    index = iota(value.shape, 0)
    bit = 1
    while bit < count:
        value = jnp.where((index & bit) != 0, pltpu.roll(value, bit, 1), value)
        bit *= 2
    return value


def column(row):
    size = row.shape[1]
    diag = iota((size, size), 0) == iota((size, size), 1)
    return jnp.sum(jnp.where(diag, row, jnp.zeros_like(row)), axis=1, keepdims=True)


def pack_kernel(
    off_hbm, live_hbm, t_hbm, bank_hbm, index_hbm, coeff_hbm, psf_hbm,
    note_ref, msg_ref, head_ref, half_ref, bank_ref, index_ref, coeff_ref, psf_ref, off_ref, live_ref, sems,
):
    rows, cols = t_hbm.shape
    edge = 2 * B
    piece = half_ref.shape[0]
    begin = pl.multiple_of(lax.axis_index("band") * piece, B)
    copies = [
        pltpu.make_async_copy(a, b, sems.at[n])
        for n, (a, b) in enumerate((
            (off_hbm, off_ref), (live_hbm, live_ref),
            (t_hbm.at[pl.ds(rows - edge, edge)], note_ref.at[pl.ds(0, edge)]),
            (t_hbm.at[pl.ds(0, edge)], note_ref.at[pl.ds(edge, edge)]),
            (t_hbm.at[pl.ds(begin, piece)], half_ref),
            (bank_hbm, bank_ref), (index_hbm, index_ref), (coeff_hbm, coeff_ref), (psf_hbm, psf_ref),
        ))
    ]
    for copy in copies:
        copy.start()
    for copy in copies:
        copy.wait()
    lane = iota((1, cols), 1)
    off = off_ref[0, 0]
    note = jnp.where(lane == 0, off // B, jnp.where(lane == 1, off % B, live_ref[0, 0])).astype(F32)
    block = note_ref[0:B, :].astype(F32)
    note_ref[0:B, :] = jnp.where(iota((B, cols), 0) == 0, note, block).astype(BF16)
    msg_ref[...] = note_ref[0:edge, :]
    head_ref[...] = note_ref[edge:, :]


def first_kernel(
    note_ref, t_hbm, sci_hbm, bank_ref, index_ref, coeff_ref, psf_ref,
    w_ref, pcol_ref, prow_ref, sci_ref, m_ref, edge_ref, filt_ref,
    t_ref, sems, src, xs, sci, diff,
):
    copies = [
        pltpu.make_async_copy(t_hbm, t_ref, sems.at[0]), pltpu.make_async_copy(sci_hbm, sci_ref, sems.at[1])
    ]
    for copy in copies:
        copy.start()
    profs, taps = bank_ref.shape
    half = taps // 2
    delta = B - half
    bank = bank_ref[...]
    index = index_ref[0].astype(F32)
    labels = iota((index.shape[1], profs), 1).astype(F32)
    pick_row = (column(index[0:1]) == labels).astype(F32).astype(BF16)
    pick_col = (column(index[1:2]) == labels).astype(F32).astype(BF16)
    weight = column(coeff_ref[...])
    rowprof = (weight * jnp.dot(pick_row, bank, preferred_element_type=F32)).astype(BF16)
    colprof = jnp.dot(pick_col, bank, preferred_element_type=F32).astype(BF16)
    span = 3 * B
    total = 4 * B * B
    place = (iota((span, taps), 0) - delta == iota((span, taps), 1)).astype(F32).astype(BF16)
    col_t = lax.dot_general(place, colprof, (((1,), (1,)), ((), ())), preferred_element_type=F32).astype(BF16)
    spread = (span - 1 - iota((taps, total), 1) // B - delta == iota((taps, total), 0)).astype(F32).astype(BF16)
    row_rep = jnp.dot(rowprof, spread, preferred_element_type=F32).astype(BF16)
    z = jnp.dot(col_t, row_rep, preferred_element_type=F32)
    lane = iota((span, total), 1)
    for bit in (1, 2, 4, 8):
        z = jnp.where((lane & bit) != 0, pltpu.roll(z, bit, 0), z)
    z = z.astype(BF16)
    for phase in range(GROUPS):
        zp = z if phase == 0 else pltpu.roll(z, total - phase * B, 1)
        for g in range(span):
            start = span - 1 - g
            if start % GROUPS != phase:
                continue
            at = (start // GROUPS) * LANES
            for qc in range(3):
                row = (g // B) * 3 * CH + qc * CH + (g % B) * B
                w_ref[row : row + B, :] = zp[qc * B : (qc + 1) * B, at : at + CH]
    size = pcol_ref.shape[0]
    lanes = iota((taps, 3 * LANES), 1)
    mirror = (lanes - LANES + iota(lanes.shape, 0) == half).astype(F32).astype(BF16)
    bands = slanted(jnp.dot(psf_ref[...], mirror, preferred_element_type=F32), LANES)
    bands = {1 - n: bands[:, n * LANES : (n + 1) * LANES].astype(BF16) for n in range(3)}
    for i in range(size // LANES):
        for j in range(size // LANES):
            block = bands.get(i - j, jnp.zeros((LANES, LANES), BF16))
            pcol_ref[i * LANES : (i + 1) * LANES, j * LANES : (j + 1) * LANES] = block
    share, depth = prow_ref.shape
    lanes = iota((taps, depth), 1)
    ahead = (lanes - iota(lanes.shape, 0) == delta).astype(F32).astype(BF16)
    prow_ref[...] = slanted(jnp.dot(psf_ref[...], ahead, preferred_element_type=F32), share).astype(BF16)
    copies[0].wait()
    edge = 2 * B
    rows, cols = t_ref.shape
    off, _ = read_note(note_ref)
    to_blocks(src, 0, t_ref[...])
    conv_blocks(src, rows // B, w_ref, xs, m_ref)
    copies[1].wait()
    to_chunks(sci, rows, sci_ref[...])
    filter_inner(sci, rows - B - off, off, off + rows, m_ref, pcol_ref, edge_ref, filt_ref, diff)


def to_chunks(dst, dst_row, value):
    value = value.astype(F32)
    rows = value.shape[0]
    for c in range(dst.shape[0]):
        dst[c, dst_row : dst_row + rows, :] = value[:, c * LANES : (c + 1) * LANES]


def tile_diff(sky, m, base, first, last):
    row = iota(m.shape, 0) + (base - B)
    return jnp.where((row >= first) & (row < last), sky - m, 0.0).astype(BF16)


def filter_inner(sci, start, first, last, m_ref, pcol_ref, edge_ref, filt_ref, diff):
    chunks, blocks = m_ref.shape[0], m_ref.shape[1] // PITCH
    rows, edge = blocks * B, 2 * B
    for c in range(chunks):
        part = slice(c * LANES, (c + 1) * LANES)
        sky = sci[c, pl.ds(start, rows + edge), :]
        inner = jnp.concatenate([m_ref[c, PITCH * a : PITCH * a + B, :] for a in range(1, blocks - 1)], axis=0)
        edge_ref[c, 0:edge, :] = sky[0:edge]
        edge_ref[c, edge:, :] = sky[rows:]
        diff[:, part] = tile_diff(sky[edge:rows], inner, edge, first, last)
    filt_ref[...] = jnp.dot(diff[...], pcol_ref[...], preferred_element_type=F32).astype(BF16)


def read_note(msg_ref):
    note = msg_ref[0:B, 0:LANES].astype(F32)
    return (note[0, 0] * B + note[0, 1]).astype(jnp.int32), note[0, 2]


def read_before(msg_ref):
    valid = lax.axis_index("patch") > 0
    off, live = read_note(msg_ref)
    return jnp.where(valid, off, 0), jnp.where(valid, live, 0.0), valid


def join_kernel(
    note_ref, msg_ref, head_ref, sci_ref, m1_ref, w_ref, pcol_ref, prow_ref, edge_a, filt_a,
    *rest,
):
    *outs, mark_ref, m_ref, src, xs, strip, diff, filt, sci, inner, edge_b, filt_b = rest
    edge = 2 * B
    rows, cols = filt_a.shape[0] + edge, filt_a.shape[1]
    off_b, live_b, valid = read_before(msg_ref)
    to_chunks(sci, 0, sci_ref[...])
    to_blocks(src, 0, jnp.where(valid, msg_ref[...].astype(F32), 0.0))
    to_blocks(src, 2, note_ref[edge:, :])
    to_blocks(src, 4, note_ref[0:edge, :])
    to_blocks(src, 6, head_ref[...])
    filter_inner(sci, rows - B - off_b, off_b - rows, off_b, m1_ref, pcol_ref, edge_b, filt_b, inner)
    conv_blocks(src, 8, w_ref, xs, strip)
    for n, a in enumerate((1, 2, 5, 6)):
        m_ref[:, B * n : B * (n + 1), :] = strip[:, PITCH * a : PITCH * a + B, :]
    off_a, live_a = read_note(note_ref)
    for s, (side, first, last) in enumerate(((edge_a, off_a, off_a + rows), (edge_b, off_b - rows, off_b))):
        for c in range(cols // LANES):
            part = slice(c * LANES, (c + 1) * LANES)
            for k, base in enumerate((0, rows)):
                span = slice(k * edge, (k + 1) * edge)
                at = (2 * s + k) * edge
                diff[at : at + edge, part] = tile_diff(side[c, span, :], m_ref[c, span, :], base, first, last)
    sides = jnp.dot(diff[...], pcol_ref[...], preferred_element_type=F32).astype(BF16)
    for s, inner in enumerate((filt_a, filt_b)):
        filt[s, 0:edge, :] = sides[2 * s * edge : (2 * s + 1) * edge]
        filt[s, edge:rows, :] = inner[...]
        filt[s, rows : rows + edge, :] = sides[(2 * s + 1) * edge : (2 * s + 2) * edge]
        filt[s, rows + edge :, :] = jnp.zeros((filt.shape[1] - rows - edge, cols), BF16)
    share, depth = prow_ref.shape
    prow = prow_ref[...].astype(F32)
    out_row = iota((share, depth), 0)
    from_a = jnp.where(live_a > 0.5, off_a, 2 * rows)
    until_b = jnp.where(live_b > 0.5, off_b, 0)
    lane = iota((B, cols), 1)
    visits, bands = lax.axis_size("visit"), lax.axis_size("band")
    hi, lo = off_b // B, off_b % B
    marks = note_ref[0:B, 0:LANES].astype(F32)
    marks = jnp.where(iota(marks.shape, 1) == 3, hi.astype(F32), marks)
    marks = jnp.where(iota(marks.shape, 1) == 4, lo.astype(F32), marks)
    marks = jnp.where(iota(marks.shape, 1) == 5, live_b, marks)
    mark_ref[...] = marks.astype(BF16)
    for j, out_ref in enumerate(outs):
        for k in range(visits):
            to_visit = partner(lax.axis_index("visit"), k, visits)
            base = (to_visit * bands + partner(lax.axis_index("band"), j, bands)) * share
            row = out_row + base
            left = jnp.where(row >= from_a, prow, 0.0).astype(BF16)
            right = jnp.where(row < until_b, prow, 0.0).astype(BF16)
            span = pl.ds(pl.multiple_of(base, B), depth)
            total = jnp.dot(left, filt[0, span, :], preferred_element_type=F32)
            total += jnp.dot(right, filt[1, span, :], preferred_element_type=F32)
            out_ref[k * share : (k + 1) * share, :] = total.astype(out_ref.dtype)
        if j:
            out_ref[visits * share :, 0:LANES] = marks.astype(BF16)
            out_ref[visits * share :, LANES:] = jnp.zeros((B, cols - LANES), BF16)


def pair_kernel(*refs):
    bands = lax.axis_size("band")
    visits = lax.axis_size("visit")
    mark_ref, keep_ref, *got = refs[: bands + 1]
    *outs, own_mark_ref = refs[bands + 1 :]
    share, cols = outs[0].shape
    rowid = iota((B, LANES), 0)
    marks = jnp.where(rowid == 0, mark_ref[...].astype(F32), 0.0)
    for n, ref in enumerate(got):
        other = ref[visits * share :, 0:LANES].astype(F32)
        marks = jnp.where(rowid == n + 1, other[0:1, :], marks)
    own_mark_ref[...] = marks.astype(BF16)
    for k, out_ref in enumerate(outs):
        span = slice(k * share, (k + 1) * share)
        total = keep_ref[span, :]
        for ref in got:
            total += ref[span, :].astype(F32)
        out_ref[...] = total.astype(out_ref.dtype)


def tile_kernel(mark_ref, sci_ref, note_ref, m1_ref, edge_ref, w_ref, *rest):
    rows, cols = sci_ref.shape
    *halves, out_hbm, src, xs, res, big, out, sems = rest
    bands = len(halves)
    blocks = rows // B // bands
    band = lax.axis_index("band")

    def place_halves(own):
        for k in range(bands):
            to_blocks(src, partner(own, k, bands) * blocks, halves[k][...])

    for own in range(bands):
        pl.when(band == own)(functools.partial(place_halves, own))
    off, _ = read_note(note_ref)
    copies = []

    def after(c):
        big[c, 0:B, :] = edge_ref[c, B : 2 * B, :]
        for a in range(1, rows // B - 1):
            big[c, B * a : B * (a + 1), :] = m1_ref[c, PITCH * a : PITCH * a + B, :]
        big[c, rows - B : rows + B, :] = edge_ref[c, 2 * B : 4 * B, :]
        for a in range(1, rows // B):
            big[c, rows + B * a : rows + B * (a + 1), :] = res[c, PITCH * a : PITCH * a + B, :]
        part = slice(c * LANES, (c + 1) * LANES)
        out[:, part] = (sci_ref[:, part].astype(F32) - big[c, pl.ds(off, rows), :]).astype(BF16)
        there = pl.ds(c * LANES, LANES)
        copies.append(pltpu.make_async_copy(out.at[:, there], out_hbm.at[:, there], sems.at[c]))
        copies[-1].start()

    conv_blocks(src, rows // B, w_ref, xs, res, after)
    for copy in copies:
        copy.wait()


def coadd_kernel(*refs):
    *parts, out_ref = refs
    marks, parts = parts[: len(parts) // 2], parts[len(parts) // 2 :]
    share, cols = out_ref.shape
    bands = lax.axis_size("band")
    base = (lax.axis_index("visit") * bands + lax.axis_index("band")) * share
    row = (iota((share, LANES), 0) + base).astype(F32)
    cover = jnp.zeros((share, LANES), F32)
    for ref in marks:
        for m in range(bands):
            mark = ref[...].astype(F32)[m : m + 1, :]
            cover += jnp.where(row >= mark[:, 0:1] * B + mark[:, 1:2], mark[:, 2:3], 0.0)
            cover += jnp.where(row < mark[:, 3:4] * B + mark[:, 4:5], mark[:, 5:6], 0.0)
    scale = lax.rsqrt(jnp.maximum(cover, 1.0))
    for c in range(cols // LANES):
        span = slice(c * LANES, (c + 1) * LANES)
        value = parts[0][:, span]
        for part in parts[1:]:
            value += part[:, span].astype(F32)
        out_ref[:, span] = value * scale


def in_hbm(*arrays):
    return [pltpu.with_memory_space_constraint(x, pltpu.HBM) for x in arrays]


def call(body, shapes, specs, scratch, flops, name, out=VM):
    return pl.pallas_call(
        body,
        out_shape=shapes,
        in_specs=specs,
        out_specs=jax.tree.map(lambda _: out, shapes),
        scratch_shapes=scratch,
        compiler_params=pltpu.CompilerParams(vmem_limit_bytes=LIMIT * 1024 * 1024),
        cost_estimate=pl.CostEstimate(flops=flops, bytes_accessed=1 << 21, transcendentals=0),
        name=name,
    )


def on_device(template, science, offsets, live_flags, bank, basis_index, coeff, psf_profile):
    rows, cols = template.shape
    sharers = lax.axis_size("visit") * lax.axis_size("band")
    share = rows // sharers
    chunks, blocks = cols // LANES, cols // B
    edge = 2 * B
    inner = rows - edge
    sds = jax.ShapeDtypeStruct
    deep = 9 * CH
    depth = -(-(share + edge) // LANES) * LANES
    sci = science[:, 0, :]
    held = in_hbm(template, sci)
    index = jnp.swapaxes(basis_index, 1, 2)
    before = shifted(science, "patch", 1)[:, 0, :]
    bands, visits = lax.axis_size("band"), lax.axis_size("visit")
    psf = psf_profile[None]
    note, msg, head, half, *small = call(
        pack_kernel,
        (
            sds((2 * edge, cols), BF16), sds((edge, cols), BF16), sds((edge, cols), BF16),
            sds((rows // bands, cols), BF16),
            *(sds(x.shape, x.dtype) for x in (bank, index, coeff, psf)),
        ),
        [HBM] * 7,
        [pltpu.SMEM((1, 1), jnp.int32), pltpu.SMEM((1, 1), jnp.int32), pltpu.SemaphoreType.DMA((10,))],
        1 << 20, "pack",
    )(offsets, live_flags, held[0], *in_hbm(bank, index, coeff, psf))
    half = shifted(half, "patch", -1)
    panels = lax.axis_size("patch")
    msg = lax.ppermute(msg, "patch", [(i, (i + 1) % panels) for i in range(panels)])
    head = shifted(head, "patch", -1)
    count = rows // B
    conv_scratch = [
        pltpu.VMEM((chunks, count * PITCH, LANES), F32),
        pltpu.VMEM((3, blocks + 2, count, CH), BF16),
        pltpu.VMEM((chunks, count * PITCH, LANES), F32),
    ]
    conv_flops = 2 * rows * cols * deep
    sky_scratch = [pltpu.VMEM((chunks, 2 * rows + B, LANES), F32), pltpu.VMEM((inner, cols), BF16)]
    sides = (sds((chunks, 2 * edge, LANES), F32), sds((inner, cols), BF16))
    w, pcol, prow, tile, m1, edge_a, filt_a = call(
        first_kernel,
        (
            sds((deep, CH), BF16), sds((cols, cols), BF16), sds((share, depth), BF16),
            sds((rows, cols), BF16), sds((chunks, count * PITCH, LANES), F32),
        ) + sides,
        [VM, HBM, HBM] + [VM] * 4,
        [pltpu.VMEM((rows, cols), BF16), pltpu.SemaphoreType.DMA((2,))] + conv_scratch[:2] + sky_scratch,
        conv_flops, "first",
    )(note, *held, *small)
    whole = visits * share
    keep, *sent, mark, m_edge = call(
        join_kernel,
        (sds((whole, cols), F32),) + (sds((whole + B, cols), BF16),) * (bands - 1)
        + (sds((B, LANES), BF16), sds((chunks, 2 * edge, LANES), F32)),
        [VM] * 10,
        [
            pltpu.VMEM((chunks, 8 * PITCH, LANES), F32),
            pltpu.VMEM((3, blocks + 2, 8, CH), F32),
            pltpu.VMEM((chunks, 8 * PITCH, LANES), F32),
            pltpu.VMEM((4 * edge, cols), BF16),
            pltpu.VMEM((2, rows - share + depth, cols), BF16),
        ] + sky_scratch + [pltpu.VMEM((chunks, 2 * edge, LANES), F32), pltpu.VMEM((inner, cols), BF16)],
        1 << 34, "join",
    )(note, msg, head, before, m1, w, pcol, prow, edge_a, filt_a)
    got = [swapped(part, "band", k + 1) for k, part in enumerate(sent)]
    halves = [half] + [swapped(half, "band", k) for k in range(1, bands)]
    own, *sent, mark = call(
        pair_kernel,
        (sds((share, cols), F32),) + (sds((share, cols), BF16),) * (visits - 1) + (sds((B, LANES), BF16),),
        [VM] * (1 + bands), [], 1 << 20, "pair",
    )(mark, keep, *got)
    got = [swapped(part, "visit", k + 1) for k, part in enumerate(sent)]
    marks = [mark] + [swapped(mark, "visit", k) for k in range(1, visits)]
    difference = call(
        tile_kernel, sds((rows, cols), BF16), [VM] * (6 + bands),
        conv_scratch + [
            pltpu.VMEM((chunks, 2 * rows, LANES), F32), pltpu.VMEM((rows, cols), BF16),
            pltpu.SemaphoreType.DMA((chunks,)),
        ],
        conv_flops, "tile", HBM,
    )(mark, tile, note, m1, m_edge, w, *halves)
    detection = call(
        coadd_kernel, sds((share, cols), F32), [VM] * (2 * visits), [], 1 << 20, "coadd"
    )(*marks, own, *got)
    return (difference[:, None, :], detection)


def solution(mesh):
    return jax.shard_map(
        on_device,
        mesh=mesh,
        in_specs=(
            P(("group", "patch"), None),
            P(("group", "patch"), ("visit", "band"), None),
            P(("group", "patch"), ("visit", "band")),
            P(("group", "patch"), ("visit", "band")),
            P(),
            P(("group", "visit", "band"), None, None),
            P(("group", "visit", "band"), None),
            P(),
        ),
        out_specs=(
            P(("group", "patch"), ("visit", "band"), None),
            P(("group", "patch", "visit", "band"), None),
        ),
        check_vma=False,
    )
```

```python
import functools

import jax
import jax.numpy as jnp
from jax import lax
from jax.experimental import pallas as pl
from jax.experimental.pallas import tpu as pltpu
from jax.sharding import PartitionSpec as P

B = 16
CH = B * B
LANES = 128
GROUPS = LANES // B
PITCH = B + 1
F32 = jnp.float32
BF16 = jnp.bfloat16


def shifted(shard, axis, by):
    devices = lax.axis_size(axis)
    pairs = [(i, i + by) for i in range(devices) if 0 <= i + by < devices]
    return lax.ppermute(shard, axis, pairs)


def partner(me, k, count):
    return me ^ k if count & (count - 1) == 0 else (me + k) % count


def swapped(shard, axis, k):
    devices = lax.axis_size(axis)
    return lax.ppermute(shard, axis, [(i, partner(i, k, devices)) for i in range(devices)])


def iota(shape, dim):
    return lax.broadcasted_iota(jnp.int32, shape, dim)


LIMIT = 14
VM = pl.BlockSpec(memory_space=pltpu.VMEM)
HBM = pl.BlockSpec(memory_space=pltpu.HBM)


def group_transpose(parts):
    parts = list(parts)
    group = iota(parts[0].shape, 1) // B
    for step in (1, 2, 4):
        low = (group & step) == 0
        for m in range(GROUPS):
            if m & step:
                continue
            x, y = parts[m], parts[m + step]
            parts[m] = jnp.where(low, x, pltpu.roll(y, step * B, 1))
            parts[m + step] = jnp.where(low, pltpu.roll(x, LANES - step * B, 1), y)
    return parts


def to_blocks(dst, block, value):
    value = value.astype(F32)
    for a in range(value.shape[0] // B):
        at = (block + a) * PITCH
        for c in range(dst.shape[0]):
            dst[c, at : at + B, :] = value[a * B : (a + 1) * B, c * LANES : (c + 1) * LANES]


def conv_blocks(src, count, w_ref, xs, dst, after=None):
    chunks = src.shape[0]
    blocks = chunks * GROUPS

    def load(c):
        for h in range(2):
            rows = [src[c, pl.ds(GROUPS * h + i, count, stride=PITCH), :] for i in range(GROUPS)]
            part = slice(h * LANES, (h + 1) * LANES)
            for g, here in enumerate(group_transpose(rows)):
                at = 1 + c * GROUPS + g
                xs[0, at, :, part] = pltpu.roll(here, 1, 0).astype(xs.dtype)
                xs[1, at, :, part] = here.astype(xs.dtype)
                xs[2, at, :, part] = pltpu.roll(here, count - 1, 0).astype(xs.dtype)

    def solve(c):
        b = c * GROUPS
        pieces = [
            xs[qr, b + qc : b + qc + GROUPS].reshape(GROUPS * count, CH).astype(BF16)
            for qr in range(3)
            for qc in range(3)
        ]
        out = jnp.dot(jnp.concatenate(pieces, axis=1), w_ref[...], preferred_element_type=F32)
        for h in range(2):
            part = slice(h * LANES, (h + 1) * LANES)
            rows = group_transpose([out[g * count : (g + 1) * count, part] for g in range(GROUPS)])
            for i in range(GROUPS):
                dst[c, pl.ds(GROUPS * h + i, count, stride=PITCH), :] = rows[i]

    for q in range(3):
        xs[q, 0] = jnp.zeros((count, CH), xs.dtype)
        xs[q, blocks + 1] = jnp.zeros((count, CH), xs.dtype)
    load(0)
    for c in range(chunks):
        if c + 1 < chunks:
            load(c + 1)
        solve(c)
        if after is not None:
            after(c)


def slanted(row, count):
    value = jnp.broadcast_to(row, (count, row.shape[1]))
    index = iota(value.shape, 0)
    bit = 1
    while bit < count:
        value = jnp.where((index & bit) != 0, pltpu.roll(value, bit, 1), value)
        bit *= 2
    return value


def column(row):
    size = row.shape[1]
    diag = iota((size, size), 0) == iota((size, size), 1)
    return jnp.sum(jnp.where(diag, row, jnp.zeros_like(row)), axis=1, keepdims=True)


def pack_kernel(
    off_hbm, live_hbm, t_hbm, bank_hbm, index_hbm, coeff_hbm, psf_hbm,
    note_ref, msg_ref, head_ref, half_ref, bank_ref, index_ref, coeff_ref, psf_ref, off_ref, live_ref, sems,
):
    rows, cols = t_hbm.shape
    edge = 2 * B
    piece = half_ref.shape[0]
    begin = pl.multiple_of(lax.axis_index("band") * piece, B)
    copies = [
        pltpu.make_async_copy(a, b, sems.at[n])
        for n, (a, b) in enumerate((
            (off_hbm, off_ref), (live_hbm, live_ref),
            (t_hbm.at[pl.ds(rows - edge, edge)], note_ref.at[pl.ds(0, edge)]),
            (t_hbm.at[pl.ds(0, edge)], note_ref.at[pl.ds(edge, edge)]),
            (t_hbm.at[pl.ds(begin, piece)], half_ref),
            (bank_hbm, bank_ref), (index_hbm, index_ref), (coeff_hbm, coeff_ref), (psf_hbm, psf_ref),
        ))
    ]
    for copy in copies:
        copy.start()
    for copy in copies:
        copy.wait()
    lane = iota((1, cols), 1)
    off = off_ref[0, 0]
    note = jnp.where(lane == 0, off // B, jnp.where(lane == 1, off % B, live_ref[0, 0])).astype(F32)
    block = note_ref[0:B, :].astype(F32)
    note_ref[0:B, :] = jnp.where(iota((B, cols), 0) == 0, note, block).astype(BF16)
    msg_ref[...] = note_ref[0:edge, :]
    head_ref[...] = note_ref[edge:, :]


def first_kernel(
    note_ref, t_hbm, sci_hbm, bank_ref, index_ref, coeff_ref, psf_ref,
    w_ref, pcol_ref, prow_ref, sci_ref, m_ref, edge_ref, filt_ref,
    t_ref, sems, src, xs, sci, diff,
):
    copies = [
        pltpu.make_async_copy(t_hbm, t_ref, sems.at[0]), pltpu.make_async_copy(sci_hbm, sci_ref, sems.at[1])
    ]
    for copy in copies:
        copy.start()
    profs, taps = bank_ref.shape
    half = taps // 2
    delta = B - half
    bank = bank_ref[...]
    index = index_ref[0].astype(F32)
    labels = iota((index.shape[1], profs), 1).astype(F32)
    pick_row = (column(index[0:1]) == labels).astype(F32).astype(BF16)
    pick_col = (column(index[1:2]) == labels).astype(F32).astype(BF16)
    weight = column(coeff_ref[...])
    rowprof = (weight * jnp.dot(pick_row, bank, preferred_element_type=F32)).astype(BF16)
    colprof = jnp.dot(pick_col, bank, preferred_element_type=F32).astype(BF16)
    span = 3 * B
    total = 4 * B * B
    place = (iota((span, taps), 0) - delta == iota((span, taps), 1)).astype(F32).astype(BF16)
    col_t = lax.dot_general(place, colprof, (((1,), (1,)), ((), ())), preferred_element_type=F32).astype(BF16)
    spread = (span - 1 - iota((taps, total), 1) // B - delta == iota((taps, total), 0)).astype(F32).astype(BF16)
    row_rep = jnp.dot(rowprof, spread, preferred_element_type=F32).astype(BF16)
    z = jnp.dot(col_t, row_rep, preferred_element_type=F32)
    lane = iota((span, total), 1)
    for bit in (1, 2, 4, 8):
        z = jnp.where((lane & bit) != 0, pltpu.roll(z, bit, 0), z)
    z = z.astype(BF16)
    for phase in range(GROUPS):
        zp = z if phase == 0 else pltpu.roll(z, total - phase * B, 1)
        for g in range(span):
            start = span - 1 - g
            if start % GROUPS != phase:
                continue
            at = (start // GROUPS) * LANES
            for qc in range(3):
                row = (g // B) * 3 * CH + qc * CH + (g % B) * B
                w_ref[row : row + B, :] = zp[qc * B : (qc + 1) * B, at : at + CH]
    size = pcol_ref.shape[0]
    lanes = iota((taps, 3 * LANES), 1)
    mirror = (lanes - LANES + iota(lanes.shape, 0) == half).astype(F32).astype(BF16)
    bands = slanted(jnp.dot(psf_ref[...], mirror, preferred_element_type=F32), LANES)
    bands = {1 - n: bands[:, n * LANES : (n + 1) * LANES].astype(BF16) for n in range(3)}
    for i in range(size // LANES):
        for j in range(size // LANES):
            block = bands.get(i - j, jnp.zeros((LANES, LANES), BF16))
            pcol_ref[i * LANES : (i + 1) * LANES, j * LANES : (j + 1) * LANES] = block
    share, depth = prow_ref.shape
    lanes = iota((taps, depth), 1)
    ahead = (lanes - iota(lanes.shape, 0) == delta).astype(F32).astype(BF16)
    prow_ref[...] = slanted(jnp.dot(psf_ref[...], ahead, preferred_element_type=F32), share).astype(BF16)
    copies[0].wait()
    edge = 2 * B
    rows, cols = t_ref.shape
    off, _ = read_note(note_ref)
    to_blocks(src, 0, t_ref[...])
    conv_blocks(src, rows // B, w_ref, xs, m_ref)
    copies[1].wait()
    to_chunks(sci, rows, sci_ref[...])
    filter_inner(sci, rows - B - off, off, off + rows, m_ref, pcol_ref, edge_ref, filt_ref, diff)


def to_chunks(dst, dst_row, value):
    value = value.astype(F32)
    rows = value.shape[0]
    for c in range(dst.shape[0]):
        dst[c, dst_row : dst_row + rows, :] = value[:, c * LANES : (c + 1) * LANES]


def tile_diff(sky, m, base, first, last):
    row = iota(m.shape, 0) + (base - B)
    return jnp.where((row >= first) & (row < last), sky - m, 0.0).astype(BF16)


def filter_inner(sci, start, first, last, m_ref, pcol_ref, edge_ref, filt_ref, diff):
    chunks, blocks = m_ref.shape[0], m_ref.shape[1] // PITCH
    rows, edge = blocks * B, 2 * B
    for c in range(chunks):
        part = slice(c * LANES, (c + 1) * LANES)
        sky = sci[c, pl.ds(start, rows + edge), :]
        inner = jnp.concatenate([m_ref[c, PITCH * a : PITCH * a + B, :] for a in range(1, blocks - 1)], axis=0)
        edge_ref[c, 0:edge, :] = sky[0:edge]
        edge_ref[c, edge:, :] = sky[rows:]
        diff[:, part] = tile_diff(sky[edge:rows], inner, edge, first, last)
    filt_ref[...] = jnp.dot(diff[...], pcol_ref[...], preferred_element_type=F32).astype(BF16)


def read_note(msg_ref):
    note = msg_ref[0:B, 0:LANES].astype(F32)
    return (note[0, 0] * B + note[0, 1]).astype(jnp.int32), note[0, 2]


def read_before(msg_ref):
    valid = lax.axis_index("patch") > 0
    off, live = read_note(msg_ref)
    return jnp.where(valid, off, 0), jnp.where(valid, live, 0.0), valid


def join_kernel(
    note_ref, msg_ref, head_ref, sci_ref, m1_ref, w_ref, pcol_ref, prow_ref, edge_a, filt_a,
    *rest,
):
    *outs, mark_ref, m_ref, src, xs, strip, diff, filt, sci, inner, edge_b, filt_b = rest
    edge = 2 * B
    rows, cols = filt_a.shape[0] + edge, filt_a.shape[1]
    off_b, live_b, valid = read_before(msg_ref)
    to_chunks(sci, 0, sci_ref[...])
    to_blocks(src, 0, jnp.where(valid, msg_ref[...].astype(F32), 0.0))
    to_blocks(src, 2, note_ref[edge:, :])
    to_blocks(src, 4, note_ref[0:edge, :])
    to_blocks(src, 6, head_ref[...])
    conv_blocks(src, 8, w_ref, xs, strip)
    filter_inner(sci, rows - B - off_b, off_b - rows, off_b, m1_ref, pcol_ref, edge_b, filt_b, inner)
    for n, a in enumerate((1, 2, 5, 6)):
        m_ref[:, B * n : B * (n + 1), :] = strip[:, PITCH * a : PITCH * a + B, :]
    off_a, live_a = read_note(note_ref)
    for s, (side, first, last) in enumerate(((edge_a, off_a, off_a + rows), (edge_b, off_b - rows, off_b))):
        for c in range(cols // LANES):
            part = slice(c * LANES, (c + 1) * LANES)
            for k, base in enumerate((0, rows)):
                span = slice(k * edge, (k + 1) * edge)
                at = (2 * s + k) * edge
                diff[at : at + edge, part] = tile_diff(side[c, span, :], m_ref[c, span, :], base, first, last)
    sides = jnp.dot(diff[...], pcol_ref[...], preferred_element_type=F32).astype(BF16)
    for s, inner in enumerate((filt_a, filt_b)):
        filt[s, 0:edge, :] = sides[2 * s * edge : (2 * s + 1) * edge]
        filt[s, edge:rows, :] = inner[...]
        filt[s, rows : rows + edge, :] = sides[(2 * s + 1) * edge : (2 * s + 2) * edge]
        filt[s, rows + edge :, :] = jnp.zeros((filt.shape[1] - rows - edge, cols), BF16)
    share, depth = prow_ref.shape
    prow = prow_ref[...].astype(F32)
    out_row = iota((share, depth), 0)
    from_a = jnp.where(live_a > 0.5, off_a, 2 * rows)
    until_b = jnp.where(live_b > 0.5, off_b, 0)
    lane = iota((B, cols), 1)
    visits, bands = lax.axis_size("visit"), lax.axis_size("band")
    hi, lo = off_b // B, off_b % B
    marks = note_ref[0:B, 0:LANES].astype(F32)
    marks = jnp.where(iota(marks.shape, 1) == 3, hi.astype(F32), marks)
    marks = jnp.where(iota(marks.shape, 1) == 4, lo.astype(F32), marks)
    marks = jnp.where(iota(marks.shape, 1) == 5, live_b, marks)
    mark_ref[...] = marks.astype(BF16)
    for j, out_ref in enumerate(outs):
        for k in range(visits):
            to_visit = partner(lax.axis_index("visit"), k, visits)
            base = (to_visit * bands + partner(lax.axis_index("band"), j, bands)) * share
            row = out_row + base
            left = jnp.where(row >= from_a, prow, 0.0).astype(BF16)
            right = jnp.where(row < until_b, prow, 0.0).astype(BF16)
            span = pl.ds(pl.multiple_of(base, B), depth)
            total = jnp.dot(left, filt[0, span, :], preferred_element_type=F32)
            total += jnp.dot(right, filt[1, span, :], preferred_element_type=F32)
            out_ref[k * share : (k + 1) * share, :] = total.astype(out_ref.dtype)
        if j:
            out_ref[visits * share :, 0:LANES] = marks.astype(BF16)
            out_ref[visits * share :, LANES:] = jnp.zeros((B, cols - LANES), BF16)


def pair_kernel(*refs):
    bands = lax.axis_size("band")
    visits = lax.axis_size("visit")
    mark_ref, keep_ref, *got = refs[: bands + 1]
    *outs, own_mark_ref = refs[bands + 1 :]
    share, cols = outs[0].shape
    rowid = iota((B, LANES), 0)
    marks = jnp.where(rowid == 0, mark_ref[...].astype(F32), 0.0)
    for n, ref in enumerate(got):
        other = ref[visits * share :, 0:LANES].astype(F32)
        marks = jnp.where(rowid == n + 1, other[0:1, :], marks)
    own_mark_ref[...] = marks.astype(BF16)
    for k, out_ref in enumerate(outs):
        span = slice(k * share, (k + 1) * share)
        total = keep_ref[span, :]
        for ref in got:
            total += ref[span, :].astype(F32)
        out_ref[...] = total.astype(out_ref.dtype)


def tile_kernel(mark_ref, sci_ref, note_ref, m1_ref, edge_ref, w_ref, *rest):
    rows, cols = sci_ref.shape
    *halves, out_hbm, src, xs, res, big, out, sems = rest
    bands = len(halves)
    blocks = rows // B // bands
    band = lax.axis_index("band")

    def place_halves(own):
        for k in range(bands):
            to_blocks(src, partner(own, k, bands) * blocks, halves[k][...])

    for own in range(bands):
        pl.when(band == own)(functools.partial(place_halves, own))
    off, _ = read_note(note_ref)
    copies = []

    def after(c):
        big[c, 0:B, :] = edge_ref[c, B : 2 * B, :]
        for a in range(1, rows // B - 1):
            big[c, B * a : B * (a + 1), :] = m1_ref[c, PITCH * a : PITCH * a + B, :]
        big[c, rows - B : rows + B, :] = edge_ref[c, 2 * B : 4 * B, :]
        for a in range(1, rows // B):
            big[c, rows + B * a : rows + B * (a + 1), :] = res[c, PITCH * a : PITCH * a + B, :]
        part = slice(c * LANES, (c + 1) * LANES)
        out[:, part] = (sci_ref[:, part].astype(F32) - big[c, pl.ds(off, rows), :]).astype(BF16)
        there = pl.ds(c * LANES, LANES)
        copies.append(pltpu.make_async_copy(out.at[:, there], out_hbm.at[:, there], sems.at[c]))
        copies[-1].start()

    conv_blocks(src, rows // B, w_ref, xs, res, after)
    for copy in copies:
        copy.wait()


def coadd_kernel(*refs):
    *parts, out_ref = refs
    marks, parts = parts[: len(parts) // 2], parts[len(parts) // 2 :]
    share, cols = out_ref.shape
    bands = lax.axis_size("band")
    base = (lax.axis_index("visit") * bands + lax.axis_index("band")) * share
    row = (iota((share, LANES), 0) + base).astype(F32)
    cover = jnp.zeros((share, LANES), F32)
    for ref in marks:
        for m in range(bands):
            mark = ref[...].astype(F32)[m : m + 1, :]
            cover += jnp.where(row >= mark[:, 0:1] * B + mark[:, 1:2], mark[:, 2:3], 0.0)
            cover += jnp.where(row < mark[:, 3:4] * B + mark[:, 4:5], mark[:, 5:6], 0.0)
    scale = lax.rsqrt(jnp.maximum(cover, 1.0))
    for c in range(cols // LANES):
        span = slice(c * LANES, (c + 1) * LANES)
        value = parts[0][:, span]
        for part in parts[1:]:
            value += part[:, span].astype(F32)
        out_ref[:, span] = value * scale


def in_hbm(*arrays):
    return [pltpu.with_memory_space_constraint(x, pltpu.HBM) for x in arrays]


def call(body, shapes, specs, scratch, flops, name, out=VM):
    return pl.pallas_call(
        body,
        out_shape=shapes,
        in_specs=specs,
        out_specs=jax.tree.map(lambda _: out, shapes),
        scratch_shapes=scratch,
        compiler_params=pltpu.CompilerParams(vmem_limit_bytes=LIMIT * 1024 * 1024),
        cost_estimate=pl.CostEstimate(flops=flops, bytes_accessed=1 << 21, transcendentals=0),
        name=name,
    )


def on_device(template, science, offsets, live_flags, bank, basis_index, coeff, psf_profile):
    rows, cols = template.shape
    sharers = lax.axis_size("visit") * lax.axis_size("band")
    share = rows // sharers
    chunks, blocks = cols // LANES, cols // B
    edge = 2 * B
    inner = rows - edge
    sds = jax.ShapeDtypeStruct
    deep = 9 * CH
    depth = -(-(share + edge) // LANES) * LANES
    sci = science[:, 0, :]
    held = in_hbm(template, sci)
    index = jnp.swapaxes(basis_index, 1, 2)
    before = shifted(science, "patch", 1)[:, 0, :]
    bands, visits = lax.axis_size("band"), lax.axis_size("visit")
    psf = psf_profile[None]
    note, msg, head, half, *small = call(
        pack_kernel,
        (
            sds((2 * edge, cols), BF16), sds((edge, cols), BF16), sds((edge, cols), BF16),
            sds((rows // bands, cols), BF16),
            *(sds(x.shape, x.dtype) for x in (bank, index, coeff, psf)),
        ),
        [HBM] * 7,
        [pltpu.SMEM((1, 1), jnp.int32), pltpu.SMEM((1, 1), jnp.int32), pltpu.SemaphoreType.DMA((10,))],
        1 << 20, "pack",
    )(offsets, live_flags, held[0], *in_hbm(bank, index, coeff, psf))
    half = shifted(half, "patch", -1)
    panels = lax.axis_size("patch")
    msg = lax.ppermute(msg, "patch", [(i, (i + 1) % panels) for i in range(panels)])
    head = shifted(head, "patch", -1)
    count = rows // B
    conv_scratch = [
        pltpu.VMEM((chunks, count * PITCH, LANES), F32),
        pltpu.VMEM((3, blocks + 2, count, CH), BF16),
        pltpu.VMEM((chunks, count * PITCH, LANES), F32),
    ]
    conv_flops = 2 * rows * cols * deep
    sky_scratch = [pltpu.VMEM((chunks, 2 * rows + B, LANES), F32), pltpu.VMEM((inner, cols), BF16)]
    sides = (sds((chunks, 2 * edge, LANES), F32), sds((inner, cols), BF16))
    w, pcol, prow, tile, m1, edge_a, filt_a = call(
        first_kernel,
        (
            sds((deep, CH), BF16), sds((cols, cols), BF16), sds((share, depth), BF16),
            sds((rows, cols), BF16), sds((chunks, count * PITCH, LANES), F32),
        ) + sides,
        [VM, HBM, HBM] + [VM] * 4,
        [pltpu.VMEM((rows, cols), BF16), pltpu.SemaphoreType.DMA((2,))] + conv_scratch[:2] + sky_scratch,
        conv_flops, "first",
    )(note, *held, *small)
    whole = visits * share
    keep, *sent, mark, m_edge = call(
        join_kernel,
        (sds((whole, cols), F32),) + (sds((whole + B, cols), BF16),) * (bands - 1)
        + (sds((B, LANES), BF16), sds((chunks, 2 * edge, LANES), F32)),
        [VM] * 10,
        [
            pltpu.VMEM((chunks, 8 * PITCH, LANES), F32),
            pltpu.VMEM((3, blocks + 2, 8, CH), F32),
            pltpu.VMEM((chunks, 8 * PITCH, LANES), F32),
            pltpu.VMEM((4 * edge, cols), BF16),
            pltpu.VMEM((2, rows - share + depth, cols), BF16),
        ] + sky_scratch + [pltpu.VMEM((chunks, 2 * edge, LANES), F32), pltpu.VMEM((inner, cols), BF16)],
        1 << 34, "join",
    )(note, msg, head, before, m1, w, pcol, prow, edge_a, filt_a)
    got = [swapped(part, "band", k + 1) for k, part in enumerate(sent)]
    halves = [half] + [swapped(half, "band", k) for k in range(1, bands)]
    own, *sent, mark = call(
        pair_kernel,
        (sds((share, cols), F32),) + (sds((share, cols), BF16),) * (visits - 1) + (sds((B, LANES), BF16),),
        [VM] * (1 + bands), [], 1 << 20, "pair",
    )(mark, keep, *got)
    got = [swapped(part, "visit", k + 1) for k, part in enumerate(sent)]
    marks = [mark] + [swapped(mark, "visit", k) for k in range(1, visits)]
    difference = call(
        tile_kernel, sds((rows, cols), BF16), [VM] * (6 + bands),
        conv_scratch + [
            pltpu.VMEM((chunks, 2 * rows, LANES), F32), pltpu.VMEM((rows, cols), BF16),
            pltpu.SemaphoreType.DMA((chunks,)),
        ],
        conv_flops, "tile", HBM,
    )(mark, tile, note, m1, m_edge, w, *halves)
    detection = call(
        coadd_kernel, sds((share, cols), F32), [VM] * (2 * visits), [], 1 << 20, "coadd"
    )(*marks, own, *got)
    return (difference[:, None, :], detection)


def solution(mesh):
    return jax.shard_map(
        on_device,
        mesh=mesh,
        in_specs=(
            P(("group", "patch"), None),
            P(("group", "patch"), ("visit", "band"), None),
            P(("group", "patch"), ("visit", "band")),
            P(("group", "patch"), ("visit", "band")),
            P(),
            P(("group", "visit", "band"), None, None),
            P(("group", "visit", "band"), None),
            P(),
        ),
        out_specs=(
            P(("group", "patch"), ("visit", "band"), None),
            P(("group", "patch", "visit", "band"), None),
        ),
        check_vma=False,
    )
```
